32 devices in a mesh: dp: 8 (over y, x, core), tensor: 4 (over z).
Axes of the slice: x: 2, y: 2, z: 4, core: 2. Of those that a mesh axis runs over, the one named last changes fastest.
Arguments:
- tokens: bfloat16 [16384, 1024], P(('dp', 'tensor')), may hold values from -6 to 6
- doc_lengths: int32 [8, 4], P('dp'), may hold values from 1 to 2048, as said below
- qkv_weight: bfloat16 [2, 3, 1024, 1024], P(None, None, 'dp', 'tensor'), may hold values from -0.1875 to 0.1875
- qv_bias: bfloat16 [2, 2, 16, 64], P(None, None, 'tensor', 'dp'), may hold values from -3 to 3
- out_weight: bfloat16 [2, 1024, 1024], P(None, 'dp', 'tensor'), may hold values from -3 to 3
- up_weight: bfloat16 [2, 1024, 4096], P(None, 'dp', 'tensor'), may hold values from -0.1875 to 0.1875
- up_bias: bfloat16 [2, 64, 64], P(None, 'tensor', 'dp'), may hold values from -3 to 3
- down_weight: bfloat16 [2, 1024, 4096], P(None, 'dp', 'tensor'), may hold values from -0.09375 to 0.09375
- gains: bfloat16 [2, 2, 1024], P(None, None, ('dp', 'tensor')), may hold values from 0.4 to 1.8
- shifts: bfloat16 [2, 4, 1024], P(None, None, ('dp', 'tensor')), may hold values from -3 to 3
- cotangent: bfloat16 [16384, 1024], P(('dp', 'tensor')), may hold values from -6 to 6
Outputs:
- layer_output: bfloat16 [16384, 1024], P(('dp', 'tensor'))
- input_grad: bfloat16 [16384, 1024], P(('dp', 'tensor'))
- qkv_grad: float32 [2, 3, 1024, 1024], P(None, None, 'dp', 'tensor')
- qv_bias_grad: float32 [2, 2, 16, 64], P(None, None, 'tensor', 'dp')
- out_grad: float32 [2, 1024, 1024], P(None, 'dp', 'tensor')
- up_grad: float32 [2, 1024, 4096], P(None, 'dp', 'tensor')
- up_bias_grad: float32 [2, 64, 64], P(None, 'tensor', 'dp')
- down_grad: float32 [2, 1024, 4096], P(None, 'dp', 'tensor')
- gains_grad: float32 [2, 2, 1024], P(None, None, ('dp', 'tensor'))
- shifts_grad: float32 [2, 4, 1024], P(None, None, ('dp', 'tensor'))
- grad_rms: float32 [], replicated
The draws below stay inside these ranges and needn't reach their ends.
Inputs may be any that keep to these rules, and one draw needn't show every extreme that they name: `doc_lengths`: each row lists the 4 lengths of the documents packed into one sequence, in order; they sum to 2048.
All inputs are finite; a program needn't handle non-finite values.
Results may differ from the reference program's by a relative error of at most 0.035.
Values may be sent and summed in bfloat16 or wider, within the bound.
No kernel may reach another device: no remote copies, remote signals or barrier semaphores. Data moves between devices by JAX's collectives and lax.ppermute only.
A program may use at most 256 MiB of HBM per device.

```python
import jax
import jax.numpy as jnp
from jax import lax

D = 1024
HEADS = 16
HD = 64
FF = 4096
LAYERS = 2
SEQLEN = 2048
WINDOW = 1024
DOCS = 4
SEQS = 8
TOKENS = 16384


def length_row(row_key):
    first_key, second_key, third_key = jax.random.split(row_key, 3)
    longest = 3 * SEQLEN // 4 + jax.random.randint(first_key, (), 1, SEQLEN // 8 + 1, dtype=jnp.int32)
    remainder = SEQLEN - longest
    shuffled = jax.random.permutation(second_key, jnp.arange(SEQLEN, dtype=jnp.int32))
    places = jnp.arange(SEQLEN, dtype=jnp.int32)
    ranking = jnp.where(shuffled < remainder - 1, places, SEQLEN + places)
    picked = jnp.argsort(ranking)[:DOCS - 2]
    cuts = jnp.sort(shuffled[picked] + 1)
    bounds = jnp.concatenate([jnp.zeros((1,), jnp.int32), cuts.astype(jnp.int32), remainder[None].astype(jnp.int32)])
    pieces = bounds[1:] - bounds[:-1]
    chosen = jax.random.randint(third_key, (), 0, DOCS, dtype=jnp.int32)
    slots = jnp.arange(DOCS, dtype=jnp.int32)
    source = jnp.clip(jnp.where(slots < chosen, slots, slots - 1), 0, DOCS - 2)
    return jnp.where(slots == chosen, longest, pieces[source]).astype(jnp.int32)


def draw_doc_lengths(key, part):
    key = jax.random.fold_in(key, 11)
    row_keys = jax.random.split(key, SEQS)
    return jax.vmap(length_row)(row_keys)


def draw_gains(key, part):
    key = jax.random.fold_in(key, 23)
    ramp = 0.5 + jnp.arange(D, dtype=jnp.float32) / D
    factor = jax.random.uniform(key, (LAYERS, 2, D), jnp.float32, 0.8, 1.2)
    return (ramp * factor).astype(jnp.bfloat16)


def shard_levels(stream_key, dims, shards, least, top_value):
    factor_of = 1.0
    for dim, blocks in shards:
        steps = jax.random.uniform(jax.random.fold_in(jax.random.fold_in(stream_key, 6), dim), (blocks,), jnp.float32, least / len(shards), top_value / len(shards))
        factor_of = factor_of * jnp.repeat(jnp.exp(steps), dims[dim] // blocks).reshape((-1,) + (1,) * (len(dims) - 1 - dim))
    return factor_of


def normal_values(stream_key, extent, width, bound, shards=(), kind=jnp.bfloat16):
    array = jax.random.normal(stream_key, extent, jnp.float32) * width
    if len(shards) > 0:
        array = shard_levels(stream_key, extent, shards, -0.22, 0.18) * array
    return jnp.clip(array, min=-bound, max=bound).astype(kind)


def setup_inputs(seed: int = 0) -> dict:
    key_of = jax.random.split(jax.random.key(seed), 12)
    tokens = normal_values(key_of[0], (TOKENS, D), 1.0, 6.0, ((0, 32),))
    doc_lengths = draw_doc_lengths(jax.random.fold_in(key_of[11], 71), 0)
    qkv_weight = normal_values(key_of[2], (LAYERS, 3, D, D), D ** -0.5, 0.1875, ((2, 8), (3, 4)))
    qv_bias = normal_values(key_of[3], (LAYERS, 2, HEADS, HD), 0.5, 3.0, ((2, 4), (3, 8)))
    out_weight = normal_values(key_of[4], (LAYERS, D, D), (max(D // 256, 1)) ** -0.5, 3.0, ((1, 8), (2, 4)))
    up_weight = normal_values(key_of[5], (LAYERS, D, FF), D ** -0.5, 0.1875, ((1, 8), (2, 4)))
    up_bias = normal_values(key_of[6], (LAYERS, FF // HD, HD), 0.5, 3.0, ((1, 4), (2, 8)))
    down_weight = normal_values(key_of[7], (LAYERS, D, FF), FF ** -0.5, 0.09375, ((1, 8), (2, 4)))
    gains = draw_gains(jax.random.fold_in(key_of[11], 71), 0)
    shifts = normal_values(key_of[9], (LAYERS, 4, D), 0.5, 3.0, ((2, 32),))
    cotangent = normal_values(key_of[10], (TOKENS, D), 1.0, 6.0, ((0, 32),))
    return {"tokens": tokens, "doc_lengths": doc_lengths, "qkv_weight": qkv_weight, "qv_bias": qv_bias, "out_weight": out_weight, "up_weight": up_weight, "up_bias": up_bias, "down_weight": down_weight, "gains": gains, "shifts": shifts, "cotangent": cotangent}


@jax.custom_vjp
def low(v):
    return lax.optimization_barrier(v.astype(jnp.bfloat16)).astype(jnp.float32)

@jax.custom_vjp
def low_back(v):
    return v

def low_keep(v):
    return (low(v), None)

def low_pass(kept, grad):
    return (grad,)

def back_keep(v):
    return (v, None)

def back_low(kept, grad):
    return (low(grad),)
low.defvjp(low_keep, low_pass)
low_back.defvjp(back_keep, back_low)
precise = lax.Precision.HIGHEST
epsilon = 1e-06
neg_fill = -1000000000.0

def both_round(values_in):
    return low(low_back(values_in))

def norm_rows(values_in, gain_row, shift_row):
    row_mean = lax.optimization_barrier(jnp.mean(values_in, -1, keepdims=True))
    centred = values_in - row_mean
    variance = lax.optimization_barrier(jnp.mean(centred * centred, -1, keepdims=True))
    return centred * lax.rsqrt(variance + epsilon) * gain_row + shift_row

def segments(lengths):
    doc_ends = jnp.cumsum(lengths, axis=-1).astype(jnp.int32)
    places = jnp.arange(SEQLEN, dtype=jnp.int32)
    return lax.optimization_barrier(jnp.sum((places[..., :, None] >= doc_ends[..., None, :]).astype(jnp.int32), axis=-1)).astype(jnp.int32)

def attend(queries, key_rows, value_rows, segment):
    block_rows = min(512, SEQLEN)
    places = jnp.arange(SEQLEN, dtype=jnp.int32)

    def one_block(block_index):
        row_start = block_index * block_rows
        query_block = lax.dynamic_slice_in_dim(queries, row_start, block_rows, 0)
        rows_here = row_start + jnp.arange(block_rows, dtype=jnp.int32)
        seg_here = lax.dynamic_slice_in_dim(segment, row_start, block_rows, 0)
        allowed = (seg_here[:, None] == segment[None, :]) & (jnp.abs(rows_here[:, None] - places[None, :]) < WINDOW)
        scores = jnp.einsum('qhd,khd->hqk', query_block, key_rows, precision=precise) * HD ** (-0.5)
        scores = low_back(jnp.where(allowed[None], scores, neg_fill))
        row_max = lax.optimization_barrier(jnp.max(scores, -1, keepdims=True))
        exponent = jnp.exp(scores - row_max)
        probability = low(exponent / lax.optimization_barrier(jnp.sum(exponent, -1, keepdims=True)))
        return jnp.einsum('hqk,khd->qhd', probability, value_rows, precision=precise)
    blocks = lax.map(jax.checkpoint(one_block), jnp.arange(SEQLEN // block_rows, dtype=jnp.int32))
    return blocks.reshape(SEQLEN, HEADS, HD)

def layer(hidden, weights, segment):
    qkv_layer, qv_layer, out_layer, up_layer, up_bias_layer, down_layer, gain_layer, shift_layer = weights
    rounded = low(hidden)
    projected = jnp.einsum('ld,cde->cle', rounded, qkv_layer, precision=precise)
    biases = qv_layer.reshape(2, D)
    queries = both_round(projected[0] + biases[0])
    key_rows = both_round(projected[1])
    value_rows = both_round(projected[2] + biases[1])
    context = attend(queries.reshape(SEQLEN, HEADS, HD), key_rows.reshape(SEQLEN, HEADS, HD), value_rows.reshape(SEQLEN, HEADS, HD), segment)
    context = both_round(context.reshape(SEQLEN, D))
    attention = low_back(jnp.dot(context, out_layer.T, precision=precise) + shift_layer[0])
    mid_state = norm_rows(hidden + attention, gain_layer[0], shift_layer[1])
    mid_low = low(mid_state)
    pre_act = low_back(jnp.dot(mid_low, up_layer, precision=precise) + up_bias_layer.reshape(FF))
    active = low(jax.nn.gelu(pre_act, approximate=False))
    feedforward = low_back(jnp.dot(active, down_layer.T, precision=precise) + shift_layer[2])
    return norm_rows(mid_state + feedforward, gain_layer[1], shift_layer[3])

def reference(tokens, doc_lengths, qkv_weight, qv_bias, out_weight, up_weight, up_bias, down_weight, gains, shifts, cotangent):
    params = tuple((member.astype(jnp.float32) for member in (qkv_weight, qv_bias, out_weight, up_weight, up_bias, down_weight, gains, shifts)))
    inputs = tokens.astype(jnp.float32).reshape(SEQS, SEQLEN, D)
    grads_out = cotangent.astype(jnp.float32).reshape(SEQS, SEQLEN, D)

    def model(hidden, weights, segment):
        for layer_index in range(LAYERS):
            hidden = layer(hidden, tuple((member[layer_index] for member in weights)), segment)
        return hidden

    def sequence_step(totals, sequence_items):
        hidden, grad_seq, lengths = sequence_items
        segment = segments(lengths)
        output, pullback = jax.vjp(lambda first_arg, second_arg: model(first_arg, second_arg, segment), hidden, params)
        grad_hidden, grad_params = pullback(grad_seq)
        return (jax.tree.map(jnp.add, totals, grad_params), (output, grad_hidden))
    zero_grads = jax.tree.map(jnp.zeros_like, params)
    totals, (outputs, grad_inputs) = lax.scan(sequence_step, zero_grads, (inputs, grads_out, doc_lengths))
    squares = sum((jnp.sum(member * member) for member in totals))
    entry_count = sum((member.size for member in totals))
    root_mean = jnp.sqrt(squares / entry_count)
    return (outputs.reshape(TOKENS, D).astype(jnp.bfloat16), grad_inputs.reshape(TOKENS, D).astype(jnp.bfloat16), totals[0], totals[1], totals[2], totals[3], totals[4], totals[5], totals[6], totals[7], root_mean)
```

```python
import functools

import jax
import jax.numpy as jnp
from jax import lax
from jax.experimental import pallas as pl
from jax.experimental.pallas import tpu as pltpu
from jax.sharding import Mesh
from jax.sharding import PartitionSpec as P

D = 1024
HD = 64
HEADS = 16
FF = 4096
LAYERS = 2
SEQLEN = 2048
WINDOW = 1024
EPS = 1e-06
FILL = -1000000000.0

F32 = jnp.float32
BF16 = jnp.bfloat16
GROUP = ("c", "zl")
ALL = ("zh", "zl", "q", "c")
VMEM_LIMIT = 52 * 1024 * 1024
NT = (((1,), (1,)), ((), ()))
NN = (((1,), (0,)), ((), ()))


def mm(left, right, dims=NN):
    return lax.dot_general(left, right, dims, preferred_element_type=F32)


def full(shape):
    return pl.BlockSpec(shape, lambda *_: (0,) * len(shape))


def call(body, grid, in_specs, out_specs, out_shape, scratch, args, scalars=(), flops=0, traffic=0, name=None):
    return pl.pallas_call(
        body,
        grid_spec=pltpu.PrefetchScalarGridSpec(
            num_scalar_prefetch=len(scalars),
            grid=grid,
            in_specs=in_specs,
            out_specs=out_specs,
            scratch_shapes=scratch,
        ),
        out_shape=out_shape,
        compiler_params=pltpu.CompilerParams(
            dimension_semantics=("arbitrary",) * len(grid), vmem_limit_bytes=VMEM_LIMIT
        ),
        cost_estimate=pl.CostEstimate(flops=int(flops), bytes_accessed=int(traffic), transcendentals=0),
        name=name,
    )(*scalars, *args)


def sds(shape, kind):
    return jax.ShapeDtypeStruct(shape, kind)


def norm_rows(values_in):
    centred = values_in - jnp.mean(values_in, -1, keepdims=True)
    variance = jnp.mean(centred * centred, -1, keepdims=True)
    inverse = lax.rsqrt(variance + EPS)
    return centred * inverse, inverse


def norm_back_rows(grad, normed, inverse, gain):
    scaled = grad * gain
    centred = scaled - jnp.mean(scaled, -1, keepdims=True) - normed * jnp.mean(scaled * normed, -1, keepdims=True)
    return centred * inverse


def fold_rows(values_in):
    return jnp.sum(values_in.reshape(-1, 8, values_in.shape[-1]), 0)


CHUNK = 64


def norm_forward_epilogue(acc, prev, vec, n_ref, low_ref, inv_ref):
    def step(index, carry):
        rows = pl.ds(index * CHUNK, CHUNK)
        total = prev[rows, :] * vec[0:1, :] + vec[1:2, :] + (acc[rows, :] + vec[2:3, :])
        normed, inverse = norm_rows(total)
        n_ref[rows, :] = normed
        low_ref[rows, :] = (normed * vec[3:4, :] + vec[4:5, :]).astype(BF16)
        inv_ref[rows, :] = jnp.broadcast_to(inverse, (CHUNK, 128))
        return carry

    lax.fori_loop(0, acc.shape[0] // CHUNK, step, 0)


def norm_backward_epilogue(get_grad, rows_total, n_ref, inv_ref, gain_ref, g_ref, low_ref, sums_ref):
    def step(index, carry):
        rows = pl.ds(index * CHUNK, CHUNK)
        grad = get_grad(rows)
        normed = n_ref[rows, :]
        result = norm_back_rows(grad, normed, inv_ref[rows, 0:1], gain_ref[0:1, :])
        low = result.astype(BF16)
        g_ref[rows, :] = result
        low_ref[rows, :] = low
        return (
            carry[0] + fold_rows(grad * normed),
            carry[1] + fold_rows(grad),
            carry[2] + fold_rows(low.astype(F32)),
        )

    zero = jnp.zeros((8, D), F32)
    sums = lax.fori_loop(0, rows_total // CHUNK, step, (zero, zero, zero))
    sums_ref[...] = jnp.zeros(sums_ref.shape, F32)
    for row, member in enumerate(sums):
        sums_ref[row : row + 1, :] = jnp.sum(member, 0, keepdims=True)


def project_blocks(place, rows_in, weight, bias):
    count, depth, width = weight.shape
    tokens = rows_in.shape[0]

    def body(place_ref, x_ref, w_ref, *rest):
        if bias is None:
            outs = rest
        else:
            bias_ref, outs = rest[0], rest[1:]
        step = pl.program_id(0)
        value = mm(x_ref[...], w_ref[0])
        if bias is not None:
            value = value + bias_ref[0]
        value = value.astype(BF16)
        for index, out in enumerate(outs):

            @pl.when(step == index)
            def _(out=out):
                out[...] = value

    pick = lambda r, place_ref: (place_ref[0] ^ r, 0, 0)
    specs = [full((tokens, depth)), pl.BlockSpec((1, depth, width), pick)]
    args = [rows_in, weight]
    if bias is not None:
        specs.append(pl.BlockSpec((1, 1, width), pick))
        args.append(bias)
    return call(
        body, (count,), specs, [full((tokens, width))] * count, [sds((tokens, width), BF16)] * count, [], args,
        (place,), 2 * tokens * depth * width * count, 2 * (count * depth * width + tokens * (depth + count * width)),
        name="project_blocks",
    )


def gelu_parts(u):
    size = jnp.abs(u)
    t = 1.0 / (1.0 + 0.2316419 * size)
    poly = t * (0.127414796 + t * (-0.142248368 + t * (0.7107068705 + t * (-0.7265760135 + t * 0.5307027145))))
    bell = jnp.exp(-0.5 * (u * u))
    tail = poly * bell
    cdf = jnp.where(u >= 0, 1.0 - tail, tail)
    return u * cdf, cdf + u * (0.3989422804014327 * bell)


def up_gelu(rows_in, weight, bias, block=512):
    count, depth, width = weight.shape
    tokens = rows_in.shape[0]
    per = width // block
    half = tokens // 2

    def body(x_ref, w_ref, b_ref, act_ref, slope_ref):
        for index in range(2):
            rows = slice(index * half, (index + 1) * half)
            act, slope = gelu_parts(mm(x_ref[rows, :], w_ref[0]) + b_ref[...])
            act_ref[rows, :] = act.astype(BF16)
            slope_ref[rows, :] = slope.astype(BF16)

    column = pl.BlockSpec((tokens, block), lambda j: (0, j))
    return call(
        body, (count * per,),
        [full((tokens, depth)), pl.BlockSpec((1, depth, block), lambda j: (j // per, 0, j % per)),
         pl.BlockSpec((1, block), lambda j: (0, j))],
        [column, column], [sds((tokens, count * width), BF16)] * 2, [], [rows_in, weight, bias], (),
        2 * tokens * depth * width * count, 2 * (count * depth * width + tokens * (depth + 2 * count * width)),
        name="up_gelu",
    )


def units_back(rows_in, weight, slope, block=512):
    count, depth, width = weight.shape
    tokens = rows_in.shape[0]
    per = width // block
    half = tokens // 2

    def body(x_ref, w_ref, s_ref, out_ref, sum_ref):
        total = jnp.zeros((8, block), F32)
        for index in range(2):
            rows = slice(index * half, (index + 1) * half)
            low = (mm(x_ref[rows, :], w_ref[0]) * s_ref[rows, :].astype(F32)).astype(BF16)
            out_ref[rows, :] = low
            total = total + fold_rows(low.astype(F32))
        sum_ref[...] = jnp.sum(total, 0, keepdims=True)

    column = pl.BlockSpec((tokens, block), lambda j: (0, j))
    return call(
        body, (count * per,),
        [full((tokens, depth)), pl.BlockSpec((1, depth, block), lambda j: (j // per, 0, j % per)), column],
        [column, pl.BlockSpec((1, block), lambda j: (0, j))],
        [sds((tokens, count * width), BF16), sds((1, count * width), F32)], [], [rows_in, weight, slope], (),
        2 * tokens * depth * width * count, 2 * (count * depth * width + tokens * (depth + 2 * count * width)),
        name="units_back",
    )


def contract_blocks(place, left, weight, extra, extra_specs, out_specs, out_shape, finish, name):
    count, depth, width = weight.shape
    listed = isinstance(left, (list, tuple))
    lefts = list(left) if listed else [left]
    tokens = lefts[0].shape[0]

    def body(place_ref, *refs):
        left_refs = refs[: len(lefts)]
        w_ref = refs[len(lefts)]
        extra_refs = refs[len(lefts) + 1 : len(lefts) + 1 + len(extra)]
        out_refs = refs[len(lefts) + 1 + len(extra) : -1]
        acc = refs[-1]
        step = pl.program_id(0)
        if listed:
            for index, left_ref in enumerate(left_refs):

                @pl.when(step == index)
                def _(left_ref=left_ref, index=index):
                    value = mm(left_ref[...], w_ref[0], NT)
                    acc[...] = value if index == 0 else acc[...] + value

        else:

            @pl.when(step == 0)
            def _():
                acc[...] = mm(left_refs[0][...], w_ref[0], NT)

            @pl.when(step != 0)
            def _():
                acc[...] += mm(left_refs[0][...], w_ref[0], NT)

        @pl.when(step == count - 1)
        def _():
            finish(acc, extra_refs, out_refs)

    if listed:
        left_specs = [full((tokens, width))] * len(lefts)
        pick = lambda r, place_ref: (place_ref[0] ^ r, 0, 0)
    else:
        left_specs = [pl.BlockSpec((tokens, width), lambda r, place_ref: (0, r))]
        pick = lambda r, place_ref: (r, 0, 0)
    return call(
        body, (count,), left_specs + [pl.BlockSpec((1, depth, width), pick)] + extra_specs, out_specs, out_shape,
        [pltpu.VMEM((tokens, depth), F32)], lefts + [weight] + extra, (place,),
        2 * tokens * depth * width * count, 2 * (count * depth * width + tokens * (4 * depth + count * width)),
        name=name,
    )


def sublayer_norm(place, left, weight, prev, vec, name):
    tokens = prev.shape[0]

    def finish(acc, extra, outs):
        norm_forward_epilogue(acc, extra[0], extra[1], outs[0], outs[1], outs[2])

    return contract_blocks(
        place, left, weight, [prev, vec], [full((tokens, D)), full((8, D))],
        [full((tokens, D)), full((tokens, D)), full((tokens, 128))],
        [sds((tokens, D), F32), sds((tokens, D), BF16), sds((tokens, 128), F32)], finish, name,
    )


def sublayer_norm_back(place, left, weight, residual, normed, inverse, gain, name):
    tokens = residual.shape[0]

    def finish(acc, extra, outs):
        norm_backward_epilogue(
            lambda rows: extra[0][rows, :] + acc[rows, :], tokens, extra[1], extra[2], extra[3], outs[0], outs[1], outs[2]
        )

    return contract_blocks(
        place, left, weight, [residual, normed, inverse, gain],
        [full((tokens, D)), full((tokens, D)), full((tokens, 128)), full((8, D))],
        [full((tokens, D)), full((tokens, D)), full((8, D))],
        [sds((tokens, D), F32), sds((tokens, D), BF16), sds((8, D), F32)], finish, name,
    )


def sublayer_back_last(place, left, weight, residual, name):
    tokens = residual.shape[0]

    def finish(acc, extra, outs):
        outs[0][...] = (extra[0][...] + acc[...]).astype(BF16)

    return contract_blocks(
        place, left, weight, [residual], [full((tokens, D))], [full((tokens, D))], [sds((tokens, D), BF16)], finish, name
    )[0]


def norm_back(grad, normed, inverse, gain):
    tokens = grad.shape[0]

    def body(grad_ref, n_ref, inv_ref, gain_ref, g_ref, low_ref, sums_ref):
        norm_backward_epilogue(
            lambda rows: grad_ref[rows, :].astype(F32), tokens, n_ref, inv_ref, gain_ref, g_ref, low_ref, sums_ref
        )

    return call(
        body, (1,), [full((tokens, D)), full((tokens, D)), full((tokens, 128)), full((8, D))],
        [full((tokens, D)), full((tokens, D)), full((8, D))],
        [sds((tokens, D), F32), sds((tokens, D), BF16), sds((8, D), F32)], [], [grad, normed, inverse, gain], (),
        20 * tokens * D, 12 * tokens * D, name="norm_back",
    )


def weight_grad(left, right, count, block=512):
    tokens, depth = left.shape
    width = right.shape[1] // count
    per = width // block

    def body(x_ref, y_ref, out_ref, turned):
        @pl.when(pl.program_id(0) == 0)
        def _():
            turned[...] = x_ref[...].T

        out_ref[0] = mm(turned[...], y_ref[...]).astype(BF16)

    return call(
        body, (count * per,), [full((tokens, depth)), pl.BlockSpec((tokens, block), lambda j: (0, j))],
        pl.BlockSpec((1, depth, block), lambda j: (j // per, 0, j % per)), sds((count, depth, width), BF16),
        [pltpu.VMEM((depth, tokens), BF16)], [left, right], (),
        2 * tokens * depth * width * count, 2 * (count * depth * width + tokens * (depth + count * width)),
        name="weight_grad",
    )


def weight_grad_blocks(place, left, rights, with_sums):
    tokens, depth = left.shape
    count = len(rights)
    width = rights[0].shape[1]

    def body(place_ref, x_ref, *refs):
        parts = refs[:count]
        if with_sums:
            out_ref, sum_ref, turned = refs[count:]
        else:
            out_ref, turned = refs[count:]
        step = pl.program_id(0)

        @pl.when(step == 0)
        def _():
            turned[...] = x_ref[...].T

        for index, part in enumerate(parts):

            @pl.when(step == index)
            def _(part=part):
                out_ref[0] = mm(turned[...], part[...]).astype(BF16)
                if with_sums:
                    sum_ref[0] = jnp.sum(part[...].astype(F32), 0, keepdims=True)

    pick = lambda r, place_ref: (place_ref[0] ^ r, 0, 0)
    out_specs = [pl.BlockSpec((1, depth, width), pick)]
    out_shape = [sds((count, depth, width), BF16)]
    if with_sums:
        out_specs.append(pl.BlockSpec((1, 1, width), pick))
        out_shape.append(sds((count, 1, width), F32))
    return call(
        body, (count,), [full((tokens, depth))] + [full((tokens, width))] * count, out_specs, out_shape,
        [pltpu.VMEM((depth, tokens), BF16)], [left] + list(rights), (place,),
        2 * tokens * depth * width * count, 2 * (count * depth * width + tokens * (depth + count * width)),
        name="weight_grad_blocks",
    )


BQ = 256


def reach(ends_ref, row):
    first = jnp.zeros_like(row)
    for index in range(3):
        first = jnp.where(row >= ends_ref[index], ends_ref[index], first)
    last = jnp.full_like(row, SEQLEN)
    for index in (2, 1, 0):
        last = jnp.where(row < ends_ref[index], ends_ref[index], last)
    return jnp.maximum(first, row - (WINDOW - 1)), jnp.minimum(last, row + WINDOW)


def block_reach(ends_ref, start):
    low_first, high_first = reach(ends_ref, start)
    low_last, high_last = reach(ends_ref, start + BQ - 1)
    return low_first, low_last, high_first, high_last


def row_reach(ends_ref, start):
    return reach(ends_ref, start + lax.broadcasted_iota(jnp.int32, (1, BQ), 1))


def attend_forward(place, ends, parts):
    count = len(parts)
    chunk, width3 = parts[0].shape
    width = width3 // 3
    heads = width // HD
    steps = SEQLEN // BQ
    per = chunk // BQ

    def body(place_ref, ends_ref, *refs):
        part_refs = refs[:count]
        ctx_refs = refs[count : 2 * count]
        wide_ref, lse_ref = refs[2 * count : 2 * count + 2]
        qh, kh, vt, acc, stat, stage = refs[2 * count + 2 :]
        step = pl.program_id(0)
        me = place_ref[0]

        @pl.when(step == 0)
        def _():
            for r in range(count):
                j = me ^ r
                rows = pl.ds(pl.multiple_of(j * chunk, chunk), chunk)
                for h in range(heads):
                    cols = slice(h * HD, (h + 1) * HD)
                    qh[h, rows, :] = part_refs[r][:, cols] * BF16(HD**-0.5)
                    kh[h, rows, :] = part_refs[r][:, width + h * HD : width + (h + 1) * HD]
                vt[j] = part_refs[r][:, 2 * width :].T

        start = step * BQ
        low_first, low_last, high_first, high_last = block_reach(ends_ref, start)
        low_row, high_row = row_reach(ends_ref, start)
        rows = pl.ds(pl.multiple_of(start, BQ), BQ)
        acc[...] = jnp.zeros(acc.shape, F32)
        stat[0:heads, :] = jnp.full((heads, BQ), -3.0e38, F32)
        stat[heads : 2 * heads, :] = jnp.zeros((heads, BQ), F32)

        def block(b, masked):
            keys = pl.ds(pl.multiple_of(b * chunk, chunk), chunk)
            if masked:
                place_of = b * chunk + lax.broadcasted_iota(jnp.int32, (chunk, BQ), 0)
                allowed = (place_of >= low_row) & (place_of < high_row)
            for h in range(heads):
                score = mm(kh[h, keys, :], qh[h, rows, :], NT)
                if masked:
                    score = jnp.where(allowed, score, FILL)
                old = stat[h : h + 1, :]
                new = jnp.maximum(old, jnp.max(score, 0, keepdims=True))
                weight = jnp.exp(score - new)
                decay = jnp.exp(old - new)
                stat[h : h + 1, :] = new
                stat[heads + h : heads + h + 1, :] = stat[heads + h : heads + h + 1, :] * decay + jnp.sum(
                    weight, 0, keepdims=True
                )
                part = slice(h * HD, (h + 1) * HD)
                acc[part, :] = acc[part, :] * decay + mm(vt[b, part, :], weight.astype(BF16))

        def one(b, carry):
            open_all = (b * chunk >= low_last) & ((b + 1) * chunk <= high_first)

            @pl.when(open_all)
            def _():
                block(b, False)

            @pl.when(jnp.logical_not(open_all))
            def _():
                block(b, True)

            return carry

        lax.fori_loop(low_first // chunk, (high_last + chunk - 1) // chunk, one, 0)
        for h in range(heads):
            part = slice(h * HD, (h + 1) * HD)
            total = stat[heads + h : heads + h + 1, :]
            wide_ref[part, :] = acc[part, :] / total
            lse_ref[h : h + 1, :] = stat[h : h + 1, :] + jnp.log(total)
        lse_ref[heads:, :] = jnp.zeros((8 - heads, BQ), F32)
        stage[step // per, pl.ds(pl.multiple_of((step % per) * BQ, BQ), BQ), :] = wide_ref[...].T.astype(BF16)

        @pl.when(step == steps - 1)
        def _():
            for r in range(count):
                ctx_refs[r][...] = stage[me ^ r]

    pairs = SEQLEN * SEQLEN
    return call(
        body, (steps,), [full((chunk, width3))] * count,
        [full((chunk, width))] * count
        + [pl.BlockSpec((width, BQ), lambda i, *_: (0, i)), pl.BlockSpec((8, BQ), lambda i, *_: (0, i))],
        [sds((chunk, width), BF16)] * count + [sds((width, SEQLEN), F32), sds((8, SEQLEN), F32)],
        [
            pltpu.VMEM((heads, SEQLEN, HD), BF16),
            pltpu.VMEM((heads, SEQLEN, HD), BF16),
            pltpu.VMEM((count, width, chunk), BF16),
            pltpu.VMEM((width, BQ), F32),
            pltpu.VMEM((2 * heads, BQ), F32),
            pltpu.VMEM((count, chunk, width), BF16),
        ],
        list(parts), (place, ends), 6 * pairs * heads * HD, 6 * SEQLEN * width * 2, name="attend_forward",
    )


def attend_backward(place, ends, parts, grads, wide, lse):
    count = len(parts)
    chunk, width3 = parts[0].shape
    width = width3 // 3
    heads = width // HD
    steps = SEQLEN // BQ
    per = chunk // BQ

    def body(place_ref, ends_ref, *refs):
        part_refs = refs[:count]
        grad_refs = refs[count : 2 * count]
        wide_ref, lse_ref = refs[2 * count : 2 * count + 2]
        out_refs = refs[2 * count + 2 : 3 * count + 2]
        qh, kh, vh, gh, kt, qt, gt, gq, gk, gv, stage = refs[3 * count + 2 :]
        step = pl.program_id(0)
        me = place_ref[0]

        @pl.when(step == 0)
        def _():
            for r in range(count):
                j = me ^ r
                rows = pl.ds(pl.multiple_of(j * chunk, chunk), chunk)
                for h in range(heads):
                    cols = slice(h * HD, (h + 1) * HD)
                    qh[h, rows, :] = part_refs[r][:, cols] * BF16(HD**-0.5)
                    kh[h, rows, :] = part_refs[r][:, width + h * HD : width + (h + 1) * HD]
                    vh[h, rows, :] = part_refs[r][:, 2 * width + h * HD : 2 * width + (h + 1) * HD]
                    gh[h, rows, :] = grad_refs[r][:, cols]
                kt[j] = part_refs[r][:, width : 2 * width].T
                for s in range(per):
                    sub = slice(s * BQ, (s + 1) * BQ)
                    qt[j * per + s] = (part_refs[r][sub, :width] * BF16(HD**-0.5)).T
                    gt[j * per + s] = grad_refs[r][sub, :].T
            gk[...] = jnp.zeros(gk.shape, F32)
            gv[...] = jnp.zeros(gv.shape, F32)

        start = step * BQ
        low_first, low_last, high_first, high_last = block_reach(ends_ref, start)
        low_row, high_row = row_reach(ends_ref, start)
        rows = pl.ds(pl.multiple_of(start, BQ), BQ)
        gq[...] = jnp.zeros(gq.shape, F32)
        inner = []
        for h in range(heads):
            part = slice(h * HD, (h + 1) * HD)
            inner.append(jnp.sum(gt[step, part, :].astype(F32) * wide_ref[part, :], 0, keepdims=True))

        def block(b, masked):
            keys = pl.ds(pl.multiple_of(b * chunk, chunk), chunk)
            if masked:
                place_of = b * chunk + lax.broadcasted_iota(jnp.int32, (chunk, BQ), 0)
                allowed = (place_of >= low_row) & (place_of < high_row)
            for h in range(heads):
                part = slice(h * HD, (h + 1) * HD)
                score = mm(kh[h, keys, :], qh[h, rows, :], NT)
                if masked:
                    score = jnp.where(allowed, score, FILL)
                weight = jnp.exp(score - lse_ref[h : h + 1, :])
                grad_weight = mm(vh[h, keys, :], gh[h, rows, :], NT)
                grad_score = (weight * (grad_weight - inner[h])).astype(BF16)
                gv[b, part, :] += mm(gt[step, part, :], weight.astype(BF16), NT)
                gk[b, part, :] += mm(qt[step, part, :], grad_score, NT)
                gq[part, :] += mm(kt[b, part, :], grad_score)

        def one(b, carry):
            open_all = (b * chunk >= low_last) & ((b + 1) * chunk <= high_first)

            @pl.when(open_all)
            def _():
                block(b, False)

            @pl.when(jnp.logical_not(open_all))
            def _():
                block(b, True)

            return carry

        lax.fori_loop(low_first // chunk, (high_last + chunk - 1) // chunk, one, 0)
        stage[step // per, pl.ds(pl.multiple_of((step % per) * BQ, BQ), BQ), :] = (gq[...] * HD**-0.5).T.astype(BF16)

        @pl.when(step == steps - 1)
        def _():
            for r in range(count):
                j = me ^ r
                out_refs[r][:, :width] = stage[j]
                out_refs[r][:, width : 2 * width] = gk[j].T.astype(BF16)
                out_refs[r][:, 2 * width :] = gv[j].T.astype(BF16)

    pairs = SEQLEN * SEQLEN
    return call(
        body, (steps,),
        [full((chunk, width3))] * count + [full((chunk, width))] * count
        + [pl.BlockSpec((width, BQ), lambda i, *_: (0, i)), pl.BlockSpec((8, BQ), lambda i, *_: (0, i))],
        [full((chunk, width3))] * count, [sds((chunk, width3), BF16)] * count,
        [pltpu.VMEM((heads, SEQLEN, HD), BF16)] * 4
        + [
            pltpu.VMEM((count, width, chunk), BF16),
            pltpu.VMEM((steps, width, BQ), BF16),
            pltpu.VMEM((steps, width, BQ), BF16),
            pltpu.VMEM((width, BQ), F32),
            pltpu.VMEM((count, width, chunk), F32),
            pltpu.VMEM((count, width, chunk), F32),
            pltpu.VMEM((count, chunk, width), BF16),
        ],
        list(parts) + list(grads) + [wide, lse], (place, ends), 14 * pairs * heads * HD, 20 * SEQLEN * width,
        name="attend_backward",
    )


def regroup(values_in):
    count = lax.axis_size("zh")
    perm = [(a * count + b, b * count + a) for a in range(count) for b in range(count)]
    return lax.ppermute(values_in, ("c", "zh"), perm)


def swap_members(parts):
    count = len(parts)
    out = [parts[0]]
    for r in range(1, count):
        out.append(lax.ppermute(parts[r], GROUP, [(a, a ^ r) for a in range(count)]))
    return out


def gather_blocks(shard):
    members = lax.axis_size("zh") * lax.axis_size("zl")
    gathered = lax.all_gather(shard, ALL, axis=0, tiled=True)
    return gathered.reshape(members, -1, shard.shape[1])


def scatter_sum(blocks):
    return lax.psum_scatter(blocks.reshape(-1, blocks.shape[2]), ALL, scatter_dimension=0, tiled=True).astype(F32)


def on_device(
    tokens, doc_lengths, qkv_weight, qv_bias, out_weight, up_weight, up_bias, down_weight, gains, shifts, cotangent
):
    layers = qkv_weight.shape[0]
    tz = lax.axis_size("zh") * lax.axis_size("zl")
    dp = lax.axis_size("q") * lax.axis_size("c")
    place = lax.axis_index(GROUP).astype(jnp.int32).reshape(1)

    x_low = regroup(tokens)
    lengths = regroup(doc_lengths)
    ends = jnp.cumsum(lengths[0], dtype=jnp.int32)

    pieces = [qv_bias, up_bias, gains, shifts]
    sizes = [piece.size // layers for piece in pieces]
    small = jnp.concatenate([piece.reshape(layers, -1) for piece in pieces], axis=1)
    small_all = lax.all_gather(small, ALL, axis=0, tiled=False).reshape(tz, dp, layers, -1).astype(F32)
    cuts = [0]
    for size in sizes:
        cuts.append(cuts[-1] + size)
    parts = [small_all[..., cuts[i] : cuts[i + 1]] for i in range(4)]
    hz = qv_bias.shape[2]
    qv_full = parts[0].reshape(tz, dp, layers, 2, hz, -1).transpose(2, 3, 0, 4, 1, 5).reshape(layers, 2, tz, -1)
    bias_qkv = jnp.stack([qv_full[:, 0], jnp.zeros_like(qv_full[:, 0]), qv_full[:, 1]], axis=2)
    bias_qkv = bias_qkv.reshape(layers, tz, 1, -1)
    up_bias_full = (
        parts[1].reshape(tz, dp, layers, up_bias.shape[1], -1).transpose(2, 0, 3, 1, 4).reshape(layers, 1, FF)
    )
    gain_full = parts[2].reshape(tz, dp, layers, 2, -1).transpose(2, 3, 1, 0, 4).reshape(layers, 2, D)
    shift_full = parts[3].reshape(tz, dp, layers, 4, -1).transpose(2, 3, 1, 0, 4).reshape(layers, 4, D)

    weights = []
    for l in range(layers):
        qkv_cols = qkv_weight[l].transpose(1, 0, 2).reshape(qkv_weight.shape[2], -1)
        weights.append(
            (
                gather_blocks(qkv_cols),
                gather_blocks(out_weight[l]),
                gather_blocks(up_weight[l]),
                gather_blocks(down_weight[l]),
            )
        )
    grad_rows = regroup(cotangent)

    one, zero = jnp.ones((D,), F32), jnp.zeros((D,), F32)
    pad = [zero, zero, zero]
    prev = tokens_wide = x_low.astype(F32)
    prev_gain, prev_shift = one, zero
    kept = []
    for l in range(layers):
        w_qkv, w_out, w_up, w_down = weights[l]
        qkv = swap_members(project_blocks(place, x_low, w_qkv, bias_qkv[l]))
        *ctx, wide, lse = attend_forward(place, ends, qkv)
        ctx = swap_members(ctx)
        vec = jnp.stack([prev_gain, prev_shift, shift_full[l, 0], gain_full[l, 0], shift_full[l, 1]] + pad)
        n1, hs, r1 = sublayer_norm(place, ctx, w_out, prev, vec, "out_norm")
        act, slope = up_gelu(hs, w_up, up_bias_full[l])
        vec = jnp.stack([gain_full[l, 0], shift_full[l, 1], shift_full[l, 2], gain_full[l, 1], shift_full[l, 3]] + pad)
        n2, y_low, r2 = sublayer_norm(place, act, w_down, n1, vec, "down_norm")
        kept.append((x_low, qkv, ctx, wide, lse, n1, hs, r1, act, slope, n2, r2))
        x_low, prev, prev_gain, prev_shift = y_low, n2, gain_full[l, 1], shift_full[l, 3]
    layer_output = regroup(x_low)

    gain_rows = [[jnp.broadcast_to(gain_full[l, i], (8, D)) for i in range(2)] for l in range(layers)]
    g2, gf, sums2 = norm_back(grad_rows, kept[-1][10], kept[-1][11], gain_rows[-1][1])
    results = [None] * layers
    small_grads = [None] * layers
    for l in reversed(range(layers)):
        w_qkv, w_out, w_up, w_down = weights[l]
        x_in, qkv, ctx, wide, lse, n1, hs, r1, act, slope, n2, r2 = kept[l]
        gu, up_bias_sum = units_back(gf, w_down, slope)
        d_down = scatter_sum(weight_grad(gf, act, tz))
        g1, ga, sums1 = sublayer_norm_back(place, gu, w_up, g2, n1, r1, gain_rows[l][0], "up_back")
        d_up = scatter_sum(weight_grad(hs, gu, tz))
        gc = swap_members(project_blocks(place, ga, w_out, None))
        d_out = scatter_sum(weight_grad_blocks(place, ga, ctx, False)[0])
        gqkv = swap_members(attend_backward(place, ends, qkv, gc, wide, lse))
        d_qkv, qkv_sums = weight_grad_blocks(place, x_in, gqkv, True)
        d_qkv = scatter_sum(d_qkv)
        qv_sums = qkv_sums.reshape(tz, 3, hz, dp, -1)
        pieces = [
            jnp.stack([qv_sums[:, 0], qv_sums[:, 2]], axis=1).transpose(0, 3, 1, 2, 4).reshape(tz, dp, -1),
            up_bias_sum.reshape(tz, up_bias.shape[1], dp, -1).transpose(0, 2, 1, 3).reshape(tz, dp, -1),
            jnp.stack([sums1[0], sums2[0]]).reshape(2, dp, tz, -1).transpose(2, 1, 0, 3).reshape(tz, dp, -1),
            jnp.stack([sums1[2], sums1[1], sums2[2], sums2[1]])
            .reshape(4, dp, tz, -1)
            .transpose(2, 1, 0, 3)
            .reshape(tz, dp, -1),
        ]
        small_grads[l] = jnp.concatenate(pieces, axis=-1)
        if l > 0:
            g2, gf, sums2 = sublayer_norm_back(
                place, gqkv, w_qkv, g1, kept[l - 1][10], kept[l - 1][11], gain_rows[l - 1][1], "qkv_back"
            )
        else:
            input_grad = regroup(sublayer_back_last(place, gqkv, w_qkv, g1, "qkv_back"))
        results[l] = (d_qkv.reshape(d_qkv.shape[0], 3, -1).transpose(1, 0, 2), d_out, d_up, d_down)

    small_out = lax.psum_scatter(
        jnp.stack(small_grads, axis=2).reshape(tz * dp, -1), ALL, scatter_dimension=0, tiled=True
    ).reshape(layers, -1)
    qkv_grad, out_grad, up_grad, down_grad = (jnp.stack([entry[i] for entry in results]) for i in range(4))
    qv_bias_grad = small_out[:, cuts[0] : cuts[1]].reshape(qv_bias.shape)
    up_bias_grad = small_out[:, cuts[1] : cuts[2]].reshape(up_bias.shape)
    gains_grad = small_out[:, cuts[2] : cuts[3]].reshape(gains.shape)
    shifts_grad = small_out[:, cuts[3] : cuts[4]].reshape(shifts.shape)
    all_grads = (qkv_grad, qv_bias_grad, out_grad, up_grad, up_bias_grad, down_grad, gains_grad, shifts_grad)
    local_squares = sum(jnp.sum(member * member) for member in all_grads)
    entry_count = LAYERS * (4 * D * D + 2 * D * FF + FF + 8 * D)
    grad_rms = jnp.sqrt(lax.psum(local_squares, ALL) / entry_count)
    return (
        layer_output, input_grad, qkv_grad, qv_bias_grad, out_grad, up_grad, up_bias_grad, down_grad, gains_grad,
        shifts_grad, grad_rms,
    )


def solution(mesh):
    dp, tensor = mesh.shape["dp"], mesh.shape["tensor"]
    fine = Mesh(mesh.devices.reshape(dp // 2, 2, 2, tensor // 2), ("q", "c", "zh", "zl"))
    data, model = ("q", "c"), ("zh", "zl")
    both = data + model
    weight3, weight4 = P(None, data, model), P(None, None, data, model)
    in_specs = (
        P(both, None), P(data, None), weight4, P(None, None, model, data), weight3, weight3, P(None, model, data),
        weight3, P(None, None, both), P(None, None, both), P(both, None),
    )
    out_specs = (
        P(both, None), P(both, None), weight4, P(None, None, model, data), weight3, weight3, P(None, model, data),
        weight3, P(None, None, both), P(None, None, both), P(),
    )
    return jax.shard_map(on_device, mesh=fine, in_specs=in_specs, out_specs=out_specs, check_vma=False)
```

```python
import jax
import jax.numpy as jnp
from jax import lax
from jax.experimental import pallas as pl
from jax.experimental.pallas import tpu as pltpu
from jax.sharding import Mesh
from jax.sharding import PartitionSpec as P

D = 1024
HD = 64
HEADS = 16
FF = 4096
LAYERS = 2
SEQLEN = 2048
WINDOW = 1024
EPS = 1e-06
FILL = -1000000000.0

F32 = jnp.float32
BF16 = jnp.bfloat16
GROUP = ("c", "zl")
MODEL = ("zh", "zl")
ALL = ("zh", "zl", "q", "c")
VMEM_LIMIT = 56 * 1024 * 1024
NT = (((1,), (1,)), ((), ()))
NN = (((1,), (0,)), ((), ()))
ROWS = 128
CHUNK = 64
BQ = 256


def mm(left, right, dims=NN):
    return lax.dot_general(left, right, dims, preferred_element_type=F32)


def full(shape):
    return pl.BlockSpec(shape, lambda *_: (0,) * len(shape))


ANY = pl.BlockSpec(memory_space=pl.ANY)


def sds(shape, kind):
    return jax.ShapeDtypeStruct(shape, kind)


def call(body, grid, in_specs, out_specs, out_shape, scratch, args, scalars, flops, traffic, name):
    return pl.pallas_call(
        body,
        grid_spec=pltpu.PrefetchScalarGridSpec(
            num_scalar_prefetch=len(scalars),
            grid=grid,
            in_specs=in_specs,
            out_specs=out_specs,
            scratch_shapes=scratch,
        ),
        out_shape=out_shape,
        compiler_params=pltpu.CompilerParams(
            dimension_semantics=("arbitrary",) * len(grid), vmem_limit_bytes=VMEM_LIMIT
        ),
        cost_estimate=pl.CostEstimate(flops=int(flops), bytes_accessed=int(traffic), transcendentals=0),
        name=name,
    )(*scalars, *args)


S_P, S_Q, S_C, S_ZH, S_Z = range(5)


def norm_rows(values_in):
    centred = values_in - jnp.mean(values_in, -1, keepdims=True)
    variance = jnp.mean(centred * centred, -1, keepdims=True)
    inverse = lax.rsqrt(variance + EPS)
    return centred * inverse, inverse


def norm_back_rows(grad, normed, inverse, gain):
    scaled = grad * gain
    centred = scaled - jnp.mean(scaled, -1, keepdims=True) - normed * jnp.mean(scaled * normed, -1, keepdims=True)
    return centred * inverse


def fold_rows(values_in):
    return jnp.sum(values_in.reshape(-1, 8, values_in.shape[-1]), 0)


def norm_forward(get_total, tokens, vec, n_ref, low_ref, inv_ref):
    def step(index, carry):
        rows = pl.ds(pl.multiple_of(index * CHUNK, CHUNK), CHUNK)
        normed, inverse = norm_rows(get_total(rows))
        n_ref[rows, :] = normed
        low_ref[rows, :] = (normed * vec[3:4, :] + vec[4:5, :]).astype(BF16)
        inv_ref[rows, :] = jnp.broadcast_to(inverse, (CHUNK, 128))
        return carry

    lax.fori_loop(0, tokens // CHUNK, step, 0)


def norm_backward(get_grad, tokens, n_ref, inv_ref, gain_ref, g_ref, low_ref, sums_ref):
    def step(index, carry):
        rows = pl.ds(pl.multiple_of(index * CHUNK, CHUNK), CHUNK)
        grad = get_grad(rows)
        normed = n_ref[rows, :]
        result = norm_back_rows(grad, normed, inv_ref[rows, 0:1], gain_ref[0:1, :])
        low = result.astype(BF16)
        g_ref[rows, :] = result
        low_ref[rows, :] = low
        return (
            carry[0] + fold_rows(grad * normed),
            carry[1] + fold_rows(grad),
            carry[2] + fold_rows(low.astype(F32)),
        )

    zero = jnp.zeros((8, D), F32)
    sums = lax.fori_loop(0, tokens // CHUNK, step, (zero, zero, zero))
    sums_ref[...] = jnp.zeros(sums_ref.shape, F32)
    for row, member in enumerate(sums):
        sums_ref[row : row + 1, :] = jnp.sum(member, 0, keepdims=True)


class Streamed:
    def __init__(self, refs, matrix, buffer, sems, scal):
        self.refs, self.matrix, self.buffer, self.sems, self.scal = refs, matrix, buffer, sems, scal

    def copies(self, s):
        slot = lax.rem(s, 2)
        plain, early, late = [], [], []
        for k in range(2):
            own, near_x, near_y, far_a, far_b = self.refs[5 * k : 5 * k + 5]

            def copy(src, r, k=k):
                row = ((self.scal[S_Q] ^ r) * 2 + (self.scal[S_C] ^ k)) * ROWS
                return pltpu.make_async_copy(
                    src, self.buffer.at[slot, pl.ds(pl.multiple_of(row, ROWS), ROWS), :], self.sems.at[slot, 4 * k + r]
                )

            for r, ref in enumerate((own, near_x, near_y)):
                plain.append(copy(ref.at[s, self.matrix], r))
            early.append(copy(far_a.at[jnp.minimum(s, 1), self.matrix], 3))
            late.append(copy(far_b.at[jnp.maximum(s - 2, 0), self.matrix], 3))
        return plain, early, late

    def each(self, s, act):
        plain, early, late = self.copies(s)
        for copy in plain:
            act(copy)

        @pl.when(s < 2)
        def _():
            for copy in early:
                act(copy)

        @pl.when(s >= 2)
        def _():
            for copy in late:
                act(copy)

    def start(self, s):
        self.each(s, lambda copy: copy.start())

    def wait(self, s):
        self.each(s, lambda copy: copy.wait())

    def turn(self, s, count):
        @pl.when(s == 0)
        def _():
            self.start(s)

        @pl.when(s + 1 < count)
        def _():
            self.start(s + 1)


def piece_shapes(width):
    return [pltpu.VMEM((2, D, width), BF16), pltpu.SemaphoreType.DMA((2, 8))]


def gelu_parts(u):
    size = jnp.abs(u)
    t = 1.0 / (1.0 + 0.2316419 * size)
    poly = t * (0.127414796 + t * (-0.142248368 + t * (0.7107068705 + t * (-0.7265760135 + t * 0.5307027145))))
    bell = jnp.exp(-0.5 * (u * u))
    tail = poly * bell
    cdf = jnp.where(u >= 0, 1.0 - tail, tail)
    return u * cdf, cdf + u * (0.3989422804014327 * bell)


def tiles(tokens, width):
    for i in range(2):
        for j in range(2):
            yield slice(i * tokens // 2, (i + 1) * tokens // 2), slice(j * width // 2, (j + 1) * width // 2)


def norm_up(scal, prev, parts, vec, weight, matrix, bias, count):
    tokens = prev.shape[0]
    width = FF // count

    def body(scal_ref, prev_ref, *refs):
        part_refs, refs = refs[: len(parts)], refs[len(parts) :]
        vec_ref, bias_ref, refs = refs[0], refs[1], refs[2:]
        pieces, (n_ref, low_ref, inv_ref, act_ref, slope_ref, buffer, sems) = refs[:10], refs[10:]
        s = pl.program_id(0)
        stream = Streamed(pieces, matrix, buffer, sems, scal_ref)
        stream.turn(s, count)

        @pl.when(s == 0)
        def _():
            def total(rows):
                attn = part_refs[0][rows, :].astype(F32)
                for part in part_refs[1:]:
                    attn = attn + part[rows, :].astype(F32)
                return prev_ref[rows, :] * vec_ref[0:1, :] + vec_ref[1:2, :] + (attn + vec_ref[2:3, :])

            norm_forward(total, tokens, vec_ref, n_ref, low_ref, inv_ref)

        stream.wait(s)
        slot = lax.rem(s, 2)
        for rows, cols in tiles(tokens, width):
            act, slope = gelu_parts(mm(low_ref[rows, :], buffer[slot, :, cols]) + bias_ref[0, :, cols])
            act_ref[rows, cols] = act.astype(BF16)
            slope_ref[rows, cols] = slope.astype(BF16)

    column = pl.BlockSpec((tokens, width), lambda s, _: (0, s))
    return call(
        body, (count,),
        [full((tokens, D))] * (1 + len(parts))
        + [full((8, D)), pl.BlockSpec((1, 1, width), lambda s, scal_ref: (scal_ref[S_Z] ^ s, 0, 0))] + [ANY] * 10,
        [full((tokens, D)), full((tokens, D)), full((tokens, 128)), column, column],
        [sds((tokens, D), F32), sds((tokens, D), BF16), sds((tokens, 128), F32)] + [sds((tokens, FF), BF16)] * 2,
        piece_shapes(width), [prev, *parts, vec, bias, *weight], (scal,), 2 * tokens * D * FF,
        2 * (D * FF + tokens * (10 * D + 2 * FF)), "norm_up",
    )


def down_norm(scal, act, weight, matrix, prev, vec, count):
    tokens = prev.shape[0]
    width = FF // count

    def body(scal_ref, act_ref, prev_ref, vec_ref, *refs):
        pieces, (n_ref, low_ref, inv_ref, buffer, sems, acc) = refs[:10], refs[10:]
        s = pl.program_id(0)
        stream = Streamed(pieces, matrix, buffer, sems, scal_ref)
        stream.turn(s, count)
        stream.wait(s)
        value = mm(act_ref[...], buffer[lax.rem(s, 2)], NT)

        @pl.when(s == 0)
        def _():
            acc[...] = value

        @pl.when(s > 0)
        def _():
            acc[...] += value

        @pl.when(s == count - 1)
        def _():
            def total(rows):
                return prev_ref[rows, :] * vec_ref[0:1, :] + vec_ref[1:2, :] + (acc[rows, :] + vec_ref[2:3, :])

            norm_forward(total, tokens, vec_ref, n_ref, low_ref, inv_ref)

    return call(
        body, (count,),
        [pl.BlockSpec((tokens, width), lambda s, _: (0, s)), full((tokens, D)), full((8, D))] + [ANY] * 10,
        [full((tokens, D)), full((tokens, D)), full((tokens, 128))],
        [sds((tokens, D), F32), sds((tokens, D), BF16), sds((tokens, 128), F32)],
        piece_shapes(width) + [pltpu.VMEM((tokens, D), F32)], [act, prev, vec, *weight], (scal,), 2 * tokens * D * FF,
        2 * (D * FF + tokens * (5 * D + FF)), "down_norm",
    )


def units_back(scal, grad, weight, matrix, slope, count):
    tokens = grad.shape[0]
    width = FF // count

    def body(scal_ref, grad_ref, slope_ref, *refs):
        pieces, (out_ref, sum_ref, buffer, sems) = refs[:10], refs[10:]
        s = pl.program_id(0)
        stream = Streamed(pieces, matrix, buffer, sems, scal_ref)
        stream.turn(s, count)
        stream.wait(s)
        slot = lax.rem(s, 2)
        sums = {}
        for rows, cols in tiles(tokens, width):
            low = (mm(grad_ref[rows, :], buffer[slot, :, cols]) * slope_ref[rows, cols].astype(F32)).astype(BF16)
            out_ref[rows, cols] = low
            part = fold_rows(low.astype(F32))
            sums[cols.start] = sums[cols.start] + part if cols.start in sums else part
            if rows.start > 0:
                sum_ref[0, :, cols] = jnp.sum(sums[cols.start], 0, keepdims=True)

    column = pl.BlockSpec((tokens, width), lambda s, _: (0, s))
    return call(
        body, (count,), [full((tokens, D)), column] + [ANY] * 10,
        [column, pl.BlockSpec((1, 1, width), lambda s, scal_ref: (scal_ref[S_Z] ^ s, 0, 0))],
        [sds((tokens, FF), BF16), sds((count, 1, width), F32)], piece_shapes(width), [grad, slope, *weight], (scal,),
        2 * tokens * D * FF, 2 * (D * FF + tokens * (D + 2 * FF)), "units_back",
    )


def up_back(scal, gu, weight, matrix, residual, normed, inverse, gain, count):
    tokens = residual.shape[0]
    width = FF // count

    def body(scal_ref, gu_ref, res_ref, n_ref, inv_ref, gain_ref, *refs):
        pieces, (g_ref, low_ref, sums_ref, buffer, sems, acc) = refs[:10], refs[10:]
        s = pl.program_id(0)
        stream = Streamed(pieces, matrix, buffer, sems, scal_ref)
        stream.turn(s, count)
        stream.wait(s)
        value = mm(gu_ref[...], buffer[lax.rem(s, 2)], NT)

        @pl.when(s == 0)
        def _():
            acc[...] = value

        @pl.when(s > 0)
        def _():
            acc[...] += value

        @pl.when(s == count - 1)
        def _():
            norm_backward(
                lambda rows: res_ref[rows, :] + acc[rows, :], tokens, n_ref, inv_ref, gain_ref, g_ref, low_ref, sums_ref
            )

    return call(
        body, (count,),
        [pl.BlockSpec((tokens, width), lambda s, _: (0, s)), full((tokens, D)), full((tokens, D)), full((tokens, 128)),
         full((8, D))] + [ANY] * 10,
        [full((tokens, D)), full((tokens, D)), full((8, D))],
        [sds((tokens, D), F32), sds((tokens, D), BF16), sds((8, D), F32)],
        piece_shapes(width) + [pltpu.VMEM((tokens, D), F32)], [gu, residual, normed, inverse, gain, *weight], (scal,),
        2 * tokens * D * FF, 2 * (D * FF + tokens * (8 * D + FF)), "up_back",
    )


def norm_back(scal, grad, normed, inverse, gain):
    tokens = grad.shape[0]

    def body(scal_ref, grad_ref, n_ref, inv_ref, gain_ref, g_ref, low_ref, sums_ref):
        norm_backward(
            lambda rows: grad_ref[rows, :].astype(F32), tokens, n_ref, inv_ref, gain_ref, g_ref, low_ref, sums_ref
        )

    return call(
        body, (1,), [full((tokens, D)), full((tokens, D)), full((tokens, 128)), full((8, D))],
        [full((tokens, D)), full((tokens, D)), full((8, D))],
        [sds((tokens, D), F32), sds((tokens, D), BF16), sds((8, D), F32)], [], [grad, normed, inverse, gain], (scal,),
        20 * tokens * D, 12 * tokens * D, "norm_back",
    )


def sum_norm_back(scal, residual, parts, normed, inverse, gain):
    tokens = residual.shape[0]

    def body(scal_ref, res_ref, *refs):
        part_refs, (n_ref, inv_ref, gain_ref, g_ref, low_ref, sums_ref) = refs[: len(parts)], refs[len(parts) :]

        def grad(rows):
            total = part_refs[0][rows, :].astype(F32)
            for part in part_refs[1:]:
                total = total + part[rows, :].astype(F32)
            return res_ref[rows, :] + total

        norm_backward(grad, tokens, n_ref, inv_ref, gain_ref, g_ref, low_ref, sums_ref)

    return call(
        body, (1,), [full((tokens, D))] * (2 + len(parts)) + [full((tokens, 128)), full((8, D))],
        [full((tokens, D)), full((tokens, D)), full((8, D))],
        [sds((tokens, D), F32), sds((tokens, D), BF16), sds((8, D), F32)], [],
        [residual, *parts, normed, inverse, gain], (scal,), 20 * tokens * D, 22 * tokens * D, "sum_norm_back",
    )


def turn_rows(scal_ref, x_ref, turned, core):
    for r in range(4):
        row = ((scal_ref[S_Q] ^ r) * 2 + core) * ROWS
        turned[r * ROWS : (r + 1) * ROWS, :] = x_ref[:, pl.ds(pl.multiple_of(row, ROWS), ROWS)].T


def grad_theirs(scal, left, right, count):
    tokens = left.shape[0]
    width = right.shape[1] // count

    def body(scal_ref, x_ref, y_ref, out_ref, turned):
        @pl.when(pl.program_id(0) == 0)
        def _():
            turn_rows(scal_ref, x_ref, turned, scal_ref[S_C] ^ 1)

        out_ref[:, 0] = mm(turned[...], y_ref[...]).astype(BF16).reshape(4, ROWS, width)

    return call(
        body, (count,), [full((tokens, D)), pl.BlockSpec((tokens, width), lambda s, _: (0, s))],
        pl.BlockSpec((4, 1, ROWS, width), lambda s, _: (0, s, 0, 0)), sds((4, count, ROWS, width), BF16),
        [pltpu.VMEM((4 * ROWS, tokens), BF16)], [left, right], (scal,), tokens * D * width * count,
        D * width * count + 2 * tokens * (D + count * width), "grad_theirs",
    )


def grad_mine(scal, left, right, received, count):
    tokens = left.shape[0]
    width = right.shape[1] // count
    half = count // 2

    def body(scal_ref, x_ref, y_ref, *refs):
        if received is None:
            own, to_x, to_y, rest_x, rest_y, turned = refs
        else:
            got_ref, own, to_x, to_y, rest_x, rest_y, turned = refs
        s = pl.program_id(0)

        @pl.when(s == 0)
        def _():
            turn_rows(scal_ref, x_ref, turned, scal_ref[S_C])

        value = mm(turned[...], y_ref[...]).reshape(4, ROWS, width)
        if received is not None:
            value = value + got_ref[:, 0].astype(F32)
        value = value.astype(BF16)
        own[s] = value[0]

        @pl.when(s < half)
        def _():
            to_x[s] = value[1]
            to_x[half + s] = value[3]
            rest_y[s] = value[2]

        @pl.when(s >= half)
        def _():
            rest_x[s - half] = value[1]
            to_y[s - half] = value[2]
            to_y[s] = value[3]

    specs = [full((tokens, D)), pl.BlockSpec((tokens, width), lambda s, _: (0, s))]
    args = [left, right]
    if received is not None:
        specs.append(pl.BlockSpec((4, 1, ROWS, width), lambda s, _: (0, s, 0, 0)))
        args.append(received)
    shapes = [(count, ROWS, width)] * 3 + [(half, ROWS, width)] * 2
    return call(
        body, (count,), specs, [full(shape) for shape in shapes], [sds(shape, BF16) for shape in shapes],
        [pltpu.VMEM((4 * ROWS, tokens), BF16)], args, (scal,), tokens * D * width * count,
        2 * D * width * count + 2 * tokens * (D + count * width), "grad_mine",
    )


def fetch_heads_weight(scal_ref, pieces, cols, buffer, sems):
    copies = []
    for r in range(4):
        for k in range(2):
            row = ((scal_ref[S_Q] ^ r) * 2 + (scal_ref[S_ZH] ^ k)) * ROWS
            copies.append(
                pltpu.make_async_copy(
                    pieces[r].at[k, :, cols], buffer.at[pl.ds(pl.multiple_of(row, ROWS), ROWS), :], sems.at[2 * r + k]
                )
            )
    for copy in copies:
        copy.start()
    for copy in copies:
        copy.wait()


def by_member(shape):
    return pl.BlockSpec((1,) + shape, lambda r, scal_ref: (scal_ref[S_P] ^ r, 0, 0))


def heads_weight_scratch(width):
    return [pltpu.VMEM((D, width), BF16), pltpu.SemaphoreType.DMA((8,))]


def project_in(scal, lefts, weight, cols, bias, name):
    count = len(lefts)
    tokens = lefts[0].shape[0]
    width = cols.stop - cols.start

    def body(scal_ref, *refs):
        left_refs, refs = refs[:count], refs[count:]
        if bias is not None:
            bias_ref, refs = refs[0], refs[1:]
        pieces, (out_ref, buffer, sems) = refs[:4], refs[4:]
        step = pl.program_id(0)

        @pl.when(step == 0)
        def _():
            fetch_heads_weight(scal_ref, pieces, cols, buffer, sems)

        for r, left in enumerate(left_refs):

            @pl.when(step == r)
            def _(left=left):
                value = mm(left[...], buffer[...])
                if bias is not None:
                    value = value + bias_ref[...]
                out_ref[0] = value.astype(BF16)

    extra, extra_specs = ([], []) if bias is None else ([bias], [full((1, width))])
    return call(
        body, (count,), [full((tokens, D))] * count + extra_specs + [ANY] * 4, by_member((tokens, width)),
        sds((count, tokens, width), BF16), heads_weight_scratch(width), [*lefts, *extra, *weight], (scal,),
        2 * tokens * D * width * count, 2 * (D * width + count * tokens * (D + width)), name,
    )


def project_out(scal, blocks, weight, cols, name):
    count, tokens, width = blocks.shape

    def body(scal_ref, block_ref, *refs):
        pieces, outs, (buffer, sems) = refs[:4], refs[4 : 4 + count], refs[4 + count :]
        step = pl.program_id(0)

        @pl.when(step == 0)
        def _():
            fetch_heads_weight(scal_ref, pieces, cols, buffer, sems)

        for r, out in enumerate(outs):

            @pl.when(step == r)
            def _(out=out):
                out[...] = mm(block_ref[0], buffer[...], NT).astype(BF16)

    return call(
        body, (count,), [by_member((tokens, width))] + [ANY] * 4, [full((tokens, D))] * count,
        [sds((tokens, D), BF16)] * count, heads_weight_scratch(width), [blocks, *weight], (scal,),
        2 * tokens * D * width * count, 2 * (D * width + count * tokens * (D + width)), name,
    )


def heads_grad(scal, xs, gqkv, gas, ctx):
    count, tokens, width = gqkv.shape
    out_width = ctx.shape[2]

    def body(scal_ref, *refs):
        x_refs, refs = refs[:count], refs[count:]
        ga_refs, refs = refs[:count], refs[count:]
        g_ref, ctx_ref = refs[:2]
        outs, (sum_ref, acc, acc_out) = refs[2:6], refs[6:]
        step = pl.program_id(0)
        for r in range(count):

            @pl.when(step == r)
            def _(r=r):
                value = mm(x_refs[r][...].T, g_ref[0])
                value_out = mm(ga_refs[r][...].T, ctx_ref[0])
                sums = jnp.sum(g_ref[0].astype(F32), 0, keepdims=True)
                if r == 0:
                    acc[...] = value
                    acc_out[...] = value_out
                    sum_ref[...] = sums
                else:
                    acc[...] += value
                    acc_out[...] += value_out
                    sum_ref[...] += sums

        @pl.when(step == count - 1)
        def _():
            for r in range(4):
                for k in range(2):
                    row = ((scal_ref[S_Q] ^ r) * 2 + (scal_ref[S_ZH] ^ k)) * ROWS
                    rows = pl.ds(pl.multiple_of(row, ROWS), ROWS)
                    outs[r][k, :, :width] = acc[rows, :].astype(BF16)
                    outs[r][k, :, width:] = acc_out[rows, :].astype(BF16)

    shape = (2, ROWS, width + out_width)
    return call(
        body, (count,), [full((tokens, D))] * (2 * count) + [by_member((tokens, width)), by_member((tokens, out_width))],
        [full(shape)] * 4 + [full((1, width))], [sds(shape, BF16)] * 4 + [sds((1, width), F32)],
        [pltpu.VMEM((D, width), F32), pltpu.VMEM((D, out_width), F32)], [*xs, *gas, gqkv, ctx], (scal,),
        2 * tokens * D * (width + out_width) * count, 4 * count * tokens * (D + width), "heads_grad",
    )


def reach(ends_ref, row):
    first = jnp.zeros_like(row)
    for index in range(3):
        first = jnp.where(row >= ends_ref[index], ends_ref[index], first)
    last = jnp.full_like(row, SEQLEN)
    for index in (2, 1, 0):
        last = jnp.where(row < ends_ref[index], ends_ref[index], last)
    return jnp.maximum(first, row - (WINDOW - 1)), jnp.minimum(last, row + WINDOW)


def over_keys(ends_ref, start, chunk, block):
    low_first, high_first = reach(ends_ref, start)
    low_last, high_last = reach(ends_ref, start + BQ - 1)
    low_row, high_row = reach(ends_ref, start + lax.broadcasted_iota(jnp.int32, (1, BQ), 1))

    def one(b, carry):
        open_all = (b * chunk >= low_last) & ((b + 1) * chunk <= high_first)

        @pl.when(open_all)
        def _():
            block(b, None)

        @pl.when(jnp.logical_not(open_all))
        def _():
            key = b * chunk + lax.broadcasted_iota(jnp.int32, (chunk, BQ), 0)
            block(b, (key >= low_row) & (key < high_row))

        return carry

    lax.fori_loop(low_first // chunk, (high_last + chunk - 1) // chunk, one, 0)


def attend_forward(ends, qkv):
    count, chunk, width3 = qkv.shape
    width = width3 // 3
    heads = width // HD
    steps = SEQLEN // BQ
    per = chunk // BQ

    def body(ends_ref, qkv_ref, ctx_ref, wide_ref, lse_ref, qh, kh, vt, acc, tops, sums, scores):
        step = pl.program_id(0)

        @pl.when(step == 0)
        def _():
            for j in range(count):
                rows = slice(j * chunk, (j + 1) * chunk)
                for h in range(heads):
                    qh[h, rows, :] = qkv_ref[j, :, h * HD : (h + 1) * HD] * BF16(HD**-0.5)
                    kh[h, rows, :] = qkv_ref[j, :, width + h * HD : width + (h + 1) * HD]
                vt[j] = qkv_ref[j, :, 2 * width :].T

        start = step * BQ
        rows = pl.ds(pl.multiple_of(start, BQ), BQ)
        acc[...] = jnp.zeros(acc.shape, F32)
        tops[...] = jnp.full(tops.shape, -3.0e38, F32)
        sums[...] = jnp.zeros(sums.shape, F32)

        def score(b, allowed):
            keys = pl.ds(pl.multiple_of(b * chunk, chunk), chunk)
            for h in range(heads):
                value = mm(kh[h, keys, :], qh[h, rows, :], NT)
                if allowed is not None:
                    value = jnp.where(allowed, value, FILL)
                scores[h, b] = value
                tops[h] = jnp.maximum(tops[h], jnp.max(value.reshape(-1, 8, BQ), 0))

        over_keys(ends_ref, start, chunk, score)
        top = [jnp.max(tops[h], 0, keepdims=True) for h in range(heads)]

        def weigh(b, carry):
            for h in range(heads):
                part = slice(h * HD, (h + 1) * HD)
                weight = jnp.exp(scores[h, b] - top[h])
                sums[h] += fold_rows(weight)
                acc[part, :] += mm(vt[b, part, :], weight.astype(BF16))
            return carry

        low_first, _ = reach(ends_ref, start)
        _, high_last = reach(ends_ref, start + BQ - 1)
        lax.fori_loop(low_first // chunk, (high_last + chunk - 1) // chunk, weigh, 0)
        for h in range(heads):
            part = slice(h * HD, (h + 1) * HD)
            total = jnp.sum(sums[h], 0, keepdims=True)
            wide_ref[part, :] = acc[part, :] / total
            lse_ref[h : h + 1, :] = top[h] + jnp.log(total)
        lse_ref[heads:, :] = jnp.zeros((8 - heads, BQ), F32)
        ctx_ref[0] = wide_ref[...].T.astype(BF16)

    pairs = SEQLEN * SEQLEN
    return call(
        body, (steps,), [full((count, chunk, width3))],
        [pl.BlockSpec((1, BQ, width), lambda i, _: (i // per, i % per, 0)),
         pl.BlockSpec((width, BQ), lambda i, _: (0, i)), pl.BlockSpec((8, BQ), lambda i, _: (0, i))],
        [sds((count, chunk, width), BF16), sds((width, SEQLEN), F32), sds((8, SEQLEN), F32)],
        [
            pltpu.VMEM((heads, SEQLEN, HD), BF16),
            pltpu.VMEM((heads, SEQLEN, HD), BF16),
            pltpu.VMEM((count, width, chunk), BF16),
            pltpu.VMEM((width, BQ), F32),
            pltpu.VMEM((heads, 8, BQ), F32),
            pltpu.VMEM((heads, 8, BQ), F32),
            pltpu.VMEM((heads, count, chunk, BQ), F32),
        ],
        [qkv], (ends,), 16 * pairs * heads * HD, 6 * SEQLEN * width * 2, "attend_forward",
    )


def attend_backward(ends, qkv, grads, wide, lse):
    count, chunk, width3 = qkv.shape
    width = width3 // 3
    heads = width // HD
    steps = SEQLEN // BQ
    per = chunk // BQ

    def body(ends_ref, qkv_ref, grad_ref, wide_ref, lse_ref, out_ref, qh, kh, vh, gh, kt, qt, gt, gq, gk, gv):
        step = pl.program_id(0)

        @pl.when(step == 0)
        def _():
            for j in range(count):
                rows = slice(j * chunk, (j + 1) * chunk)
                for h in range(heads):
                    cols = slice(h * HD, (h + 1) * HD)
                    qh[h, rows, :] = qkv_ref[j, :, cols] * BF16(HD**-0.5)
                    kh[h, rows, :] = qkv_ref[j, :, width + h * HD : width + (h + 1) * HD]
                    vh[h, rows, :] = qkv_ref[j, :, 2 * width + h * HD : 2 * width + (h + 1) * HD]
                    gh[h, rows, :] = grad_ref[j, :, cols]
                kt[j] = qkv_ref[j, :, width : 2 * width].T
                for s in range(per):
                    sub = slice(s * BQ, (s + 1) * BQ)
                    qt[j * per + s] = (qkv_ref[j, sub, :width] * BF16(HD**-0.5)).T
                    gt[j * per + s] = grad_ref[j, sub, :].T
            gk[...] = jnp.zeros(gk.shape, F32)
            gv[...] = jnp.zeros(gv.shape, F32)

        start = step * BQ
        rows = pl.ds(pl.multiple_of(start, BQ), BQ)
        gq[...] = jnp.zeros(gq.shape, F32)
        inner = []
        for h in range(heads):
            part = slice(h * HD, (h + 1) * HD)
            inner.append(jnp.sum(gt[step, part, :].astype(F32) * wide_ref[part, :], 0, keepdims=True))

        def block(b, allowed):
            keys = pl.ds(pl.multiple_of(b * chunk, chunk), chunk)
            for h in range(heads):
                part = slice(h * HD, (h + 1) * HD)
                score = mm(kh[h, keys, :], qh[h, rows, :], NT)
                grad_weight = mm(vh[h, keys, :], gh[h, rows, :], NT)
                if allowed is not None:
                    score = jnp.where(allowed, score, FILL)
                weight = jnp.exp(score - lse_ref[h : h + 1, :])
                grad_score = (weight * (grad_weight - inner[h])).astype(BF16)
                gv[b, part, :] += mm(gt[step, part, :], weight.astype(BF16), NT)
                gk[b, part, :] += mm(qt[step, part, :], grad_score, NT)
                gq[part, :] += mm(kt[b, part, :], grad_score)

        over_keys(ends_ref, start, chunk, block)
        out_ref[step // per, pl.ds(pl.multiple_of((step % per) * BQ, BQ), BQ), :width] = (
            (gq[...] * HD**-0.5).T.astype(BF16)
        )

        @pl.when(step == steps - 1)
        def _():
            for j in range(count):
                out_ref[j, :, width : 2 * width] = gk[j].T.astype(BF16)
                out_ref[j, :, 2 * width :] = gv[j].T.astype(BF16)

    pairs = SEQLEN * SEQLEN
    return call(
        body, (steps,),
        [full((count, chunk, width3)), full((count, chunk, width)), pl.BlockSpec((width, BQ), lambda i, _: (0, i)),
         pl.BlockSpec((8, BQ), lambda i, _: (0, i))],
        full((count, chunk, width3)), sds((count, chunk, width3), BF16),
        [pltpu.VMEM((heads, SEQLEN, HD), BF16)] * 4
        + [
            pltpu.VMEM((count, width, chunk), BF16),
            pltpu.VMEM((steps, width, BQ), BF16),
            pltpu.VMEM((steps, width, BQ), BF16),
            pltpu.VMEM((width, BQ), F32),
            pltpu.VMEM((count, width, chunk), F32),
            pltpu.VMEM((count, width, chunk), F32),
        ],
        [qkv, grads, wide, lse], (ends,), 28 * pairs * heads * HD, 20 * SEQLEN * width, "attend_backward",
    )


def flip(values_in, axes, mask):
    return lax.ppermute(values_in, axes, [(a, a ^ mask) for a in range(lax.axis_size(axes))])


def turn(values_in):
    return lax.ppermute(values_in, ("c", "zh"), [(2 * a + b, 2 * b + a) for a in range(2) for b in range(2)])


def cross(values_in):
    return lax.ppermute(values_in, ("c", "zh"), [(2 * a + b, 2 * b + 1 - a) for a in range(2) for b in range(2)])


def uncross(values_in):
    return lax.ppermute(values_in, ("c", "zh"), [(2 * b + 1 - a, 2 * a + b) for a in range(2) for b in range(2)])


def from_members(values_in, axes):
    return [values_in] + [flip(values_in, axes, r) for r in range(1, lax.axis_size(axes))]


def to_members(parts, axes):
    return [parts[0]] + [flip(part, axes, r) for r, part in enumerate(parts) if r > 0]


def add(*parts):
    total = parts[0].astype(F32)
    for part in parts[1:]:
        total = total + part.astype(F32)
    return total


def is_small():
    return lax.axis_size("q") == 4


def order_by(values_in, axis, position, count):
    bit = 1
    while bit < count:
        shape = values_in.shape
        split = shape[:axis] + (count // (2 * bit), 2, bit) + shape[axis + 1 :]
        cut = values_in.reshape(split)
        values_in = jnp.where((position & bit) != 0, jnp.flip(cut, axis + 1), cut).reshape(shape)
        bit *= 2
    return values_in


def gather_heads_weight(shard, zh):
    pair = jnp.stack([turn(shard), cross(shard)])
    if is_small():
        return from_members(pair, "q")
    every = order_by(lax.all_gather(pair, "q"), 1, zh, 2).reshape(4, 2, ROWS, -1)
    return [every[r] for r in range(4)]


def scatter_heads_grad(buckets, zh):
    if is_small():
        got = to_members(buckets, "q")
        first, second = (add(*(member[k] for member in got)).astype(BF16) for k in range(2))
    else:
        every = jnp.stack(buckets).reshape(lax.axis_size("q"), 2, -1, buckets[0].shape[-1])
        rows = order_by(lax.psum_scatter(every, "q", scatter_dimension=0, tiled=False), 0, zh, 2)
        first, second = rows[0], rows[1]
    return add(turn(first), uncross(second))


def gather_units_weight(shard):
    if is_small():
        two = jnp.stack([shard, flip(shard, "zl", 1)])
        own = jnp.concatenate([two, flip(two, "zh", 1)])
        near_x, near_y = flip(own, "q", 1), flip(own, "q", 2)
        far_a, far_b = flip(near_y[:2], "q", 1), flip(near_x[2:], "q", 2)
        mine = [own, near_x, near_y, far_a, far_b]
        return mine + [flip(piece, "c", 1) for piece in mine]
    matrices, _, width = shard.shape
    members = lax.axis_size(MODEL)
    every = lax.all_gather(shard, ALL).reshape(members, -1, matrices, shard.shape[1], width).transpose(0, 2, 1, 3, 4)
    every = every.reshape(members, matrices, 4, 2, ROWS, width)
    pieces = []
    for k in range(2):
        pieces += [every[:, :, r, k] for r in range(3)] + [every[:2, :, 3, k], every[2:, :, 3, k]]
    return pieces


def scatter_units_grad(scal, left, right, count):
    if is_small():
        got = flip(grad_theirs(scal, left, right, count), "c", 1)
        own, to_x, to_y, rest_x, rest_y = grad_mine(scal, left, right, got, count)
        half = count // 2
        from_x, from_y = flip(to_x, "q", 1), flip(to_y, "q", 2)
        late_x = flip(add(rest_x, from_y[half:]).astype(BF16), "q", 1)
        late_y = flip(add(rest_y, from_x[half:]).astype(BF16), "q", 2)
        near = add(own[:half], from_x[:half], late_y)
        far = add(own[half:], late_x, from_y[:half]).astype(BF16)
        both = near + flip(far, "zh", 1).astype(F32)
        return both[0] + flip(both[1].astype(BF16), "zl", 1).astype(F32)
    theirs = grad_theirs(scal, left, right, count)
    own, to_x, to_y, rest_x, rest_y = grad_mine(scal, left, right, None, count)
    half = count // 2
    mine = jnp.stack(
        [own, jnp.concatenate([to_x[:half], rest_x]), jnp.concatenate([rest_y, to_y[:half]]),
         jnp.concatenate([to_x[half:], to_y[half:]])]
    )
    every = jnp.stack([mine, theirs], axis=1).transpose(2, 0, 1, 3, 4).reshape(-1, mine.shape[-1])
    return lax.psum_scatter(every, ALL, scatter_dimension=0, tiled=True).astype(F32)


SMALL_AXES = ("q", MODEL, "c")


def gather_small(shard, where):
    tz, dp = lax.axis_size(MODEL), lax.axis_size(("q", "c"))
    if not is_small():
        return lax.all_gather(shard, ALL).reshape(tz, dp, -1)
    every = shard.reshape(1, -1)
    for axes in SMALL_AXES:
        every = jnp.stack(from_members(every, axes))
    every = every.reshape(2, 4, 4, -1)
    for axis, position in enumerate(where[::-1]):
        every = order_by(every, axis, position, every.shape[axis])
    return every.transpose(1, 2, 0, 3).reshape(tz, dp, -1)


def scatter_small(values_in, where):
    if not is_small():
        return lax.psum_scatter(values_in.reshape(-1, values_in.shape[-1]), ALL, scatter_dimension=0, tiled=True)[0]
    every = values_in.reshape(4, 4, 2, -1).transpose(1, 0, 2, 3)
    for axis, position in enumerate(where):
        every = order_by(every, axis, position, every.shape[axis])
    for axes in SMALL_AXES:
        every = add(*to_members([every[r] for r in range(every.shape[0])], axes))
    return every


def sum_all(value):
    if not is_small():
        return lax.psum(value, ALL)
    value = jnp.broadcast_to(value, (8, 128))
    for axes in SMALL_AXES:
        parts = jnp.stack(from_members(value, axes))
        value = jnp.sum(order_by(parts, 0, lax.axis_index(axes), parts.shape[0]), 0)
    return value[0, 0]


def on_device(
    tokens, doc_lengths, qkv_weight, qv_bias, out_weight, up_weight, up_bias, down_weight, gains, shifts, cotangent
):
    layers = qkv_weight.shape[0]
    tz, dp = lax.axis_size(MODEL), lax.axis_size(("q", "c"))
    place, zh = lax.axis_index(GROUP), lax.axis_index("zh")
    where = (lax.axis_index("q"), lax.axis_index(MODEL), lax.axis_index("c"))
    if is_small():
        spots = [place, where[0], where[2], zh, where[1]]
    else:
        spots = [place] + [jnp.zeros((), jnp.int32)] * 4
    scal = jnp.stack([spot.astype(jnp.int32) for spot in spots])

    x_low = turn(tokens)
    ends = jnp.cumsum(turn(doc_lengths)[0], dtype=jnp.int32)

    pieces = [qv_bias, up_bias, gains, shifts]
    sizes = [piece.size // layers for piece in pieces]
    small = jnp.concatenate([piece.reshape(layers, -1) for piece in pieces], axis=1)
    small_all = gather_small(small.reshape(-1), where).reshape(tz, dp, layers, -1).astype(F32)
    cuts = [0]
    for size in sizes:
        cuts.append(cuts[-1] + size)
    parts = [small_all[..., cuts[i] : cuts[i + 1]] for i in range(4)]
    hz = qv_bias.shape[2]
    qv_here = lax.dynamic_index_in_dim(parts[0], place, 0, False)
    qv_here = qv_here.reshape(dp, layers, 2, hz, -1).transpose(1, 2, 3, 0, 4).reshape(layers, 2, -1)
    bias_qkv = jnp.concatenate([qv_here[:, :1], jnp.zeros_like(qv_here[:, :1]), qv_here[:, 1:]], axis=1)
    bias_qkv = bias_qkv.reshape(layers, 1, -1)
    up_bias_full = parts[1].reshape(tz, dp, layers, up_bias.shape[1], -1).transpose(2, 0, 3, 1, 4)
    up_bias_full = up_bias_full.reshape(layers, tz, 1, -1)
    gain_full = parts[2].reshape(tz, dp, layers, 2, -1).transpose(2, 3, 1, 0, 4).reshape(layers, 2, D)
    shift_full = parts[3].reshape(tz, dp, layers, 4, -1).transpose(2, 3, 1, 0, 4).reshape(layers, 4, D)

    qkv_cols = 3 * out_weight.shape[2]
    heads_weight, units_weight = [], []
    for l in range(layers):
        shard = jnp.concatenate([qkv_weight[l].transpose(1, 0, 2).reshape(-1, qkv_cols), out_weight[l]], axis=1)
        heads_weight.append(gather_heads_weight(shard, zh))
        if l == 0:
            up = (gather_units_weight(up_weight[l][None]), 0)
            down = (gather_units_weight(down_weight[l][None]), 0)
        else:
            both = gather_units_weight(jnp.stack([up_weight[l], down_weight[l]]))
            up, down = (both, 0), (both, 1)
        units_weight.append((up, down))
    top_grad = turn(cotangent)
    in_cols, out_cols = slice(0, qkv_cols), slice(qkv_cols, qkv_cols + out_weight.shape[2])

    one, zero = jnp.ones((D,), F32), jnp.zeros((D,), F32)
    pad = [zero, zero, zero]
    prev, prev_gain, prev_shift = x_low.astype(F32), one, zero
    kept = []
    for l in range(layers):
        w_heads, (w_up, w_down) = heads_weight[l], units_weight[l]
        xs = from_members(x_low, GROUP)
        qkv = project_in(scal, xs, w_heads, in_cols, bias_qkv[l], "project_qkv")
        ctx, wide, lse = attend_forward(ends, qkv)
        attn = to_members(project_out(scal, ctx, w_heads, out_cols, "project_attn"), GROUP)
        vec = jnp.stack([prev_gain, prev_shift, shift_full[l, 0], gain_full[l, 0], shift_full[l, 1]] + pad)
        n1, hs, r1, act, slope = norm_up(scal, prev, attn, vec, *w_up, up_bias_full[l], tz)
        vec = jnp.stack([gain_full[l, 0], shift_full[l, 1], shift_full[l, 2], gain_full[l, 1], shift_full[l, 3]] + pad)
        n2, y_low, r2 = down_norm(scal, act, *w_down, n1, vec, tz)
        kept.append((xs, qkv, ctx, wide, lse, n1, hs, r1, act, slope, n2, r2))
        x_low, prev, prev_gain, prev_shift = y_low, n2, gain_full[l, 1], shift_full[l, 3]
    layer_output = turn(x_low)

    gain_rows = [[jnp.broadcast_to(gain_full[l, i], (8, D)) for i in range(2)] for l in range(layers)]
    g2, gf, sums2 = norm_back(scal, top_grad, kept[-1][10], kept[-1][11], gain_rows[-1][1])
    results = [None] * layers
    small_grads = [None] * layers
    for l in reversed(range(layers)):
        w_heads, (w_up, w_down) = heads_weight[l], units_weight[l]
        xs, qkv, ctx, wide, lse, n1, hs, r1, act, slope, n2, r2 = kept[l]
        gu, up_bias_sum = units_back(scal, gf, *w_down, slope, tz)
        g1, ga, sums1 = up_back(scal, gu, *w_up, g2, n1, r1, gain_rows[l][0], tz)
        gas = from_members(ga, GROUP)
        d_down = scatter_units_grad(scal, gf, act, tz)
        d_up = scatter_units_grad(scal, hs, gu, tz)
        gc = project_in(scal, gas, w_heads, out_cols, None, "project_gc")
        gqkv = attend_backward(ends, qkv, gc, wide, lse)
        back = to_members(project_out(scal, gqkv, w_heads, in_cols, "project_gx"), GROUP)
        *buckets, qkv_sums = heads_grad(scal, xs, gqkv, gas, ctx)
        d_heads = scatter_heads_grad(buckets, zh)
        qv_sums = qkv_sums.reshape(3, hz, dp, -1)
        qv_sums = jnp.stack([qv_sums[0], qv_sums[2]]).transpose(2, 0, 1, 3).reshape(1, dp, -1)
        mine = (jnp.arange(tz) == place).astype(F32).reshape(tz, 1, 1)
        small_grads[l] = jnp.concatenate(
            [
                mine * qv_sums,
                up_bias_sum.reshape(tz, up_bias.shape[1], dp, -1).transpose(0, 2, 1, 3).reshape(tz, dp, -1),
                jnp.stack([sums1[0], sums2[0]]).reshape(2, dp, tz, -1).transpose(2, 1, 0, 3).reshape(tz, dp, -1),
                jnp.stack([sums1[2], sums1[1], sums2[2], sums2[1]])
                .reshape(4, dp, tz, -1).transpose(2, 1, 0, 3).reshape(tz, dp, -1),
            ],
            axis=-1,
        )
        if l > 0:
            g2, gf, sums2 = sum_norm_back(scal, g1, back, kept[l - 1][10], kept[l - 1][11], gain_rows[l - 1][1])
        else:
            input_grad = turn((g1 + add(*back)).astype(BF16))
        rows = d_heads.shape[0]
        results[l] = (
            d_heads[:, :qkv_cols].reshape(rows, 3, -1).transpose(1, 0, 2), d_heads[:, qkv_cols:], d_up, d_down
        )

    small_out = scatter_small(jnp.stack(small_grads, axis=2).reshape(tz, dp, -1), where).reshape(layers, -1)
    qkv_grad, out_grad, up_grad, down_grad = (jnp.stack([entry[i] for entry in results]) for i in range(4))
    qv_bias_grad = small_out[:, cuts[0] : cuts[1]].reshape(qv_bias.shape)
    up_bias_grad = small_out[:, cuts[1] : cuts[2]].reshape(up_bias.shape)
    gains_grad = small_out[:, cuts[2] : cuts[3]].reshape(gains.shape)
    shifts_grad = small_out[:, cuts[3] : cuts[4]].reshape(shifts.shape)
    all_grads = (qkv_grad, qv_bias_grad, out_grad, up_grad, up_bias_grad, down_grad, gains_grad, shifts_grad)
    local_squares = sum(jnp.sum(member * member) for member in all_grads)
    entry_count = LAYERS * (4 * D * D + 2 * D * FF + FF + 8 * D)
    grad_rms = jnp.sqrt(sum_all(local_squares) / entry_count)
    return (
        layer_output, input_grad, qkv_grad, qv_bias_grad, out_grad, up_grad, up_bias_grad, down_grad, gains_grad,
        shifts_grad, grad_rms,
    )


def solution(mesh):
    dp, tensor = mesh.shape["dp"], mesh.shape["tensor"]
    fine = Mesh(mesh.devices.reshape(dp // 2, 2, 2, tensor // 2), ("q", "c", "zh", "zl"))
    data, model = ("q", "c"), ("zh", "zl")
    both = data + model
    weight3, weight4 = P(None, data, model), P(None, None, data, model)
    in_specs = (
        P(both, None), P(data, None), weight4, P(None, None, model, data), weight3, weight3, P(None, model, data),
        weight3, P(None, None, both), P(None, None, both), P(both, None),
    )
    out_specs = (
        P(both, None), P(both, None), weight4, P(None, None, model, data), weight3, weight3, P(None, model, data),
        weight3, P(None, None, both), P(None, None, both), P(),
    )
    return jax.shard_map(on_device, mesh=fine, in_specs=in_specs, out_specs=out_specs, check_vma=False)
```

```python
import jax
import jax.numpy as jnp
from jax import lax
from jax.experimental import pallas as pl
from jax.experimental.pallas import tpu as pltpu
from jax.sharding import Mesh
from jax.sharding import PartitionSpec as P

D = 1024
HD = 64
HEADS = 16
FF = 4096
LAYERS = 2
SEQLEN = 2048
WINDOW = 1024
EPS = 1e-06
FILL = -1000000000.0

F32 = jnp.float32
BF16 = jnp.bfloat16
GROUP = ("c", "zl")
MODEL = ("zh", "zl")
ALL = ("zh", "zl", "q", "c")
VMEM_LIMIT = 56 * 1024 * 1024
COST = 1000
NT = (((1,), (1,)), ((), ()))
NN = (((1,), (0,)), ((), ()))
ROWS = 128
CHUNK = 64
BQ = 256


def mm(left, right, dims=NN):
    return lax.dot_general(left, right, dims, preferred_element_type=F32)


def full(shape):
    return pl.BlockSpec(shape, lambda *_: (0,) * len(shape))


ANY = pl.BlockSpec(memory_space=pl.ANY)


def sds(shape, kind):
    return jax.ShapeDtypeStruct(shape, kind)


class Flow:
    def __init__(self, scal):
        self.scal, self.before, self.held = scal, [], {}

    def wait(self, *arrays):
        self.before += arrays

    def hold(self, **arrays):
        self.held.update(arrays)

    def free(self, name):
        return self.held.pop(name)


def call(flow, body, grid, in_specs, out_specs, out_shape, scratch, args, flops, traffic, name, scalars=None):
    scalars = (flow.scal,) if scalars is None else scalars
    single = not isinstance(out_specs, (list, tuple))
    out_specs = [out_specs] if single else list(out_specs)
    out_shape = [out_shape] if single else list(out_shape)
    before, held = flow.before, list(flow.held.items())
    ns, nb, nh, no = len(scalars), len(before), len(held), len(out_specs)
    first, last = ns + nb + nh, ns + nb + nh + len(args) + no

    def wrapped(*refs):
        body(*refs[:ns], *refs[first:last], *refs[last + nh :])

    result = pl.pallas_call(
        wrapped,
        grid_spec=pltpu.PrefetchScalarGridSpec(
            num_scalar_prefetch=ns,
            grid=grid,
            in_specs=[ANY] * (nb + nh) + list(in_specs),
            out_specs=out_specs + [ANY] * nh,
            scratch_shapes=scratch,
        ),
        out_shape=out_shape + [sds(array.shape, array.dtype) for _, array in held],
        input_output_aliases={ns + nb + i: no + i for i in range(nh)},
        compiler_params=pltpu.CompilerParams(
            dimension_semantics=("arbitrary",) * len(grid), vmem_limit_bytes=VMEM_LIMIT
        ),
        cost_estimate=pl.CostEstimate(flops=COST, bytes_accessed=COST, transcendentals=0),
        name=name,
    )(*scalars, *before, *[array for _, array in held], *args)
    flow.before = []
    flow.held = {key: value for (key, _), value in zip(held, result[no:])}
    return result[0] if single else result[:no]


def gate(flow):
    if flow.held:
        call(flow, lambda *refs: None, (1,), [], [], [], [], [], 0, 0, "gate")


S_P, S_Q, S_C, S_ZH, S_Z = range(5)


def norm_rows(values_in):
    centred = values_in - jnp.mean(values_in, -1, keepdims=True)
    variance = jnp.mean(centred * centred, -1, keepdims=True)
    inverse = lax.rsqrt(variance + EPS)
    return centred * inverse, inverse


def norm_back_rows(grad, normed, inverse, gain):
    scaled = grad * gain
    centred = scaled - jnp.mean(scaled, -1, keepdims=True) - normed * jnp.mean(scaled * normed, -1, keepdims=True)
    return centred * inverse


def fold_rows(values_in):
    return jnp.sum(values_in.reshape(-1, 8, values_in.shape[-1]), 0)


def norm_forward(get_total, tokens, vec, n_ref, low_ref, inv_ref):
    def step(index, carry):
        rows = pl.ds(pl.multiple_of(index * CHUNK, CHUNK), CHUNK)
        normed, inverse = norm_rows(get_total(rows))
        n_ref[rows, :] = normed
        low_ref[rows, :] = (normed * vec[3:4, :] + vec[4:5, :]).astype(BF16)
        inv_ref[rows, :] = jnp.broadcast_to(inverse, (CHUNK, 128))
        return carry

    lax.fori_loop(0, tokens // CHUNK, step, 0)


def norm_backward(get_grad, tokens, n_ref, inv_ref, gain_ref, g_ref, low_ref, sums_ref):
    def step(index, carry):
        rows = pl.ds(pl.multiple_of(index * CHUNK, CHUNK), CHUNK)
        grad = get_grad(rows)
        normed = n_ref[rows, :]
        result = norm_back_rows(grad, normed, inv_ref[rows, 0:1], gain_ref[0:1, :])
        low = result.astype(BF16)
        g_ref[rows, :] = result
        low_ref[rows, :] = low
        return (
            carry[0] + fold_rows(grad * normed),
            carry[1] + fold_rows(grad),
            carry[2] + fold_rows(low.astype(F32)),
        )

    zero = jnp.zeros((8, D), F32)
    sums = lax.fori_loop(0, tokens // CHUNK, step, (zero, zero, zero))
    sums_ref[...] = jnp.zeros(sums_ref.shape, F32)
    for row, member in enumerate(sums):
        sums_ref[row : row + 1, :] = jnp.sum(member, 0, keepdims=True)


def away(s):
    return (s & 1) * 2 + s // 2


class Streamed:
    def __init__(self, refs, matrix, buffer, sems, scal):
        self.refs, self.matrix, self.buffer, self.sems, self.scal = refs, matrix, buffer, sems, scal

    def copies(self, s):
        slot = lax.rem(s, 2)
        plain, early, late = [], [], []
        for k in range(2):
            own, near_x, near_y, far_a, far_b = self.refs[5 * k : 5 * k + 5]

            def copy(src, r, k=k):
                row = ((self.scal[S_Q] ^ r) * 2 + (self.scal[S_C] ^ k)) * ROWS
                return pltpu.make_async_copy(
                    src, self.buffer.at[slot, pl.ds(pl.multiple_of(row, ROWS), ROWS), :], self.sems.at[slot, 4 * k + r]
                )

            for r, ref in enumerate((own, near_x, near_y)):
                plain.append(copy(ref.at[s, self.matrix], r))
            early.append(copy(far_a.at[jnp.minimum(s, 1), self.matrix], 3))
            late.append(copy(far_b.at[jnp.maximum(s - 2, 0), self.matrix], 3))
        return plain, early, late

    def each(self, s, act):
        plain, early, late = self.copies(s)
        for copy in plain:
            act(copy)

        @pl.when(s < 2)
        def _():
            for copy in early:
                act(copy)

        @pl.when(s >= 2)
        def _():
            for copy in late:
                act(copy)

    def start(self, s):
        self.each(s, lambda copy: copy.start())

    def wait(self, s):
        self.each(s, lambda copy: copy.wait())

    def turn(self, s, count):
        @pl.when(s == 0)
        def _():
            self.start(s)

        @pl.when(s + 1 < count)
        def _():
            self.start(s + 1)


def piece_shapes(width):
    return [pltpu.VMEM((2, D, width), BF16), pltpu.SemaphoreType.DMA((2, 8))]


def gelu_parts(u):
    size = jnp.abs(u)
    t = 1.0 / (1.0 + 0.2316419 * size)
    poly = t * (0.127414796 + t * (-0.142248368 + t * (0.7107068705 + t * (-0.7265760135 + t * 0.5307027145))))
    bell = jnp.exp(-0.5 * (u * u))
    tail = poly * bell
    cdf = jnp.where(u >= 0, 1.0 - tail, tail)
    return u * cdf, cdf + u * (0.3989422804014327 * bell)


def tiles(tokens, width):
    for i in range(2):
        for j in range(2):
            yield slice(i * tokens // 2, (i + 1) * tokens // 2), slice(j * width // 2, (j + 1) * width // 2)


def norm_up(flow, prev, parts, vec, weight, matrix, bias, count):
    tokens = prev.shape[0]
    width = FF // count

    def body(scal_ref, prev_ref, *refs):
        part_refs, refs = refs[: len(parts)], refs[len(parts) :]
        vec_ref, bias_ref, refs = refs[0], refs[1], refs[2:]
        pieces, (n_ref, low_ref, inv_ref, act_ref, slope_ref, buffer, sems) = refs[:10], refs[10:]
        s = pl.program_id(0)
        stream = Streamed(pieces, matrix, buffer, sems, scal_ref)
        stream.turn(s, count)

        @pl.when(s == 0)
        def _():
            def total(rows):
                attn = part_refs[0][rows, :].astype(F32)
                for part in part_refs[1:]:
                    attn = attn + part[rows, :].astype(F32)
                return prev_ref[rows, :] * vec_ref[0:1, :] + vec_ref[1:2, :] + (attn + vec_ref[2:3, :])

            norm_forward(total, tokens, vec_ref, n_ref, low_ref, inv_ref)

        stream.wait(s)
        slot = lax.rem(s, 2)
        for rows, cols in tiles(tokens, width):
            act, slope = gelu_parts(mm(low_ref[rows, :], buffer[slot, :, cols]) + bias_ref[0, :, cols])
            act_ref[rows, cols] = act.astype(BF16)
            slope_ref[rows, cols] = slope.astype(BF16)

    column = pl.BlockSpec((tokens, width), lambda s, _: (0, s))
    return call(
        flow, body, (count,),
        [full((tokens, D))] * (1 + len(parts))
        + [full((8, D)), pl.BlockSpec((1, 1, width), lambda s, scal_ref: (scal_ref[S_Z] ^ away(s), 0, 0))] + [ANY] * 10,
        [full((tokens, D)), full((tokens, D)), full((tokens, 128)), column, column],
        [sds((tokens, D), F32), sds((tokens, D), BF16), sds((tokens, 128), F32)] + [sds((tokens, FF), BF16)] * 2,
        piece_shapes(width), [prev, *parts, vec, bias, *weight], 2 * tokens * D * FF,
        2 * (D * FF + tokens * (10 * D + 2 * FF)), "norm_up",
    )


def down_norm(flow, act, weight, matrix, prev, vec, count):
    tokens = prev.shape[0]
    width = FF // count

    def body(scal_ref, act_ref, prev_ref, vec_ref, *refs):
        pieces, (n_ref, low_ref, inv_ref, buffer, sems, acc) = refs[:10], refs[10:]
        s = pl.program_id(0)
        stream = Streamed(pieces, matrix, buffer, sems, scal_ref)
        stream.turn(s, count)
        stream.wait(s)
        value = mm(act_ref[...], buffer[lax.rem(s, 2)], NT)

        @pl.when(s == 0)
        def _():
            acc[...] = value

        @pl.when(s > 0)
        def _():
            acc[...] += value

        @pl.when(s == count - 1)
        def _():
            def total(rows):
                return prev_ref[rows, :] * vec_ref[0:1, :] + vec_ref[1:2, :] + (acc[rows, :] + vec_ref[2:3, :])

            norm_forward(total, tokens, vec_ref, n_ref, low_ref, inv_ref)

    return call(
        flow, body, (count,),
        [pl.BlockSpec((tokens, width), lambda s, _: (0, s)), full((tokens, D)), full((8, D))] + [ANY] * 10,
        [full((tokens, D)), full((tokens, D)), full((tokens, 128))],
        [sds((tokens, D), F32), sds((tokens, D), BF16), sds((tokens, 128), F32)],
        piece_shapes(width) + [pltpu.VMEM((tokens, D), F32)], [act, prev, vec, *weight], 2 * tokens * D * FF,
        2 * (D * FF + tokens * (5 * D + FF)), "down_norm",
    )


def units_back(flow, grad, weight, matrix, slope, count):
    tokens = grad.shape[0]
    width = FF // count

    def body(scal_ref, grad_ref, slope_ref, *refs):
        pieces, (out_ref, sum_ref, buffer, sems) = refs[:10], refs[10:]
        s = pl.program_id(0)
        stream = Streamed(pieces, matrix, buffer, sems, scal_ref)
        stream.turn(s, count)
        stream.wait(s)
        slot = lax.rem(s, 2)
        sums = {}
        for rows, cols in tiles(tokens, width):
            low = (mm(grad_ref[rows, :], buffer[slot, :, cols]) * slope_ref[rows, cols].astype(F32)).astype(BF16)
            out_ref[rows, cols] = low
            part = fold_rows(low.astype(F32))
            sums[cols.start] = sums[cols.start] + part if cols.start in sums else part
            if rows.start > 0:
                sum_ref[0, :, cols] = jnp.sum(sums[cols.start], 0, keepdims=True)

    column = pl.BlockSpec((tokens, width), lambda s, _: (0, s))
    return call(
        flow, body, (count,), [full((tokens, D)), column] + [ANY] * 10,
        [column, pl.BlockSpec((1, 1, width), lambda s, scal_ref: (scal_ref[S_Z] ^ away(s), 0, 0))],
        [sds((tokens, FF), BF16), sds((count, 1, width), F32)], piece_shapes(width), [grad, slope, *weight],
        2 * tokens * D * FF, 2 * (D * FF + tokens * (D + 2 * FF)), "units_back",
    )


def up_back(flow, gu, weight, matrix, residual, normed, inverse, gain, count):
    tokens = residual.shape[0]
    width = FF // count

    def body(scal_ref, gu_ref, res_ref, n_ref, inv_ref, gain_ref, *refs):
        pieces, (g_ref, low_ref, sums_ref, buffer, sems, acc) = refs[:10], refs[10:]
        s = pl.program_id(0)
        stream = Streamed(pieces, matrix, buffer, sems, scal_ref)
        stream.turn(s, count)
        stream.wait(s)
        value = mm(gu_ref[...], buffer[lax.rem(s, 2)], NT)

        @pl.when(s == 0)
        def _():
            acc[...] = value

        @pl.when(s > 0)
        def _():
            acc[...] += value

        @pl.when(s == count - 1)
        def _():
            norm_backward(
                lambda rows: res_ref[rows, :] + acc[rows, :], tokens, n_ref, inv_ref, gain_ref, g_ref, low_ref, sums_ref
            )

    return call(
        flow, body, (count,),
        [pl.BlockSpec((tokens, width), lambda s, _: (0, s)), full((tokens, D)), full((tokens, D)), full((tokens, 128)),
         full((8, D))] + [ANY] * 10,
        [full((tokens, D)), full((tokens, D)), full((8, D))],
        [sds((tokens, D), F32), sds((tokens, D), BF16), sds((8, D), F32)],
        piece_shapes(width) + [pltpu.VMEM((tokens, D), F32)], [gu, residual, normed, inverse, gain, *weight],
        2 * tokens * D * FF, 2 * (D * FF + tokens * (8 * D + FF)), "up_back",
    )


def norm_back(flow, grad, normed, inverse, gain):
    tokens = grad.shape[0]

    def body(scal_ref, grad_ref, n_ref, inv_ref, gain_ref, g_ref, low_ref, sums_ref):
        norm_backward(
            lambda rows: grad_ref[rows, :].astype(F32), tokens, n_ref, inv_ref, gain_ref, g_ref, low_ref, sums_ref
        )

    return call(
        flow, body, (1,), [full((tokens, D)), full((tokens, D)), full((tokens, 128)), full((8, D))],
        [full((tokens, D)), full((tokens, D)), full((8, D))],
        [sds((tokens, D), F32), sds((tokens, D), BF16), sds((8, D), F32)], [], [grad, normed, inverse, gain],
        20 * tokens * D, 12 * tokens * D, "norm_back",
    )


def sum_norm_back(flow, residual, parts, normed, inverse, gain):
    tokens = residual.shape[0]

    def body(scal_ref, res_ref, *refs):
        part_refs, (n_ref, inv_ref, gain_ref, g_ref, low_ref, sums_ref) = refs[: len(parts)], refs[len(parts) :]

        def grad(rows):
            total = part_refs[0][rows, :].astype(F32)
            for part in part_refs[1:]:
                total = total + part[rows, :].astype(F32)
            return res_ref[rows, :] + total

        norm_backward(grad, tokens, n_ref, inv_ref, gain_ref, g_ref, low_ref, sums_ref)

    return call(
        flow, body, (1,), [full((tokens, D))] * (2 + len(parts)) + [full((tokens, 128)), full((8, D))],
        [full((tokens, D)), full((tokens, D)), full((8, D))],
        [sds((tokens, D), F32), sds((tokens, D), BF16), sds((8, D), F32)], [],
        [residual, *parts, normed, inverse, gain], 20 * tokens * D, 22 * tokens * D, "sum_norm_back",
    )


def turn_rows(scal_ref, x_ref, turned, core):
    for r in range(4):
        row = ((scal_ref[S_Q] ^ r) * 2 + core) * ROWS
        turned[r * ROWS : (r + 1) * ROWS, :] = x_ref[:, pl.ds(pl.multiple_of(row, ROWS), ROWS)].T


def unit_grads(flow, down, up, received, count, sibling):
    tokens = down[0].shape[0]
    width = down[1].shape[1] // count
    half = count // 2
    steps = 2 * count

    def body(scal_ref, x0_ref, y0_ref, x1_ref, y1_ref, *refs):
        turned, t = refs[-1], pl.program_id(0)
        m, s = t // count, lax.rem(t, count)
        core = scal_ref[S_C] ^ 1 if sibling else scal_ref[S_C]

        @pl.when(t == 0)
        def _():
            turn_rows(scal_ref, x0_ref, turned, core)

        @pl.when(t == count)
        def _():
            turn_rows(scal_ref, x1_ref, turned, core)

        def store(y_ref):
            value = mm(turned[...], y_ref[...]).reshape(4, ROWS, width)
            if sibling:
                refs[0][:, 0] = value.astype(BF16)
                return
            if received is not None:
                value = value + refs[0][:, 0].astype(F32)
            value = value.astype(BF16)
            own, to_x, to_y, rest_x, rest_y = refs[-6:-1]
            own[t] = value[0]

            @pl.when(s < half)
            def _():
                to_x[t] = value[1]
                to_x[half + t] = value[3]
                rest_y[m * half + s] = value[2]

            @pl.when(s >= half)
            def _():
                rest_x[m * half + s - half] = value[1]
                to_y[t - half] = value[2]
                to_y[t] = value[3]

        @pl.when(m == 0)
        def _():
            store(y0_ref)

        @pl.when(m == 1)
        def _():
            store(y1_ref)

    left = full((tokens, D))
    specs = [left, pl.BlockSpec((tokens, width), lambda t, _: (0, jnp.minimum(t, count - 1))),
             left, pl.BlockSpec((tokens, width), lambda t, _: (0, jnp.maximum(t - count, 0)))]
    args = [*down, *up]
    one = pl.BlockSpec((4, 1, ROWS, width), lambda t, _: (0, t, 0, 0))
    if sibling:
        out_specs, out_shape = one, sds((4, steps, ROWS, width), BF16)
    else:
        if received is not None:
            specs.append(one)
            args.append(received)
        shapes = [(steps, ROWS, width)] * 3 + [(count, ROWS, width)] * 2
        out_specs, out_shape = [full(shape) for shape in shapes], [sds(shape, BF16) for shape in shapes]
    return call(
        flow, body, (steps,), specs, out_specs, out_shape, [pltpu.VMEM((4 * ROWS, tokens), BF16)], args,
        0, 0, "grads_theirs" if sibling else "grads_mine",
    )


def fetch_heads_weight(scal_ref, pieces, cols, buffer, sems):
    copies = []
    for r in range(4):
        for k in range(2):
            row = ((scal_ref[S_Q] ^ r) * 2 + (scal_ref[S_ZH] ^ k)) * ROWS
            copies.append(
                pltpu.make_async_copy(
                    pieces[r].at[k, :, cols], buffer.at[pl.ds(pl.multiple_of(row, ROWS), ROWS), :], sems.at[2 * r + k]
                )
            )
    for copy in copies:
        copy.start()
    for copy in copies:
        copy.wait()


def by_member(shape):
    return pl.BlockSpec((1,) + shape, lambda r, scal_ref: (scal_ref[S_P] ^ r, 0, 0))


def heads_weight_scratch(width):
    return [pltpu.VMEM((D, width), BF16), pltpu.SemaphoreType.DMA((8,))]


def project_in(flow, lefts, weight, cols, bias, name):
    count = len(lefts)
    tokens = lefts[0].shape[0]
    width = cols.stop - cols.start

    def body(scal_ref, *refs):
        left_refs, refs = refs[:count], refs[count:]
        if bias is not None:
            bias_ref, refs = refs[0], refs[1:]
        pieces, (out_ref, buffer, sems) = refs[:4], refs[4:]
        step = pl.program_id(0)

        @pl.when(step == 0)
        def _():
            fetch_heads_weight(scal_ref, pieces, cols, buffer, sems)

        for r, left in enumerate(left_refs):

            @pl.when(step == r)
            def _(left=left):
                value = mm(left[...], buffer[...])
                if bias is not None:
                    value = value + bias_ref[...]
                out_ref[0] = value.astype(BF16)

    extra, extra_specs = ([], []) if bias is None else ([bias], [full((1, width))])
    return call(
        flow, body, (count,), [full((tokens, D))] * count + extra_specs + [ANY] * 4, by_member((tokens, width)),
        sds((count, tokens, width), BF16), heads_weight_scratch(width), [*lefts, *extra, *weight],
        2 * tokens * D * width * count, 2 * (D * width + count * tokens * (D + width)), name,
    )


def project_out(flow, blocks, weight, cols, name):
    count, tokens, width = blocks.shape

    def body(scal_ref, block_ref, *refs):
        pieces, outs, (buffer, sems) = refs[:4], refs[4 : 4 + count], refs[4 + count :]
        step = pl.program_id(0)

        @pl.when(step == 0)
        def _():
            fetch_heads_weight(scal_ref, pieces, cols, buffer, sems)

        for r, out in enumerate(outs):

            @pl.when(step == r)
            def _(out=out):
                out[...] = mm(block_ref[0], buffer[...], NT).astype(BF16)

    return call(
        flow, body, (count,), [by_member((tokens, width))] + [ANY] * 4, [full((tokens, D))] * count,
        [sds((tokens, D), BF16)] * count, heads_weight_scratch(width), [blocks, *weight],
        2 * tokens * D * width * count, 2 * (D * width + count * tokens * (D + width)), name,
    )


def heads_grad(flow, xs, gqkv, gas, ctx):
    count, tokens, width = gqkv.shape
    out_width = ctx.shape[2]

    def body(scal_ref, *refs):
        x_refs, refs = refs[:count], refs[count:]
        ga_refs, refs = refs[:count], refs[count:]
        g_ref, ctx_ref = refs[:2]
        outs, (sum_ref, acc, acc_out) = refs[2:6], refs[6:]
        step = pl.program_id(0)
        for r in range(count):

            @pl.when(step == r)
            def _(r=r):
                value = mm(x_refs[r][...].T, g_ref[0])
                value_out = mm(ga_refs[r][...].T, ctx_ref[0])
                sums = jnp.sum(g_ref[0].astype(F32), 0, keepdims=True)
                if r == 0:
                    acc[...] = value
                    acc_out[...] = value_out
                    sum_ref[...] = sums
                else:
                    acc[...] += value
                    acc_out[...] += value_out
                    sum_ref[...] += sums

        @pl.when(step == count - 1)
        def _():
            for r in range(4):
                for k in range(2):
                    row = ((scal_ref[S_Q] ^ r) * 2 + (scal_ref[S_ZH] ^ k)) * ROWS
                    rows = pl.ds(pl.multiple_of(row, ROWS), ROWS)
                    outs[r][k, :, :width] = acc[rows, :].astype(BF16)
                    outs[r][k, :, width:] = acc_out[rows, :].astype(BF16)

    shape = (2, ROWS, width + out_width)
    return call(
        flow, body, (count,), [full((tokens, D))] * (2 * count) + [by_member((tokens, width)), by_member((tokens, out_width))],
        [full(shape)] * 4 + [full((1, width))], [sds(shape, BF16)] * 4 + [sds((1, width), F32)],
        [pltpu.VMEM((D, width), F32), pltpu.VMEM((D, out_width), F32)], [*xs, *gas, gqkv, ctx],
        2 * tokens * D * (width + out_width) * count, 4 * count * tokens * (D + width), "heads_grad",
    )


def reach(ends_ref, row):
    first = jnp.zeros_like(row)
    for index in range(3):
        first = jnp.where(row >= ends_ref[index], ends_ref[index], first)
    last = jnp.full_like(row, SEQLEN)
    for index in (2, 1, 0):
        last = jnp.where(row < ends_ref[index], ends_ref[index], last)
    return jnp.maximum(first, row - (WINDOW - 1)), jnp.minimum(last, row + WINDOW)


def over_keys(ends_ref, start, chunk, block):
    low_first, high_first = reach(ends_ref, start)
    low_last, high_last = reach(ends_ref, start + BQ - 1)
    low_row, high_row = reach(ends_ref, start + lax.broadcasted_iota(jnp.int32, (1, BQ), 1))

    def one(b, carry):
        open_all = (b * chunk >= low_last) & ((b + 1) * chunk <= high_first)

        @pl.when(open_all)
        def _():
            block(b, None)

        @pl.when(jnp.logical_not(open_all))
        def _():
            key = b * chunk + lax.broadcasted_iota(jnp.int32, (chunk, BQ), 0)
            block(b, (key >= low_row) & (key < high_row))

        return carry

    lax.fori_loop(low_first // chunk, (high_last + chunk - 1) // chunk, one, 0)


def attend_forward(flow, ends, qkv):
    count, chunk, width3 = qkv.shape
    width = width3 // 3
    heads = width // HD
    steps = SEQLEN // BQ
    per = chunk // BQ

    def body(ends_ref, qkv_ref, ctx_ref, wide_ref, lse_ref, qh, kh, vt, acc, tops, sums, scores):
        step = pl.program_id(0)

        @pl.when(step == 0)
        def _():
            for j in range(count):
                rows = slice(j * chunk, (j + 1) * chunk)
                for h in range(heads):
                    qh[h, rows, :] = qkv_ref[j, :, h * HD : (h + 1) * HD] * BF16(HD**-0.5)
                    kh[h, rows, :] = qkv_ref[j, :, width + h * HD : width + (h + 1) * HD]
                vt[j] = qkv_ref[j, :, 2 * width :].T

        start = step * BQ
        rows = pl.ds(pl.multiple_of(start, BQ), BQ)
        acc[...] = jnp.zeros(acc.shape, F32)
        tops[...] = jnp.full(tops.shape, -3.0e38, F32)
        sums[...] = jnp.zeros(sums.shape, F32)

        def score(b, allowed):
            keys = pl.ds(pl.multiple_of(b * chunk, chunk), chunk)
            for h in range(heads):
                value = mm(kh[h, keys, :], qh[h, rows, :], NT)
                if allowed is not None:
                    value = jnp.where(allowed, value, FILL)
                scores[h, b] = value
                tops[h] = jnp.maximum(tops[h], jnp.max(value.reshape(-1, 8, BQ), 0))

        over_keys(ends_ref, start, chunk, score)
        top = [jnp.max(tops[h], 0, keepdims=True) for h in range(heads)]

        def weigh(b, carry):
            for h in range(heads):
                part = slice(h * HD, (h + 1) * HD)
                weight = jnp.exp(scores[h, b] - top[h])
                sums[h] += fold_rows(weight)
                acc[part, :] += mm(vt[b, part, :], weight.astype(BF16))
            return carry

        low_first, _ = reach(ends_ref, start)
        _, high_last = reach(ends_ref, start + BQ - 1)
        lax.fori_loop(low_first // chunk, (high_last + chunk - 1) // chunk, weigh, 0)
        for h in range(heads):
            part = slice(h * HD, (h + 1) * HD)
            total = jnp.sum(sums[h], 0, keepdims=True)
            wide_ref[part, :] = acc[part, :] / total
            lse_ref[h : h + 1, :] = top[h] + jnp.log(total)
        lse_ref[heads:, :] = jnp.zeros((8 - heads, BQ), F32)
        ctx_ref[0] = wide_ref[...].T.astype(BF16)

    pairs = SEQLEN * SEQLEN
    return call(
        flow, body, (steps,), [full((count, chunk, width3))],
        [pl.BlockSpec((1, BQ, width), lambda i, _: (i // per, i % per, 0)),
         pl.BlockSpec((width, BQ), lambda i, _: (0, i)), pl.BlockSpec((8, BQ), lambda i, _: (0, i))],
        [sds((count, chunk, width), BF16), sds((width, SEQLEN), F32), sds((8, SEQLEN), F32)],
        [
            pltpu.VMEM((heads, SEQLEN, HD), BF16),
            pltpu.VMEM((heads, SEQLEN, HD), BF16),
            pltpu.VMEM((count, width, chunk), BF16),
            pltpu.VMEM((width, BQ), F32),
            pltpu.VMEM((heads, 8, BQ), F32),
            pltpu.VMEM((heads, 8, BQ), F32),
            pltpu.VMEM((heads, count, chunk, BQ), F32),
        ],
        [qkv], 16 * pairs * heads * HD, 6 * SEQLEN * width * 2, "attend_forward", (ends,),
    )


def attend_backward(flow, ends, qkv, grads, wide, lse):
    count, chunk, width3 = qkv.shape
    width = width3 // 3
    heads = width // HD
    steps = SEQLEN // BQ
    per = chunk // BQ

    def body(ends_ref, qkv_ref, grad_ref, wide_ref, lse_ref, out_ref, qh, kh, vh, gh, kt, qt, gt, gq, gk, gv):
        step = pl.program_id(0)

        @pl.when(step == 0)
        def _():
            for j in range(count):
                rows = slice(j * chunk, (j + 1) * chunk)
                for h in range(heads):
                    cols = slice(h * HD, (h + 1) * HD)
                    qh[h, rows, :] = qkv_ref[j, :, cols] * BF16(HD**-0.5)
                    kh[h, rows, :] = qkv_ref[j, :, width + h * HD : width + (h + 1) * HD]
                    vh[h, rows, :] = qkv_ref[j, :, 2 * width + h * HD : 2 * width + (h + 1) * HD]
                    gh[h, rows, :] = grad_ref[j, :, cols]
                kt[j] = qkv_ref[j, :, width : 2 * width].T
                for s in range(per):
                    sub = slice(s * BQ, (s + 1) * BQ)
                    qt[j * per + s] = (qkv_ref[j, sub, :width] * BF16(HD**-0.5)).T
                    gt[j * per + s] = grad_ref[j, sub, :].T
            gk[...] = jnp.zeros(gk.shape, F32)
            gv[...] = jnp.zeros(gv.shape, F32)

        start = step * BQ
        rows = pl.ds(pl.multiple_of(start, BQ), BQ)
        gq[...] = jnp.zeros(gq.shape, F32)
        inner = []
        for h in range(heads):
            part = slice(h * HD, (h + 1) * HD)
            inner.append(jnp.sum(gt[step, part, :].astype(F32) * wide_ref[part, :], 0, keepdims=True))

        def block(b, allowed):
            keys = pl.ds(pl.multiple_of(b * chunk, chunk), chunk)
            for h in range(heads):
                part = slice(h * HD, (h + 1) * HD)
                score = mm(kh[h, keys, :], qh[h, rows, :], NT)
                grad_weight = mm(vh[h, keys, :], gh[h, rows, :], NT)
                if allowed is not None:
                    score = jnp.where(allowed, score, FILL)
                weight = jnp.exp(score - lse_ref[h : h + 1, :])
                grad_score = (weight * (grad_weight - inner[h])).astype(BF16)
                gv[b, part, :] += mm(gt[step, part, :], weight.astype(BF16), NT)
                gk[b, part, :] += mm(qt[step, part, :], grad_score, NT)
                gq[part, :] += mm(kt[b, part, :], grad_score)

        over_keys(ends_ref, start, chunk, block)
        out_ref[step // per, pl.ds(pl.multiple_of((step % per) * BQ, BQ), BQ), :width] = (
            (gq[...] * HD**-0.5).T.astype(BF16)
        )

        @pl.when(step == steps - 1)
        def _():
            for j in range(count):
                out_ref[j, :, width : 2 * width] = gk[j].T.astype(BF16)
                out_ref[j, :, 2 * width :] = gv[j].T.astype(BF16)

    pairs = SEQLEN * SEQLEN
    return call(
        flow, body, (steps,),
        [full((count, chunk, width3)), full((count, chunk, width)), pl.BlockSpec((width, BQ), lambda i, _: (0, i)),
         pl.BlockSpec((8, BQ), lambda i, _: (0, i))],
        full((count, chunk, width3)), sds((count, chunk, width3), BF16),
        [pltpu.VMEM((heads, SEQLEN, HD), BF16)] * 4
        + [
            pltpu.VMEM((count, width, chunk), BF16),
            pltpu.VMEM((steps, width, BQ), BF16),
            pltpu.VMEM((steps, width, BQ), BF16),
            pltpu.VMEM((width, BQ), F32),
            pltpu.VMEM((count, width, chunk), F32),
            pltpu.VMEM((count, width, chunk), F32),
        ],
        [qkv, grads, wide, lse], 28 * pairs * heads * HD, 20 * SEQLEN * width, "attend_backward", (ends,),
    )


def flip(values_in, axes, mask):
    return lax.ppermute(values_in, axes, [(a, a ^ mask) for a in range(lax.axis_size(axes))])


def turn(values_in):
    return lax.ppermute(values_in, ("c", "zh"), [(2 * a + b, 2 * b + a) for a in range(2) for b in range(2)])


def cross(values_in):
    return lax.ppermute(values_in, ("c", "zh"), [(2 * a + b, 2 * b + 1 - a) for a in range(2) for b in range(2)])


def uncross(values_in):
    return lax.ppermute(values_in, ("c", "zh"), [(2 * b + 1 - a, 2 * a + b) for a in range(2) for b in range(2)])


def from_members(values_in, axes):
    return [values_in] + [flip(values_in, axes, r) for r in range(1, lax.axis_size(axes))]


def to_members(parts, axes):
    return [parts[0]] + [flip(part, axes, r) for r, part in enumerate(parts) if r > 0]


def add(*parts):
    total = parts[0].astype(F32)
    for part in parts[1:]:
        total = total + part.astype(F32)
    return total


def is_small():
    return lax.axis_size("q") == 4


def order_by(values_in, axis, position, count):
    bit = 1
    while bit < count:
        shape = values_in.shape
        split = shape[:axis] + (count // (2 * bit), 2, bit) + shape[axis + 1 :]
        cut = values_in.reshape(split)
        values_in = jnp.where((position & bit) != 0, jnp.flip(cut, axis + 1), cut).reshape(shape)
        bit *= 2
    return values_in


def all_heads_weight(shard, zh):
    pair = jnp.stack([turn(shard), cross(shard)])
    every = order_by(lax.all_gather(pair, "q"), 1, zh, 2).reshape(4, 2, ROWS, -1)
    return [every[r] for r in range(4)]


def sum_heads_grad(buckets, zh):
    if is_small():
        got = to_members(buckets, "q")
        return [add(*(member[k] for member in got)).astype(BF16) for k in range(2)]
    every = jnp.stack(buckets).reshape(lax.axis_size("q"), 2, -1, buckets[0].shape[-1])
    rows = order_by(lax.psum_scatter(every, "q", scatter_dimension=0, tiled=False), 0, zh, 2)
    return [rows[0], rows[1]]


SLOTS = (0, 2, 1, 3)


def all_units_weight(shard):
    matrices, _, width = shard.shape
    members = lax.axis_size(MODEL)
    every = lax.all_gather(shard, ALL).reshape(members, -1, matrices, shard.shape[1], width).transpose(0, 2, 1, 3, 4)
    every = every.reshape(members, matrices, 4, 2, ROWS, width)
    every = jnp.stack([every[slot] for slot in SLOTS])
    pieces = []
    for k in range(2):
        pieces += [every[:, :, r, k] for r in range(3)] + [every[:2, :, 3, k], every[2:, :, 3, k]]
    return pieces


class UnitsWeight:
    def __init__(self, shard):
        self.shard = shard

    def far_z(self):
        self.two = jnp.stack([self.shard, flip(self.shard, "zh", 1)])

    def near_z(self):
        self.own = jnp.concatenate([self.two, flip(self.two, "zl", 1)])

    def near(self):
        self.near_x, self.near_y = flip(self.own, "q", 1), flip(self.own, "q", 2)

    def far(self):
        self.far_a, self.far_b = flip(self.near_y[:2], "q", 1), flip(self.near_x[2:], "q", 2)

    def pieces(self):
        mine = [self.own, self.near_x, self.near_y, self.far_a, self.far_b]
        return mine + [flip(piece, "c", 1) for piece in mine]


class UnitsGrads:
    def __init__(self, flow, down, up, count):
        self.flow, self.down, self.up, self.count = flow, down, up, count

    def sibling(self):
        self.theirs = unit_grads(self.flow, self.down, self.up, None, self.count, True)
        self.got = flip(self.theirs, "c", 1) if is_small() else None

    def mine(self):
        made = unit_grads(self.flow, self.down, self.up, self.got, self.count, False)
        self.made = made
        self.own, self.to_x, self.to_y, self.rest_x, self.rest_y = (
            part.reshape(2, -1, ROWS, part.shape[-1]) for part in made
        )

    def near(self):
        self.from_x, self.from_y = flip(self.to_x, "q", 1), flip(self.to_y, "q", 2)
        return [self.from_x, self.from_y]

    def far(self):
        half = self.count // 2
        self.late_x = flip(add(self.rest_x, self.from_y[:, half:]).astype(BF16), "q", 1)
        self.late_y = flip(add(self.rest_y, self.from_x[:, half:]).astype(BF16), "q", 2)
        return [self.late_x, self.late_y]

    def near_z(self):
        half = self.count // 2
        self.here = add(self.own[:, :half], self.from_x[:, :half], self.late_y)
        self.there = flip(add(self.own[:, half:], self.late_x, self.from_y[:, :half]).astype(BF16), "zl", 1)
        return [self.there]

    def far_z(self):
        both = self.here + self.there.astype(F32)
        self.stays, self.last = both[:, 0], flip(both[:, 1].astype(BF16), "zh", 1)
        return [self.last]

    def total(self):
        if is_small():
            return self.stays + self.last.astype(F32)
        half = self.count // 2
        mine = jnp.stack(
            [self.own, jnp.concatenate([self.to_x[:, :half], self.rest_x], 1),
             jnp.concatenate([self.rest_y, self.to_y[:, :half]], 1),
             jnp.concatenate([self.to_x[:, half:], self.to_y[:, half:]], 1)]
        )
        theirs = self.theirs.reshape(4, 2, self.count, ROWS, -1)
        every = jnp.stack([mine, theirs], axis=2)
        every = every.transpose(3, 0, 2, 4, 1, 5)
        every = jnp.stack([every[slot] for slot in SLOTS]).reshape(-1, 2, mine.shape[-1])
        return lax.psum_scatter(every, ALL, scatter_dimension=0, tiled=True).astype(F32).transpose(1, 0, 2)


SMALL_AXES = ("q", MODEL, "c")


def gather_small(shard, where):
    tz, dp = lax.axis_size(MODEL), lax.axis_size(("q", "c"))
    if not is_small():
        return lax.all_gather(shard, ALL).reshape(tz, dp, -1)
    every = shard.reshape(1, -1)
    for axes in SMALL_AXES:
        every = jnp.stack(from_members(every, axes))
    every = every.reshape(2, 4, 4, -1)
    for axis, position in enumerate(where[::-1]):
        every = order_by(every, axis, position, every.shape[axis])
    return every.transpose(1, 2, 0, 3).reshape(tz, dp, -1)


def scatter_small(values_in, where):
    if not is_small():
        return lax.psum_scatter(values_in.reshape(-1, values_in.shape[-1]), ALL, scatter_dimension=0, tiled=True)[0]
    every = values_in.reshape(4, 4, 2, -1).transpose(1, 0, 2, 3)
    for axis, position in enumerate(where):
        every = order_by(every, axis, position, every.shape[axis])
    for axes in SMALL_AXES:
        every = add(*to_members([every[r] for r in range(every.shape[0])], axes))
    return every


def sum_all(value):
    if not is_small():
        return lax.psum(value, ALL)
    value = jnp.broadcast_to(value, (8, 128))
    for axes in SMALL_AXES:
        parts = jnp.stack(from_members(value, axes))
        value = jnp.sum(order_by(parts, 0, lax.axis_index(axes), parts.shape[0]), 0)
    return value[0, 0]


def finish(above, arrived, zh):
    units, buckets = above
    if arrived is None:
        halves = sum_heads_grad(buckets, zh)
        arrived = [turn(halves[0]), uncross(halves[1])]
    d_heads = add(*arrived)
    rows, cols = d_heads.shape[0], d_heads.shape[1] * 3 // 4
    down_up = units.total()
    return d_heads[:, :cols].reshape(rows, 3, -1).transpose(1, 0, 2), d_heads[:, cols:], down_up[1], down_up[0]


def on_device(
    tokens, doc_lengths, qkv_weight, qv_bias, out_weight, up_weight, up_bias, down_weight, gains, shifts, cotangent
):
    layers = qkv_weight.shape[0]
    tz, dp = lax.axis_size(MODEL), lax.axis_size(("q", "c"))
    place, zh = lax.axis_index(GROUP), lax.axis_index("zh")
    where = (lax.axis_index("q"), lax.axis_index(MODEL), lax.axis_index("c"))
    if is_small():
        spots = [place, where[0], where[2], zh, where[1]]
    else:
        spots = [place] + [jnp.zeros((), jnp.int32)] * 4
    scal = jnp.stack([spot.astype(jnp.int32) for spot in spots])

    flow = Flow(scal)
    small_slice = is_small()
    qkv_cols = 3 * out_weight.shape[2]
    heads_shard = [
        jnp.concatenate([qkv_weight[l].transpose(1, 0, 2).reshape(-1, qkv_cols), out_weight[l]], axis=1)
        for l in range(layers)
    ]
    x_low = turn(tokens)
    ends = jnp.cumsum(turn(doc_lengths)[0], dtype=jnp.int32)
    units_shard = [up_weight[0][None], down_weight[0][None], jnp.stack([up_weight[1], down_weight[1]])]
    if small_slice:
        pair = jnp.stack([turn(heads_shard[0]), cross(heads_shard[0])])
        up0, down0, both1 = (UnitsWeight(shard) for shard in units_shard)
        up0.far_z()
        flow.wait(x_low, pair)
        flow.hold(down0=down0.shard, both1=both1.shard, heads1=heads_shard[1], top=cotangent, low=x_low, two=up0.two)
        gate(flow)
        x_low, up0.two, down0.shard = flow.free("low"), flow.free("two"), flow.free("down0")
        heads_weight = [from_members(pair, "q")]
        up0.near_z()
        down0.far_z()
    else:
        heads_weight = [all_heads_weight(shard, zh) for shard in heads_shard]
        every = [all_units_weight(shard) for shard in units_shard]
        units_weight = [((every[0], 0), (every[1], 0)), ((every[2], 0), (every[2], 1))]
        top_grad = turn(cotangent)

    pieces = [qv_bias, up_bias, gains, shifts]
    sizes = [piece.size // layers for piece in pieces]
    small = jnp.concatenate([piece.reshape(layers, -1) for piece in pieces], axis=1)
    small_all = gather_small(small.reshape(-1), where).reshape(tz, dp, layers, -1).astype(F32)
    cuts = [0]
    for size in sizes:
        cuts.append(cuts[-1] + size)
    parts = [small_all[..., cuts[i] : cuts[i + 1]] for i in range(4)]
    hz = qv_bias.shape[2]
    qv_here = lax.dynamic_index_in_dim(parts[0], place, 0, False)
    qv_here = qv_here.reshape(dp, layers, 2, hz, -1).transpose(1, 2, 3, 0, 4).reshape(layers, 2, -1)
    bias_qkv = jnp.concatenate([qv_here[:, :1], jnp.zeros_like(qv_here[:, :1]), qv_here[:, 1:]], axis=1)
    bias_qkv = bias_qkv.reshape(layers, 1, -1)
    up_bias_full = parts[1].reshape(tz, dp, layers, up_bias.shape[1], -1).transpose(2, 0, 3, 1, 4)
    up_bias_full = up_bias_full.reshape(layers, tz, 1, -1)
    gain_full = parts[2].reshape(tz, dp, layers, 2, -1).transpose(2, 3, 1, 0, 4).reshape(layers, 2, D)
    shift_full = parts[3].reshape(tz, dp, layers, 4, -1).transpose(2, 3, 1, 0, 4).reshape(layers, 4, D)

    in_cols, out_cols = slice(0, qkv_cols), slice(qkv_cols, qkv_cols + out_weight.shape[2])

    one, zero = jnp.ones((D,), F32), jnp.zeros((D,), F32)
    pad = [zero, zero, zero]
    prev, prev_gain, prev_shift = x_low.astype(F32), one, zero
    kept = []
    for l in range(layers):
        xs = from_members(x_low, GROUP)
        if small_slice and l == 0:
            flow.wait(up0.own)
            flow.hold(down0=down0.two)
        if small_slice and l == 1:
            flow.wait(*xs, *heads_members)
            gate(flow)
            both1.own = flow.free("both1")
            both1.near()
            heads_weight.append(heads_members)
        w_heads = heads_weight[l]
        qkv = project_in(flow, xs, w_heads, in_cols, bias_qkv[l], "project_qkv")
        if small_slice and l == 0:
            up0.near()
            down0.two, both1.shard = flow.free("down0"), flow.free("both1")
            down0.near_z()
            both1.far_z()
        if small_slice and l == 1:
            top_grad = turn(flow.free("top"))
        ctx, wide, lse = attend_forward(flow, ends, qkv)
        if small_slice and l == 0:
            flow.wait(up0.near_x, up0.near_y, down0.own, both1.two)
            flow.hold(both1=both1.two)
            up0.far()
            down0.near()
        if small_slice and l == 1:
            flow.wait(both1.near_x, both1.near_y, top_grad)
            both1.far()
        attn = to_members(project_out(flow, ctx, w_heads, out_cols, "project_attn"), GROUP)
        if small_slice and l == 0:
            w_up = (up0.pieces(), 0)
            flow.wait(*attn[1:], *w_up[0], down0.near_x, down0.near_y)
            gate(flow)
            both1.two, shard = flow.free("both1"), flow.free("heads1")
            both1.near_z()
            down0.far()
            pair = jnp.stack([turn(shard), cross(shard)])
        elif small_slice:
            every = both1.pieces()
            w_up, w_down = (every, 0), (every, 1)
        else:
            w_up, w_down = units_weight[l]
        vec = jnp.stack([prev_gain, prev_shift, shift_full[l, 0], gain_full[l, 0], shift_full[l, 1]] + pad)
        n1, hs, r1, act, slope = norm_up(flow, prev, attn, vec, *w_up, up_bias_full[l], tz)
        if small_slice and l == 0:
            w_down = (down0.pieces(), 0)
            flow.wait(both1.own, pair)
            flow.hold(both1=both1.own)
            heads_members = from_members(pair, "q")
        vec = jnp.stack([gain_full[l, 0], shift_full[l, 1], shift_full[l, 2], gain_full[l, 1], shift_full[l, 3]] + pad)
        n2, y_low, r2 = down_norm(flow, act, *w_down, n1, vec, tz)
        kept.append((xs, qkv, ctx, wide, lse, n1, hs, r1, act, slope, n2, r2, w_heads, w_up, w_down))
        x_low, prev, prev_gain, prev_shift = y_low, n2, gain_full[l, 1], shift_full[l, 3]
    layer_output = turn(x_low)

    gain_rows = [[jnp.broadcast_to(gain_full[l, i], (8, D)) for i in range(2)] for l in range(layers)]
    g2, gf, sums2 = norm_back(flow, top_grad, kept[-1][10], kept[-1][11], gain_rows[-1][1])
    results = [None] * layers
    small_grads = [None] * layers
    above = None
    for l in reversed(range(layers)):
        xs, qkv, ctx, wide, lse, n1, hs, r1, act, slope, n2, r2, w_heads, w_up, w_down = kept[l]
        gu, up_bias_sum = units_back(flow, gf, *w_down, slope, tz)
        units = UnitsGrads(flow, (gf, act), (hs, gu), tz)
        if small_slice and l == layers - 1:
            flow.wait(layer_output)
        units.sibling()
        flow.wait(units.theirs)
        if small_slice and above is not None:
            flow.wait(*above[0].near_z())
            halves = sum_heads_grad(above[1], zh)
            flow.wait(*halves)
        g1, ga, sums1 = up_back(flow, gu, *w_up, g2, n1, r1, gain_rows[l][0], tz)
        gas = from_members(ga, GROUP)
        flow.wait(ga)
        units.mine()
        if small_slice:
            flow.wait(*units.made)
        if small_slice and above is not None:
            arrived = [turn(halves[0]), uncross(halves[1])]
            flow.wait(*above[0].far_z(), *arrived)
        gc = project_in(flow, gas, w_heads, out_cols, None, "project_gc")
        gqkv = attend_backward(flow, ends, qkv, gc, wide, lse)
        if small_slice:
            flow.wait(*units.near())
        back = project_out(flow, gqkv, w_heads, in_cols, "project_gx")
        flow.wait(back[0])
        back = to_members(back, GROUP)
        *buckets, qkv_sums = heads_grad(flow, xs, gqkv, gas, ctx)
        qv_sums = qkv_sums.reshape(3, hz, dp, -1)
        qv_sums = jnp.stack([qv_sums[0], qv_sums[2]]).transpose(2, 0, 1, 3).reshape(1, dp, -1)
        mine = (jnp.arange(tz) == place).astype(F32).reshape(tz, 1, 1)
        small_grads[l] = jnp.concatenate(
            [
                mine * qv_sums,
                up_bias_sum.reshape(tz, up_bias.shape[1], dp, -1).transpose(0, 2, 1, 3).reshape(tz, dp, -1),
                jnp.stack([sums1[0], sums2[0]]).reshape(2, dp, tz, -1).transpose(2, 1, 0, 3).reshape(tz, dp, -1),
                jnp.stack([sums1[2], sums1[1], sums2[2], sums2[1]])
                .reshape(4, dp, tz, -1).transpose(2, 1, 0, 3).reshape(tz, dp, -1),
            ],
            axis=-1,
        )
        if small_slice:
            late = units.far()
        if above is not None:
            results[l + 1] = finish(above, arrived if small_slice else None, zh)
        above = (units, buckets)
        if l > 0:
            flow.wait(buckets[0])
            if small_slice:
                flow.wait(*late)
            g2, gf, sums2 = sum_norm_back(flow, g1, back, kept[l - 1][10], kept[l - 1][11], gain_rows[l - 1][1])
        else:
            if small_slice:
                flow.wait(*back)
                flow.hold(small=jnp.stack(small_grads, axis=2).reshape(tz, dp, -1), **{f"b{r}": buckets[r] for r in (1, 2, 3)})
                gate(flow)
                small_sums = flow.free("small")
                buckets = buckets[:1] + [flow.free(f"b{r}") for r in (1, 2, 3)]
                above = (units, buckets)
            else:
                small_sums = jnp.stack(small_grads, axis=2).reshape(tz, dp, -1)
            input_grad = turn((g1 + add(*back)).astype(BF16))
            if small_slice:
                units.near_z()
                units.far_z()
                halves = sum_heads_grad(buckets, zh)
                arrived = [turn(halves[0]), uncross(halves[1])]
            results[l] = finish(above, arrived if small_slice else None, zh)

    small_out = scatter_small(small_sums, where).reshape(layers, -1)
    qkv_grad, out_grad, up_grad, down_grad = (jnp.stack([entry[i] for entry in results]) for i in range(4))
    qv_bias_grad = small_out[:, cuts[0] : cuts[1]].reshape(qv_bias.shape)
    up_bias_grad = small_out[:, cuts[1] : cuts[2]].reshape(up_bias.shape)
    gains_grad = small_out[:, cuts[2] : cuts[3]].reshape(gains.shape)
    shifts_grad = small_out[:, cuts[3] : cuts[4]].reshape(shifts.shape)
    all_grads = (qkv_grad, qv_bias_grad, out_grad, up_grad, up_bias_grad, down_grad, gains_grad, shifts_grad)
    local_squares = sum(jnp.sum(member * member) for member in all_grads)
    entry_count = LAYERS * (4 * D * D + 2 * D * FF + FF + 8 * D)
    grad_rms = jnp.sqrt(sum_all(local_squares) / entry_count)
    return (
        layer_output, input_grad, qkv_grad, qv_bias_grad, out_grad, up_grad, up_bias_grad, down_grad, gains_grad,
        shifts_grad, grad_rms,
    )


def solution(mesh):
    dp, tensor = mesh.shape["dp"], mesh.shape["tensor"]
    fine = Mesh(mesh.devices.reshape(dp // 2, 2, 2, tensor // 2), ("q", "c", "zh", "zl"))
    data, model = ("q", "c"), ("zh", "zl")
    both = data + model
    weight3, weight4 = P(None, data, model), P(None, None, data, model)
    in_specs = (
        P(both, None), P(data, None), weight4, P(None, None, model, data), weight3, weight3, P(None, model, data),
        weight3, P(None, None, both), P(None, None, both), P(both, None),
    )
    out_specs = (
        P(both, None), P(both, None), weight4, P(None, None, model, data), weight3, weight3, P(None, model, data),
        weight3, P(None, None, both), P(None, None, both), P(),
    )
    return jax.shard_map(on_device, mesh=fine, in_specs=in_specs, out_specs=out_specs, check_vma=False)
```

```python
import jax
import jax.numpy as jnp
from jax import lax
from jax.experimental import pallas as pl
from jax.experimental.pallas import tpu as pltpu
from jax.sharding import Mesh
from jax.sharding import PartitionSpec as P

D = 1024
HD = 64
HEADS = 16
FF = 4096
LAYERS = 2
SEQLEN = 2048
WINDOW = 1024
EPS = 1e-06
FILL = -1000000000.0

F32 = jnp.float32
BF16 = jnp.bfloat16
GROUP = ("c", "zl")
MODEL = ("zh", "zl")
ALL = ("zh", "zl", "q", "c")
VMEM_LIMIT = 56 * 1024 * 1024
TIMES = {
    "gate": 0.1, "norm_up": 20.0, "down_norm": 20.0, "units_back": 20.0, "up_back": 20.0, "norm_back": 6.0,
    "sum_norm_back": 20.0, "grads_theirs": 0.2, "grads_mine": 0.2, "project_qkv": 0.2, "project_gc": 0.2,
    "project_attn": 0.2, "project_gx": 0.2, "heads_grad": 0.2, "attend_forward": 40.0, "attend_backward": 60.0,
}
PEAK = 0.35e9
NT = (((1,), (1,)), ((), ()))
NN = (((1,), (0,)), ((), ()))
ROWS = 128
CHUNK = 64
BQ = 256


def mm(left, right, dims=NN):
    return lax.dot_general(left, right, dims, preferred_element_type=F32)


def full(shape):
    return pl.BlockSpec(shape, lambda *_: (0,) * len(shape))


ANY = pl.BlockSpec(memory_space=pl.ANY)


def sds(shape, kind):
    return jax.ShapeDtypeStruct(shape, kind)


class Flow:
    def __init__(self, scal):
        self.scal, self.before, self.held = scal, [], {}

    def wait(self, *arrays):
        self.before += arrays

    def hold(self, **arrays):
        self.held.update(arrays)

    def free(self, name):
        return self.held.pop(name)


def call(flow, body, grid, in_specs, out_specs, out_shape, scratch, args, flops, traffic, name, scalars=None):
    scalars = (flow.scal,) if scalars is None else scalars
    single = not isinstance(out_specs, (list, tuple))
    out_specs = [out_specs] if single else list(out_specs)
    out_shape = [out_shape] if single else list(out_shape)
    before, held = flow.before, list(flow.held.items())
    ns, nb, nh, no = len(scalars), len(before), len(held), len(out_specs)
    first, last = ns + nb + nh, ns + nb + nh + len(args) + no

    def wrapped(*refs):
        body(*refs[:ns], *refs[first:last], *refs[last + nh :])

    result = pl.pallas_call(
        wrapped,
        grid_spec=pltpu.PrefetchScalarGridSpec(
            num_scalar_prefetch=ns,
            grid=grid,
            in_specs=[ANY] * (nb + nh) + list(in_specs),
            out_specs=out_specs + [ANY] * nh,
            scratch_shapes=scratch,
        ),
        out_shape=out_shape + [sds(array.shape, array.dtype) for _, array in held],
        input_output_aliases={ns + nb + i: no + i for i in range(nh)},
        compiler_params=pltpu.CompilerParams(
            dimension_semantics=("arbitrary",) * len(grid), vmem_limit_bytes=VMEM_LIMIT
        ),
        cost_estimate=pl.CostEstimate(flops=int(TIMES[name] * PEAK), bytes_accessed=1024, transcendentals=0),
        name=name,
    )(*scalars, *before, *[array for _, array in held], *args)
    flow.before = []
    flow.held = {key: value for (key, _), value in zip(held, result[no:])}
    return result[0] if single else result[:no]


def gate(flow):
    if flow.held:
        call(flow, lambda *refs: None, (1,), [], [], [], [], [], 0, 0, "gate")


S_P, S_Q, S_C, S_ZH, S_Z = range(5)


def norm_rows(values_in):
    centred = values_in - jnp.mean(values_in, -1, keepdims=True)
    variance = jnp.mean(centred * centred, -1, keepdims=True)
    inverse = lax.rsqrt(variance + EPS)
    return centred * inverse, inverse


def norm_back_rows(grad, normed, inverse, gain):
    scaled = grad * gain
    centred = scaled - jnp.mean(scaled, -1, keepdims=True) - normed * jnp.mean(scaled * normed, -1, keepdims=True)
    return centred * inverse


def fold_rows(values_in):
    return jnp.sum(values_in.reshape(-1, 8, values_in.shape[-1]), 0)


def read(part, rows):
    return (part[0, rows, :] if len(part.shape) == 3 else part[rows, :]).astype(F32)


def part_spec(part):
    shape = part.shape
    return full(shape) if len(shape) == 2 else pl.BlockSpec((1,) + shape[1:], lambda *_: (0, 0, 0))


ONE, ZERO, TABLE = 0, 1, 16


def gain_row(layer, index):
    return 2 + 6 * layer + index


def shift_row(layer, index):
    return 4 + 6 * layer + index


def row_of(vec_ref, row):
    return vec_ref[row : row + 1, :]


def norm_forward(get_total, tokens, vec, gain, shift, n_ref, low_ref, inv_ref):

    def step(index, carry):
        rows = pl.ds(pl.multiple_of(index * CHUNK, CHUNK), CHUNK)
        normed, inverse = norm_rows(get_total(rows))
        n_ref[rows, :] = normed
        low_ref[rows, :] = (normed * row_of(vec, gain) + row_of(vec, shift)).astype(BF16)
        inv_ref[rows, :] = jnp.broadcast_to(inverse, (CHUNK, 128))
        return carry

    lax.fori_loop(0, tokens // CHUNK, step, 0)


def norm_backward(get_grad, tokens, n_ref, inv_ref, vec, gain, g_ref, low_ref, sums_ref):
    def step(index, carry):
        rows = pl.ds(pl.multiple_of(index * CHUNK, CHUNK), CHUNK)
        grad = get_grad(rows)
        normed = n_ref[rows, :]
        result = norm_back_rows(grad, normed, inv_ref[rows, 0:1], row_of(vec, gain))
        low = result.astype(BF16)
        g_ref[rows, :] = result
        low_ref[rows, :] = low
        return (
            carry[0] + fold_rows(grad * normed),
            carry[1] + fold_rows(grad),
            carry[2] + fold_rows(low.astype(F32)),
        )

    zero = jnp.zeros((8, D), F32)
    sums = lax.fori_loop(0, tokens // CHUNK, step, (zero, zero, zero))
    sums_ref[...] = jnp.zeros(sums_ref.shape, F32)
    for row, member in enumerate(sums):
        sums_ref[row : row + 1, :] = jnp.sum(member, 0, keepdims=True)


def away(s):
    return (s & 1) * 2 + s // 2


class Streamed:
    def __init__(self, refs, buffer, sems, scal):
        self.refs, self.buffer, self.sems, self.scal = refs, buffer, sems, scal

    def copies(self, s):
        slot = lax.rem(s, 2)
        for k, ref in enumerate(self.refs):
            for q in range(4):
                row = (2 * q + (self.scal[S_C] ^ k)) * ROWS
                yield pltpu.make_async_copy(
                    ref.at[s, q], self.buffer.at[slot, pl.ds(pl.multiple_of(row, ROWS), ROWS), :],
                    self.sems.at[slot, 4 * k + q],
                )

    def start(self, s):
        for copy in self.copies(s):
            copy.start()

    def wait(self, s):
        for copy in self.copies(s):
            copy.wait()

    def turn(self, s, count):
        @pl.when(s == 0)
        def _():
            self.start(s)

        @pl.when(s + 1 < count)
        def _():
            self.start(s + 1)


def piece_shapes(width):
    return [pltpu.VMEM((2, D, width), BF16), pltpu.SemaphoreType.DMA((2, 8))]


def gelu_parts(u):
    size = jnp.abs(u)
    t = 1.0 / (1.0 + 0.2316419 * size)
    poly = t * (0.127414796 + t * (-0.142248368 + t * (0.7107068705 + t * (-0.7265760135 + t * 0.5307027145))))
    bell = jnp.exp(-0.5 * (u * u))
    tail = poly * bell
    cdf = jnp.where(u >= 0, 1.0 - tail, tail)
    return u * cdf, cdf + u * (0.3989422804014327 * bell)


def tiles(tokens, width):
    for i in range(2):
        for j in range(2):
            yield slice(i * tokens // 2, (i + 1) * tokens // 2), slice(j * width // 2, (j + 1) * width // 2)


def norm_up(flow, prev, parts, vec, rows_used, weight, bias, count):
    tokens = prev.shape[0]
    width = FF // count

    def body(scal_ref, prev_ref, *refs):
        part_refs, refs = refs[: len(parts)], refs[len(parts) :]
        vec_ref, bias_ref, refs = refs[0], refs[1], refs[2:]
        pieces, (n_ref, low_ref, inv_ref, act_ref, slope_ref, buffer, sems) = refs[:2], refs[2:]
        s = pl.program_id(0)
        stream = Streamed(pieces, buffer, sems, scal_ref)
        stream.turn(s, count)

        @pl.when(s == 0)
        def _():
            def total(rows):
                attn = read(part_refs[0], rows)
                for part in part_refs[1:]:
                    attn = attn + read(part, rows)
                before = read(prev_ref, rows) * row_of(vec_ref, rows_used[0]) + row_of(vec_ref, rows_used[1])
                return before + (attn + row_of(vec_ref, rows_used[2]))

            norm_forward(total, tokens, vec_ref, *rows_used[3:], n_ref, low_ref, inv_ref)

        stream.wait(s)
        slot = lax.rem(s, 2)
        for rows, cols in tiles(tokens, width):
            act, slope = gelu_parts(mm(low_ref[rows, :], buffer[slot, :, cols]) + bias_ref[0, :, cols])
            act_ref[rows, cols] = act.astype(BF16)
            slope_ref[rows, cols] = slope.astype(BF16)

    column = pl.BlockSpec((tokens, width), lambda s, _: (0, s))
    return call(
        flow, body, (count,),
        [full((tokens, D))] + [part_spec(part) for part in parts]
        + [full((TABLE, D)), pl.BlockSpec((1, 1, width), lambda s, _: (s, 0, 0))] + [ANY] * 2,
        [full((tokens, D)), full((tokens, D)), full((tokens, 128)), column, column],
        [sds((tokens, D), F32), sds((tokens, D), BF16), sds((tokens, 128), F32)] + [sds((tokens, FF), BF16)] * 2,
        piece_shapes(width), [prev, *parts, vec, bias, *weight], 2 * tokens * D * FF,
        2 * (D * FF + tokens * (10 * D + 2 * FF)), "norm_up",
    )


def down_norm(flow, act, weight, prev, vec, rows_used, count):
    tokens = prev.shape[0]
    width = FF // count

    def body(scal_ref, act_ref, prev_ref, vec_ref, *refs):
        pieces, (n_ref, low_ref, inv_ref, buffer, sems, acc) = refs[:2], refs[2:]
        s = pl.program_id(0)
        stream = Streamed(pieces, buffer, sems, scal_ref)
        stream.turn(s, count)
        stream.wait(s)
        value = mm(act_ref[...], buffer[lax.rem(s, 2)], NT)

        @pl.when(s == 0)
        def _():
            acc[...] = value

        @pl.when(s > 0)
        def _():
            acc[...] += value

        @pl.when(s == count - 1)
        def _():
            def total(rows):
                before = prev_ref[rows, :] * row_of(vec_ref, rows_used[0]) + row_of(vec_ref, rows_used[1])
                return before + (acc[rows, :] + row_of(vec_ref, rows_used[2]))

            norm_forward(total, tokens, vec_ref, *rows_used[3:], n_ref, low_ref, inv_ref)

    return call(
        flow, body, (count,),
        [pl.BlockSpec((tokens, width), lambda s, _: (0, s)), full((tokens, D)), full((TABLE, D))] + [ANY] * 2,
        [full((tokens, D)), full((tokens, D)), full((tokens, 128))],
        [sds((tokens, D), F32), sds((tokens, D), BF16), sds((tokens, 128), F32)],
        piece_shapes(width) + [pltpu.VMEM((tokens, D), F32)], [act, prev, vec, *weight], 2 * tokens * D * FF,
        2 * (D * FF + tokens * (5 * D + FF)), "down_norm",
    )


def units_back(flow, grad, weight, slope, count):
    tokens = grad.shape[0]
    width = FF // count

    def body(scal_ref, grad_ref, slope_ref, *refs):
        pieces, (out_ref, sum_ref, buffer, sems) = refs[:2], refs[2:]
        s = pl.program_id(0)
        stream = Streamed(pieces, buffer, sems, scal_ref)
        stream.turn(s, count)
        stream.wait(s)
        slot = lax.rem(s, 2)
        sums = {}
        for rows, cols in tiles(tokens, width):
            low = (mm(grad_ref[rows, :], buffer[slot, :, cols]) * slope_ref[rows, cols].astype(F32)).astype(BF16)
            out_ref[rows, cols] = low
            part = fold_rows(low.astype(F32))
            sums[cols.start] = sums[cols.start] + part if cols.start in sums else part
            if rows.start > 0:
                sum_ref[0, :, cols] = jnp.sum(sums[cols.start], 0, keepdims=True)

    column = pl.BlockSpec((tokens, width), lambda s, _: (0, s))
    return call(
        flow, body, (count,), [full((tokens, D)), column] + [ANY] * 2,
        [column, pl.BlockSpec((1, 1, width), lambda s, _: (s, 0, 0))],
        [sds((tokens, FF), BF16), sds((count, 1, width), F32)], piece_shapes(width), [grad, slope, *weight],
        2 * tokens * D * FF, 2 * (D * FF + tokens * (D + 2 * FF)), "units_back",
    )


def up_back(flow, gu, weight, residual, normed, inverse, vec, gain, count):
    tokens = residual.shape[0]
    width = FF // count

    def body(scal_ref, gu_ref, res_ref, n_ref, inv_ref, vec_ref, *refs):
        pieces, (g_ref, low_ref, sums_ref, buffer, sems, acc) = refs[:2], refs[2:]
        s = pl.program_id(0)
        stream = Streamed(pieces, buffer, sems, scal_ref)
        stream.turn(s, count)
        stream.wait(s)
        value = mm(gu_ref[...], buffer[lax.rem(s, 2)], NT)

        @pl.when(s == 0)
        def _():
            acc[...] = value

        @pl.when(s > 0)
        def _():
            acc[...] += value

        @pl.when(s == count - 1)
        def _():
            norm_backward(
                lambda rows: res_ref[rows, :] + acc[rows, :], tokens, n_ref, inv_ref, vec_ref, gain, g_ref, low_ref,
                sums_ref,
            )

    return call(
        flow, body, (count,),
        [pl.BlockSpec((tokens, width), lambda s, _: (0, s)), full((tokens, D)), full((tokens, D)), full((tokens, 128)),
         full((TABLE, D))] + [ANY] * 2,
        [full((tokens, D)), full((tokens, D)), full((8, D))],
        [sds((tokens, D), F32), sds((tokens, D), BF16), sds((8, D), F32)],
        piece_shapes(width) + [pltpu.VMEM((tokens, D), F32)], [gu, residual, normed, inverse, vec, *weight],
        2 * tokens * D * FF, 2 * (D * FF + tokens * (8 * D + FF)), "up_back",
    )


def norm_back(flow, grad, normed, inverse, vec, gain):
    tokens = grad.shape[0]

    def body(scal_ref, grad_ref, n_ref, inv_ref, vec_ref, g_ref, low_ref, sums_ref):
        norm_backward(lambda rows: read(grad_ref, rows), tokens, n_ref, inv_ref, vec_ref, gain, g_ref, low_ref, sums_ref)

    return call(
        flow, body, (1,), [full((tokens, D)), full((tokens, D)), full((tokens, 128)), full((TABLE, D))],
        [full((tokens, D)), full((tokens, D)), full((8, D))],
        [sds((tokens, D), F32), sds((tokens, D), BF16), sds((8, D), F32)], [], [grad, normed, inverse, vec],
        20 * tokens * D, 12 * tokens * D, "norm_back",
    )


def sum_norm_back(flow, residual, parts, normed, inverse, vec, gain):
    tokens = residual.shape[0]

    def body(scal_ref, res_ref, *refs):
        part_refs, (n_ref, inv_ref, vec_ref, g_ref, low_ref, sums_ref) = refs[: len(parts)], refs[len(parts) :]

        def grad(rows):
            total = read(part_refs[0], rows)
            for part in part_refs[1:]:
                total = total + read(part, rows)
            return res_ref[rows, :] + total

        norm_backward(grad, tokens, n_ref, inv_ref, vec_ref, gain, g_ref, low_ref, sums_ref)

    return call(
        flow, body, (1,), [full((tokens, D))] + [part_spec(part) for part in parts]
        + [full((tokens, D)), full((tokens, 128)), full((TABLE, D))],
        [full((tokens, D)), full((tokens, D)), full((8, D))],
        [sds((tokens, D), F32), sds((tokens, D), BF16), sds((8, D), F32)], [],
        [residual, *parts, normed, inverse, vec], 20 * tokens * D, 22 * tokens * D, "sum_norm_back",
    )


def turn_rows(scal_ref, x_ref, turned, core):
    for r in range(4):
        row = ((scal_ref[S_Q] ^ r) * 2 + core) * ROWS
        turned[r * ROWS : (r + 1) * ROWS, :] = x_ref[:, pl.ds(pl.multiple_of(row, ROWS), ROWS)].T


def unit_grads(flow, down, up, received, count, sibling):
    tokens = down[0].shape[0]
    width = down[1].shape[1] // count
    half = count // 2
    steps = 2 * count

    def body(scal_ref, x0_ref, y0_ref, x1_ref, y1_ref, *refs):
        turned, t = refs[-1], pl.program_id(0)
        m, s = t // count, lax.rem(t, count)
        core = scal_ref[S_C] ^ 1 if sibling else scal_ref[S_C]

        @pl.when(t == 0)
        def _():
            turn_rows(scal_ref, x0_ref, turned, core)

        @pl.when(t == count)
        def _():
            turn_rows(scal_ref, x1_ref, turned, core)

        def store(y_ref):
            value = mm(turned[...], y_ref[...]).reshape(4, ROWS, width)
            if sibling:
                refs[0][:, 0] = value.astype(BF16)
                return
            if received is not None:
                value = value + refs[0][:, 0].astype(F32)
            value = value.astype(BF16)
            own, to_x, to_y, rest_x, rest_y = refs[-6:-1]
            spot = lax.rem(s, half) * 2 + m
            own[s // half * count + spot] = value[0]

            @pl.when(s < half)
            def _():
                to_x[spot] = value[1]
                to_x[count + spot] = value[3]
                rest_y[spot] = value[2]

            @pl.when(s >= half)
            def _():
                rest_x[spot] = value[1]
                to_y[spot] = value[2]
                to_y[count + spot] = value[3]

        @pl.when(m == 0)
        def _():
            store(y0_ref)

        @pl.when(m == 1)
        def _():
            store(y1_ref)

    left = full((tokens, D))
    pick_down = lambda t, scal_ref: (0, scal_ref[S_Z] ^ away(jnp.minimum(t, count - 1)))
    pick_up = lambda t, scal_ref: (0, scal_ref[S_Z] ^ away(jnp.maximum(t - count, 0)))
    specs = [left, pl.BlockSpec((tokens, width), pick_down), left, pl.BlockSpec((tokens, width), pick_up)]
    args = [*down, *up]
    one = pl.BlockSpec((4, 1, ROWS, width), lambda t, _: (0, t, 0, 0))
    if sibling:
        out_specs, out_shape = one, sds((4, steps, ROWS, width), BF16)
    else:
        if received is not None:
            specs.append(one)
            args.append(received)
        shapes = [(steps, ROWS, width)] * 3 + [(count, ROWS, width)] * 2
        out_specs, out_shape = [full(shape) for shape in shapes], [sds(shape, BF16) for shape in shapes]
    return call(
        flow, body, (steps,), specs, out_specs, out_shape, [pltpu.VMEM((4 * ROWS, tokens), BF16)], args,
        0, 0, "grads_theirs" if sibling else "grads_mine",
    )


def fetch_heads_weight(scal_ref, pieces, cols, buffer, sems):
    copies = []
    for r in range(4):
        for k in range(2):
            row = ((scal_ref[S_Q] ^ r) * 2 + (scal_ref[S_ZH] ^ k)) * ROWS
            copies.append(
                pltpu.make_async_copy(
                    pieces[r].at[k, pl.ds(0, ROWS), cols], buffer.at[pl.ds(pl.multiple_of(row, ROWS), ROWS), :],
                    sems.at[2 * r + k],
                )
            )
    for copy in copies:
        copy.start()
    for copy in copies:
        copy.wait()


def by_member(shape):
    return pl.BlockSpec((1,) + shape, lambda r, scal_ref: (scal_ref[S_P] ^ r, 0, 0))


def heads_weight_scratch(width):
    return [pltpu.VMEM((D, width), BF16), pltpu.SemaphoreType.DMA((8,))]


def project_in(flow, lefts, across, weight, cols, bias, name):
    tokens = lefts[0].shape[0]
    width = cols.stop - cols.start

    def body(scal_ref, left_ref, right_ref, *refs):
        if bias is not None:
            bias_ref, refs = refs[0], refs[1:]
        pieces, (out_ref, buffer, sems) = refs[:4], refs[4:]
        step = pl.program_id(0)

        @pl.when(step == 0)
        def _():
            fetch_heads_weight(scal_ref, pieces, cols, buffer, sems)

        for r, left in enumerate((left_ref, right_ref)):

            @pl.when(step == r)
            def _(left=left):
                value = mm(left[...], buffer[...])
                if bias is not None:
                    value = value + bias_ref[...]
                out_ref[0] = value.astype(BF16)

    extra, extra_specs = ([], []) if bias is None else ([bias], [full((1, width))])
    return call(
        flow, body, (2,), [full((tokens, D))] * 2 + extra_specs + [ANY] * 4,
        pl.BlockSpec((1, tokens, width), lambda r, scal_ref: ((scal_ref[S_P] >> 1) ^ r, 0, 0)),
        sds((2, tokens, width), BF16), heads_weight_scratch(width), [*lefts, *extra, *weight], 0, 0, name,
    )


def project_out(flow, blocks, members, weight, cols, stacked, name):
    count, tokens, width = blocks.shape

    def body(scal_ref, block_ref, *refs):
        pieces, outs, (buffer, sems) = refs[:4], refs[4:-2], refs[-2:]
        step = pl.program_id(0)

        @pl.when(step == 0)
        def _():
            fetch_heads_weight(scal_ref, pieces, cols, buffer, sems)

        value = mm(block_ref[0], buffer[...], NT).astype(BF16)
        if stacked:
            outs[0][0] = value
            return
        for r, out in enumerate(outs):

            @pl.when(step == r)
            def _(out=out):
                out[...] = value

    first, last = members
    pick = lambda r, scal_ref: (scal_ref[S_P] ^ (first + r * (last - first)), 0, 0)
    if stacked:
        out_specs, out_shape = pl.BlockSpec((1, tokens, D), lambda r, _: (r, 0, 0)), sds((2, tokens, D), BF16)
    else:
        out_specs, out_shape = [full((tokens, D))] * 2, [sds((tokens, D), BF16)] * 2
    return call(
        flow, body, (2,), [pl.BlockSpec((1, tokens, width), pick)] + [ANY] * 4, out_specs, out_shape,
        heads_weight_scratch(width), [blocks, *weight], 0, 0, name,
    )


def heads_grad(flow, xs, gqkv, gas, ctx):
    count, tokens, width = gqkv.shape
    out_width = ctx.shape[2]

    def body(scal_ref, *refs):
        x_refs, refs = refs[:count], refs[count:]
        ga_refs, refs = refs[:count], refs[count:]
        g_ref, ctx_ref = refs[:2]
        outs, (sum_ref, acc, acc_out) = refs[2:4], refs[4:]
        step = pl.program_id(0)
        for r in range(count):

            @pl.when(step == r)
            def _(r=r):
                value = mm(x_refs[r][...].T, g_ref[0])
                value_out = mm(ga_refs[r][...].T, ctx_ref[0])
                sums = jnp.sum(g_ref[0].astype(F32), 0, keepdims=True)
                if r == 0:
                    acc[...] = value
                    acc_out[...] = value_out
                    sum_ref[...] = sums
                else:
                    acc[...] += value
                    acc_out[...] += value_out
                    sum_ref[...] += sums

        @pl.when(step == count - 1)
        def _():
            for r in range(4):
                for k in range(2):
                    row = ((scal_ref[S_Q] ^ r) * 2 + (scal_ref[S_ZH] ^ k)) * ROWS
                    rows = pl.ds(pl.multiple_of(row, ROWS), ROWS)
                    outs[r % 2][r // 2, k, :, :width] = acc[rows, :].astype(BF16)
                    outs[r % 2][r // 2, k, :, width:] = acc_out[rows, :].astype(BF16)

    shape = (2, 2, ROWS, width + out_width)
    return call(
        flow, body, (count,), [full((tokens, D))] * (2 * count) + [by_member((tokens, width)), by_member((tokens, out_width))],
        [full(shape)] * 2 + [full((1, width))], [sds(shape, BF16)] * 2 + [sds((1, width), F32)],
        [pltpu.VMEM((D, width), F32), pltpu.VMEM((D, out_width), F32)], [*xs, *gas, gqkv, ctx],
        2 * tokens * D * (width + out_width) * count, 4 * count * tokens * (D + width), "heads_grad",
    )


def reach(ends_ref, row):
    first = jnp.zeros_like(row)
    for index in range(3):
        first = jnp.where(row >= ends_ref[index], ends_ref[index], first)
    last = jnp.full_like(row, SEQLEN)
    for index in (2, 1, 0):
        last = jnp.where(row < ends_ref[index], ends_ref[index], last)
    return jnp.maximum(first, row - (WINDOW - 1)), jnp.minimum(last, row + WINDOW)


def chunks_of(scal_ref, near_ref, far_ref):
    here = scal_ref[S_P] & 1
    for core in range(2):
        yield 2 * core + here, near_ref.at[core]
        yield 2 * core + 1 - here, far_ref.at[core]


def over_keys(ends_ref, start, chunk, block):
    low_first, high_first = reach(ends_ref, start)
    low_last, high_last = reach(ends_ref, start + BQ - 1)
    low_row, high_row = reach(ends_ref, start + lax.broadcasted_iota(jnp.int32, (1, BQ), 1))

    def one(b, carry):
        open_all = (b * chunk >= low_last) & ((b + 1) * chunk <= high_first)

        @pl.when(open_all)
        def _():
            block(b, None)

        @pl.when(jnp.logical_not(open_all))
        def _():
            key = b * chunk + lax.broadcasted_iota(jnp.int32, (chunk, BQ), 0)
            block(b, (key >= low_row) & (key < high_row))

        return carry

    lax.fori_loop(low_first // chunk, (high_last + chunk - 1) // chunk, one, 0)


def attend_forward(flow, ends, qkv):
    _, chunk, width3 = qkv[0].shape
    count = SEQLEN // chunk
    width = width3 // 3
    heads = width // HD
    steps = SEQLEN // BQ
    per = chunk // BQ

    def body(scal_ref, ends_ref, near_ref, far_ref, ctx_ref, wide_ref, lse_ref, qh, kh, vt, acc, tops, sums, scores):
        step = pl.program_id(0)

        @pl.when(step == 0)
        def _():
            for j, block in chunks_of(scal_ref, near_ref, far_ref):
                rows = pl.ds(pl.multiple_of(j * chunk, chunk), chunk)
                for h in range(heads):
                    qh[h, rows, :] = block[:, h * HD : (h + 1) * HD] * BF16(HD**-0.5)
                    kh[h, rows, :] = block[:, width + h * HD : width + (h + 1) * HD]
                vt[j] = block[:, 2 * width :].T

        start = step * BQ
        rows = pl.ds(pl.multiple_of(start, BQ), BQ)
        acc[...] = jnp.zeros(acc.shape, F32)
        tops[...] = jnp.full(tops.shape, -3.0e38, F32)
        sums[...] = jnp.zeros(sums.shape, F32)

        def score(b, allowed):
            keys = pl.ds(pl.multiple_of(b * chunk, chunk), chunk)
            for h in range(heads):
                value = mm(kh[h, keys, :], qh[h, rows, :], NT)
                if allowed is not None:
                    value = jnp.where(allowed, value, FILL)
                scores[h, b] = value
                tops[h] = jnp.maximum(tops[h], jnp.max(value.reshape(-1, 8, BQ), 0))

        over_keys(ends_ref, start, chunk, score)
        top = [jnp.max(tops[h], 0, keepdims=True) for h in range(heads)]

        def weigh(b, carry):
            for h in range(heads):
                part = slice(h * HD, (h + 1) * HD)
                weight = jnp.exp(scores[h, b] - top[h])
                sums[h] += fold_rows(weight)
                acc[part, :] += mm(vt[b, part, :], weight.astype(BF16))
            return carry

        low_first, _ = reach(ends_ref, start)
        _, high_last = reach(ends_ref, start + BQ - 1)
        lax.fori_loop(low_first // chunk, (high_last + chunk - 1) // chunk, weigh, 0)
        for h in range(heads):
            part = slice(h * HD, (h + 1) * HD)
            total = jnp.sum(sums[h], 0, keepdims=True)
            wide_ref[part, :] = acc[part, :] / total
            lse_ref[h : h + 1, :] = top[h] + jnp.log(total)
        lse_ref[heads:, :] = jnp.zeros((8 - heads, BQ), F32)
        ctx_ref[0] = wide_ref[...].T.astype(BF16)

    pairs = SEQLEN * SEQLEN
    return call(
        flow, body, (steps,), [full((2, chunk, width3))] * 2,
        [pl.BlockSpec((1, BQ, width), lambda i, *_: (i // per, i % per, 0)),
         pl.BlockSpec((width, BQ), lambda i, *_: (0, i)), pl.BlockSpec((8, BQ), lambda i, *_: (0, i))],
        [sds((count, chunk, width), BF16), sds((width, SEQLEN), F32), sds((8, SEQLEN), F32)],
        [
            pltpu.VMEM((heads, SEQLEN, HD), BF16),
            pltpu.VMEM((heads, SEQLEN, HD), BF16),
            pltpu.VMEM((count, width, chunk), BF16),
            pltpu.VMEM((width, BQ), F32),
            pltpu.VMEM((heads, 8, BQ), F32),
            pltpu.VMEM((heads, 8, BQ), F32),
            pltpu.VMEM((heads, count, chunk, BQ), F32),
        ],
        [*qkv], 16 * pairs * heads * HD, 6 * SEQLEN * width * 2, "attend_forward", (flow.scal, ends),
    )


def attend_backward(flow, ends, qkv, grads, wide, lse):
    _, chunk, width3 = qkv[0].shape
    count = SEQLEN // chunk
    width = width3 // 3
    heads = width // HD
    steps = SEQLEN // BQ
    per = chunk // BQ

    def body(
        scal_ref, ends_ref, near_ref, far_ref, grad_near, grad_far, wide_ref, lse_ref, out_ref, qh, kh, vh, gh, kt, qt, gt,
        gq, gk, gv,
    ):
        step = pl.program_id(0)

        @pl.when(step == 0)
        def _():
            blocks = chunks_of(scal_ref, near_ref, far_ref)
            grad_blocks = chunks_of(scal_ref, grad_near, grad_far)
            for (j, block), (_, grad_block) in zip(blocks, grad_blocks):
                rows = pl.ds(pl.multiple_of(j * chunk, chunk), chunk)
                for h in range(heads):
                    cols = slice(h * HD, (h + 1) * HD)
                    qh[h, rows, :] = block[:, cols] * BF16(HD**-0.5)
                    kh[h, rows, :] = block[:, width + h * HD : width + (h + 1) * HD]
                    vh[h, rows, :] = block[:, 2 * width + h * HD : 2 * width + (h + 1) * HD]
                    gh[h, rows, :] = grad_block[:, cols]
                kt[j] = block[:, width : 2 * width].T
                for s in range(per):
                    sub = slice(s * BQ, (s + 1) * BQ)
                    qt[j * per + s] = (block[sub, :width] * BF16(HD**-0.5)).T
                    gt[j * per + s] = grad_block[sub, :].T
            gk[...] = jnp.zeros(gk.shape, F32)
            gv[...] = jnp.zeros(gv.shape, F32)

        start = step * BQ
        rows = pl.ds(pl.multiple_of(start, BQ), BQ)
        gq[...] = jnp.zeros(gq.shape, F32)
        inner = []
        for h in range(heads):
            part = slice(h * HD, (h + 1) * HD)
            inner.append(jnp.sum(gt[step, part, :].astype(F32) * wide_ref[part, :], 0, keepdims=True))

        def block(b, allowed):
            keys = pl.ds(pl.multiple_of(b * chunk, chunk), chunk)
            for h in range(heads):
                part = slice(h * HD, (h + 1) * HD)
                score = mm(kh[h, keys, :], qh[h, rows, :], NT)
                grad_weight = mm(vh[h, keys, :], gh[h, rows, :], NT)
                if allowed is not None:
                    score = jnp.where(allowed, score, FILL)
                weight = jnp.exp(score - lse_ref[h : h + 1, :])
                grad_score = (weight * (grad_weight - inner[h])).astype(BF16)
                gv[b, part, :] += mm(gt[step, part, :], weight.astype(BF16), NT)
                gk[b, part, :] += mm(qt[step, part, :], grad_score, NT)
                gq[part, :] += mm(kt[b, part, :], grad_score)

        over_keys(ends_ref, start, chunk, block)
        out_ref[step // per, pl.ds(pl.multiple_of((step % per) * BQ, BQ), BQ), :width] = (
            (gq[...] * HD**-0.5).T.astype(BF16)
        )

        @pl.when(step == steps - 1)
        def _():
            for j in range(count):
                out_ref[j, :, width : 2 * width] = gk[j].T.astype(BF16)
                out_ref[j, :, 2 * width :] = gv[j].T.astype(BF16)

    pairs = SEQLEN * SEQLEN
    return call(
        flow, body, (steps,),
        [full((2, chunk, width3))] * 2 + [full((2, chunk, width))] * 2
        + [pl.BlockSpec((width, BQ), lambda i, *_: (0, i)), pl.BlockSpec((8, BQ), lambda i, *_: (0, i))],
        full((count, chunk, width3)), sds((count, chunk, width3), BF16),
        [pltpu.VMEM((heads, SEQLEN, HD), BF16)] * 4
        + [
            pltpu.VMEM((count, width, chunk), BF16),
            pltpu.VMEM((steps, width, BQ), BF16),
            pltpu.VMEM((steps, width, BQ), BF16),
            pltpu.VMEM((width, BQ), F32),
            pltpu.VMEM((count, width, chunk), F32),
            pltpu.VMEM((count, width, chunk), F32),
        ],
        [*qkv, *grads, wide, lse], 28 * pairs * heads * HD, 20 * SEQLEN * width, "attend_backward", (flow.scal, ends),
    )


def flip(values_in, axes, mask):
    return lax.ppermute(values_in, axes, [(a, a ^ mask) for a in range(lax.axis_size(axes))])


def turn(values_in):
    return lax.ppermute(values_in, ("c", "zh"), [(2 * a + b, 2 * b + a) for a in range(2) for b in range(2)])


def cross(values_in):
    return lax.ppermute(values_in, ("c", "zh"), [(2 * a + b, 2 * b + 1 - a) for a in range(2) for b in range(2)])


def uncross(values_in):
    return lax.ppermute(values_in, ("c", "zh"), [(2 * b + 1 - a, 2 * a + b) for a in range(2) for b in range(2)])


def from_members(values_in, axes):
    return [values_in] + [flip(values_in, axes, r) for r in range(1, lax.axis_size(axes))]


def to_members(parts, axes):
    return [parts[0]] + [flip(part, axes, r) for r, part in enumerate(parts) if r > 0]


def add(*parts):
    total = parts[0].astype(F32)
    for part in parts[1:]:
        total = total + part.astype(F32)
    return total


def is_small():
    return lax.axis_size("q") == 4


def order_by(values_in, axis, position, count):
    bit = 1
    while bit < count:
        shape = values_in.shape
        split = shape[:axis] + (count // (2 * bit), 2, bit) + shape[axis + 1 :]
        cut = values_in.reshape(split)
        values_in = jnp.where((position & bit) != 0, jnp.flip(cut, axis + 1), cut).reshape(shape)
        bit *= 2
    return values_in


def gather_group(values_in):
    across, sibling = flip(values_in, GROUP, 1), flip(values_in, GROUP, 2)
    return [values_in, across, sibling, flip(across, GROUP, 2)]


def sum_group(keep, send):
    got = flip(send, GROUP, 2)
    passed = add(keep[1], got[1]).astype(BF16)
    return [keep[0], got, flip(passed, GROUP, 1)], passed


EXTRA = 16


def heads_shard_of(qkv, out, bias):
    weights = jnp.concatenate([qkv.transpose(1, 0, 2).reshape(out.shape[0], -1), out], axis=1)
    below = jnp.pad(bias.reshape(1, -1), ((0, EXTRA - 1), (0, weights.shape[1] - bias.size)))
    return jnp.concatenate([weights, below])


def heads_bias(rows, heads):
    bias = rows.reshape(rows.shape[0], 2, heads, -1).transpose(1, 2, 0, 3).reshape(2, -1).astype(F32)
    return jnp.concatenate([bias[0], jnp.zeros_like(bias[0]), bias[1]])[None]


def heads_bias_near(members, size, heads, where, zh):
    rows = jnp.stack([member[:, ROWS, :size] for member in members])
    return heads_bias(order_by(order_by(rows, 0, where[0], 4), 1, zh, 2).reshape(8, size), heads)


def all_heads_weight(shard, size, heads, zh):
    pair = jnp.stack([turn(shard), cross(shard)])
    every = order_by(lax.all_gather(pair, "q"), 1, zh, 2)
    count = shard.shape[0] - EXTRA
    weights = every[:, :, :count].reshape(4, 2, ROWS, -1)
    return [weights[r] for r in range(4)], heads_bias(every[:, :, count, :size].reshape(-1, size), heads)


class HeadsGrad:
    def __init__(self, keep, send):
        self.keep, self.send = keep, send

    def along_x(self):
        self.got = flip(self.send, "q", 1)
        return self.got

    def along_y(self):
        self.here = add(self.keep[0], self.got[0])
        self.got = flip(add(self.keep[1], self.got[1]).astype(BF16), "q", 2)
        return self.got

    def halves(self, zh):
        if is_small():
            total = add(self.here, self.got).astype(BF16)
            return total[0], total[1]
        buckets = [self.keep[0], self.send[0], self.keep[1], self.send[1]]
        every = jnp.stack(buckets).reshape(lax.axis_size("q"), 2, -1, buckets[0].shape[-1])
        rows = order_by(lax.psum_scatter(every, "q", scatter_dimension=0, tiled=False), 0, zh, 2)
        return rows[0], rows[1]


SLOTS = (0, 2, 1, 3)


def units_weight(shard):
    if is_small():
        return lax.all_gather(shard, MODEL + ("q",)).reshape(-1, 4, ROWS, shard.shape[1]), None
    members = lax.axis_size(MODEL)
    every = lax.all_gather(shard, ALL, tiled=True).reshape(members, 4, 2, ROWS, shard.shape[1])
    return every[:, :, 0], every[:, :, 1]


class UnitsGrads:
    def __init__(self, flow, down, up, count):
        self.flow, self.down, self.up, self.count = flow, down, up, count

    def compute_theirs(self):
        self.theirs = unit_grads(self.flow, self.down, self.up, None, self.count, True)

    def send_theirs(self):
        self.got = flip(self.theirs, "c", 1) if is_small() else None

    def sibling(self):
        self.compute_theirs()
        self.send_theirs()

    def mine(self):
        self.made = unit_grads(self.flow, self.down, self.up, self.got, self.count, False)
        self.own, self.to_x, self.to_y, self.rest_x, self.rest_y = self.made

    def near(self):
        self.from_x, self.from_y = flip(self.to_x, "q", 1), flip(self.to_y, "q", 2)
        return [self.from_x, self.from_y]

    def far(self):
        half = self.count
        self.late_x = flip(add(self.rest_x, self.from_y[half:]).astype(BF16), "q", 1)
        self.late_y = flip(add(self.rest_y, self.from_x[half:]).astype(BF16), "q", 2)
        return [self.late_x, self.late_y]

    def near_z(self):
        half = self.count
        self.here = add(self.own[:half], self.from_x[:half], self.late_y)
        self.there = flip(add(self.own[half:], self.late_x, self.from_y[:half]).astype(BF16), "zl", 1)
        return [self.there]

    def far_z(self):
        half = self.count // 2
        self.stays = add(self.here[:half], self.there[:half])
        self.last = flip(add(self.here[half:], self.there[half:]).astype(BF16), "zh", 1)
        return [self.last]

    def total(self):
        if is_small():
            return self.stays + self.last.astype(F32)
        half = self.count
        mine = jnp.stack(
            [self.own, jnp.concatenate([self.to_x[:half], self.rest_x]), jnp.concatenate([self.rest_y, self.to_y[:half]]),
             jnp.concatenate([self.to_x[half:], self.to_y[half:]])]
        ).reshape(4, self.count, 2, ROWS, -1)
        theirs = self.theirs.reshape(4, 2, self.count, ROWS, -1).transpose(0, 2, 1, 3, 4)
        every = jnp.stack([mine, theirs], axis=1)
        every = every.transpose(2, 0, 1, 4, 3, 5)
        every = jnp.stack([every[slot] for slot in SLOTS]).reshape(-1, 2, mine.shape[-1])
        return lax.psum_scatter(every, ALL, scatter_dimension=0, tiled=True).astype(F32).transpose(1, 0, 2)


SMALL_AXES = ("q", MODEL, "c")
SMALL_STEPS = (("q", 1), ("q", 2), ("zl", 1), ("zh", 1), ("c", 1))


def small_step(values_in, step):
    axis, mask = SMALL_STEPS[step]
    return jnp.concatenate([values_in, flip(values_in, axis, mask)])


def order_small(every, where):
    every = every.reshape(2, 2, 2, 4, -1)
    every = every.reshape(2, 4, 4, -1)
    for axis, position in enumerate(where[::-1]):
        every = order_by(every, axis, position, every.shape[axis])
    return every.transpose(1, 2, 0, 3).reshape(16 // 4, 8, -1)


def scatter_small(values_in, where):
    if not is_small():
        return lax.psum_scatter(values_in.reshape(-1, values_in.shape[-1]), ALL, scatter_dimension=0, tiled=True)[0]
    every = values_in.reshape(4, 4, 2, -1).transpose(1, 0, 2, 3)
    for axis, position in enumerate(where):
        every = order_by(every, axis, position, every.shape[axis])
    every = every.transpose(2, 1, 0, 3).reshape(32, -1)
    for axis, mask in SMALL_STEPS[::-1]:
        half = every.shape[0] // 2
        every = every[:half] + flip(every[half:], axis, mask)
    return every[0]


def sum_all(value):
    if not is_small():
        return lax.psum(value, ALL)
    for axes in SMALL_AXES:
        parts = jnp.stack(from_members(value, axes))
        value = jnp.sum(order_by(parts, 0, lax.axis_index(axes), parts.shape[0]), 0)
    return value[0, 0]


def on_device(
    tokens, doc_lengths, qkv_weight, qv_bias, out_weight, up_weight, up_bias, down_weight, gains, shifts, cotangent
):
    layers = qkv_weight.shape[0]
    tz, dp = lax.axis_size(MODEL), lax.axis_size(("q", "c"))
    place, zh = lax.axis_index(GROUP), lax.axis_index("zh")
    where = (lax.axis_index("q"), lax.axis_index(MODEL), lax.axis_index("c"))
    if is_small():
        spots = [place, where[0], where[2], zh, where[1]]
    else:
        spots = [place] + [jnp.zeros((), jnp.int32)] * 4
    scal = jnp.stack([spot.astype(jnp.int32) for spot in spots])

    flow = Flow(scal)
    small_slice = is_small()
    qkv_cols, out_cols = 3 * out_weight.shape[2], out_weight.shape[2]
    in_cols, out_cols = slice(0, qkv_cols), slice(qkv_cols, qkv_cols + out_cols)
    hz, bias_size = qv_bias.shape[2], qv_bias.size // layers
    heads_shard = [heads_shard_of(qkv_weight[l], out_weight[l], qv_bias[l]) for l in range(layers)]
    pieces = [up_bias, gains, shifts]
    sizes = [piece.size // layers for piece in pieces]
    cuts = [0]
    for size in sizes:
        cuts.append(cuts[-1] + size)
    small = jnp.concatenate([piece.reshape(layers, -1) for piece in pieces], axis=1).reshape(1, -1)

    def spread_small(every):
        every = every.reshape(tz, dp, layers, -1).astype(F32)
        parts = [every[..., cuts[i] : cuts[i + 1]] for i in range(3)]
        biases = parts[0].reshape(tz, dp, layers, up_bias.shape[1], -1).transpose(2, 0, 3, 1, 4)
        gain = parts[1].reshape(tz, dp, layers, 2, -1).transpose(2, 3, 1, 0, 4).reshape(layers, 2, D)
        shift = parts[2].reshape(tz, dp, layers, 4, -1).transpose(2, 3, 1, 0, 4).reshape(layers, 4, D)
        table = jnp.concatenate([gain, shift], axis=1).reshape(layers * 6, D)
        head = jnp.concatenate([jnp.ones((1, D), F32), jnp.zeros((1, D), F32)])
        return biases.reshape(layers, tz, 1, -1), jnp.pad(jnp.concatenate([head, table]), ((0, TABLE - 2 - 6 * layers), (0, 0)))

    weights = [(units_weight(up_weight[l]), units_weight(down_weight[l])) for l in range(layers)]
    if small_slice:
        pair = jnp.stack([turn(heads_shard[0]), cross(heads_shard[0])])
        x_low = turn(tokens)
        ends = jnp.cumsum(turn(doc_lengths)[0], dtype=jnp.int32)
        members = from_members(pair, "q")
        small = small_step(small, 0)
        flow.wait(x_low, small)
        flow.hold(heads1=heads_shard[1], top=cotangent, low=x_low, small=small)
        gate(flow)
        x_low = flow.free("low")
        small = small_step(flow.free("small"), 1)
        weights_of = [(members, heads_bias_near(members, bias_size, hz, where, zh))]
    else:
        x_low = turn(tokens)
        ends = jnp.cumsum(turn(doc_lengths)[0], dtype=jnp.int32)
        weights_of = [all_heads_weight(shard, bias_size, hz, zh) for shard in heads_shard]
        top_grad = turn(cotangent)
        up_bias_full, table = spread_small(lax.all_gather(small, ALL))

    prev, prev_gain, prev_shift = x_low, ONE, ZERO
    kept = []
    for l in range(layers):
        first, last = small_slice and l == 0, small_slice and l == 1
        xs = gather_group(x_low)
        w_heads, bias = weights_of[l]
        w_up, w_down = weights[l]
        if first:
            flow.wait(small)
            flow.hold(small=small)
        qkv_near = project_in(flow, (xs[0], xs[2]), False, w_heads, in_cols, bias, "project_qkv")
        flow.wait(qkv_near)
        if first:
            small = small_step(flow.free("small"), 2)
            flow.wait(small)
            flow.hold(small=small)
        qkv_far = project_in(flow, (xs[1], xs[3]), True, w_heads, in_cols, bias, "project_qkv")
        qkv = (qkv_near, qkv_far)
        if first:
            small = small_step(flow.free("small"), 3)
        if last:
            top_grad = turn(flow.free("top"))
        if small_slice:
            flow.hold(up=w_up[0])
        ctx, wide, lse = attend_forward(flow, ends, qkv)
        if small_slice:
            mine = flow.free("up")
            w_up = mine, flip(mine, "c", 1)
        if first:
            flow.wait(small)
            flow.hold(small=small)
            shard = flow.free("heads1")
            pair = jnp.stack([turn(shard), cross(shard)])
        if last:
            flow.wait(top_grad)
        if small_slice:
            flow.hold(down=w_down[0])
        send = project_out(flow, ctx, (2, 3), w_heads, out_cols, True, "project_attn")
        flow.wait(send)
        if small_slice:
            mine = flow.free("down")
            w_down = mine, flip(mine, "c", 1)
        keep = project_out(flow, ctx, (0, 1), w_heads, out_cols, False, "project_attn")
        attn, _ = sum_group(keep, send)
        if first:
            up_bias_full, table = spread_small(order_small(small_step(flow.free("small"), 4), where))
            flow.wait(pair)
        used = (prev_gain, prev_shift, shift_row(l, 0), gain_row(l, 0), shift_row(l, 1))
        n1, hs, r1, act, slope = norm_up(flow, prev, attn, table, used, w_up, up_bias_full[l], tz)
        if first:
            members = from_members(pair, "q")
            weights_of.append((members, heads_bias_near(members, bias_size, hz, where, zh)))
        used = (gain_row(l, 0), shift_row(l, 1), shift_row(l, 2), gain_row(l, 1), shift_row(l, 3))
        n2, y_low, r2 = down_norm(flow, act, w_down, n1, table, used, tz)
        kept.append((xs, qkv, ctx, wide, lse, n1, hs, r1, act, slope, n2, r2, w_heads, w_up, w_down))
        x_low, prev, prev_gain, prev_shift = y_low, n2, gain_row(l, 1), shift_row(l, 3)
    layer_output = turn(x_low)

    g2, gf, sums2 = norm_back(flow, top_grad, kept[-1][10], kept[-1][11], table, gain_row(layers - 1, 1))
    small_grads = [None] * layers
    units_of, heads_of = [None] * layers, [None] * layers
    above = above_heads = None
    for l in reversed(range(layers)):
        top = l == layers - 1
        xs, qkv, ctx, wide, lse, n1, hs, r1, act, slope, n2, r2, w_heads, w_up, w_down = kept[l]
        beside = small_slice and not top
        gu, up_bias_sum = units_back(flow, gf, w_down, slope, tz)
        units = UnitsGrads(flow, (gf, act), (hs, gu), tz)
        if top:
            flow.wait(layer_output)
        else:
            if beside:
                flow.wait(*above.near())
                flow.hold(heads=above_heads.send)
            units.sibling()
            flow.wait(units.theirs)
            if beside:
                above_heads.send = flow.free("heads")
                above_heads.along_x()
                late = above.far()
        g1, ga, sums1 = up_back(flow, gu, w_up, g2, n1, r1, table, gain_row(l, 0), tz)
        gas = gather_group(ga)
        flow.wait(ga)
        if top:
            units.compute_theirs()
        else:
            units.mine()
            flow.wait(*units.made)
            if beside:
                flow.wait(*late, above_heads.got)
        gc_near = project_in(flow, (gas[0], gas[2]), False, w_heads, out_cols, None, "project_gc")
        flow.wait(gc_near)
        if top:
            flow.hold(theirs=units.theirs)
        gc_far = project_in(flow, (gas[1], gas[3]), True, w_heads, out_cols, None, "project_gc")
        if top:
            units.theirs = flow.free("theirs")
            units.send_theirs()
        gqkv = attend_backward(flow, ends, qkv, (gc_near, gc_far), wide, lse)
        if beside:
            flow.wait(*units.near(), *above.near_z(), above_heads.along_y())
        send = project_out(flow, gqkv, (2, 3), w_heads, in_cols, True, "project_gx")
        flow.wait(send)
        keep = project_out(flow, gqkv, (0, 1), w_heads, in_cols, False, "project_gx")
        back, passed = sum_group(keep, send)
        flow.wait(passed)
        if top:
            units.mine()
            flow.wait(*units.made)
        elif small_slice:
            flow.hold(there=above.there)
        *buckets, qkv_sums = heads_grad(flow, xs, gqkv, gas, ctx)
        heads = HeadsGrad(*buckets)
        units_of[l], heads_of[l] = units, heads
        qv_sums = qkv_sums.reshape(3, hz, dp, -1)
        qv_sums = jnp.stack([qv_sums[0], qv_sums[2]]).transpose(2, 0, 1, 3).reshape(1, dp, -1)
        mine = (jnp.arange(tz) == place).astype(F32).reshape(tz, 1, 1)
        small_grads[l] = jnp.concatenate(
            [
                mine * qv_sums,
                up_bias_sum.reshape(tz, up_bias.shape[1], dp, -1).transpose(0, 2, 1, 3).reshape(tz, dp, -1),
                jnp.stack([sums1[0], sums2[0]]).reshape(2, dp, tz, -1).transpose(2, 1, 0, 3).reshape(tz, dp, -1),
                jnp.stack([sums1[2], sums1[1], sums2[2], sums2[1]])
                .reshape(4, dp, tz, -1).transpose(2, 1, 0, 3).reshape(tz, dp, -1),
            ],
            axis=-1,
        )
        if l > 0:
            above, above_heads = units, heads
            flow.wait(heads.send)
            g2, gf, sums2 = sum_norm_back(flow, g1, back, kept[l - 1][10], kept[l - 1][11], table, gain_row(l - 1, 1))
    small_sums = jnp.stack(small_grads, axis=2).reshape(tz, dp, -1)
    if small_slice:
        units.far()
        above.there = flow.free("there")
        above.far_z()
        flow.hold(late_x=units.late_x, late_y=units.late_y, heads=heads.send)
        gate(flow)
        units.late_x, units.late_y, heads.send = flow.free("late_x"), flow.free("late_y"), flow.free("heads")
        heads.along_x()
        units.near_z()
        flow.wait(back[2])
        flow.hold(small=small_sums, there=units.there, got=heads.got)
        gate(flow)
        small_sums, units.there, heads.got = flow.free("small"), flow.free("there"), flow.free("got")
        heads.along_y()
        units.far_z()
    input_grad = turn(add(g1, back[0], back[1][0], back[2]).astype(BF16))
    halves = [member.halves(zh) for member in heads_of]
    d_heads = add(turn(jnp.stack([half[0] for half in halves])), uncross(jnp.stack([half[1] for half in halves])))
    qkv_grad = d_heads[:, :, : in_cols.stop].reshape(layers, d_heads.shape[1], 3, -1).transpose(0, 2, 1, 3)
    out_grad = d_heads[:, :, in_cols.stop :]
    totals = [member.total() for member in units_of]
    down_grad, up_grad = (jnp.stack([total[i] for total in totals]) for i in range(2))

    small_out = scatter_small(small_sums, where).reshape(layers, -1)
    rest = small_out[:, bias_size:]
    qv_bias_grad = small_out[:, :bias_size].reshape(qv_bias.shape)
    up_bias_grad = rest[:, cuts[0] : cuts[1]].reshape(up_bias.shape)
    gains_grad = rest[:, cuts[1] : cuts[2]].reshape(gains.shape)
    shifts_grad = rest[:, cuts[2] : cuts[3]].reshape(shifts.shape)
    all_grads = (qkv_grad, qv_bias_grad, out_grad, up_grad, up_bias_grad, down_grad, gains_grad, shifts_grad)
    local_squares = sum(jnp.sum(member * member) for member in all_grads)
    entry_count = LAYERS * (4 * D * D + 2 * D * FF + FF + 8 * D)
    if small_slice:
        flow.wait(input_grad)
        flow.hold(squares=jnp.broadcast_to(local_squares, (8, 128)))
        gate(flow)
        local_squares = flow.free("squares")
    grad_rms = jnp.sqrt(sum_all(local_squares) / entry_count)
    return (
        layer_output, input_grad, qkv_grad, qv_bias_grad, out_grad, up_grad, up_bias_grad, down_grad, gains_grad,
        shifts_grad, grad_rms,
    )


def solution(mesh):
    dp, tensor = mesh.shape["dp"], mesh.shape["tensor"]
    fine = Mesh(mesh.devices.reshape(dp // 2, 2, 2, tensor // 2), ("q", "c", "zh", "zl"))
    data, model = ("q", "c"), ("zh", "zl")
    both = data + model
    weight3, weight4 = P(None, data, model), P(None, None, data, model)
    in_specs = (
        P(both, None), P(data, None), weight4, P(None, None, model, data), weight3, weight3, P(None, model, data),
        weight3, P(None, None, both), P(None, None, both), P(both, None),
    )
    out_specs = (
        P(both, None), P(both, None), weight4, P(None, None, model, data), weight3, weight3, P(None, model, data),
        weight3, P(None, None, both), P(None, None, both), P(),
    )
    return jax.shard_map(on_device, mesh=fine, in_specs=in_specs, out_specs=out_specs, check_vma=False)
```

```python
import jax
import jax.numpy as jnp
from jax import lax
from jax.experimental import pallas as pl
from jax.experimental.pallas import tpu as pltpu
from jax.sharding import Mesh
from jax.sharding import PartitionSpec as P

D = 1024
HD = 64
HEADS = 16
FF = 4096
LAYERS = 2
SEQLEN = 2048
WINDOW = 1024
EPS = 1e-06
FILL = -1000000000.0

F32 = jnp.float32
BF16 = jnp.bfloat16
GROUP = ("c", "zl")
MODEL = ("zh", "zl")
ALL = ("zh", "zl", "q", "c")
VMEM_LIMIT = 56 * 1024 * 1024
TIMES = {
    "gate": 0.1, "norm_up": 20.0, "down_norm": 20.0, "units_back": 20.0, "up_back": 20.0, "norm_back": 6.0,
    "sum_norm_back": 20.0, "grads_theirs": 0.2, "grads_mine": 0.2, "project_qkv": 0.2, "project_gc": 0.2,
    "project_attn": 0.2, "project_gx": 0.2, "heads_grad": 0.2, "attend_forward": 40.0, "attend_backward": 30.0,
}
PEAK = 0.35e9
NT = (((1,), (1,)), ((), ()))
NN = (((1,), (0,)), ((), ()))
ROWS = 128
CHUNK = 64
BQ = 256
PAIR = 2 * HD


def mm(left, right, dims=NN):
    return lax.dot_general(left, right, dims, preferred_element_type=F32)


def full(shape):
    return pl.BlockSpec(shape, lambda *_: (0,) * len(shape))


ANY = pl.BlockSpec(memory_space=pl.ANY)


def sds(shape, kind):
    return jax.ShapeDtypeStruct(shape, kind)


class Flow:
    def __init__(self, scal):
        self.scal, self.before, self.held = scal, [], {}

    def wait(self, *arrays):
        self.before += arrays

    def hold(self, **arrays):
        self.held.update(arrays)

    def free(self, name):
        return self.held.pop(name)


def call(flow, body, grid, in_specs, out_specs, out_shape, scratch, args, flops, traffic, name, scalars=None):
    scalars = (flow.scal,) if scalars is None else scalars
    single = not isinstance(out_specs, (list, tuple))
    out_specs = [out_specs] if single else list(out_specs)
    out_shape = [out_shape] if single else list(out_shape)
    before, held = flow.before, list(flow.held.items())
    ns, nb, nh, no = len(scalars), len(before), len(held), len(out_specs)
    first, last = ns + nb + nh, ns + nb + nh + len(args) + no

    def wrapped(*refs):
        body(*refs[:ns], *refs[first:last], *refs[last + nh :])

    result = pl.pallas_call(
        wrapped,
        grid_spec=pltpu.PrefetchScalarGridSpec(
            num_scalar_prefetch=ns,
            grid=grid,
            in_specs=[ANY] * (nb + nh) + list(in_specs),
            out_specs=out_specs + [ANY] * nh,
            scratch_shapes=scratch,
        ),
        out_shape=out_shape + [sds(array.shape, array.dtype) for _, array in held],
        input_output_aliases={ns + nb + i: no + i for i in range(nh)},
        compiler_params=pltpu.CompilerParams(
            dimension_semantics=("arbitrary",) * len(grid), vmem_limit_bytes=VMEM_LIMIT
        ),
        cost_estimate=pl.CostEstimate(flops=int(TIMES[name] * PEAK), bytes_accessed=1024, transcendentals=0),
        name=name,
    )(*scalars, *before, *[array for _, array in held], *args)
    flow.before = []
    flow.held = {key: value for (key, _), value in zip(held, result[no:])}
    return result[0] if single else result[:no]


def gate(flow):
    if flow.held:
        call(flow, lambda *refs: None, (1,), [], [], [], [], [], 0, 0, "gate")


S_P, S_Q, S_C, S_ZH, S_Z = range(5)


def norm_rows(values_in):
    centred = values_in - jnp.mean(values_in, -1, keepdims=True)
    variance = jnp.mean(centred * centred, -1, keepdims=True)
    inverse = lax.rsqrt(variance + EPS)
    return centred * inverse, inverse


def norm_back_rows(grad, normed, inverse, gain):
    scaled = grad * gain
    centred = scaled - jnp.mean(scaled, -1, keepdims=True) - normed * jnp.mean(scaled * normed, -1, keepdims=True)
    return centred * inverse


def fold_rows(values_in):
    return jnp.sum(values_in.reshape(-1, 8, values_in.shape[-1]), 0)


def read(part, rows):
    return (part[0, rows, :] if len(part.shape) == 3 else part[rows, :]).astype(F32)


def part_spec(part):
    shape = part.shape
    return full(shape) if len(shape) == 2 else pl.BlockSpec((1,) + shape[1:], lambda *_: (0, 0, 0))


ONE, ZERO, TABLE = 0, 1, 16


def gain_row(layer, index):
    return 2 + 6 * layer + index


def shift_row(layer, index):
    return 4 + 6 * layer + index


def row_of(vec_ref, row):
    return vec_ref[row : row + 1, :]


def norm_forward(get_total, tokens, vec, gain, shift, n_ref, low_ref, inv_ref):

    def step(index, carry):
        rows = pl.ds(pl.multiple_of(index * CHUNK, CHUNK), CHUNK)
        normed, inverse = norm_rows(get_total(rows))
        n_ref[rows, :] = normed
        low_ref[rows, :] = (normed * row_of(vec, gain) + row_of(vec, shift)).astype(BF16)
        inv_ref[rows, :] = jnp.broadcast_to(inverse, (CHUNK, 128))
        return carry

    lax.fori_loop(0, tokens // CHUNK, step, 0)


def norm_backward(get_grad, tokens, n_ref, inv_ref, vec, gain, g_ref, low_ref, sums_ref):
    def step(index, carry):
        rows = pl.ds(pl.multiple_of(index * CHUNK, CHUNK), CHUNK)
        grad = get_grad(rows)
        normed = n_ref[rows, :]
        result = norm_back_rows(grad, normed, inv_ref[rows, 0:1], row_of(vec, gain))
        low = result.astype(BF16)
        g_ref[rows, :] = result
        low_ref[rows, :] = low
        return (
            carry[0] + fold_rows(grad * normed),
            carry[1] + fold_rows(grad),
            carry[2] + fold_rows(low.astype(F32)),
        )

    zero = jnp.zeros((8, D), F32)
    sums = lax.fori_loop(0, tokens // CHUNK, step, (zero, zero, zero))
    sums_ref[...] = jnp.zeros(sums_ref.shape, F32)
    for row, member in enumerate(sums):
        sums_ref[row : row + 1, :] = jnp.sum(member, 0, keepdims=True)


def away(s):
    return (s & 1) * 2 + s // 2


class Streamed:
    def __init__(self, refs, matrix, buffer, sems, scal):
        self.refs, self.matrix, self.buffer, self.sems, self.scal = refs, matrix, buffer, sems, scal

    def copies(self, s):
        slot = lax.rem(s, 2)
        for k in range(2):
            main, far = self.refs[2 * k : 2 * k + 2]
            for r in range(4):
                row = ((self.scal[S_Q] ^ r) * 2 + (self.scal[S_C] ^ k)) * ROWS
                source = far.at[s, self.matrix] if r == 3 else main.at[r, s, self.matrix]
                yield pltpu.make_async_copy(
                    source, self.buffer.at[slot, pl.ds(pl.multiple_of(row, ROWS), ROWS), :], self.sems.at[slot, 4 * k + r]
                )

    def start(self, s):
        for copy in self.copies(s):
            copy.start()

    def wait(self, s):
        for copy in self.copies(s):
            copy.wait()

    def turn(self, s, count):
        @pl.when(s == 0)
        def _():
            self.start(s)

        @pl.when(s + 1 < count)
        def _():
            self.start(s + 1)


def piece_shapes(width):
    return [pltpu.VMEM((2, D, width), BF16), pltpu.SemaphoreType.DMA((2, 8))]


def gelu_parts(u):
    size = jnp.abs(u)
    t = 1.0 / (1.0 + 0.2316419 * size)
    poly = t * (0.127414796 + t * (-0.142248368 + t * (0.7107068705 + t * (-0.7265760135 + t * 0.5307027145))))
    bell = jnp.exp(-0.5 * (u * u))
    tail = poly * bell
    cdf = jnp.where(u >= 0, 1.0 - tail, tail)
    return u * cdf, cdf + u * (0.3989422804014327 * bell)


def tiles(tokens, width):
    for i in range(2):
        for j in range(2):
            yield slice(i * tokens // 2, (i + 1) * tokens // 2), slice(j * width // 2, (j + 1) * width // 2)


def norm_up(flow, prev, parts, vec, rows_used, weight, matrix, bias, count):
    tokens = prev.shape[0]
    width = FF // count

    def body(scal_ref, prev_ref, *refs):
        part_refs, refs = refs[: len(parts)], refs[len(parts) :]
        vec_ref, bias_ref, refs = refs[0], refs[1], refs[2:]
        pieces, (n_ref, low_ref, inv_ref, act_ref, slope_ref, buffer, sems) = refs[:4], refs[4:]
        s = pl.program_id(0)
        stream = Streamed(pieces, matrix, buffer, sems, scal_ref)
        stream.turn(s, count)

        @pl.when(s == 0)
        def _():
            def total(rows):
                attn = read(part_refs[0], rows)
                for part in part_refs[1:]:
                    attn = attn + read(part, rows)
                before = read(prev_ref, rows) * row_of(vec_ref, rows_used[0]) + row_of(vec_ref, rows_used[1])
                return before + (attn + row_of(vec_ref, rows_used[2]))

            norm_forward(total, tokens, vec_ref, *rows_used[3:], n_ref, low_ref, inv_ref)

        stream.wait(s)
        slot = lax.rem(s, 2)
        for rows, cols in tiles(tokens, width):
            act, slope = gelu_parts(mm(low_ref[rows, :], buffer[slot, :, cols]) + bias_ref[0, :, cols])
            act_ref[rows, cols] = act.astype(BF16)
            slope_ref[rows, cols] = slope.astype(BF16)

    column = pl.BlockSpec((tokens, width), lambda s, _: (0, s))
    return call(
        flow, body, (count,),
        [full((tokens, D))] + [part_spec(part) for part in parts]
        + [full((TABLE, D)), pl.BlockSpec((1, 1, width), lambda s, scal_ref: (scal_ref[S_Z] ^ away(s), 0, 0))] + [ANY] * 4,
        [full((tokens, D)), full((tokens, D)), full((tokens, 128)), column, column],
        [sds((tokens, D), F32), sds((tokens, D), BF16), sds((tokens, 128), F32)] + [sds((tokens, FF), BF16)] * 2,
        piece_shapes(width), [prev, *parts, vec, bias, *weight], 2 * tokens * D * FF,
        2 * (D * FF + tokens * (10 * D + 2 * FF)), "norm_up",
    )


def down_norm(flow, act, weight, matrix, prev, vec, rows_used, count):
    tokens = prev.shape[0]
    width = FF // count

    def body(scal_ref, act_ref, prev_ref, vec_ref, *refs):
        pieces, (n_ref, low_ref, inv_ref, buffer, sems, acc) = refs[:4], refs[4:]
        s = pl.program_id(0)
        stream = Streamed(pieces, matrix, buffer, sems, scal_ref)
        stream.turn(s, count)
        stream.wait(s)
        value = mm(act_ref[...], buffer[lax.rem(s, 2)], NT)

        @pl.when(s == 0)
        def _():
            acc[...] = value

        @pl.when(s > 0)
        def _():
            acc[...] += value

        @pl.when(s == count - 1)
        def _():
            def total(rows):
                before = prev_ref[rows, :] * row_of(vec_ref, rows_used[0]) + row_of(vec_ref, rows_used[1])
                return before + (acc[rows, :] + row_of(vec_ref, rows_used[2]))

            norm_forward(total, tokens, vec_ref, *rows_used[3:], n_ref, low_ref, inv_ref)

    return call(
        flow, body, (count,),
        [pl.BlockSpec((tokens, width), lambda s, _: (0, s)), full((tokens, D)), full((TABLE, D))] + [ANY] * 4,
        [full((tokens, D)), full((tokens, D)), full((tokens, 128))],
        [sds((tokens, D), F32), sds((tokens, D), BF16), sds((tokens, 128), F32)],
        piece_shapes(width) + [pltpu.VMEM((tokens, D), F32)], [act, prev, vec, *weight], 2 * tokens * D * FF,
        2 * (D * FF + tokens * (5 * D + FF)), "down_norm",
    )


def units_back(flow, grad, weight, matrix, slope, count):
    tokens = grad.shape[0]
    width = FF // count

    def body(scal_ref, grad_ref, slope_ref, *refs):
        pieces, (out_ref, sum_ref, buffer, sems) = refs[:4], refs[4:]
        s = pl.program_id(0)
        stream = Streamed(pieces, matrix, buffer, sems, scal_ref)
        stream.turn(s, count)
        stream.wait(s)
        slot = lax.rem(s, 2)
        sums = {}
        for rows, cols in tiles(tokens, width):
            low = (mm(grad_ref[rows, :], buffer[slot, :, cols]) * slope_ref[rows, cols].astype(F32)).astype(BF16)
            out_ref[rows, cols] = low
            part = fold_rows(low.astype(F32))
            sums[cols.start] = sums[cols.start] + part if cols.start in sums else part
            if rows.start > 0:
                sum_ref[0, :, cols] = jnp.sum(sums[cols.start], 0, keepdims=True)

    column = pl.BlockSpec((tokens, width), lambda s, _: (0, s))
    return call(
        flow, body, (count,), [full((tokens, D)), column] + [ANY] * 4,
        [column, pl.BlockSpec((1, 1, width), lambda s, scal_ref: (scal_ref[S_Z] ^ away(s), 0, 0))],
        [sds((tokens, FF), BF16), sds((count, 1, width), F32)], piece_shapes(width), [grad, slope, *weight],
        2 * tokens * D * FF, 2 * (D * FF + tokens * (D + 2 * FF)), "units_back",
    )


def up_back(flow, gu, weight, matrix, residual, normed, inverse, vec, gain, count):
    tokens = residual.shape[0]
    width = FF // count

    def body(scal_ref, gu_ref, res_ref, n_ref, inv_ref, vec_ref, *refs):
        pieces, (g_ref, low_ref, sums_ref, buffer, sems, acc) = refs[:4], refs[4:]
        s = pl.program_id(0)
        stream = Streamed(pieces, matrix, buffer, sems, scal_ref)
        stream.turn(s, count)
        stream.wait(s)
        value = mm(gu_ref[...], buffer[lax.rem(s, 2)], NT)

        @pl.when(s == 0)
        def _():
            acc[...] = value

        @pl.when(s > 0)
        def _():
            acc[...] += value

        @pl.when(s == count - 1)
        def _():
            norm_backward(
                lambda rows: res_ref[rows, :] + acc[rows, :], tokens, n_ref, inv_ref, vec_ref, gain, g_ref, low_ref,
                sums_ref,
            )

    return call(
        flow, body, (count,),
        [pl.BlockSpec((tokens, width), lambda s, _: (0, s)), full((tokens, D)), full((tokens, D)), full((tokens, 128)),
         full((TABLE, D))] + [ANY] * 4,
        [full((tokens, D)), full((tokens, D)), full((8, D))],
        [sds((tokens, D), F32), sds((tokens, D), BF16), sds((8, D), F32)],
        piece_shapes(width) + [pltpu.VMEM((tokens, D), F32)], [gu, residual, normed, inverse, vec, *weight],
        2 * tokens * D * FF, 2 * (D * FF + tokens * (8 * D + FF)), "up_back",
    )


def norm_back(flow, grad, normed, inverse, vec, gain):
    tokens = grad.shape[0]

    def body(scal_ref, grad_ref, n_ref, inv_ref, vec_ref, g_ref, low_ref, sums_ref):
        norm_backward(lambda rows: read(grad_ref, rows), tokens, n_ref, inv_ref, vec_ref, gain, g_ref, low_ref, sums_ref)

    return call(
        flow, body, (1,), [full((tokens, D)), full((tokens, D)), full((tokens, 128)), full((TABLE, D))],
        [full((tokens, D)), full((tokens, D)), full((8, D))],
        [sds((tokens, D), F32), sds((tokens, D), BF16), sds((8, D), F32)], [], [grad, normed, inverse, vec],
        20 * tokens * D, 12 * tokens * D, "norm_back",
    )


def sum_norm_back(flow, residual, parts, normed, inverse, vec, gain):
    tokens = residual.shape[0]

    def body(scal_ref, res_ref, *refs):
        part_refs, (n_ref, inv_ref, vec_ref, g_ref, low_ref, sums_ref) = refs[: len(parts)], refs[len(parts) :]

        def grad(rows):
            total = read(part_refs[0], rows)
            for part in part_refs[1:]:
                total = total + read(part, rows)
            return res_ref[rows, :] + total

        norm_backward(grad, tokens, n_ref, inv_ref, vec_ref, gain, g_ref, low_ref, sums_ref)

    return call(
        flow, body, (1,), [full((tokens, D))] + [part_spec(part) for part in parts]
        + [full((tokens, D)), full((tokens, 128)), full((TABLE, D))],
        [full((tokens, D)), full((tokens, D)), full((8, D))],
        [sds((tokens, D), F32), sds((tokens, D), BF16), sds((8, D), F32)], [],
        [residual, *parts, normed, inverse, vec], 20 * tokens * D, 22 * tokens * D, "sum_norm_back",
    )


def turn_rows(scal_ref, x_ref, turned, core):
    for r in range(4):
        row = ((scal_ref[S_Q] ^ r) * 2 + core) * ROWS
        turned[r * ROWS : (r + 1) * ROWS, :] = x_ref[:, pl.ds(pl.multiple_of(row, ROWS), ROWS)].T


def unit_grads(flow, down, up, received, count, sibling):
    tokens = down[0].shape[0]
    width = down[1].shape[1] // count
    half = count // 2
    steps = 2 * count

    def body(scal_ref, x0_ref, y0_ref, x1_ref, y1_ref, *refs):
        turned, t = refs[-1], pl.program_id(0)
        m, s = t // count, lax.rem(t, count)
        core = scal_ref[S_C] ^ 1 if sibling else scal_ref[S_C]

        @pl.when(t == 0)
        def _():
            turn_rows(scal_ref, x0_ref, turned, core)

        @pl.when(t == count)
        def _():
            turn_rows(scal_ref, x1_ref, turned, core)

        def store(y_ref):
            value = mm(turned[...], y_ref[...]).reshape(4, ROWS, width)
            if sibling:
                refs[0][:, 0] = value.astype(BF16)
                return
            if received is not None:
                value = value + refs[0][:, 0].astype(F32)
            value = value.astype(BF16)
            own, to_x, to_y, rest_x, rest_y = refs[-6:-1]
            spot = lax.rem(s, half) * 2 + m
            own[s // half * count + spot] = value[0]

            @pl.when(s < half)
            def _():
                to_x[spot] = value[1]
                to_x[count + spot] = value[3]
                rest_y[spot] = value[2]

            @pl.when(s >= half)
            def _():
                rest_x[spot] = value[1]
                to_y[spot] = value[2]
                to_y[count + spot] = value[3]

        @pl.when(m == 0)
        def _():
            store(y0_ref)

        @pl.when(m == 1)
        def _():
            store(y1_ref)

    left = full((tokens, D))
    pick_down = lambda t, _: (0, jnp.minimum(t, count - 1))
    pick_up = lambda t, _: (0, jnp.maximum(t - count, 0))
    specs = [left, pl.BlockSpec((tokens, width), pick_down), left, pl.BlockSpec((tokens, width), pick_up)]
    args = [*down, *up]
    one = pl.BlockSpec((4, 1, ROWS, width), lambda t, _: (0, t, 0, 0))
    if sibling:
        out_specs, out_shape = one, sds((4, steps, ROWS, width), BF16)
    else:
        if received is not None:
            specs.append(one)
            args.append(received)
        shapes = [(steps, ROWS, width)] * 3 + [(count, ROWS, width)] * 2
        out_specs, out_shape = [full(shape) for shape in shapes], [sds(shape, BF16) for shape in shapes]
    return call(
        flow, body, (steps,), specs, out_specs, out_shape, [pltpu.VMEM((4 * ROWS, tokens), BF16)], args,
        0, 0, "grads_theirs" if sibling else "grads_mine",
    )


def fetch_heads_weight(scal_ref, pieces, cols, buffer, sems):
    copies = []
    for r in range(4):
        for k in range(2):
            row = ((scal_ref[S_Q] ^ r) * 2 + (scal_ref[S_ZH] ^ k)) * ROWS
            copies.append(
                pltpu.make_async_copy(
                    pieces[r // 2].at[r % 2, k, pl.ds(0, ROWS), cols], buffer.at[pl.ds(pl.multiple_of(row, ROWS), ROWS), :],
                    sems.at[2 * r + k],
                )
            )
    for copy in copies:
        copy.start()
    for copy in copies:
        copy.wait()


def by_member(shape):
    return pl.BlockSpec((1,) + shape, lambda r, scal_ref: (scal_ref[S_P] ^ r, 0, 0))


def heads_weight_scratch(width):
    return [pltpu.VMEM((D, width), BF16), pltpu.SemaphoreType.DMA((8,))]


def project_in(flow, lefts, across, weight, cols, bias, name):
    tokens = lefts[0].shape[0]
    width = cols.stop - cols.start

    def body(scal_ref, left_ref, right_ref, *refs):
        if bias is not None:
            bias_ref, refs = refs[0], refs[1:]
        pieces, (out_ref, buffer, sems) = refs[:2], refs[2:]
        step = pl.program_id(0)

        @pl.when(step == 0)
        def _():
            fetch_heads_weight(scal_ref, pieces, cols, buffer, sems)

        for r, left in enumerate((left_ref, right_ref)):

            @pl.when(step == r)
            def _(left=left):
                value = mm(left[...], buffer[...])
                if bias is not None:
                    value = value + bias_ref[...]
                out_ref[0] = value.astype(BF16)

    extra, extra_specs = ([], []) if bias is None else ([bias], [full((1, width))])
    return call(
        flow, body, (2,), [full((tokens, D))] * 2 + extra_specs + [ANY] * 2,
        pl.BlockSpec((1, tokens, width), lambda r, scal_ref: ((scal_ref[S_P] >> 1) ^ r, 0, 0)),
        sds((2, tokens, width), BF16), heads_weight_scratch(width), [*lefts, *extra, *weight], 0, 0, name,
    )


def project_out(flow, blocks, members, weight, cols, stacked, name):
    count, tokens, width = blocks[0].shape

    def body(scal_ref, *refs):
        block_refs, refs = refs[: len(blocks)], refs[len(blocks) :]
        pieces, outs, (buffer, sems) = refs[:2], refs[2:-2], refs[-2:]
        step = pl.program_id(0)

        @pl.when(step == 0)
        def _():
            fetch_heads_weight(scal_ref, pieces, cols, buffer, sems)

        value = mm(block_refs[0][0], buffer[:, :width], NT)
        for index in range(1, len(blocks)):
            value = value + mm(block_refs[index][0], buffer[:, index * width : (index + 1) * width], NT)
        value = value.astype(BF16)
        if stacked:
            outs[0][0] = value
            return
        for r, out in enumerate(outs):

            @pl.when(step == r)
            def _(out=out):
                out[...] = value

    first, last = members
    pick = lambda r, scal_ref: (scal_ref[S_P] ^ (first + r * (last - first)), 0, 0)
    if stacked:
        out_specs, out_shape = pl.BlockSpec((1, tokens, D), lambda r, _: (r, 0, 0)), sds((2, tokens, D), BF16)
    else:
        out_specs, out_shape = [full((tokens, D))] * 2, [sds((tokens, D), BF16)] * 2
    return call(
        flow, body, (2,), [pl.BlockSpec((1, tokens, width), pick)] * len(blocks) + [ANY] * 2, out_specs, out_shape,
        heads_weight_scratch(width * len(blocks)), [*blocks, *weight], 0, 0, name,
    )


def heads_grad(flow, xs, parts, gas, ctx):
    count, tokens, width = parts[0].shape
    out_width = ctx.shape[2]
    cuts = [slice(i * width, (i + 1) * width) for i in range(len(parts))]
    total = width * len(parts)

    def body(scal_ref, *refs):
        x_refs, refs = refs[:count], refs[count:]
        ga_refs, refs = refs[:count], refs[count:]
        part_refs, refs = refs[: len(parts)], refs[len(parts) :]
        ctx_ref, outs, (sum_ref, acc, acc_out) = refs[0], refs[1:3], refs[3:]
        step = pl.program_id(0)
        for r in range(count):

            @pl.when(step == r)
            def _(r=r):
                turned = x_refs[r][...].T
                value_out = mm(ga_refs[r][...].T, ctx_ref[0])
                for cut, part in zip(cuts, part_refs):
                    value = mm(turned, part[0])
                    sums = jnp.sum(part[0].astype(F32), 0, keepdims=True)
                    acc[:, cut] = value if r == 0 else acc[:, cut] + value
                    sum_ref[:, cut] = sums if r == 0 else sum_ref[:, cut] + sums
                acc_out[...] = value_out if r == 0 else acc_out[...] + value_out

        @pl.when(step == count - 1)
        def _():
            for r in range(4):
                for k in range(2):
                    row = ((scal_ref[S_Q] ^ r) * 2 + (scal_ref[S_ZH] ^ k)) * ROWS
                    rows = pl.ds(pl.multiple_of(row, ROWS), ROWS)
                    outs[r % 2][r // 2, k, :, :total] = acc[rows, :].astype(BF16)
                    outs[r % 2][r // 2, k, :, total:] = acc_out[rows, :].astype(BF16)

    shape = (2, 2, ROWS, total + out_width)
    return call(
        flow, body, (count,),
        [full((tokens, D))] * (2 * count) + [by_member((tokens, width))] * len(parts) + [by_member((tokens, out_width))],
        [full(shape)] * 2 + [full((1, total))], [sds(shape, BF16)] * 2 + [sds((1, total), F32)],
        [pltpu.VMEM((D, total), F32), pltpu.VMEM((D, out_width), F32)], [*xs, *gas, *parts, ctx], 0, 0, "heads_grad",
    )


def reach(ends_ref, row):
    first = jnp.zeros_like(row)
    for index in range(3):
        first = jnp.where(row >= ends_ref[index], ends_ref[index], first)
    last = jnp.full_like(row, SEQLEN)
    for index in (2, 1, 0):
        last = jnp.where(row < ends_ref[index], ends_ref[index], last)
    return jnp.maximum(first, row - (WINDOW - 1)), jnp.minimum(last, row + WINDOW)


def chunks_of(scal_ref, near_ref, far_ref):
    here = scal_ref[S_P] & 1
    for core in range(2):
        yield 2 * core + here, near_ref.at[core]
        yield 2 * core + 1 - here, far_ref.at[core]


def over_keys(ends_ref, start, chunk, keys_first, block):
    low_first, high_first = reach(ends_ref, start)
    low_last, high_last = reach(ends_ref, start + BQ - 1)
    axis = 1 if keys_first else 0
    low_row, high_row = reach(ends_ref, start + lax.broadcasted_iota(jnp.int32, (1, BQ) if keys_first else (BQ, 1), axis))
    shape = (chunk, BQ) if keys_first else (BQ, chunk)

    def one(b, carry):
        open_all = (b * chunk >= low_last) & ((b + 1) * chunk <= high_first)

        @pl.when(open_all)
        def _():
            block(b, None)

        @pl.when(jnp.logical_not(open_all))
        def _():
            key = b * chunk + lax.broadcasted_iota(jnp.int32, shape, 1 - axis)
            block(b, (key >= low_row) & (key < high_row))

        return carry

    lax.fori_loop(low_first // chunk, (high_last + chunk - 1) // chunk, one, 0)


def attend_forward(flow, ends, qkv):
    _, chunk, width3 = qkv[0].shape
    count = SEQLEN // chunk
    width = width3 // 3
    heads = width // HD
    steps = SEQLEN // BQ
    per = chunk // BQ

    def body(scal_ref, ends_ref, near_ref, far_ref, ctx_ref, wide_ref, lse_ref, qt, kh, vt, acc, tops, sums, scores):
        step = pl.program_id(0)

        @pl.when(step == 0)
        def _():
            for j, block in chunks_of(scal_ref, near_ref, far_ref):
                rows = pl.ds(pl.multiple_of(j * chunk, chunk), chunk)
                for pair in range(heads // 2):
                    base = 3 * PAIR * pair
                    part = slice(pair * PAIR, (pair + 1) * PAIR)
                    vt[j, part, :] = block[:, base + 2 * PAIR : base + 3 * PAIR].T
                    for s in range(per):
                        queries = block[s * BQ : (s + 1) * BQ, base : base + PAIR] * BF16(HD**-0.5)
                        qt[j * per + s, part, :] = queries.T
                    for h in range(2):
                        kh[2 * pair + h, rows, :] = block[:, base + PAIR + h * HD : base + PAIR + (h + 1) * HD]

        start = step * BQ
        acc[...] = jnp.zeros(acc.shape, F32)
        tops[...] = jnp.full(tops.shape, -3.0e38, F32)
        sums[...] = jnp.zeros(sums.shape, F32)

        def score(b, allowed):
            keys = pl.ds(pl.multiple_of(b * chunk, chunk), chunk)
            for h in range(heads):
                value = mm(kh[h, keys, :], qt[step, h * HD : (h + 1) * HD, :])
                if allowed is not None:
                    value = jnp.where(allowed, value, FILL)
                scores[h, b] = value
                tops[h] = jnp.maximum(tops[h], jnp.max(value.reshape(-1, 8, BQ), 0))

        over_keys(ends_ref, start, chunk, True, score)
        top = [jnp.max(tops[h], 0, keepdims=True) for h in range(heads)]

        def weigh(b, carry):
            for h in range(heads):
                part = slice(h * HD, (h + 1) * HD)
                weight = jnp.exp(scores[h, b] - top[h])
                sums[h] += fold_rows(weight)
                acc[part, :] += mm(vt[b, part, :], weight.astype(BF16))
            return carry

        low_first, _ = reach(ends_ref, start)
        _, high_last = reach(ends_ref, start + BQ - 1)
        lax.fori_loop(low_first // chunk, (high_last + chunk - 1) // chunk, weigh, 0)
        lse_ref[...] = jnp.zeros(lse_ref.shape, F32)
        for h in range(heads):
            part = slice(h * HD, (h + 1) * HD)
            total = jnp.sum(sums[h], 0, keepdims=True)
            acc[part, :] = acc[part, :] / total
            lse_ref[0, h : h + 1, :] = top[h] + jnp.log(total)
        wide = acc[...].T
        wide_ref[0] = wide
        ctx_ref[0] = wide.astype(BF16)

    row_block = lambda i, *_: (i // per, i % per, 0)
    return call(
        flow, body, (steps,), [full((2, chunk, width3))] * 2,
        [pl.BlockSpec((1, BQ, width), row_block), pl.BlockSpec((1, BQ, width), row_block),
         pl.BlockSpec((1, 8, BQ), lambda i, *_: (i, 0, 0))],
        [sds((count, chunk, width), BF16), sds((count, chunk, width), F32), sds((steps, 8, BQ), F32)],
        [
            pltpu.VMEM((steps, width, BQ), BF16),
            pltpu.VMEM((heads, SEQLEN, HD), BF16),
            pltpu.VMEM((count, width, chunk), BF16),
            pltpu.VMEM((width, BQ), F32),
            pltpu.VMEM((heads, 8, BQ), F32),
            pltpu.VMEM((heads, 8, BQ), F32),
            pltpu.VMEM((heads, count, chunk, BQ), F32),
        ],
        [*qkv], 0, 0, "attend_forward", (flow.scal, ends),
    )


def attend_backward(flow, ends, pair, qkv, grads, wide, lse):
    chunk = qkv[0].shape[1]
    count = SEQLEN // chunk
    steps = SEQLEN // BQ
    per = chunk // BQ

    def body(
        scal_ref, ends_ref, near_ref, far_ref, grad_near, grad_far, wide_ref, lse_ref, out_ref, qh, kh, gh, kt, vt, qt, gt,
        gq, gk, gv,
    ):
        step = pl.program_id(0)

        @pl.when(step == 0)
        def _():
            blocks = chunks_of(scal_ref, near_ref, far_ref)
            grad_blocks = chunks_of(scal_ref, grad_near, grad_far)
            for (j, block), (_, grad_block) in zip(blocks, grad_blocks):
                rows = pl.ds(pl.multiple_of(j * chunk, chunk), chunk)
                queries = block[:, :PAIR] * BF16(HD**-0.5)
                keys = block[:, PAIR : 2 * PAIR]
                back = grad_block[...]
                for h in range(2):
                    cols = slice(h * HD, (h + 1) * HD)
                    qh[h, rows, :] = queries[:, cols]
                    kh[h, rows, :] = keys[:, cols]
                    gh[h, rows, :] = back[:, cols]
                kt[j] = keys.T
                vt[j] = block[:, 2 * PAIR :].T
                for s in range(per):
                    sub = slice(s * BQ, (s + 1) * BQ)
                    qt[j * per + s] = queries[sub, :].T
                    gt[j * per + s] = back[sub, :].T
            gk[...] = jnp.zeros(gk.shape, F32)
            gv[...] = jnp.zeros(gv.shape, F32)

        start = step * BQ
        rows = pl.ds(pl.multiple_of(start, BQ), BQ)
        gq[...] = jnp.zeros(gq.shape, F32)
        sums = lse_ref[0].T
        inner, logs = [], []
        for h in range(2):
            product = gh[h, rows, :].astype(F32) * wide_ref[0, :, h * HD : (h + 1) * HD]
            inner.append(jnp.sum(product, 1, keepdims=True))
            logs.append(sums[:, 2 * pair + h : 2 * pair + h + 1])

        def block(b, allowed):
            keys = pl.ds(pl.multiple_of(b * chunk, chunk), chunk)
            for h in range(2):
                part = slice(h * HD, (h + 1) * HD)
                score = mm(qh[h, rows, :], kt[b, part, :])
                grad_weight = mm(gh[h, rows, :], vt[b, part, :])
                if allowed is not None:
                    score = jnp.where(allowed, score, FILL)
                weight = jnp.exp(score - logs[h])
                grad_score = (weight * (grad_weight - inner[h])).astype(BF16)
                gv[b, part, :] += mm(gt[step, part, :], weight.astype(BF16))
                gk[b, part, :] += mm(qt[step, part, :], grad_score)
                gq[h] += mm(grad_score, kh[h, keys, :])

        over_keys(ends_ref, start, chunk, False, block)
        place = pl.ds(pl.multiple_of((step % per) * BQ, BQ), BQ)
        for h in range(2):
            out_ref[step // per, place, h * HD : (h + 1) * HD] = (gq[h] * HD**-0.5).astype(BF16)

        @pl.when(step == steps - 1)
        def _():
            for j in range(count):
                out_ref[j, :, PAIR : 2 * PAIR] = gk[j].T.astype(BF16)
                out_ref[j, :, 2 * PAIR :] = gv[j].T.astype(BF16)

    out = (count, chunk, 3 * PAIR)
    return call(
        flow, body, (steps,),
        [pl.BlockSpec((2, chunk, 3 * PAIR), lambda i, *_: (0, 0, pair))] * 2
        + [pl.BlockSpec((2, chunk, PAIR), lambda i, *_: (0, 0, pair))] * 2
        + [pl.BlockSpec((1, BQ, PAIR), lambda i, *_: (i // per, i % per, pair)),
           pl.BlockSpec((1, 8, BQ), lambda i, *_: (i, 0, 0))],
        full(out), sds(out, BF16),
        [pltpu.VMEM((2, SEQLEN, HD), BF16)] * 3
        + [pltpu.VMEM((count, PAIR, chunk), BF16)] * 2
        + [pltpu.VMEM((steps, PAIR, BQ), BF16)] * 2
        + [pltpu.VMEM((2, BQ, HD), F32)]
        + [pltpu.VMEM((count, PAIR, chunk), F32)] * 2,
        [*qkv, *grads, wide, lse], 0, 0, "attend_backward", (flow.scal, ends),
    )


def flip(values_in, axes, mask):
    return lax.ppermute(values_in, axes, [(a, a ^ mask) for a in range(lax.axis_size(axes))])


def turn(values_in):
    return lax.ppermute(values_in, ("c", "zh"), [(2 * a + b, 2 * b + a) for a in range(2) for b in range(2)])


def cross(values_in):
    return lax.ppermute(values_in, ("c", "zh"), [(2 * a + b, 2 * b + 1 - a) for a in range(2) for b in range(2)])


def uncross(values_in):
    return lax.ppermute(values_in, ("c", "zh"), [(2 * b + 1 - a, 2 * a + b) for a in range(2) for b in range(2)])


def from_members(values_in, axes):
    return [values_in] + [flip(values_in, axes, r) for r in range(1, lax.axis_size(axes))]


def to_members(parts, axes):
    return [parts[0]] + [flip(part, axes, r) for r, part in enumerate(parts) if r > 0]


def add(*parts):
    total = parts[0].astype(F32)
    for part in parts[1:]:
        total = total + part.astype(F32)
    return total


def is_small():
    return lax.axis_size("q") == 4


def order_by(values_in, axis, position, count):
    bit = 1
    while bit < count:
        shape = values_in.shape
        split = shape[:axis] + (count // (2 * bit), 2, bit) + shape[axis + 1 :]
        cut = values_in.reshape(split)
        values_in = jnp.where((position & bit) != 0, jnp.flip(cut, axis + 1), cut).reshape(shape)
        bit *= 2
    return values_in


def gather_group(values_in):
    across, sibling = flip(values_in, GROUP, 1), flip(values_in, GROUP, 2)
    return [values_in, across, sibling]


def forward(flow, members, *before):
    flow.wait(*before)
    flow.hold(across=members[1])
    gate(flow)
    members[1] = flow.free("across")
    members.append(flip(members[1], GROUP, 2))


def sum_group(keep, send):
    got = flip(send, GROUP, 2)
    passed = add(keep[1], got[1]).astype(BF16)
    return [keep[0], got, flip(passed, GROUP, 1)], passed


EXTRA = 16


def heads_shard_of(qkv, out, bias):
    rows = out.shape[0]
    paired = qkv.reshape(3, rows, -1, PAIR).transpose(1, 2, 0, 3).reshape(rows, -1)
    weights = jnp.concatenate([paired, out], axis=1)
    below = jnp.pad(bias.reshape(1, -1), ((0, EXTRA - 1), (0, weights.shape[1] - bias.size)))
    return jnp.concatenate([weights, below])


def heads_bias(rows, heads):
    bias = rows.reshape(rows.shape[0], 2, heads, -1).transpose(1, 2, 0, 3).reshape(2, -1).astype(F32)
    bias = jnp.stack([bias[0], jnp.zeros_like(bias[0]), bias[1]])
    return bias.reshape(3, -1, PAIR).transpose(1, 0, 2).reshape(1, -1)


def heads_along_x(pair):
    return jnp.stack([pair, flip(pair, "q", 1)])


def heads_along_y(near, size, heads, where, zh):
    far = flip(near, "q", 2)
    rows = jnp.concatenate([near[:, :, ROWS, :size], far[:, :, ROWS, :size]])
    return [near, far], heads_bias(order_by(order_by(rows, 0, where[0], 4), 1, zh, 2).reshape(8, size), heads)


def all_heads_weight(shard, size, heads, zh):
    pair = jnp.stack([turn(shard), cross(shard)])
    every = order_by(lax.all_gather(pair, "q"), 1, zh, 2)
    count = shard.shape[0] - EXTRA
    weights = every[:, :, :count].reshape(4, 2, ROWS, -1)
    return [weights[:2], weights[2:]], heads_bias(every[:, :, count, :size].reshape(-1, size), heads)


class HeadsGrad:
    def __init__(self, keep, send):
        self.keep, self.send = keep, send

    def along_x(self):
        self.got = flip(self.send, "q", 1)
        return self.got

    def along_y(self):
        self.here = add(self.keep[0], self.got[0])
        self.got = flip(add(self.keep[1], self.got[1]).astype(BF16), "q", 2)
        return self.got

    def halves(self, zh):
        if is_small():
            total = add(self.here, self.got).astype(BF16)
            return total[0], total[1]
        buckets = [self.keep[0], self.send[0], self.keep[1], self.send[1]]
        every = jnp.stack(buckets).reshape(lax.axis_size("q"), 2, -1, buckets[0].shape[-1])
        rows = order_by(lax.psum_scatter(every, "q", scatter_dimension=0, tiled=False), 0, zh, 2)
        return rows[0], rows[1]


SLOTS = (0, 2, 1, 3)


def all_units_weight(shard):
    matrices, _, width = shard.shape
    members = lax.axis_size(MODEL)
    every = lax.all_gather(shard, ALL).reshape(members, -1, matrices, shard.shape[1], width).transpose(0, 2, 1, 3, 4)
    every = every.reshape(members, matrices, 4, 2, ROWS, width)
    every = jnp.stack([every[slot] for slot in SLOTS])
    pieces = []
    for k in range(2):
        pieces += [jnp.stack([every[:, :, r, k] for r in range(3)]), every[:, :, 3, k]]
    return pieces


class UnitsWeight:
    def __init__(self, shard):
        self.shard = shard

    def start_far_z(self):
        self.other = flip(self.shard, "zh", 1)

    def join_far_z(self, shard):
        self.two = jnp.stack([shard, self.other])

    def far_z(self):
        self.start_far_z()
        self.join_far_z(self.shard)

    def start_z(self):
        self.other = flip(self.two, "zl", 1)

    def join_z(self, two):
        self.own = jnp.concatenate([two, self.other])

    def near_z(self):
        self.start_z()
        self.join_z(self.two)

    def near(self):
        self.near_x, self.near_y = flip(self.own, "q", 1), flip(self.own, "q", 2)

    def corner(self):
        self.far_a, self.far_b = flip(self.near_y[:2], "q", 1), flip(self.near_x[2:], "q", 2)

    def swap_main(self):
        self.main = jnp.stack([self.own, self.near_x, self.near_y])
        self.main_sibling = flip(self.main, "c", 1)

    def swap_corner(self):
        self.far = jnp.concatenate([self.far_a, self.far_b])
        self.far_sibling = flip(self.far, "c", 1)

    def pieces(self):
        return [self.main, self.far, self.main_sibling, self.far_sibling]


class UnitsGrads:
    def __init__(self, flow, down, up, count):
        self.flow, self.down, self.up, self.count = flow, down, up, count

    def compute_theirs(self):
        self.theirs = unit_grads(self.flow, self.down, self.up, None, self.count, True)

    def send_theirs(self):
        self.got = flip(self.theirs, "c", 1) if is_small() else None

    def sibling(self):
        self.compute_theirs()
        self.send_theirs()

    def mine(self):
        self.made = unit_grads(self.flow, self.down, self.up, self.got, self.count, False)
        self.own, self.to_x, self.to_y, self.rest_x, self.rest_y = self.made

    def near(self):
        self.from_x, self.from_y = flip(self.to_x, "q", 1), flip(self.to_y, "q", 2)
        return [self.from_x, self.from_y]

    def far(self):
        half = self.count
        self.late_x = flip(add(self.rest_x, self.from_y[half:]).astype(BF16), "q", 1)
        self.late_y = flip(add(self.rest_y, self.from_x[half:]).astype(BF16), "q", 2)
        return [self.late_x, self.late_y]

    def near_z(self):
        half = self.count
        self.here = add(self.own[:half], self.from_x[:half], self.late_y)
        self.there = flip(add(self.own[half:], self.late_x, self.from_y[:half]).astype(BF16), "zl", 1)
        return [self.there]

    def far_z(self):
        half = self.count // 2
        self.stays = add(self.here[:half], self.there[:half])
        self.last = flip(add(self.here[half:], self.there[half:]).astype(BF16), "zh", 1)
        return [self.last]

    def total(self):
        if is_small():
            return self.stays + self.last.astype(F32)
        half = self.count
        mine = jnp.stack(
            [self.own, jnp.concatenate([self.to_x[:half], self.rest_x]), jnp.concatenate([self.rest_y, self.to_y[:half]]),
             jnp.concatenate([self.to_x[half:], self.to_y[half:]])]
        ).reshape(4, self.count, 2, ROWS, -1)
        theirs = self.theirs.reshape(4, 2, self.count, ROWS, -1).transpose(0, 2, 1, 3, 4)
        every = jnp.stack([mine, theirs], axis=1)
        every = every.transpose(2, 0, 1, 4, 3, 5)
        every = jnp.stack([every[slot] for slot in SLOTS]).reshape(-1, 2, mine.shape[-1])
        return lax.psum_scatter(every, ALL, scatter_dimension=0, tiled=True).astype(F32).transpose(1, 0, 2)


SMALL_AXES = ("q", MODEL, "c")
SMALL_STEPS = (("q", 1), ("q", 2), ("zl", 1), ("zh", 1), ("c", 1))


def small_step(values_in, step):
    axis, mask = SMALL_STEPS[step]
    return jnp.concatenate([values_in, flip(values_in, axis, mask)])


def order_small(every, where):
    every = every.reshape(2, 2, 2, 4, -1)
    every = every.reshape(2, 4, 4, -1)
    for axis, position in enumerate(where[::-1]):
        every = order_by(every, axis, position, every.shape[axis])
    return every.transpose(1, 2, 0, 3).reshape(16 // 4, 8, -1)


def spread_by_distance(values_in, where):
    every = values_in.reshape(4, 4, 2, -1).transpose(1, 0, 2, 3)
    for axis, position in enumerate(where):
        every = order_by(every, axis, position, every.shape[axis])
    return every.transpose(2, 1, 0, 3).reshape(32, -1)


def fold_small(every, first, last):
    for axis, mask in SMALL_STEPS[::-1][first:last]:
        half = every.shape[0] // 2
        every = every[:half] + flip(every[half:], axis, mask)
    return every


def sum_all(value):
    if not is_small():
        return lax.psum(value, ALL)
    for axes in SMALL_AXES:
        parts = jnp.stack(from_members(value, axes))
        value = jnp.sum(order_by(parts, 0, lax.axis_index(axes), parts.shape[0]), 0)
    return value[0, 0]


def on_device(
    tokens, doc_lengths, qkv_weight, qv_bias, out_weight, up_weight, up_bias, down_weight, gains, shifts, cotangent
):
    layers = qkv_weight.shape[0]
    tz, dp = lax.axis_size(MODEL), lax.axis_size(("q", "c"))
    place, zh = lax.axis_index(GROUP), lax.axis_index("zh")
    where = (lax.axis_index("q"), lax.axis_index(MODEL), lax.axis_index("c"))
    if is_small():
        spots = [place, where[0], where[2], zh, where[1]]
    else:
        spots = [place] + [jnp.zeros((), jnp.int32)] * 4
    scal = jnp.stack([spot.astype(jnp.int32) for spot in spots])

    flow = Flow(scal)
    small_slice = is_small()
    qkv_cols, out_cols = 3 * out_weight.shape[2], out_weight.shape[2]
    in_cols, out_cols = slice(0, qkv_cols), slice(qkv_cols, qkv_cols + out_cols)
    hz, bias_size = qv_bias.shape[2], qv_bias.size // layers
    heads_shard = [heads_shard_of(qkv_weight[l], out_weight[l], qv_bias[l]) for l in range(layers)]
    pieces = [up_bias, gains, shifts]
    sizes = [piece.size // layers for piece in pieces]
    cuts = [0]
    for size in sizes:
        cuts.append(cuts[-1] + size)
    small = jnp.concatenate([piece.reshape(layers, -1) for piece in pieces], axis=1).reshape(1, -1)

    def spread_small(every):
        every = every.reshape(tz, dp, layers, -1).astype(F32)
        parts = [every[..., cuts[i] : cuts[i + 1]] for i in range(3)]
        biases = parts[0].reshape(tz, dp, layers, up_bias.shape[1], -1).transpose(2, 0, 3, 1, 4)
        gain = parts[1].reshape(tz, dp, layers, 2, -1).transpose(2, 3, 1, 0, 4).reshape(layers, 2, D)
        shift = parts[2].reshape(tz, dp, layers, 4, -1).transpose(2, 3, 1, 0, 4).reshape(layers, 4, D)
        table = jnp.concatenate([gain, shift], axis=1).reshape(layers * 6, D)
        head = jnp.concatenate([jnp.ones((1, D), F32), jnp.zeros((1, D), F32)])
        return biases.reshape(layers, tz, 1, -1), jnp.pad(jnp.concatenate([head, table]), ((0, TABLE - 2 - 6 * layers), (0, 0)))

    if small_slice:
        pair = jnp.stack([turn(heads_shard[0]), cross(heads_shard[0])])
        x_low = turn(tokens)
        ends = jnp.cumsum(turn(doc_lengths)[0], dtype=jnp.int32)
        near = heads_along_x(pair)
        small = small_step(small, 0)
        up0, down0 = UnitsWeight(up_weight[0][None]), UnitsWeight(down_weight[0][None])
        both1 = UnitsWeight(jnp.stack([up_weight[1], down_weight[1]]))
        flow.wait(x_low, small)
        flow.hold(
            up0=up0.shard, down0=down0.shard, down0_twin=down0.shard, both1=both1.shard, heads1=heads_shard[1], top=cotangent,
            low=x_low, small=small,
        )
        gate(flow)
        x_low, up0.shard = flow.free("low"), flow.free("up0")
        up0.far_z()
        small = small_step(flow.free("small"), 1)
        weights_of = [heads_along_y(near, bias_size, hz, where, zh)]
    else:
        x_low = turn(tokens)
        ends = jnp.cumsum(turn(doc_lengths)[0], dtype=jnp.int32)
        weights_of = [all_heads_weight(shard, bias_size, hz, zh) for shard in heads_shard]
        every = [all_units_weight(jnp.stack([up_weight[l], down_weight[l]])) for l in range(layers)]
        top_grad = turn(cotangent)
        up_bias_full, table = spread_small(lax.all_gather(small, ALL))

    prev, prev_gain, prev_shift = x_low, ONE, ZERO
    kept = []
    for l in range(layers):
        first, last = small_slice and l == 0, small_slice and l == 1
        xs = gather_group(x_low)
        w_heads, bias = weights_of[l]
        if first:
            flow.wait(up0.two, small)
            flow.hold(small=small, two=up0.two, two_twin=up0.two)
        if last:
            flow.wait(both1.own)
            flow.hold(own=both1.own)
        qkv_near = project_in(flow, (xs[0], xs[2]), False, w_heads, in_cols, bias, "project_qkv")
        if first:
            up0.two, down0.shard = flow.free("two"), flow.free("down0")
            up0.start_z()
            down0.start_far_z()
            small = small_step(flow.free("small"), 2)
        if last:
            both1.own = flow.free("own")
            both1.near()
        forward(flow, xs, qkv_near)
        if first:
            flow.hold(small=small)
        qkv_far = project_in(flow, (xs[1], xs[3]), True, w_heads, in_cols, bias, "project_qkv")
        qkv = (qkv_near, qkv_far)
        if first:
            small = small_step(flow.free("small"), 3)
            both1.shard = flow.free("both1")
            down0.join_far_z(flow.free("down0_twin"))
            up0.join_z(flow.free("two_twin"))
            up0.near()
            down0.near_z()
            both1.far_z()
        if last:
            top_grad = turn(flow.free("top"))
        ctx, wide, lse = attend_forward(flow, ends, qkv)
        if first:
            flow.wait(up0.near_x, up0.near_y)
            flow.hold(small=small, down0=down0.own, both1=both1.two)
            up0.corner()
        if last:
            flow.wait(both1.near_x, both1.near_y, top_grad)
            flow.hold(own=both1.own)
            both1.corner()
        send = project_out(flow, [ctx], (2, 3), w_heads, out_cols, True, "project_attn")
        flow.wait(send)
        if first:
            shard = flow.free("heads1")
            pair = jnp.stack([turn(shard), cross(shard)])
        if last:
            both1.own = flow.free("own")
            both1.swap_main()
        keep = project_out(flow, [ctx], (0, 1), w_heads, out_cols, False, "project_attn")
        attn, passed = sum_group(keep, send)
        if first:
            flow.wait(passed, up0.far_a, up0.far_b)
            flow.hold(pair=pair, pair_twin=pair)
            gate(flow)
            up0.swap_main()
            up0.swap_corner()
            down0.own = flow.free("down0")
            down0.near()
            up_bias_full, table = spread_small(order_small(small_step(flow.free("small"), 4), where))
            flow.wait(down0.near_x, down0.near_y)
            w_up = up0.pieces(), 0
        elif last:
            flow.wait(passed)
            flow.hold(far_a=both1.far_a)
            flow.wait(attn[2])
            gate(flow)
            both1.far_a = flow.free("far_a")
            both1.swap_corner()
            w_up, w_down = (both1.pieces(), 0), (both1.pieces(), 1)
        else:
            w_up, w_down = (every[l], 0), (every[l], 1)
        used = (prev_gain, prev_shift, shift_row(l, 0), gain_row(l, 0), shift_row(l, 1))
        n1, hs, r1, act, slope = norm_up(flow, prev, attn, table, used, *w_up, up_bias_full[l], tz)
        if first:
            down0.corner()
            down0.swap_main()
            flow.wait(n1)
            flow.hold(far_a=down0.far_a)
            gate(flow)
            down0.far_a = flow.free("far_a")
            down0.swap_corner()
            both1.two, pair = flow.free("both1"), flow.free("pair")
            both1.near_z()
            beside = flip(pair, "q", 1)
            w_down = down0.pieces(), 0
        used = (gain_row(l, 0), shift_row(l, 1), shift_row(l, 2), gain_row(l, 1), shift_row(l, 3))
        n2, y_low, r2 = down_norm(flow, act, *w_down, n1, table, used, tz)
        kept.append((xs, qkv, ctx, wide, lse, n1, hs, r1, act, slope, n2, r2, w_heads, w_up, w_down))
        if first:
            near = jnp.stack([flow.free("pair_twin"), beside])
            weights_of.append(heads_along_y(near, bias_size, hz, where, zh))
        x_low, prev, prev_gain, prev_shift = y_low, n2, gain_row(l, 1), shift_row(l, 3)
    layer_output = turn(x_low)

    g2, gf, sums2 = norm_back(flow, top_grad, kept[-1][10], kept[-1][11], table, gain_row(layers - 1, 1))
    small_grads = [None] * layers
    units_of, heads_of = [None] * layers, [None] * layers
    above = above_heads = None
    for l in reversed(range(layers)):
        top = l == layers - 1
        xs, qkv, ctx, wide, lse, n1, hs, r1, act, slope, n2, r2, w_heads, w_up, w_down = kept[l]
        beside = small_slice and not top
        gu, up_bias_sum = units_back(flow, gf, *w_down, slope, tz)
        units = UnitsGrads(flow, (gf, act), (hs, gu), tz)
        if top:
            flow.hold(output=layer_output)
        else:
            if beside:
                flow.wait(*above.near())
                flow.hold(heads=above_heads.send)
            units.sibling()
            flow.wait(units.theirs)
            if beside:
                above_heads.send = flow.free("heads")
                above_heads.along_x()
                late = above.far()
        g1, ga, sums1 = up_back(flow, gu, *w_up, g2, n1, r1, table, gain_row(l, 0), tz)
        gas = gather_group(ga)
        flow.wait(ga)
        if top:
            layer_output = flow.free("output")
            units.compute_theirs()
            forward(flow, gas, units.theirs)
        else:
            units.mine()
            if beside:
                flow.wait(*late, above_heads.got)
            forward(flow, gas, *units.made)
        gc_near = project_in(flow, (gas[0], gas[2]), False, w_heads, out_cols, None, "project_gc")
        flow.wait(gc_near)
        if top:
            flow.hold(theirs=units.theirs)
        gc_far = project_in(flow, (gas[1], gas[3]), True, w_heads, out_cols, None, "project_gc")
        if top:
            units.theirs = flow.free("theirs")
            units.send_theirs()
        gcs = (gc_near, gc_far)
        if beside:
            flow.hold(rest_x=units.rest_x, rest_y=units.rest_y)
        gqkv = [attend_backward(flow, ends, 0, qkv, gcs, wide, lse)]
        if beside:
            units.rest_x, units.rest_y = flow.free("rest_x"), flow.free("rest_y")
        flow.wait(gqkv[0])
        if beside:
            flow.wait(*units.near(), *above.near_z(), above_heads.along_y())
            above.far_z()
            units.far()
            above_halves = above_heads.halves(zh)
        gqkv.append(attend_backward(flow, ends, 1, qkv, gcs, wide, lse))
        if beside:
            flow.wait(units.late_x, units.late_y)
            units.near_z()
        send = project_out(flow, gqkv, (2, 3), w_heads, in_cols, True, "project_gx")
        flow.wait(send)
        keep = project_out(flow, gqkv, (0, 1), w_heads, in_cols, False, "project_gx")
        back, passed = sum_group(keep, send)
        flow.wait(passed)
        if top:
            units.mine()
            flow.wait(*units.made)
        elif small_slice:
            flow.hold(h0=above_halves[0], h1=above_halves[1])
        *buckets, qkv_sums = heads_grad(flow, xs, gqkv, gas, ctx)
        heads = HeadsGrad(*buckets)
        units_of[l], heads_of[l] = units, heads
        qv_sums = qkv_sums.reshape(-1, 3, PAIR).transpose(1, 0, 2).reshape(3, hz, dp, -1)
        qv_sums = jnp.stack([qv_sums[0], qv_sums[2]]).transpose(2, 0, 1, 3).reshape(1, dp, -1)
        mine = (jnp.arange(tz) == place).astype(F32).reshape(tz, 1, 1)
        small_grads[l] = jnp.concatenate(
            [
                mine * qv_sums,
                up_bias_sum.reshape(tz, up_bias.shape[1], dp, -1).transpose(0, 2, 1, 3).reshape(tz, dp, -1),
                jnp.stack([sums1[0], sums2[0]]).reshape(2, dp, tz, -1).transpose(2, 1, 0, 3).reshape(tz, dp, -1),
                jnp.stack([sums1[2], sums1[1], sums2[2], sums2[1]])
                .reshape(4, dp, tz, -1).transpose(2, 1, 0, 3).reshape(tz, dp, -1),
            ],
            axis=-1,
        )
        if l > 0:
            above, above_heads = units, heads
            flow.wait(heads.send)
            g2, gf, sums2 = sum_norm_back(flow, g1, back, kept[l - 1][10], kept[l - 1][11], table, gain_row(l - 1, 1))
    small_sums = jnp.stack(small_grads, axis=2).reshape(tz, dp, -1)
    if small_slice:
        above_halves = flow.free("h0"), flow.free("h1")
        done = turn(above_halves[0]), uncross(above_halves[1])
        heads.along_x()
        flow.wait(units.there)
        flow.hold(small=small_sums)
        gate(flow)
        small_sums = flow.free("small")
        units.far_z()
        flow.wait(back[2], *done)
        flow.hold(small=small_sums, got=heads.got)
        gate(flow)
        small_sums, heads.got = flow.free("small"), flow.free("got")
        input_grad = turn(add(g1, back[0], back[1][0], back[2]).astype(BF16))
        heads.along_y()
        small_sums = fold_small(spread_by_distance(small_sums, where), 0, 2)
        flow.wait(heads.got)
        flow.hold(small=small_sums, grad=input_grad, last=units.last)
        gate(flow)
        small_sums, input_grad, units.last = flow.free("small"), flow.free("grad"), flow.free("last")
        halves = heads.halves(zh)
        d_heads = jnp.stack([add(turn(halves[0]), uncross(halves[1])), add(*done)])
        small_out = fold_small(small_sums, 2, 5).reshape(layers, -1)
    else:
        halves = [member.halves(zh) for member in heads_of]
        d_heads = jnp.stack([add(turn(half[0]), uncross(half[1])) for half in halves])
        input_grad = turn(add(g1, back[0], back[1][0], back[2]).astype(BF16))
        small_out = lax.psum_scatter(small_sums.reshape(tz * dp, -1), ALL, scatter_dimension=0, tiled=True)
        small_out = small_out.reshape(layers, -1)
    qkv_grad = d_heads[:, :, : in_cols.stop].reshape(layers, d_heads.shape[1], -1, 3, PAIR)
    qkv_grad = qkv_grad.transpose(0, 3, 1, 2, 4).reshape(qkv_weight.shape)
    out_grad = d_heads[:, :, in_cols.stop :]
    totals = [member.total() for member in units_of]
    down_grad, up_grad = (jnp.stack([total[i] for total in totals]) for i in range(2))

    rest = small_out[:, bias_size:]
    qv_bias_grad = small_out[:, :bias_size].reshape(qv_bias.shape)
    up_bias_grad = rest[:, cuts[0] : cuts[1]].reshape(up_bias.shape)
    gains_grad = rest[:, cuts[1] : cuts[2]].reshape(gains.shape)
    shifts_grad = rest[:, cuts[2] : cuts[3]].reshape(shifts.shape)
    all_grads = (qkv_grad, qv_bias_grad, out_grad, up_grad, up_bias_grad, down_grad, gains_grad, shifts_grad)
    local_squares = sum(jnp.sum(member * member) for member in all_grads)
    entry_count = LAYERS * (4 * D * D + 2 * D * FF + FF + 8 * D)
    if small_slice:
        local_squares = jnp.broadcast_to(local_squares, (8, 128))
    grad_rms = jnp.sqrt(sum_all(local_squares) / entry_count)
    return (
        layer_output, input_grad, qkv_grad, qv_bias_grad, out_grad, up_grad, up_bias_grad, down_grad, gains_grad,
        shifts_grad, grad_rms,
    )


def solution(mesh):
    dp, tensor = mesh.shape["dp"], mesh.shape["tensor"]
    fine = Mesh(mesh.devices.reshape(dp // 2, 2, 2, tensor // 2), ("q", "c", "zh", "zl"))
    data, model = ("q", "c"), ("zh", "zl")
    both = data + model
    weight3, weight4 = P(None, data, model), P(None, None, data, model)
    in_specs = (
        P(both, None), P(data, None), weight4, P(None, None, model, data), weight3, weight3, P(None, model, data),
        weight3, P(None, None, both), P(None, None, both), P(both, None),
    )
    out_specs = (
        P(both, None), P(both, None), weight4, P(None, None, model, data), weight3, weight3, P(None, model, data),
        weight3, P(None, None, both), P(None, None, both), P(),
    )
    return jax.shard_map(on_device, mesh=fine, in_specs=in_specs, out_specs=out_specs, check_vma=False)
```

```python
import jax
import jax.numpy as jnp
from jax import lax
from jax.experimental import pallas as pl
from jax.experimental.pallas import tpu as pltpu
from jax.sharding import Mesh
from jax.sharding import PartitionSpec as P

D = 1024
HD = 64
HEADS = 16
FF = 4096
LAYERS = 2
SEQLEN = 2048
WINDOW = 1024
EPS = 1e-06
FILL = -1000000000.0

F32 = jnp.float32
BF16 = jnp.bfloat16
GROUP = ("c", "zl")
MODEL = ("zh", "zl")
ALL = ("zh", "zl", "q", "c")
VMEM_LIMIT = 56 * 1024 * 1024
TIMES = {
    "gate": 0.1, "norm_up": 20.0, "down_norm": 20.0, "units_back": 20.0, "up_back": 20.0, "norm_back": 6.0,
    "sum_norm_back": 20.0, "grads_theirs": 0.2, "grads_mine": 0.2, "project_qkv": 0.2, "project_gc": 0.2,
    "project_attn": 0.2, "project_gx": 0.2, "heads_grad": 0.2, "attend_forward": 40.0, "attend_backward": 30.0,
}
PEAK = 0.35e9
NT = (((1,), (1,)), ((), ()))
NN = (((1,), (0,)), ((), ()))
ROWS = 128
CHUNK = 64
BQ = 512
PAIR = 2 * HD


def mm(left, right, dims=NN):
    return lax.dot_general(left, right, dims, preferred_element_type=F32)


def full(shape):
    return pl.BlockSpec(shape, lambda *_: (0,) * len(shape))


ANY = pl.BlockSpec(memory_space=pl.ANY)


def sds(shape, kind):
    return jax.ShapeDtypeStruct(shape, kind)


class Flow:
    def __init__(self, scal):
        self.scal, self.before, self.held = scal, [], {}

    def wait(self, *arrays):
        self.before += arrays

    def hold(self, **arrays):
        self.held.update(arrays)

    def free(self, name):
        return self.held.pop(name)


def call(flow, body, grid, in_specs, out_specs, out_shape, scratch, args, flops, traffic, name, scalars=None):
    scalars = (flow.scal,) if scalars is None else scalars
    single = not isinstance(out_specs, (list, tuple))
    out_specs = [out_specs] if single else list(out_specs)
    out_shape = [out_shape] if single else list(out_shape)
    before, held = flow.before, list(flow.held.items())
    ns, nb, nh, no = len(scalars), len(before), len(held), len(out_specs)
    first, last = ns + nb + nh, ns + nb + nh + len(args) + no

    def wrapped(*refs):
        body(*refs[:ns], *refs[first:last], *refs[last + nh :])

    result = pl.pallas_call(
        wrapped,
        grid_spec=pltpu.PrefetchScalarGridSpec(
            num_scalar_prefetch=ns,
            grid=grid,
            in_specs=[ANY] * (nb + nh) + list(in_specs),
            out_specs=out_specs + [ANY] * nh,
            scratch_shapes=scratch,
        ),
        out_shape=out_shape + [sds(array.shape, array.dtype) for _, array in held],
        input_output_aliases={ns + nb + i: no + i for i in range(nh)},
        compiler_params=pltpu.CompilerParams(
            dimension_semantics=("arbitrary",) * len(grid), vmem_limit_bytes=VMEM_LIMIT
        ),
        cost_estimate=pl.CostEstimate(flops=int(TIMES[name] * PEAK), bytes_accessed=1024, transcendentals=0),
        name=name,
    )(*scalars, *before, *[array for _, array in held], *args)
    flow.before = []
    flow.held = {key: value for (key, _), value in zip(held, result[no:])}
    return result[0] if single else result[:no]


def gate(flow):
    if flow.held:
        call(flow, lambda *refs: None, (1,), [], [], [], [], [], 0, 0, "gate")


S_P, S_Q, S_C, S_ZH, S_Z = range(5)


def norm_rows(values_in):
    centred = values_in - jnp.mean(values_in, -1, keepdims=True)
    variance = jnp.mean(centred * centred, -1, keepdims=True)
    inverse = lax.rsqrt(variance + EPS)
    return centred * inverse, inverse


def norm_back_rows(grad, normed, inverse, gain):
    scaled = grad * gain
    centred = scaled - jnp.mean(scaled, -1, keepdims=True) - normed * jnp.mean(scaled * normed, -1, keepdims=True)
    return centred * inverse


def fold_rows(values_in):
    return jnp.sum(values_in.reshape(-1, 8, values_in.shape[-1]), 0)


def read(part, rows):
    return (part[0, rows, :] if len(part.shape) == 3 else part[rows, :]).astype(F32)


def part_spec(part):
    shape = part.shape
    return full(shape) if len(shape) == 2 else pl.BlockSpec((1,) + shape[1:], lambda *_: (0, 0, 0))


ONE, ZERO, TABLE = 0, 1, 16


def gain_row(layer, index):
    return 2 + 6 * layer + index


def shift_row(layer, index):
    return 4 + 6 * layer + index


def row_of(vec_ref, row):
    return vec_ref[row : row + 1, :]


def norm_forward(get_total, tokens, vec, gain, shift, n_ref, low_ref, inv_ref):

    def step(index, carry):
        rows = pl.ds(pl.multiple_of(index * CHUNK, CHUNK), CHUNK)
        normed, inverse = norm_rows(get_total(rows))
        n_ref[rows, :] = normed
        low_ref[rows, :] = (normed * row_of(vec, gain) + row_of(vec, shift)).astype(BF16)
        inv_ref[rows, :] = jnp.broadcast_to(inverse, (CHUNK, 128))
        return carry

    lax.fori_loop(0, tokens // CHUNK, step, 0)


def norm_backward(get_grad, tokens, n_ref, inv_ref, vec, gain, g_ref, low_ref, sums_ref):
    def step(index, carry):
        rows = pl.ds(pl.multiple_of(index * CHUNK, CHUNK), CHUNK)
        grad = get_grad(rows)
        normed = n_ref[rows, :]
        result = norm_back_rows(grad, normed, inv_ref[rows, 0:1], row_of(vec, gain))
        low = result.astype(BF16)
        g_ref[rows, :] = result
        low_ref[rows, :] = low
        return (
            carry[0] + fold_rows(grad * normed),
            carry[1] + fold_rows(grad),
            carry[2] + fold_rows(low.astype(F32)),
        )

    zero = jnp.zeros((8, D), F32)
    sums = lax.fori_loop(0, tokens // CHUNK, step, (zero, zero, zero))
    sums_ref[...] = jnp.zeros(sums_ref.shape, F32)
    for row, member in enumerate(sums):
        sums_ref[row : row + 1, :] = jnp.sum(member, 0, keepdims=True)


def away(s):
    return (s & 1) * 2 + s // 2


class Streamed:
    def __init__(self, refs, matrix, buffer, sems, scal):
        self.refs, self.matrix, self.buffer, self.sems, self.scal = refs, matrix, buffer, sems, scal

    def copies(self, s):
        slot = lax.rem(s, 2)
        for k in range(2):
            main, far = self.refs[2 * k : 2 * k + 2]
            for r in range(4):
                row = ((self.scal[S_Q] ^ r) * 2 + (self.scal[S_C] ^ k)) * ROWS
                source = far.at[s, self.matrix] if r == 3 else main.at[r, s, self.matrix]
                yield pltpu.make_async_copy(
                    source, self.buffer.at[slot, pl.ds(pl.multiple_of(row, ROWS), ROWS), :], self.sems.at[slot, 4 * k + r]
                )

    def start(self, s):
        for copy in self.copies(s):
            copy.start()

    def wait(self, s):
        for copy in self.copies(s):
            copy.wait()

    def turn(self, s, count):
        @pl.when(s == 0)
        def _():
            self.start(s)

        @pl.when(s + 1 < count)
        def _():
            self.start(s + 1)


def piece_shapes(width):
    return [pltpu.VMEM((2, D, width), BF16), pltpu.SemaphoreType.DMA((2, 8))]


def gelu_parts(u):
    size = jnp.abs(u)
    t = 1.0 / (1.0 + 0.2316419 * size)
    poly = t * (0.127414796 + t * (-0.142248368 + t * (0.7107068705 + t * (-0.7265760135 + t * 0.5307027145))))
    bell = jnp.exp(-0.5 * (u * u))
    tail = poly * bell
    cdf = jnp.where(u >= 0, 1.0 - tail, tail)
    return u * cdf, cdf + u * (0.3989422804014327 * bell)


def tiles(tokens, width):
    for i in range(2):
        for j in range(2):
            yield slice(i * tokens // 2, (i + 1) * tokens // 2), slice(j * width // 2, (j + 1) * width // 2)


def norm_up(flow, prev, parts, vec, rows_used, weight, matrix, bias, count):
    tokens = prev.shape[0]
    width = FF // count

    def body(scal_ref, prev_ref, *refs):
        part_refs, refs = refs[: len(parts)], refs[len(parts) :]
        vec_ref, bias_ref, refs = refs[0], refs[1], refs[2:]
        pieces, (n_ref, low_ref, inv_ref, act_ref, slope_ref, buffer, sems) = refs[:4], refs[4:]
        s = pl.program_id(0)
        stream = Streamed(pieces, matrix, buffer, sems, scal_ref)
        stream.turn(s, count)

        @pl.when(s == 0)
        def _():
            def total(rows):
                attn = read(part_refs[0], rows)
                for part in part_refs[1:]:
                    attn = attn + read(part, rows)
                before = read(prev_ref, rows) * row_of(vec_ref, rows_used[0]) + row_of(vec_ref, rows_used[1])
                return before + (attn + row_of(vec_ref, rows_used[2]))

            norm_forward(total, tokens, vec_ref, *rows_used[3:], n_ref, low_ref, inv_ref)

        stream.wait(s)
        slot = lax.rem(s, 2)
        for rows, cols in tiles(tokens, width):
            act, slope = gelu_parts(mm(low_ref[rows, :], buffer[slot, :, cols]) + bias_ref[0, :, cols])
            act_ref[rows, cols] = act.astype(BF16)
            slope_ref[rows, cols] = slope.astype(BF16)

    column = pl.BlockSpec((tokens, width), lambda s, _: (0, s))
    return call(
        flow, body, (count,),
        [full((tokens, D))] + [part_spec(part) for part in parts]
        + [full((TABLE, D)), pl.BlockSpec((1, 1, width), lambda s, scal_ref: (scal_ref[S_Z] ^ away(s), 0, 0))] + [ANY] * 4,
        [full((tokens, D)), full((tokens, D)), full((tokens, 128)), column, column],
        [sds((tokens, D), F32), sds((tokens, D), BF16), sds((tokens, 128), F32)] + [sds((tokens, FF), BF16)] * 2,
        piece_shapes(width), [prev, *parts, vec, bias, *weight], 2 * tokens * D * FF,
        2 * (D * FF + tokens * (10 * D + 2 * FF)), "norm_up",
    )


def down_norm(flow, act, weight, matrix, prev, vec, rows_used, count):
    tokens = prev.shape[0]
    width = FF // count

    def body(scal_ref, act_ref, prev_ref, vec_ref, *refs):
        pieces, (n_ref, low_ref, inv_ref, buffer, sems, acc) = refs[:4], refs[4:]
        s = pl.program_id(0)
        stream = Streamed(pieces, matrix, buffer, sems, scal_ref)
        stream.turn(s, count)
        stream.wait(s)
        value = mm(act_ref[...], buffer[lax.rem(s, 2)], NT)

        @pl.when(s == 0)
        def _():
            acc[...] = value

        @pl.when(s > 0)
        def _():
            acc[...] += value

        @pl.when(s == count - 1)
        def _():
            def total(rows):
                before = prev_ref[rows, :] * row_of(vec_ref, rows_used[0]) + row_of(vec_ref, rows_used[1])
                return before + (acc[rows, :] + row_of(vec_ref, rows_used[2]))

            norm_forward(total, tokens, vec_ref, *rows_used[3:], n_ref, low_ref, inv_ref)

    return call(
        flow, body, (count,),
        [pl.BlockSpec((tokens, width), lambda s, _: (0, s)), full((tokens, D)), full((TABLE, D))] + [ANY] * 4,
        [full((tokens, D)), full((tokens, D)), full((tokens, 128))],
        [sds((tokens, D), F32), sds((tokens, D), BF16), sds((tokens, 128), F32)],
        piece_shapes(width) + [pltpu.VMEM((tokens, D), F32)], [act, prev, vec, *weight], 2 * tokens * D * FF,
        2 * (D * FF + tokens * (5 * D + FF)), "down_norm",
    )


def units_back(flow, grad, weight, matrix, slope, count):
    tokens = grad.shape[0]
    width = FF // count

    def body(scal_ref, grad_ref, slope_ref, *refs):
        pieces, (out_ref, sum_ref, buffer, sems) = refs[:4], refs[4:]
        s = pl.program_id(0)
        stream = Streamed(pieces, matrix, buffer, sems, scal_ref)
        stream.turn(s, count)
        stream.wait(s)
        slot = lax.rem(s, 2)
        sums = {}
        for rows, cols in tiles(tokens, width):
            low = (mm(grad_ref[rows, :], buffer[slot, :, cols]) * slope_ref[rows, cols].astype(F32)).astype(BF16)
            out_ref[rows, cols] = low
            part = fold_rows(low.astype(F32))
            sums[cols.start] = sums[cols.start] + part if cols.start in sums else part
            if rows.start > 0:
                sum_ref[0, :, cols] = jnp.sum(sums[cols.start], 0, keepdims=True)

    column = pl.BlockSpec((tokens, width), lambda s, _: (0, s))
    return call(
        flow, body, (count,), [full((tokens, D)), column] + [ANY] * 4,
        [column, pl.BlockSpec((1, 1, width), lambda s, scal_ref: (scal_ref[S_Z] ^ away(s), 0, 0))],
        [sds((tokens, FF), BF16), sds((count, 1, width), F32)], piece_shapes(width), [grad, slope, *weight],
        2 * tokens * D * FF, 2 * (D * FF + tokens * (D + 2 * FF)), "units_back",
    )


def up_back(flow, gu, weight, matrix, residual, normed, inverse, vec, gain, count):
    tokens = residual.shape[0]
    width = FF // count

    def body(scal_ref, gu_ref, res_ref, n_ref, inv_ref, vec_ref, *refs):
        pieces, (g_ref, low_ref, sums_ref, buffer, sems, acc) = refs[:4], refs[4:]
        s = pl.program_id(0)
        stream = Streamed(pieces, matrix, buffer, sems, scal_ref)
        stream.turn(s, count)
        stream.wait(s)
        value = mm(gu_ref[...], buffer[lax.rem(s, 2)], NT)

        @pl.when(s == 0)
        def _():
            acc[...] = value

        @pl.when(s > 0)
        def _():
            acc[...] += value

        @pl.when(s == count - 1)
        def _():
            norm_backward(
                lambda rows: res_ref[rows, :] + acc[rows, :], tokens, n_ref, inv_ref, vec_ref, gain, g_ref, low_ref,
                sums_ref,
            )

    return call(
        flow, body, (count,),
        [pl.BlockSpec((tokens, width), lambda s, _: (0, s)), full((tokens, D)), full((tokens, D)), full((tokens, 128)),
         full((TABLE, D))] + [ANY] * 4,
        [full((tokens, D)), full((tokens, D)), full((8, D))],
        [sds((tokens, D), F32), sds((tokens, D), BF16), sds((8, D), F32)],
        piece_shapes(width) + [pltpu.VMEM((tokens, D), F32)], [gu, residual, normed, inverse, vec, *weight],
        2 * tokens * D * FF, 2 * (D * FF + tokens * (8 * D + FF)), "up_back",
    )


def norm_back(flow, grad, normed, inverse, vec, gain):
    tokens = grad.shape[0]

    def body(scal_ref, grad_ref, n_ref, inv_ref, vec_ref, g_ref, low_ref, sums_ref):
        norm_backward(lambda rows: read(grad_ref, rows), tokens, n_ref, inv_ref, vec_ref, gain, g_ref, low_ref, sums_ref)

    return call(
        flow, body, (1,), [full((tokens, D)), full((tokens, D)), full((tokens, 128)), full((TABLE, D))],
        [full((tokens, D)), full((tokens, D)), full((8, D))],
        [sds((tokens, D), F32), sds((tokens, D), BF16), sds((8, D), F32)], [], [grad, normed, inverse, vec],
        20 * tokens * D, 12 * tokens * D, "norm_back",
    )


def sum_norm_back(flow, residual, parts, normed, inverse, vec, gain):
    tokens = residual.shape[0]

    def body(scal_ref, res_ref, *refs):
        part_refs, (n_ref, inv_ref, vec_ref, g_ref, low_ref, sums_ref) = refs[: len(parts)], refs[len(parts) :]

        def grad(rows):
            total = read(part_refs[0], rows)
            for part in part_refs[1:]:
                total = total + read(part, rows)
            return res_ref[rows, :] + total

        norm_backward(grad, tokens, n_ref, inv_ref, vec_ref, gain, g_ref, low_ref, sums_ref)

    return call(
        flow, body, (1,), [full((tokens, D))] + [part_spec(part) for part in parts]
        + [full((tokens, D)), full((tokens, 128)), full((TABLE, D))],
        [full((tokens, D)), full((tokens, D)), full((8, D))],
        [sds((tokens, D), F32), sds((tokens, D), BF16), sds((8, D), F32)], [],
        [residual, *parts, normed, inverse, vec], 20 * tokens * D, 22 * tokens * D, "sum_norm_back",
    )


def turn_rows(scal_ref, x_ref, turned, core):
    for r in range(4):
        row = ((scal_ref[S_Q] ^ r) * 2 + core) * ROWS
        turned[r * ROWS : (r + 1) * ROWS, :] = x_ref[:, pl.ds(pl.multiple_of(row, ROWS), ROWS)].T


def unit_grads(flow, down, up, received, count, sibling):
    tokens = down[0].shape[0]
    width = down[1].shape[1] // count
    half = count // 2
    steps = 2 * count

    def body(scal_ref, x0_ref, y0_ref, x1_ref, y1_ref, *refs):
        turned, t = refs[-1], pl.program_id(0)
        m, s = t // count, lax.rem(t, count)
        core = scal_ref[S_C] ^ 1 if sibling else scal_ref[S_C]

        @pl.when(t == 0)
        def _():
            turn_rows(scal_ref, x0_ref, turned, core)

        @pl.when(t == count)
        def _():
            turn_rows(scal_ref, x1_ref, turned, core)

        def store(y_ref):
            value = mm(turned[...], y_ref[...]).reshape(4, ROWS, width)
            if sibling:
                refs[0][:, 0] = value.astype(BF16)
                return
            if received is not None:
                value = value + refs[0][:, 0].astype(F32)
            value = value.astype(BF16)
            own, to_x, to_y, rest_x, rest_y = refs[-6:-1]
            spot = lax.rem(s, half) * 2 + m
            own[s // half * count + spot] = value[0]

            @pl.when(s < half)
            def _():
                to_x[spot] = value[1]
                to_x[count + spot] = value[3]
                rest_y[spot] = value[2]

            @pl.when(s >= half)
            def _():
                rest_x[spot] = value[1]
                to_y[spot] = value[2]
                to_y[count + spot] = value[3]

        @pl.when(m == 0)
        def _():
            store(y0_ref)

        @pl.when(m == 1)
        def _():
            store(y1_ref)

    left = full((tokens, D))
    pick_down = lambda t, _: (0, jnp.minimum(t, count - 1))
    pick_up = lambda t, _: (0, jnp.maximum(t - count, 0))
    specs = [left, pl.BlockSpec((tokens, width), pick_down), left, pl.BlockSpec((tokens, width), pick_up)]
    args = [*down, *up]
    one = pl.BlockSpec((4, 1, ROWS, width), lambda t, _: (0, t, 0, 0))
    if sibling:
        out_specs, out_shape = one, sds((4, steps, ROWS, width), BF16)
    else:
        if received is not None:
            specs.append(one)
            args.append(received)
        shapes = [(steps, ROWS, width)] * 3 + [(count, ROWS, width)] * 2
        out_specs, out_shape = [full(shape) for shape in shapes], [sds(shape, BF16) for shape in shapes]
    return call(
        flow, body, (steps,), specs, out_specs, out_shape, [pltpu.VMEM((4 * ROWS, tokens), BF16)], args,
        0, 0, "grads_theirs" if sibling else "grads_mine",
    )


def fetch_heads_weight(scal_ref, pieces, cols, buffer, sems):
    copies = []
    for r in range(4):
        for k in range(2):
            row = ((scal_ref[S_Q] ^ r) * 2 + (scal_ref[S_ZH] ^ k)) * ROWS
            copies.append(
                pltpu.make_async_copy(
                    pieces[r // 2].at[r % 2, k, pl.ds(0, ROWS), cols], buffer.at[pl.ds(pl.multiple_of(row, ROWS), ROWS), :],
                    sems.at[2 * r + k],
                )
            )
    for copy in copies:
        copy.start()
    for copy in copies:
        copy.wait()


def by_member(shape):
    return pl.BlockSpec((1,) + shape, lambda r, scal_ref: (scal_ref[S_P] ^ r, 0, 0))


def heads_weight_scratch(width):
    return [pltpu.VMEM((D, width), BF16), pltpu.SemaphoreType.DMA((8,))]


def project_in(flow, lefts, across, weight, cols, bias, name):
    tokens = lefts[0].shape[0]
    width = cols.stop - cols.start

    def body(scal_ref, left_ref, right_ref, *refs):
        if bias is not None:
            bias_ref, refs = refs[0], refs[1:]
        pieces, (out_ref, buffer, sems) = refs[:2], refs[2:]
        step = pl.program_id(0)

        @pl.when(step == 0)
        def _():
            fetch_heads_weight(scal_ref, pieces, cols, buffer, sems)

        for r, left in enumerate((left_ref, right_ref)):

            @pl.when(step == r)
            def _(left=left):
                value = mm(left[...], buffer[...])
                if bias is not None:
                    value = value + bias_ref[...]
                out_ref[0] = value.astype(BF16)

    extra, extra_specs = ([], []) if bias is None else ([bias], [full((1, width))])
    return call(
        flow, body, (2,), [full((tokens, D))] * 2 + extra_specs + [ANY] * 2,
        pl.BlockSpec((1, tokens, width), lambda r, scal_ref: ((scal_ref[S_P] >> 1) ^ r, 0, 0)),
        sds((2, tokens, width), BF16), heads_weight_scratch(width), [*lefts, *extra, *weight], 0, 0, name,
    )


def project_out(flow, blocks, members, weight, cols, stacked, name):
    count, tokens, width = blocks[0].shape

    def body(scal_ref, *refs):
        block_refs, refs = refs[: len(blocks)], refs[len(blocks) :]
        pieces, outs, (buffer, sems) = refs[:2], refs[2:-2], refs[-2:]
        step = pl.program_id(0)

        @pl.when(step == 0)
        def _():
            fetch_heads_weight(scal_ref, pieces, cols, buffer, sems)

        value = mm(block_refs[0][0], buffer[:, :width], NT)
        for index in range(1, len(blocks)):
            value = value + mm(block_refs[index][0], buffer[:, index * width : (index + 1) * width], NT)
        value = value.astype(BF16)
        if stacked:
            outs[0][0] = value
            return
        for r, out in enumerate(outs):

            @pl.when(step == r)
            def _(out=out):
                out[...] = value

    first, last = members
    pick = lambda r, scal_ref: (scal_ref[S_P] ^ (first + r * (last - first)), 0, 0)
    if stacked:
        out_specs, out_shape = pl.BlockSpec((1, tokens, D), lambda r, _: (r, 0, 0)), sds((2, tokens, D), BF16)
    else:
        out_specs, out_shape = [full((tokens, D))] * 2, [sds((tokens, D), BF16)] * 2
    return call(
        flow, body, (2,), [pl.BlockSpec((1, tokens, width), pick)] * len(blocks) + [ANY] * 2, out_specs, out_shape,
        heads_weight_scratch(width * len(blocks)), [*blocks, *weight], 0, 0, name,
    )


def heads_grad(flow, xs, parts, gas, ctx):
    count, tokens, width = parts[0].shape
    out_width = ctx.shape[2]
    cuts = [slice(i * width, (i + 1) * width) for i in range(len(parts))]
    total = width * len(parts)

    def body(scal_ref, *refs):
        x_refs, refs = refs[:count], refs[count:]
        ga_refs, refs = refs[:count], refs[count:]
        part_refs, refs = refs[: len(parts)], refs[len(parts) :]
        ctx_ref, outs, (sum_ref, acc, acc_out) = refs[0], refs[1:3], refs[3:]
        step = pl.program_id(0)
        for r in range(count):

            @pl.when(step == r)
            def _(r=r):
                turned = x_refs[r][...].T
                value_out = mm(ga_refs[r][...].T, ctx_ref[0])
                for cut, part in zip(cuts, part_refs):
                    value = mm(turned, part[0])
                    sums = jnp.sum(part[0].astype(F32), 0, keepdims=True)
                    acc[:, cut] = value if r == 0 else acc[:, cut] + value
                    sum_ref[:, cut] = sums if r == 0 else sum_ref[:, cut] + sums
                acc_out[...] = value_out if r == 0 else acc_out[...] + value_out

        @pl.when(step == count - 1)
        def _():
            for r in range(4):
                for k in range(2):
                    row = ((scal_ref[S_Q] ^ r) * 2 + (scal_ref[S_ZH] ^ k)) * ROWS
                    rows = pl.ds(pl.multiple_of(row, ROWS), ROWS)
                    outs[r % 2][r // 2, k, :, :total] = acc[rows, :].astype(BF16)
                    outs[r % 2][r // 2, k, :, total:] = acc_out[rows, :].astype(BF16)

    shape = (2, 2, ROWS, total + out_width)
    return call(
        flow, body, (count,),
        [full((tokens, D))] * (2 * count) + [by_member((tokens, width))] * len(parts) + [by_member((tokens, out_width))],
        [full(shape)] * 2 + [full((1, total))], [sds(shape, BF16)] * 2 + [sds((1, total), F32)],
        [pltpu.VMEM((D, total), F32), pltpu.VMEM((D, out_width), F32)], [*xs, *gas, *parts, ctx], 0, 0, "heads_grad",
    )


def reach(ends_ref, row):
    first = jnp.zeros_like(row)
    for index in range(3):
        first = jnp.where(row >= ends_ref[index], ends_ref[index], first)
    last = jnp.full_like(row, SEQLEN)
    for index in (2, 1, 0):
        last = jnp.where(row < ends_ref[index], ends_ref[index], last)
    return jnp.maximum(first, row - (WINDOW - 1)), jnp.minimum(last, row + WINDOW)


def chunks_of(scal_ref, near_ref, far_ref):
    here = scal_ref[S_P] & 1
    for core in range(2):
        yield 2 * core + here, near_ref.at[core]
        yield 2 * core + 1 - here, far_ref.at[core]


def over_keys(ends_ref, start, chunk, keys_first, block):
    low_first, high_first = reach(ends_ref, start)
    low_last, high_last = reach(ends_ref, start + BQ - 1)
    axis = 1 if keys_first else 0
    low_row, high_row = reach(ends_ref, start + lax.broadcasted_iota(jnp.int32, (1, BQ) if keys_first else (BQ, 1), axis))
    shape = (chunk, BQ) if keys_first else (BQ, chunk)

    def one(b, carry):
        open_all = (b * chunk >= low_last) & ((b + 1) * chunk <= high_first)

        @pl.when(open_all)
        def _():
            block(b, None)

        @pl.when(jnp.logical_not(open_all))
        def _():
            key = b * chunk + lax.broadcasted_iota(jnp.int32, shape, 1 - axis)
            block(b, (key >= low_row) & (key < high_row))

        return carry

    lax.fori_loop(low_first // chunk, (high_last + chunk - 1) // chunk, one, 0)


def attend_forward(flow, ends, qkv):
    _, chunk, width3 = qkv[0].shape
    count = SEQLEN // chunk
    width = width3 // 3
    heads = width // HD
    steps = SEQLEN // BQ
    per = chunk // BQ

    def body(scal_ref, ends_ref, near_ref, far_ref, ctx_ref, wide_ref, lse_ref, qt, kh, vt, acc, tops, sums, scores):
        step = pl.program_id(0)

        @pl.when(step == 0)
        def _():
            for j, block in chunks_of(scal_ref, near_ref, far_ref):
                rows = pl.ds(pl.multiple_of(j * chunk, chunk), chunk)
                for pair in range(heads // 2):
                    base = 3 * PAIR * pair
                    part = slice(pair * PAIR, (pair + 1) * PAIR)
                    vt[j, part, :] = block[:, base + 2 * PAIR : base + 3 * PAIR].T
                    for s in range(per):
                        queries = block[s * BQ : (s + 1) * BQ, base : base + PAIR] * BF16(HD**-0.5)
                        qt[j * per + s, part, :] = queries.T
                    for h in range(2):
                        kh[2 * pair + h, rows, :] = block[:, base + PAIR + h * HD : base + PAIR + (h + 1) * HD]

        start = step * BQ
        acc[...] = jnp.zeros(acc.shape, F32)
        tops[...] = jnp.full(tops.shape, -3.0e38, F32)
        sums[...] = jnp.zeros(sums.shape, F32)

        def score(b, allowed):
            keys = pl.ds(pl.multiple_of(b * chunk, chunk), chunk)
            for h in range(heads):
                value = mm(kh[h, keys, :], qt[step, h * HD : (h + 1) * HD, :])
                if allowed is not None:
                    value = jnp.where(allowed, value, FILL)
                scores[h, b] = value
                tops[h] = jnp.maximum(tops[h], jnp.max(value.reshape(-1, 8, BQ), 0))

        over_keys(ends_ref, start, chunk, True, score)
        top = [jnp.max(tops[h], 0, keepdims=True) for h in range(heads)]

        def weigh(b, carry):
            for h in range(heads):
                part = slice(h * HD, (h + 1) * HD)
                weight = jnp.exp(scores[h, b] - top[h])
                sums[h] += fold_rows(weight)
                acc[part, :] += mm(vt[b, part, :], weight.astype(BF16))
            return carry

        low_first, _ = reach(ends_ref, start)
        _, high_last = reach(ends_ref, start + BQ - 1)
        lax.fori_loop(low_first // chunk, (high_last + chunk - 1) // chunk, weigh, 0)
        lse_ref[...] = jnp.zeros(lse_ref.shape, F32)
        for h in range(heads):
            part = slice(h * HD, (h + 1) * HD)
            total = jnp.sum(sums[h], 0, keepdims=True)
            acc[part, :] = acc[part, :] / total
            lse_ref[0, h : h + 1, :] = top[h] + jnp.log(total)
        wide = acc[...].T
        wide_ref[0] = wide
        ctx_ref[0] = wide.astype(BF16)

    row_block = lambda i, *_: (i // per, i % per, 0)
    return call(
        flow, body, (steps,), [full((2, chunk, width3))] * 2,
        [pl.BlockSpec((1, BQ, width), row_block), pl.BlockSpec((1, BQ, width), row_block),
         pl.BlockSpec((1, 8, BQ), lambda i, *_: (i, 0, 0))],
        [sds((count, chunk, width), BF16), sds((count, chunk, width), F32), sds((steps, 8, BQ), F32)],
        [
            pltpu.VMEM((steps, width, BQ), BF16),
            pltpu.VMEM((heads, SEQLEN, HD), BF16),
            pltpu.VMEM((count, width, chunk), BF16),
            pltpu.VMEM((width, BQ), F32),
            pltpu.VMEM((heads, 8, BQ), F32),
            pltpu.VMEM((heads, 8, BQ), F32),
            pltpu.VMEM((heads, count, chunk, BQ), F32),
        ],
        [*qkv], 0, 0, "attend_forward", (flow.scal, ends),
    )


def attend_backward(flow, ends, pair, qkv, grads, wide, lse):
    chunk = qkv[0].shape[1]
    count = SEQLEN // chunk
    steps = SEQLEN // BQ
    per = chunk // BQ

    def body(
        scal_ref, ends_ref, near_ref, far_ref, grad_near, grad_far, wide_ref, lse_ref, out_ref, qh, kh, gh, kt, vt, qt, gt,
        gq, gk, gv,
    ):
        step = pl.program_id(0)

        @pl.when(step == 0)
        def _():
            blocks = chunks_of(scal_ref, near_ref, far_ref)
            grad_blocks = chunks_of(scal_ref, grad_near, grad_far)
            for (j, block), (_, grad_block) in zip(blocks, grad_blocks):
                rows = pl.ds(pl.multiple_of(j * chunk, chunk), chunk)
                queries = block[:, :PAIR] * BF16(HD**-0.5)
                keys = block[:, PAIR : 2 * PAIR]
                back = grad_block[...]
                for h in range(2):
                    cols = slice(h * HD, (h + 1) * HD)
                    qh[h, rows, :] = queries[:, cols]
                    kh[h, rows, :] = keys[:, cols]
                    gh[h, rows, :] = back[:, cols]
                kt[j] = keys.T
                vt[j] = block[:, 2 * PAIR :].T
                for s in range(per):
                    sub = slice(s * BQ, (s + 1) * BQ)
                    qt[j * per + s] = queries[sub, :].T
                    gt[j * per + s] = back[sub, :].T
            gk[...] = jnp.zeros(gk.shape, F32)
            gv[...] = jnp.zeros(gv.shape, F32)

        start = step * BQ
        rows = pl.ds(pl.multiple_of(start, BQ), BQ)
        gq[...] = jnp.zeros(gq.shape, F32)
        sums = lse_ref[0].T
        inner, logs = [], []
        for h in range(2):
            product = gh[h, rows, :].astype(F32) * wide_ref[0, :, h * HD : (h + 1) * HD]
            inner.append(jnp.sum(product, 1, keepdims=True))
            logs.append(sums[:, 2 * pair + h : 2 * pair + h + 1])

        def block(b, allowed):
            keys = pl.ds(pl.multiple_of(b * chunk, chunk), chunk)
            for h in range(2):
                part = slice(h * HD, (h + 1) * HD)
                score = mm(qh[h, rows, :], kt[b, part, :])
                grad_weight = mm(gh[h, rows, :], vt[b, part, :])
                if allowed is not None:
                    score = jnp.where(allowed, score, FILL)
                weight = jnp.exp(score - logs[h])
                grad_score = (weight * (grad_weight - inner[h])).astype(BF16)
                gv[b, part, :] += mm(gt[step, part, :], weight.astype(BF16))
                gk[b, part, :] += mm(qt[step, part, :], grad_score)
                gq[h] += mm(grad_score, kh[h, keys, :])

        over_keys(ends_ref, start, chunk, False, block)
        place = pl.ds(pl.multiple_of((step % per) * BQ, BQ), BQ)
        for h in range(2):
            out_ref[step // per, place, h * HD : (h + 1) * HD] = (gq[h] * HD**-0.5).astype(BF16)

        @pl.when(step == steps - 1)
        def _():
            for j in range(count):
                out_ref[j, :, PAIR : 2 * PAIR] = gk[j].T.astype(BF16)
                out_ref[j, :, 2 * PAIR :] = gv[j].T.astype(BF16)

    out = (count, chunk, 3 * PAIR)
    return call(
        flow, body, (steps,),
        [pl.BlockSpec((2, chunk, 3 * PAIR), lambda i, *_: (0, 0, pair))] * 2
        + [pl.BlockSpec((2, chunk, PAIR), lambda i, *_: (0, 0, pair))] * 2
        + [pl.BlockSpec((1, BQ, PAIR), lambda i, *_: (i // per, i % per, pair)),
           pl.BlockSpec((1, 8, BQ), lambda i, *_: (i, 0, 0))],
        full(out), sds(out, BF16),
        [pltpu.VMEM((2, SEQLEN, HD), BF16)] * 3
        + [pltpu.VMEM((count, PAIR, chunk), BF16)] * 2
        + [pltpu.VMEM((steps, PAIR, BQ), BF16)] * 2
        + [pltpu.VMEM((2, BQ, HD), F32)]
        + [pltpu.VMEM((count, PAIR, chunk), F32)] * 2,
        [*qkv, *grads, wide, lse], 0, 0, "attend_backward", (flow.scal, ends),
    )


def flip(values_in, axes, mask):
    return lax.ppermute(values_in, axes, [(a, a ^ mask) for a in range(lax.axis_size(axes))])


def turn(values_in):
    return lax.ppermute(values_in, ("c", "zh"), [(2 * a + b, 2 * b + a) for a in range(2) for b in range(2)])


def cross(values_in):
    return lax.ppermute(values_in, ("c", "zh"), [(2 * a + b, 2 * b + 1 - a) for a in range(2) for b in range(2)])


def uncross(values_in):
    return lax.ppermute(values_in, ("c", "zh"), [(2 * b + 1 - a, 2 * a + b) for a in range(2) for b in range(2)])


def from_members(values_in, axes):
    return [values_in] + [flip(values_in, axes, r) for r in range(1, lax.axis_size(axes))]


def to_members(parts, axes):
    return [parts[0]] + [flip(part, axes, r) for r, part in enumerate(parts) if r > 0]


def add(*parts):
    total = parts[0].astype(F32)
    for part in parts[1:]:
        total = total + part.astype(F32)
    return total


def is_small():
    return lax.axis_size("q") == 4


def order_by(values_in, axis, position, count):
    bit = 1
    while bit < count:
        shape = values_in.shape
        split = shape[:axis] + (count // (2 * bit), 2, bit) + shape[axis + 1 :]
        cut = values_in.reshape(split)
        values_in = jnp.where((position & bit) != 0, jnp.flip(cut, axis + 1), cut).reshape(shape)
        bit *= 2
    return values_in


def gather_group(values_in):
    across, sibling = flip(values_in, GROUP, 1), flip(values_in, GROUP, 2)
    return [values_in, across, sibling]


def forward(flow, members, *before):
    flow.wait(*before)
    flow.hold(across=members[1])
    gate(flow)
    members[1] = flow.free("across")
    members.append(flip(members[1], GROUP, 2))


def sum_group(keep, send):
    got = flip(send, GROUP, 2)
    passed = add(keep[1], got[1]).astype(BF16)
    return [keep[0], got, flip(passed, GROUP, 1)], passed


EXTRA = 16


def heads_shard_of(qkv, out, bias):
    rows = out.shape[0]
    paired = qkv.reshape(3, rows, -1, PAIR).transpose(1, 2, 0, 3).reshape(rows, -1)
    weights = jnp.concatenate([paired, out], axis=1)
    below = jnp.pad(bias.reshape(1, -1), ((0, EXTRA - 1), (0, weights.shape[1] - bias.size)))
    return jnp.concatenate([weights, below])


def heads_bias(rows, heads):
    bias = rows.reshape(rows.shape[0], 2, heads, -1).transpose(1, 2, 0, 3).reshape(2, -1).astype(F32)
    bias = jnp.stack([bias[0], jnp.zeros_like(bias[0]), bias[1]])
    return bias.reshape(3, -1, PAIR).transpose(1, 0, 2).reshape(1, -1)


def heads_along_x(pair):
    return jnp.stack([pair, flip(pair, "q", 1)])


def heads_along_y(near, size, heads, where, zh):
    far = flip(near, "q", 2)
    rows = jnp.concatenate([near[:, :, ROWS, :size], far[:, :, ROWS, :size]])
    return [near, far], heads_bias(order_by(order_by(rows, 0, where[0], 4), 1, zh, 2).reshape(8, size), heads)


def all_heads_weight(shard, size, heads, zh):
    pair = jnp.stack([turn(shard), cross(shard)])
    every = order_by(lax.all_gather(pair, "q"), 1, zh, 2)
    count = shard.shape[0] - EXTRA
    weights = every[:, :, :count].reshape(4, 2, ROWS, -1)
    return [weights[:2], weights[2:]], heads_bias(every[:, :, count, :size].reshape(-1, size), heads)


class HeadsGrad:
    def __init__(self, keep, send):
        self.keep, self.send = keep, send

    def along_x(self):
        self.got = flip(self.send, "q", 1)
        return self.got

    def along_y(self):
        self.got_x = self.got
        self.got = flip(add(self.keep[1], self.got[1]).astype(BF16), "q", 2)
        return self.got

    def halves(self, zh):
        if is_small():
            return tuple(add(self.keep[0, k], self.got_x[0, k], self.got[k]).astype(BF16) for k in range(2))
        buckets = [self.keep[0], self.send[0], self.keep[1], self.send[1]]
        every = jnp.stack(buckets).reshape(lax.axis_size("q"), 2, -1, buckets[0].shape[-1])
        rows = order_by(lax.psum_scatter(every, "q", scatter_dimension=0, tiled=False), 0, zh, 2)
        return rows[0], rows[1]


SLOTS = (0, 2, 1, 3)


def all_units_weight(shard):
    matrices, _, width = shard.shape
    members = lax.axis_size(MODEL)
    every = lax.all_gather(shard, ALL).reshape(members, -1, matrices, shard.shape[1], width).transpose(0, 2, 1, 3, 4)
    every = every.reshape(members, matrices, 4, 2, ROWS, width)
    every = jnp.stack([every[slot] for slot in SLOTS])
    pieces = []
    for k in range(2):
        pieces += [jnp.stack([every[:, :, r, k] for r in range(3)]), every[:, :, 3, k]]
    return pieces


class UnitsWeight:
    def __init__(self, shard):
        self.shard = shard

    def start_far_z(self):
        self.other = flip(self.shard, "zh", 1)

    def join_far_z(self, shard):
        self.two = jnp.stack([shard, self.other])

    def far_z(self):
        self.start_far_z()
        self.join_far_z(self.shard)

    def start_z(self):
        self.other = flip(self.two, "zl", 1)

    def join_z(self, two):
        self.own = jnp.concatenate([two, self.other])

    def near_z(self):
        self.start_z()
        self.join_z(self.two)

    def near(self):
        self.near_x, self.near_y = flip(self.own, "q", 1), flip(self.own, "q", 2)

    def corner(self):
        self.far_a, self.far_b = flip(self.near_y[:2], "q", 1), flip(self.near_x[2:], "q", 2)

    def swap_main(self):
        self.main = jnp.stack([self.own, self.near_x, self.near_y])
        self.main_sibling = flip(self.main, "c", 1)

    def swap_corner(self):
        self.far = jnp.concatenate([self.far_a, self.far_b])
        self.far_sibling = flip(self.far, "c", 1)

    def pieces(self):
        return [self.main, self.far, self.main_sibling, self.far_sibling]


class UnitsGrads:
    def __init__(self, flow, down, up, count):
        self.flow, self.down, self.up, self.count = flow, down, up, count

    def compute_theirs(self):
        self.theirs = unit_grads(self.flow, self.down, self.up, None, self.count, True)

    def send_theirs(self):
        self.got = flip(self.theirs, "c", 1) if is_small() else None

    def sibling(self):
        self.compute_theirs()
        self.send_theirs()

    def mine(self):
        self.made = unit_grads(self.flow, self.down, self.up, self.got, self.count, False)
        self.own, self.to_x, self.to_y, self.rest_x, self.rest_y = self.made

    def near(self):
        self.from_x, self.from_y = flip(self.to_x, "q", 1), flip(self.to_y, "q", 2)
        return [self.from_x, self.from_y]

    def far(self):
        half = self.count
        self.late_x = flip(add(self.rest_x, self.from_y[half:]).astype(BF16), "q", 1)
        self.late_y = flip(add(self.rest_y, self.from_x[half:]).astype(BF16), "q", 2)
        return [self.late_x, self.late_y]

    def near_z(self):
        half = self.count
        self.there = flip(add(self.own[half:], self.late_x, self.from_y[:half]).astype(BF16), "zl", 1)
        return [self.there]

    def far_z(self):
        self.last = flip(self.near_sum(slice(self.count // 2, self.count)).astype(BF16), "zh", 1)
        return [self.last]

    def near_sum(self, blocks):
        return add(self.own[blocks], self.from_x[blocks], self.late_y[blocks], self.there[blocks])

    def total(self):
        if is_small():
            return self.near_sum(slice(0, self.count // 2)) + self.last.astype(F32)
        half = self.count
        mine = jnp.stack(
            [self.own, jnp.concatenate([self.to_x[:half], self.rest_x]), jnp.concatenate([self.rest_y, self.to_y[:half]]),
             jnp.concatenate([self.to_x[half:], self.to_y[half:]])]
        ).reshape(4, self.count, 2, ROWS, -1)
        theirs = self.theirs.reshape(4, 2, self.count, ROWS, -1).transpose(0, 2, 1, 3, 4)
        every = jnp.stack([mine, theirs], axis=1)
        every = every.transpose(2, 0, 1, 4, 3, 5)
        every = jnp.stack([every[slot] for slot in SLOTS]).reshape(-1, 2, mine.shape[-1])
        return lax.psum_scatter(every, ALL, scatter_dimension=0, tiled=True).astype(F32).transpose(1, 0, 2)


SMALL_AXES = ("q", MODEL, "c")
SMALL_STEPS = (("q", 1), ("q", 2), ("zl", 1), ("zh", 1), ("c", 1))


def small_step(values_in, step):
    axis, mask = SMALL_STEPS[step]
    return jnp.concatenate([values_in, flip(values_in, axis, mask)])


def order_small(every, where):
    every = every.reshape(2, 2, 2, 4, -1)
    every = every.reshape(2, 4, 4, -1)
    for axis, position in enumerate(where[::-1]):
        every = order_by(every, axis, position, every.shape[axis])
    return every.transpose(1, 2, 0, 3).reshape(16 // 4, 8, -1)


def spread_by_distance(values_in, where):
    every = values_in.reshape(4, 4, 2, -1).transpose(1, 0, 2, 3)
    for axis, position in enumerate(where):
        every = order_by(every, axis, position, every.shape[axis])
    return every.transpose(2, 1, 0, 3).reshape(32, -1)


def fold_small(every, first, last):
    for axis, mask in SMALL_STEPS[::-1][first:last]:
        half = every.shape[0] // 2
        every = every[:half] + flip(every[half:], axis, mask)
    return every


def sum_all(value):
    if not is_small():
        return lax.psum(value, ALL)
    for axes in SMALL_AXES:
        parts = jnp.stack(from_members(value, axes))
        value = jnp.sum(order_by(parts, 0, lax.axis_index(axes), parts.shape[0]), 0)
    return value[0, 0]


def on_device(
    tokens, doc_lengths, qkv_weight, qv_bias, out_weight, up_weight, up_bias, down_weight, gains, shifts, cotangent
):
    layers = qkv_weight.shape[0]
    tz, dp = lax.axis_size(MODEL), lax.axis_size(("q", "c"))
    place, zh = lax.axis_index(GROUP), lax.axis_index("zh")
    where = (lax.axis_index("q"), lax.axis_index(MODEL), lax.axis_index("c"))
    if is_small():
        spots = [place, where[0], where[2], zh, where[1]]
    else:
        spots = [place] + [jnp.zeros((), jnp.int32)] * 4
    scal = jnp.stack([spot.astype(jnp.int32) for spot in spots])

    flow = Flow(scal)
    small_slice = is_small()
    qkv_cols, out_cols = 3 * out_weight.shape[2], out_weight.shape[2]
    in_cols, out_cols = slice(0, qkv_cols), slice(qkv_cols, qkv_cols + out_cols)
    hz, bias_size = qv_bias.shape[2], qv_bias.size // layers
    heads_shard = [heads_shard_of(qkv_weight[l], out_weight[l], qv_bias[l]) for l in range(layers)]
    pieces = [up_bias, gains, shifts]
    sizes = [piece.size // layers for piece in pieces]
    cuts = [0]
    for size in sizes:
        cuts.append(cuts[-1] + size)
    small = jnp.concatenate([piece.reshape(layers, -1) for piece in pieces], axis=1).reshape(1, -1)

    def spread_small(every):
        every = every.reshape(tz, dp, layers, -1).astype(F32)
        parts = [every[..., cuts[i] : cuts[i + 1]] for i in range(3)]
        biases = parts[0].reshape(tz, dp, layers, up_bias.shape[1], -1).transpose(2, 0, 3, 1, 4)
        gain = parts[1].reshape(tz, dp, layers, 2, -1).transpose(2, 3, 1, 0, 4).reshape(layers, 2, D)
        shift = parts[2].reshape(tz, dp, layers, 4, -1).transpose(2, 3, 1, 0, 4).reshape(layers, 4, D)
        table = jnp.concatenate([gain, shift], axis=1).reshape(layers * 6, D)
        head = jnp.concatenate([jnp.ones((1, D), F32), jnp.zeros((1, D), F32)])
        return biases.reshape(layers, tz, 1, -1), jnp.pad(jnp.concatenate([head, table]), ((0, TABLE - 2 - 6 * layers), (0, 0)))

    if small_slice:
        pair = jnp.stack([turn(heads_shard[0]), cross(heads_shard[0])])
        x_low = turn(tokens)
        ends = jnp.cumsum(turn(doc_lengths)[0], dtype=jnp.int32)
        near = heads_along_x(pair)
        small = small_step(small, 0)
        up0, down0 = UnitsWeight(up_weight[0][None]), UnitsWeight(down_weight[0][None])
        both1 = UnitsWeight(jnp.stack([up_weight[1], down_weight[1]]))
        flow.hold(
            up0=up0.shard, down0=down0.shard, down0_twin=down0.shard, both1=both1.shard, heads1=heads_shard[1], low=x_low,
            small=small,
        )
        gate(flow)
        x_low, up0.shard = flow.free("low"), flow.free("up0")
        up0.far_z()
        small = small_step(small_step(flow.free("small"), 1), 2)
        weights_of = [heads_along_y(near, bias_size, hz, where, zh)]
    else:
        x_low = turn(tokens)
        ends = jnp.cumsum(turn(doc_lengths)[0], dtype=jnp.int32)
        weights_of = [all_heads_weight(shard, bias_size, hz, zh) for shard in heads_shard]
        every = [all_units_weight(jnp.stack([up_weight[l], down_weight[l]])) for l in range(layers)]
        top_grad = turn(cotangent)
        up_bias_full, table = spread_small(lax.all_gather(small, ALL))

    prev, prev_gain, prev_shift = x_low, ONE, ZERO
    kept = []
    for l in range(layers):
        first, last = small_slice and l == 0, small_slice and l == 1
        xs = gather_group(x_low)
        w_heads, bias = weights_of[l]
        if first:
            flow.wait(up0.two, small)
            flow.hold(small=small, two=up0.two, two_twin=up0.two)
        if last:
            flow.wait(both1.own)
            flow.hold(own=both1.own)
        qkv_near = project_in(flow, (xs[0], xs[2]), False, w_heads, in_cols, bias, "project_qkv")
        if first:
            up0.two, down0.shard = flow.free("two"), flow.free("down0")
            up0.start_z()
            down0.start_far_z()
            small = small_step(flow.free("small"), 3)
        if last:
            both1.own = flow.free("own")
            both1.near()
        if last:
            flow.hold(top=cotangent)
        forward(flow, xs, qkv_near)
        if first:
            flow.hold(small=small)
        qkv_far = project_in(flow, (xs[1], xs[3]), True, w_heads, in_cols, bias, "project_qkv")
        qkv = (qkv_near, qkv_far)
        if first:
            down0.join_far_z(flow.free("down0_twin"))
            up0.join_z(flow.free("two_twin"))
            up0.near()
            down0.near_z()
            both1.shard = flow.free("both1")
            both1.far_z()
        if last:
            top_grad = turn(flow.free("top"))
        ctx, wide, lse = attend_forward(flow, ends, qkv)
        if first:
            flow.wait(up0.near_x, up0.near_y, down0.own, both1.two)
            flow.hold(both1=both1.two)
            up0.corner()
            down0.near()
        if last:
            flow.wait(both1.near_x, both1.near_y, top_grad)
            flow.hold(own=both1.own)
            both1.corner()
        send = project_out(flow, [ctx], (2, 3), w_heads, out_cols, True, "project_attn")
        flow.wait(send)
        keep = project_out(flow, [ctx], (0, 1), w_heads, out_cols, False, "project_attn")
        attn, passed = sum_group(keep, send)
        if first:
            flow.wait(passed, up0.far_a, up0.far_b)
            flow.hold(own=up0.own)
            gate(flow)
            up0.own = flow.free("own")
            up0.swap_main()
            up0.swap_corner()
            up_bias_full, table = spread_small(order_small(small_step(flow.free("small"), 4), where))
            flow.wait(down0.near_x, down0.near_y)
            down0.corner()
            down0.swap_main()
            shard = flow.free("heads1")
            pair = jnp.stack([turn(shard), cross(shard)])
            w_up = up0.pieces(), 0
        elif last:
            flow.wait(passed)
            gate(flow)
            both1.own = flow.free("own")
            both1.swap_main()
            flow.hold(far_a=both1.far_a)
            flow.wait(attn[2])
            gate(flow)
            both1.far_a = flow.free("far_a")
            both1.swap_corner()
            w_up, w_down = (both1.pieces(), 0), (both1.pieces(), 1)
        else:
            w_up, w_down = (every[l], 0), (every[l], 1)
        used = (prev_gain, prev_shift, shift_row(l, 0), gain_row(l, 0), shift_row(l, 1))
        n1, hs, r1, act, slope = norm_up(flow, prev, attn, table, used, *w_up, up_bias_full[l], tz)
        if first:
            both1.two = flow.free("both1")
            flow.wait(n1)
            flow.hold(far_a=down0.far_a, pair=pair, pair_twin=pair)
            gate(flow)
            down0.far_a = flow.free("far_a")
            down0.swap_corner()
            beside = flip(flow.free("pair"), "q", 1)
            both1.near_z()
            w_down = down0.pieces(), 0
        used = (gain_row(l, 0), shift_row(l, 1), shift_row(l, 2), gain_row(l, 1), shift_row(l, 3))
        n2, y_low, r2 = down_norm(flow, act, *w_down, n1, table, used, tz)
        kept.append((xs, qkv, ctx, wide, lse, n1, hs, r1, act, slope, n2, r2, w_heads, w_up, w_down))
        if first:
            near = jnp.stack([flow.free("pair_twin"), beside])
            weights_of.append(heads_along_y(near, bias_size, hz, where, zh))
        x_low, prev, prev_gain, prev_shift = y_low, n2, gain_row(l, 1), shift_row(l, 3)
    layer_output = turn(x_low)

    g2, gf, sums2 = norm_back(flow, top_grad, kept[-1][10], kept[-1][11], table, gain_row(layers - 1, 1))
    small_grads = [None] * layers
    units_of, heads_of = [None] * layers, [None] * layers
    above = above_heads = None
    for l in reversed(range(layers)):
        top = l == layers - 1
        xs, qkv, ctx, wide, lse, n1, hs, r1, act, slope, n2, r2, w_heads, w_up, w_down = kept[l]
        beside = small_slice and not top
        gu, up_bias_sum = units_back(flow, gf, *w_down, slope, tz)
        units = UnitsGrads(flow, (gf, act), (hs, gu), tz)
        if top:
            flow.hold(output=layer_output)
        else:
            if beside:
                flow.wait(*above.near())
                flow.hold(heads=above_heads.send)
            units.sibling()
            flow.wait(units.theirs)
            if beside:
                above_heads.send = flow.free("heads")
                above_heads.along_x()
                late = above.far()
        g1, ga, sums1 = up_back(flow, gu, *w_up, g2, n1, r1, table, gain_row(l, 0), tz)
        gas = gather_group(ga)
        flow.wait(ga)
        if top:
            layer_output = flow.free("output")
            units.compute_theirs()
            forward(flow, gas, units.theirs)
        else:
            units.mine()
            if beside:
                flow.wait(*late, above_heads.got)
            forward(flow, gas, *units.made)
        gc_near = project_in(flow, (gas[0], gas[2]), False, w_heads, out_cols, None, "project_gc")
        flow.wait(gc_near)
        if top:
            flow.hold(theirs=units.theirs)
        gc_far = project_in(flow, (gas[1], gas[3]), True, w_heads, out_cols, None, "project_gc")
        if top:
            units.theirs = flow.free("theirs")
            units.send_theirs()
        gcs = (gc_near, gc_far)
        if beside:
            flow.hold(rest_x=units.rest_x, rest_y=units.rest_y)
        gqkv = [attend_backward(flow, ends, 0, qkv, gcs, wide, lse)]
        if beside:
            units.rest_x, units.rest_y = flow.free("rest_x"), flow.free("rest_y")
        flow.wait(gqkv[0])
        if beside:
            flow.wait(*units.near(), *above.near_z(), above_heads.along_y())
            above.far_z()
            units.far()
            above_halves = above_heads.halves(zh)
            done = turn(above_halves[0]), uncross(above_halves[1])
            flow.hold(own=units.own)
        gqkv.append(attend_backward(flow, ends, 1, qkv, gcs, wide, lse))
        if beside:
            units.own = flow.free("own")
            flow.wait(units.late_x, units.late_y, above.last, *done)
            units.near_z()
        send = project_out(flow, gqkv, (2, 3), w_heads, in_cols, True, "project_gx")
        flow.wait(send)
        if beside:
            flow.hold(own=units.own)
        keep = project_out(flow, gqkv, (0, 1), w_heads, in_cols, False, "project_gx")
        back, passed = sum_group(keep, send)
        flow.wait(passed)
        if top:
            units.mine()
            flow.wait(*units.made)
        elif small_slice:
            units.own = flow.free("own")
            units.far_z()
        *buckets, qkv_sums = heads_grad(flow, xs, gqkv, gas, ctx)
        heads = HeadsGrad(*buckets)
        units_of[l], heads_of[l] = units, heads
        qv_sums = qkv_sums.reshape(-1, 3, PAIR).transpose(1, 0, 2).reshape(3, hz, dp, -1)
        qv_sums = jnp.stack([qv_sums[0], qv_sums[2]]).transpose(2, 0, 1, 3).reshape(1, dp, -1)
        mine = (jnp.arange(tz) == place).astype(F32).reshape(tz, 1, 1)
        small_grads[l] = jnp.concatenate(
            [
                mine * qv_sums,
                up_bias_sum.reshape(tz, up_bias.shape[1], dp, -1).transpose(0, 2, 1, 3).reshape(tz, dp, -1),
                jnp.stack([sums1[0], sums2[0]]).reshape(2, dp, tz, -1).transpose(2, 1, 0, 3).reshape(tz, dp, -1),
                jnp.stack([sums1[2], sums1[1], sums2[2], sums2[1]])
                .reshape(4, dp, tz, -1).transpose(2, 1, 0, 3).reshape(tz, dp, -1),
            ],
            axis=-1,
        )
        if l > 0:
            above, above_heads = units, heads
            flow.wait(heads.send)
            g2, gf, sums2 = sum_norm_back(flow, g1, back, kept[l - 1][10], kept[l - 1][11], table, gain_row(l - 1, 1))
    small_sums = jnp.stack(small_grads, axis=2).reshape(tz, dp, -1)
    if small_slice:
        heads.along_x()
        flow.wait(back[2], units.last)
        flow.hold(small=small_sums, got=heads.got, own=units.own)
        gate(flow)
        small_sums, heads.got, units.own = flow.free("small"), flow.free("got"), flow.free("own")
        input_grad = turn(add(g1, back[0], back[1][0], back[2]).astype(BF16))
        heads.along_y()
        small_sums = fold_small(spread_by_distance(small_sums, where), 0, 2)
        flow.wait(heads.got)
        flow.hold(small=small_sums, grad=input_grad)
        gate(flow)
        small_sums, input_grad = flow.free("small"), flow.free("grad")
        halves = heads.halves(zh)
        d_heads = jnp.stack([add(turn(halves[0]), uncross(halves[1])), add(*done)])
        small_out = fold_small(small_sums, 2, 5).reshape(layers, -1)
    else:
        halves = [member.halves(zh) for member in heads_of]
        d_heads = jnp.stack([add(turn(half[0]), uncross(half[1])) for half in halves])
        input_grad = turn(add(g1, back[0], back[1][0], back[2]).astype(BF16))
        small_out = lax.psum_scatter(small_sums.reshape(tz * dp, -1), ALL, scatter_dimension=0, tiled=True)
        small_out = small_out.reshape(layers, -1)
    qkv_grad = d_heads[:, :, : in_cols.stop].reshape(layers, d_heads.shape[1], -1, 3, PAIR)
    qkv_grad = qkv_grad.transpose(0, 3, 1, 2, 4).reshape(qkv_weight.shape)
    out_grad = d_heads[:, :, in_cols.stop :]
    totals = [member.total() for member in units_of]
    down_grad, up_grad = (jnp.stack([total[i] for total in totals]) for i in range(2))

    rest = small_out[:, bias_size:]
    qv_bias_grad = small_out[:, :bias_size].reshape(qv_bias.shape)
    up_bias_grad = rest[:, cuts[0] : cuts[1]].reshape(up_bias.shape)
    gains_grad = rest[:, cuts[1] : cuts[2]].reshape(gains.shape)
    shifts_grad = rest[:, cuts[2] : cuts[3]].reshape(shifts.shape)
    all_grads = (qkv_grad, qv_bias_grad, out_grad, up_grad, up_bias_grad, down_grad, gains_grad, shifts_grad)
    local_squares = sum(jnp.sum(member * member) for member in all_grads)
    entry_count = LAYERS * (4 * D * D + 2 * D * FF + FF + 8 * D)
    if small_slice:
        local_squares = jnp.broadcast_to(local_squares, (8, 128))
    grad_rms = jnp.sqrt(sum_all(local_squares) / entry_count)
    return (
        layer_output, input_grad, qkv_grad, qv_bias_grad, out_grad, up_grad, up_bias_grad, down_grad, gains_grad,
        shifts_grad, grad_rms,
    )


def solution(mesh):
    dp, tensor = mesh.shape["dp"], mesh.shape["tensor"]
    fine = Mesh(mesh.devices.reshape(dp // 2, 2, 2, tensor // 2), ("q", "c", "zh", "zl"))
    data, model = ("q", "c"), ("zh", "zl")
    both = data + model
    weight3, weight4 = P(None, data, model), P(None, None, data, model)
    in_specs = (
        P(both, None), P(data, None), weight4, P(None, None, model, data), weight3, weight3, P(None, model, data),
        weight3, P(None, None, both), P(None, None, both), P(both, None),
    )
    out_specs = (
        P(both, None), P(both, None), weight4, P(None, None, model, data), weight3, weight3, P(None, model, data),
        weight3, P(None, None, both), P(None, None, both), P(),
    )
    return jax.shard_map(on_device, mesh=fine, in_specs=in_specs, out_specs=out_specs, check_vma=False)
```

```python
import jax
import jax.numpy as jnp
from jax import lax
from jax.experimental import pallas as pl
from jax.experimental.pallas import tpu as pltpu
from jax.sharding import Mesh
from jax.sharding import PartitionSpec as P

D = 1024
HD = 64
HEADS = 16
FF = 4096
LAYERS = 2
SEQLEN = 2048
WINDOW = 1024
EPS = 1e-06
FILL = -1000000000.0

F32 = jnp.float32
BF16 = jnp.bfloat16
GROUP = ("c", "zl")
MODEL = ("zh", "zl")
ALL = ("zh", "zl", "q", "c")
VMEM_LIMIT = 56 * 1024 * 1024
TIMES = {
    "gate": 0.1, "norm_up": 20.0, "down_norm": 20.0, "units_back": 20.0, "up_back": 20.0, "norm_back": 6.0,
    "sum_norm_back": 20.0, "grads_theirs": 0.2, "grads_mine": 0.2, "project_qkv": 0.2, "project_gc": 0.2,
    "project_attn": 0.2, "project_gx": 0.2, "heads_grad": 0.2, "attend_forward": 40.0, "attend_backward": 30.0,
}
PEAK = 0.35e9
NT = (((1,), (1,)), ((), ()))
NN = (((1,), (0,)), ((), ()))
ROWS = 128
CHUNK = 64
BQ = 512
PAIR = 2 * HD


def mm(left, right, dims=NN):
    return lax.dot_general(left, right, dims, preferred_element_type=F32)


def full(shape):
    return pl.BlockSpec(shape, lambda *_: (0,) * len(shape))


ANY = pl.BlockSpec(memory_space=pl.ANY)


def sds(shape, kind):
    return jax.ShapeDtypeStruct(shape, kind)


class Flow:
    def __init__(self, scal):
        self.scal, self.before, self.held = scal, [], {}

    def wait(self, *arrays):
        self.before += arrays

    def hold(self, **arrays):
        self.held.update(arrays)

    def free(self, name):
        return self.held.pop(name)


def call(flow, body, grid, in_specs, out_specs, out_shape, scratch, args, flops, traffic, name, scalars=None):
    scalars = (flow.scal,) if scalars is None else scalars
    single = not isinstance(out_specs, (list, tuple))
    out_specs = [out_specs] if single else list(out_specs)
    out_shape = [out_shape] if single else list(out_shape)
    before, held = flow.before, list(flow.held.items())
    ns, nb, nh, no = len(scalars), len(before), len(held), len(out_specs)
    first, last = ns + nb + nh, ns + nb + nh + len(args) + no

    def wrapped(*refs):
        body(*refs[:ns], *refs[first:last], *refs[last + nh :])

    result = pl.pallas_call(
        wrapped,
        grid_spec=pltpu.PrefetchScalarGridSpec(
            num_scalar_prefetch=ns,
            grid=grid,
            in_specs=[ANY] * (nb + nh) + list(in_specs),
            out_specs=out_specs + [ANY] * nh,
            scratch_shapes=scratch,
        ),
        out_shape=out_shape + [sds(array.shape, array.dtype) for _, array in held],
        input_output_aliases={ns + nb + i: no + i for i in range(nh)},
        compiler_params=pltpu.CompilerParams(
            dimension_semantics=("arbitrary",) * len(grid), vmem_limit_bytes=VMEM_LIMIT
        ),
        cost_estimate=pl.CostEstimate(flops=int(TIMES[name] * PEAK), bytes_accessed=1024, transcendentals=0),
        name=name,
    )(*scalars, *before, *[array for _, array in held], *args)
    flow.before = []
    flow.held = {key: value for (key, _), value in zip(held, result[no:])}
    return result[0] if single else result[:no]


def gate(flow):
    if flow.held:
        call(flow, lambda *refs: None, (1,), [], [], [], [], [], 0, 0, "gate")


S_P, S_Q, S_C, S_ZH, S_Z = range(5)


def norm_rows(values_in):
    centred = values_in - jnp.mean(values_in, -1, keepdims=True)
    variance = jnp.mean(centred * centred, -1, keepdims=True)
    inverse = lax.rsqrt(variance + EPS)
    return centred * inverse, inverse


def norm_back_rows(grad, normed, inverse, gain):
    scaled = grad * gain
    centred = scaled - jnp.mean(scaled, -1, keepdims=True) - normed * jnp.mean(scaled * normed, -1, keepdims=True)
    return centred * inverse


def fold_rows(values_in):
    return jnp.sum(values_in.reshape(-1, 8, values_in.shape[-1]), 0)


def read(part, rows):
    return (part[0, rows, :] if len(part.shape) == 3 else part[rows, :]).astype(F32)


def part_spec(part):
    shape = part.shape
    return full(shape) if len(shape) == 2 else pl.BlockSpec((1,) + shape[1:], lambda *_: (0, 0, 0))


ONE, ZERO, TABLE = 0, 1, 16


def gain_row(layer, index):
    return 2 + 6 * layer + index


def shift_row(layer, index):
    return 4 + 6 * layer + index


def row_of(vec_ref, row):
    return vec_ref[row : row + 1, :]


def norm_forward(get_total, tokens, vec, gain, shift, n_ref, low_ref, inv_ref):

    def step(index, carry):
        rows = pl.ds(pl.multiple_of(index * CHUNK, CHUNK), CHUNK)
        normed, inverse = norm_rows(get_total(rows))
        n_ref[rows, :] = normed
        low_ref[rows, :] = (normed * row_of(vec, gain) + row_of(vec, shift)).astype(BF16)
        inv_ref[rows, :] = jnp.broadcast_to(inverse, (CHUNK, 128))
        return carry

    lax.fori_loop(0, tokens // CHUNK, step, 0)


def norm_backward(get_grad, tokens, n_ref, inv_ref, vec, gain, g_ref, low_ref, sums_ref):
    def step(index, carry):
        rows = pl.ds(pl.multiple_of(index * CHUNK, CHUNK), CHUNK)
        grad = get_grad(rows)
        normed = n_ref[rows, :]
        result = norm_back_rows(grad, normed, inv_ref[rows, 0:1], row_of(vec, gain))
        low = result.astype(BF16)
        g_ref[rows, :] = result
        low_ref[rows, :] = low
        return (
            carry[0] + fold_rows(grad * normed),
            carry[1] + fold_rows(grad),
            carry[2] + fold_rows(low.astype(F32)),
        )

    zero = jnp.zeros((8, D), F32)
    sums = lax.fori_loop(0, tokens // CHUNK, step, (zero, zero, zero))
    sums_ref[...] = jnp.zeros(sums_ref.shape, F32)
    for row, member in enumerate(sums):
        sums_ref[row : row + 1, :] = jnp.sum(member, 0, keepdims=True)


def away(s):
    return (s & 1) * 2 + s // 2


class Streamed:
    def __init__(self, refs, matrix, buffer, sems, scal):
        self.refs, self.matrix, self.buffer, self.sems, self.scal = refs, matrix, buffer, sems, scal

    def copies(self, s):
        slot = lax.rem(s, 2)
        plain, early, late = [], [], []
        for k in range(2):
            own, near_x, near_y, far_a, far_b = self.refs[5 * k : 5 * k + 5]

            def copy(source, r, k=k):
                row = ((self.scal[S_Q] ^ r) * 2 + (self.scal[S_C] ^ k)) * ROWS
                return pltpu.make_async_copy(
                    source, self.buffer.at[slot, pl.ds(pl.multiple_of(row, ROWS), ROWS), :], self.sems.at[slot, 4 * k + r]
                )

            for r, ref in enumerate((own, near_x, near_y)):
                plain.append(copy(ref.at[s, self.matrix], r))
            early.append(copy(far_a.at[jnp.minimum(s, 1), self.matrix], 3))
            late.append(copy(far_b.at[jnp.maximum(s - 2, 0), self.matrix], 3))
        return plain, early, late

    def each(self, s, act):
        plain, early, late = self.copies(s)
        for copy in plain:
            act(copy)

        @pl.when(s < 2)
        def _():
            for copy in early:
                act(copy)

        @pl.when(s >= 2)
        def _():
            for copy in late:
                act(copy)

    def start(self, s):
        self.each(s, lambda copy: copy.start())

    def wait(self, s):
        self.each(s, lambda copy: copy.wait())

    def turn(self, s, count):
        @pl.when(s == 0)
        def _():
            self.start(s)

        @pl.when(s + 1 < count)
        def _():
            self.start(s + 1)


def piece_shapes(width):
    return [pltpu.VMEM((2, D, width), BF16), pltpu.SemaphoreType.DMA((2, 8))]


def gelu_parts(u):
    size = jnp.abs(u)
    t = 1.0 / (1.0 + 0.2316419 * size)
    poly = t * (0.127414796 + t * (-0.142248368 + t * (0.7107068705 + t * (-0.7265760135 + t * 0.5307027145))))
    bell = jnp.exp(-0.5 * (u * u))
    tail = poly * bell
    cdf = jnp.where(u >= 0, 1.0 - tail, tail)
    return u * cdf, cdf + u * (0.3989422804014327 * bell)


def tiles(tokens, width):
    for i in range(2):
        for j in range(2):
            yield slice(i * tokens // 2, (i + 1) * tokens // 2), slice(j * width // 2, (j + 1) * width // 2)


def norm_up(flow, prev, parts, vec, rows_used, weight, matrix, bias, count):
    tokens = prev.shape[0]
    width = FF // count

    def body(scal_ref, prev_ref, *refs):
        part_refs, refs = refs[: len(parts)], refs[len(parts) :]
        vec_ref, bias_ref, refs = refs[0], refs[1], refs[2:]
        pieces, (n_ref, low_ref, inv_ref, act_ref, slope_ref, buffer, sems) = refs[:10], refs[10:]
        s = pl.program_id(0)
        stream = Streamed(pieces, matrix, buffer, sems, scal_ref)
        stream.turn(s, count)

        @pl.when(s == 0)
        def _():
            def total(rows):
                attn = read(part_refs[0], rows)
                for part in part_refs[1:]:
                    attn = attn + read(part, rows)
                before = read(prev_ref, rows) * row_of(vec_ref, rows_used[0]) + row_of(vec_ref, rows_used[1])
                return before + (attn + row_of(vec_ref, rows_used[2]))

            norm_forward(total, tokens, vec_ref, *rows_used[3:], n_ref, low_ref, inv_ref)

        stream.wait(s)
        slot = lax.rem(s, 2)
        for rows, cols in tiles(tokens, width):
            act, slope = gelu_parts(mm(low_ref[rows, :], buffer[slot, :, cols]) + bias_ref[0, :, cols])
            act_ref[rows, cols] = act.astype(BF16)
            slope_ref[rows, cols] = slope.astype(BF16)

    column = pl.BlockSpec((tokens, width), lambda s, _: (0, s))
    return call(
        flow, body, (count,),
        [full((tokens, D))] + [part_spec(part) for part in parts]
        + [full((TABLE, D)), pl.BlockSpec((1, 1, width), lambda s, scal_ref: (scal_ref[S_Z] ^ away(s), 0, 0))] + [ANY] * 10,
        [full((tokens, D)), full((tokens, D)), full((tokens, 128)), column, column],
        [sds((tokens, D), F32), sds((tokens, D), BF16), sds((tokens, 128), F32)] + [sds((tokens, FF), BF16)] * 2,
        piece_shapes(width), [prev, *parts, vec, bias, *weight], 2 * tokens * D * FF,
        2 * (D * FF + tokens * (10 * D + 2 * FF)), "norm_up",
    )


def down_norm(flow, act, weight, matrix, prev, vec, rows_used, count):
    tokens = prev.shape[0]
    width = FF // count

    def body(scal_ref, act_ref, prev_ref, vec_ref, *refs):
        pieces, (n_ref, low_ref, inv_ref, buffer, sems, acc) = refs[:10], refs[10:]
        s = pl.program_id(0)
        stream = Streamed(pieces, matrix, buffer, sems, scal_ref)
        stream.turn(s, count)
        stream.wait(s)
        value = mm(act_ref[...], buffer[lax.rem(s, 2)], NT)

        @pl.when(s == 0)
        def _():
            acc[...] = value

        @pl.when(s > 0)
        def _():
            acc[...] += value

        @pl.when(s == count - 1)
        def _():
            def total(rows):
                before = prev_ref[rows, :] * row_of(vec_ref, rows_used[0]) + row_of(vec_ref, rows_used[1])
                return before + (acc[rows, :] + row_of(vec_ref, rows_used[2]))

            norm_forward(total, tokens, vec_ref, *rows_used[3:], n_ref, low_ref, inv_ref)

    return call(
        flow, body, (count,),
        [pl.BlockSpec((tokens, width), lambda s, _: (0, s)), full((tokens, D)), full((TABLE, D))] + [ANY] * 10,
        [full((tokens, D)), full((tokens, D)), full((tokens, 128))],
        [sds((tokens, D), F32), sds((tokens, D), BF16), sds((tokens, 128), F32)],
        piece_shapes(width) + [pltpu.VMEM((tokens, D), F32)], [act, prev, vec, *weight], 2 * tokens * D * FF,
        2 * (D * FF + tokens * (5 * D + FF)), "down_norm",
    )


def units_back(flow, grad, weight, matrix, slope, count):
    tokens = grad.shape[0]
    width = FF // count

    def body(scal_ref, grad_ref, slope_ref, *refs):
        pieces, (out_ref, sum_ref, buffer, sems) = refs[:10], refs[10:]
        s = pl.program_id(0)
        stream = Streamed(pieces, matrix, buffer, sems, scal_ref)
        stream.turn(s, count)
        stream.wait(s)
        slot = lax.rem(s, 2)
        sums = {}
        for rows, cols in tiles(tokens, width):
            low = (mm(grad_ref[rows, :], buffer[slot, :, cols]) * slope_ref[rows, cols].astype(F32)).astype(BF16)
            out_ref[rows, cols] = low
            part = fold_rows(low.astype(F32))
            sums[cols.start] = sums[cols.start] + part if cols.start in sums else part
            if rows.start > 0:
                sum_ref[0, :, cols] = jnp.sum(sums[cols.start], 0, keepdims=True)

    column = pl.BlockSpec((tokens, width), lambda s, _: (0, s))
    return call(
        flow, body, (count,), [full((tokens, D)), column] + [ANY] * 10,
        [column, pl.BlockSpec((1, 1, width), lambda s, scal_ref: (scal_ref[S_Z] ^ away(s), 0, 0))],
        [sds((tokens, FF), BF16), sds((count, 1, width), F32)], piece_shapes(width), [grad, slope, *weight],
        2 * tokens * D * FF, 2 * (D * FF + tokens * (D + 2 * FF)), "units_back",
    )


def up_back(flow, gu, weight, matrix, residual, normed, inverse, vec, gain, count):
    tokens = residual.shape[0]
    width = FF // count

    def body(scal_ref, gu_ref, res_ref, n_ref, inv_ref, vec_ref, *refs):
        pieces, (g_ref, low_ref, sums_ref, buffer, sems, acc) = refs[:10], refs[10:]
        s = pl.program_id(0)
        stream = Streamed(pieces, matrix, buffer, sems, scal_ref)
        stream.turn(s, count)
        stream.wait(s)
        value = mm(gu_ref[...], buffer[lax.rem(s, 2)], NT)

        @pl.when(s == 0)
        def _():
            acc[...] = value

        @pl.when(s > 0)
        def _():
            acc[...] += value

        @pl.when(s == count - 1)
        def _():
            norm_backward(
                lambda rows: res_ref[rows, :] + acc[rows, :], tokens, n_ref, inv_ref, vec_ref, gain, g_ref, low_ref,
                sums_ref,
            )

    return call(
        flow, body, (count,),
        [pl.BlockSpec((tokens, width), lambda s, _: (0, s)), full((tokens, D)), full((tokens, D)), full((tokens, 128)),
         full((TABLE, D))] + [ANY] * 10,
        [full((tokens, D)), full((tokens, D)), full((8, D))],
        [sds((tokens, D), F32), sds((tokens, D), BF16), sds((8, D), F32)],
        piece_shapes(width) + [pltpu.VMEM((tokens, D), F32)], [gu, residual, normed, inverse, vec, *weight],
        2 * tokens * D * FF, 2 * (D * FF + tokens * (8 * D + FF)), "up_back",
    )


def norm_back(flow, grad, normed, inverse, vec, gain):
    tokens = grad.shape[0]

    def body(scal_ref, grad_ref, n_ref, inv_ref, vec_ref, g_ref, low_ref, sums_ref):
        norm_backward(lambda rows: read(grad_ref, rows), tokens, n_ref, inv_ref, vec_ref, gain, g_ref, low_ref, sums_ref)

    return call(
        flow, body, (1,), [full((tokens, D)), full((tokens, D)), full((tokens, 128)), full((TABLE, D))],
        [full((tokens, D)), full((tokens, D)), full((8, D))],
        [sds((tokens, D), F32), sds((tokens, D), BF16), sds((8, D), F32)], [], [grad, normed, inverse, vec],
        20 * tokens * D, 12 * tokens * D, "norm_back",
    )


def sum_norm_back(flow, residual, parts, normed, inverse, vec, gain):
    tokens = residual.shape[0]

    def body(scal_ref, res_ref, *refs):
        part_refs, (n_ref, inv_ref, vec_ref, g_ref, low_ref, sums_ref) = refs[: len(parts)], refs[len(parts) :]

        def grad(rows):
            total = read(part_refs[0], rows)
            for part in part_refs[1:]:
                total = total + read(part, rows)
            return res_ref[rows, :] + total

        norm_backward(grad, tokens, n_ref, inv_ref, vec_ref, gain, g_ref, low_ref, sums_ref)

    return call(
        flow, body, (1,), [full((tokens, D))] + [part_spec(part) for part in parts]
        + [full((tokens, D)), full((tokens, 128)), full((TABLE, D))],
        [full((tokens, D)), full((tokens, D)), full((8, D))],
        [sds((tokens, D), F32), sds((tokens, D), BF16), sds((8, D), F32)], [],
        [residual, *parts, normed, inverse, vec], 20 * tokens * D, 22 * tokens * D, "sum_norm_back",
    )


def turn_rows(scal_ref, x_ref, turned, core):
    for r in range(4):
        row = ((scal_ref[S_Q] ^ r) * 2 + core) * ROWS
        turned[r * ROWS : (r + 1) * ROWS, :] = x_ref[:, pl.ds(pl.multiple_of(row, ROWS), ROWS)].T


def unit_grads(flow, down, up, received, count, sibling):
    tokens = down[0].shape[0]
    width = down[1].shape[1] // count
    half = count // 2
    steps = 2 * count

    def body(scal_ref, x0_ref, y0_ref, x1_ref, y1_ref, *refs):
        turned, t = refs[-1], pl.program_id(0)
        m, s = t // count, lax.rem(t, count)
        core = scal_ref[S_C] ^ 1 if sibling else scal_ref[S_C]

        @pl.when(t == 0)
        def _():
            turn_rows(scal_ref, x0_ref, turned, core)

        @pl.when(t == count)
        def _():
            turn_rows(scal_ref, x1_ref, turned, core)

        def store(y_ref):
            value = mm(turned[...], y_ref[...]).reshape(4, ROWS, width)
            if sibling:
                refs[0][:, 0] = value.astype(BF16)
                return
            if received is not None:
                value = value + refs[0][:, 0].astype(F32)
            value = value.astype(BF16)
            own, to_x, to_y, rest_x, rest_y = refs[-6:-1]
            spot = lax.rem(s, half) * 2 + m
            own[s // half * count + spot] = value[0]

            @pl.when(s < half)
            def _():
                to_x[spot] = value[1]
                to_x[count + spot] = value[3]
                rest_y[spot] = value[2]

            @pl.when(s >= half)
            def _():
                rest_x[spot] = value[1]
                to_y[spot] = value[2]
                to_y[count + spot] = value[3]

        @pl.when(m == 0)
        def _():
            store(y0_ref)

        @pl.when(m == 1)
        def _():
            store(y1_ref)

    left = full((tokens, D))
    pick_down = lambda t, _: (0, jnp.minimum(t, count - 1))
    pick_up = lambda t, _: (0, jnp.maximum(t - count, 0))
    specs = [left, pl.BlockSpec((tokens, width), pick_down), left, pl.BlockSpec((tokens, width), pick_up)]
    args = [*down, *up]
    one = pl.BlockSpec((4, 1, ROWS, width), lambda t, _: (0, t, 0, 0))
    if sibling:
        out_specs, out_shape = one, sds((4, steps, ROWS, width), BF16)
    else:
        if received is not None:
            specs.append(one)
            args.append(received)
        shapes = [(steps, ROWS, width)] * 3 + [(count, ROWS, width)] * 2
        out_specs, out_shape = [full(shape) for shape in shapes], [sds(shape, BF16) for shape in shapes]
    return call(
        flow, body, (steps,), specs, out_specs, out_shape, [pltpu.VMEM((4 * ROWS, tokens), BF16)], args,
        0, 0, "grads_theirs" if sibling else "grads_mine",
    )


def fetch_heads_weight(scal_ref, pieces, cols, buffer, sems):
    copies = []
    for r in range(4):
        for k in range(2):
            row = ((scal_ref[S_Q] ^ r) * 2 + (scal_ref[S_ZH] ^ k)) * ROWS
            copies.append(
                pltpu.make_async_copy(
                    pieces[r // 2].at[r % 2, k, pl.ds(0, ROWS), cols], buffer.at[pl.ds(pl.multiple_of(row, ROWS), ROWS), :],
                    sems.at[2 * r + k],
                )
            )
    for copy in copies:
        copy.start()
    for copy in copies:
        copy.wait()


def by_member(shape):
    return pl.BlockSpec((1,) + shape, lambda r, scal_ref: (scal_ref[S_P] ^ r, 0, 0))


def heads_weight_scratch(width):
    return [pltpu.VMEM((D, width), BF16), pltpu.SemaphoreType.DMA((8,))]


def project_in(flow, lefts, across, weight, cols, bias, name):
    tokens = lefts[0].shape[0]
    width = cols.stop - cols.start

    def body(scal_ref, left_ref, right_ref, *refs):
        if bias is not None:
            bias_ref, refs = refs[0], refs[1:]
        pieces, (out_ref, buffer, sems) = refs[:2], refs[2:]
        step = pl.program_id(0)

        @pl.when(step == 0)
        def _():
            fetch_heads_weight(scal_ref, pieces, cols, buffer, sems)

        for r, left in enumerate((left_ref, right_ref)):

            @pl.when(step == r)
            def _(left=left):
                value = mm(left[...], buffer[...])
                if bias is not None:
                    value = value + bias_ref[...]
                out_ref[0] = value.astype(BF16)

    extra, extra_specs = ([], []) if bias is None else ([bias], [full((1, width))])
    return call(
        flow, body, (2,), [full((tokens, D))] * 2 + extra_specs + [ANY] * 2,
        pl.BlockSpec((1, tokens, width), lambda r, scal_ref: ((scal_ref[S_P] >> 1) ^ r, 0, 0)),
        sds((2, tokens, width), BF16), heads_weight_scratch(width), [*lefts, *extra, *weight], 0, 0, name,
    )


def project_out(flow, blocks, members, weight, cols, stacked, name):
    count, tokens, width = blocks[0].shape

    def body(scal_ref, *refs):
        block_refs, refs = refs[: len(blocks)], refs[len(blocks) :]
        pieces, outs, (buffer, sems) = refs[:2], refs[2:-2], refs[-2:]
        step = pl.program_id(0)

        @pl.when(step == 0)
        def _():
            fetch_heads_weight(scal_ref, pieces, cols, buffer, sems)

        value = mm(block_refs[0][0], buffer[:, :width], NT)
        for index in range(1, len(blocks)):
            value = value + mm(block_refs[index][0], buffer[:, index * width : (index + 1) * width], NT)
        value = value.astype(BF16)
        if stacked:
            outs[0][0] = value
            return
        for r, out in enumerate(outs):

            @pl.when(step == r)
            def _(out=out):
                out[...] = value

    first, last = members
    pick = lambda r, scal_ref: (scal_ref[S_P] ^ (first + r * (last - first)), 0, 0)
    if stacked:
        out_specs, out_shape = pl.BlockSpec((1, tokens, D), lambda r, _: (r, 0, 0)), sds((2, tokens, D), BF16)
    else:
        out_specs, out_shape = [full((tokens, D))] * 2, [sds((tokens, D), BF16)] * 2
    return call(
        flow, body, (2,), [pl.BlockSpec((1, tokens, width), pick)] * len(blocks) + [ANY] * 2, out_specs, out_shape,
        heads_weight_scratch(width * len(blocks)), [*blocks, *weight], 0, 0, name,
    )


def heads_grad(flow, xs, parts, gas, ctx):
    count, tokens, width = parts[0].shape
    out_width = ctx.shape[2]
    cuts = [slice(i * width, (i + 1) * width) for i in range(len(parts))]
    total = width * len(parts)

    def body(scal_ref, *refs):
        x_refs, refs = refs[:count], refs[count:]
        ga_refs, refs = refs[:count], refs[count:]
        part_refs, refs = refs[: len(parts)], refs[len(parts) :]
        ctx_ref, outs, (sum_ref, acc, acc_out) = refs[0], refs[1:3], refs[3:]
        step = pl.program_id(0)
        for r in range(count):

            @pl.when(step == r)
            def _(r=r):
                turned = x_refs[r][...].T
                value_out = mm(ga_refs[r][...].T, ctx_ref[0])
                for cut, part in zip(cuts, part_refs):
                    value = mm(turned, part[0])
                    sums = jnp.sum(part[0].astype(F32), 0, keepdims=True)
                    acc[:, cut] = value if r == 0 else acc[:, cut] + value
                    sum_ref[:, cut] = sums if r == 0 else sum_ref[:, cut] + sums
                acc_out[...] = value_out if r == 0 else acc_out[...] + value_out

        @pl.when(step == count - 1)
        def _():
            for r in range(4):
                for k in range(2):
                    row = ((scal_ref[S_Q] ^ r) * 2 + (scal_ref[S_ZH] ^ k)) * ROWS
                    rows = pl.ds(pl.multiple_of(row, ROWS), ROWS)
                    outs[r % 2][r // 2, k, :, :total] = acc[rows, :].astype(BF16)
                    outs[r % 2][r // 2, k, :, total:] = acc_out[rows, :].astype(BF16)

    shape = (2, 2, ROWS, total + out_width)
    return call(
        flow, body, (count,),
        [full((tokens, D))] * (2 * count) + [by_member((tokens, width))] * len(parts) + [by_member((tokens, out_width))],
        [full(shape)] * 2 + [full((1, total))], [sds(shape, BF16)] * 2 + [sds((1, total), F32)],
        [pltpu.VMEM((D, total), F32), pltpu.VMEM((D, out_width), F32)], [*xs, *gas, *parts, ctx], 0, 0, "heads_grad",
    )


def reach(ends_ref, row):
    first = jnp.zeros_like(row)
    for index in range(3):
        first = jnp.where(row >= ends_ref[index], ends_ref[index], first)
    last = jnp.full_like(row, SEQLEN)
    for index in (2, 1, 0):
        last = jnp.where(row < ends_ref[index], ends_ref[index], last)
    return jnp.maximum(first, row - (WINDOW - 1)), jnp.minimum(last, row + WINDOW)


def chunks_of(scal_ref, near_ref, far_ref):
    here = scal_ref[S_P] & 1
    for core in range(2):
        yield 2 * core + here, near_ref.at[core]
        yield 2 * core + 1 - here, far_ref.at[core]


def over_keys(ends_ref, start, chunk, keys_first, block):
    low_first, high_first = reach(ends_ref, start)
    low_last, high_last = reach(ends_ref, start + BQ - 1)
    axis = 1 if keys_first else 0
    low_row, high_row = reach(ends_ref, start + lax.broadcasted_iota(jnp.int32, (1, BQ) if keys_first else (BQ, 1), axis))
    shape = (chunk, BQ) if keys_first else (BQ, chunk)

    def one(b, carry):
        open_all = (b * chunk >= low_last) & ((b + 1) * chunk <= high_first)

        @pl.when(open_all)
        def _():
            block(b, None)

        @pl.when(jnp.logical_not(open_all))
        def _():
            key = b * chunk + lax.broadcasted_iota(jnp.int32, shape, 1 - axis)
            block(b, (key >= low_row) & (key < high_row))

        return carry

    lax.fori_loop(low_first // chunk, (high_last + chunk - 1) // chunk, one, 0)


def attend_forward(flow, ends, qkv):
    _, chunk, width3 = qkv[0].shape
    count = SEQLEN // chunk
    width = width3 // 3
    heads = width // HD
    steps = SEQLEN // BQ
    per = chunk // BQ

    def body(scal_ref, ends_ref, near_ref, far_ref, ctx_ref, wide_ref, lse_ref, qt, kh, vt, acc, tops, sums, scores):
        step = pl.program_id(0)

        @pl.when(step == 0)
        def _():
            for j, block in chunks_of(scal_ref, near_ref, far_ref):
                rows = pl.ds(pl.multiple_of(j * chunk, chunk), chunk)
                for pair in range(heads // 2):
                    base = 3 * PAIR * pair
                    part = slice(pair * PAIR, (pair + 1) * PAIR)
                    vt[j, part, :] = block[:, base + 2 * PAIR : base + 3 * PAIR].T
                    for s in range(per):
                        queries = block[s * BQ : (s + 1) * BQ, base : base + PAIR] * BF16(HD**-0.5)
                        qt[j * per + s, part, :] = queries.T
                    for h in range(2):
                        kh[2 * pair + h, rows, :] = block[:, base + PAIR + h * HD : base + PAIR + (h + 1) * HD]

        start = step * BQ
        acc[...] = jnp.zeros(acc.shape, F32)
        tops[...] = jnp.full(tops.shape, -3.0e38, F32)
        sums[...] = jnp.zeros(sums.shape, F32)

        def score(b, allowed):
            keys = pl.ds(pl.multiple_of(b * chunk, chunk), chunk)
            for h in range(heads):
                value = mm(kh[h, keys, :], qt[step, h * HD : (h + 1) * HD, :])
                if allowed is not None:
                    value = jnp.where(allowed, value, FILL)
                scores[h, b] = value
                tops[h] = jnp.maximum(tops[h], jnp.max(value.reshape(-1, 8, BQ), 0))

        over_keys(ends_ref, start, chunk, True, score)
        top = [jnp.max(tops[h], 0, keepdims=True) for h in range(heads)]

        def weigh(b, carry):
            for h in range(heads):
                part = slice(h * HD, (h + 1) * HD)
                weight = jnp.exp(scores[h, b] - top[h])
                sums[h] += fold_rows(weight)
                acc[part, :] += mm(vt[b, part, :], weight.astype(BF16))
            return carry

        low_first, _ = reach(ends_ref, start)
        _, high_last = reach(ends_ref, start + BQ - 1)
        lax.fori_loop(low_first // chunk, (high_last + chunk - 1) // chunk, weigh, 0)
        lse_ref[...] = jnp.zeros(lse_ref.shape, F32)
        for h in range(heads):
            part = slice(h * HD, (h + 1) * HD)
            total = jnp.sum(sums[h], 0, keepdims=True)
            acc[part, :] = acc[part, :] / total
            lse_ref[0, h : h + 1, :] = top[h] + jnp.log(total)
        wide = acc[...].T
        wide_ref[0] = wide
        ctx_ref[0] = wide.astype(BF16)

    row_block = lambda i, *_: (i // per, i % per, 0)
    return call(
        flow, body, (steps,), [full((2, chunk, width3))] * 2,
        [pl.BlockSpec((1, BQ, width), row_block), pl.BlockSpec((1, BQ, width), row_block),
         pl.BlockSpec((1, 8, BQ), lambda i, *_: (i, 0, 0))],
        [sds((count, chunk, width), BF16), sds((count, chunk, width), F32), sds((steps, 8, BQ), F32)],
        [
            pltpu.VMEM((steps, width, BQ), BF16),
            pltpu.VMEM((heads, SEQLEN, HD), BF16),
            pltpu.VMEM((count, width, chunk), BF16),
            pltpu.VMEM((width, BQ), F32),
            pltpu.VMEM((heads, 8, BQ), F32),
            pltpu.VMEM((heads, 8, BQ), F32),
            pltpu.VMEM((heads, count, chunk, BQ), F32),
        ],
        [*qkv], 0, 0, "attend_forward", (flow.scal, ends),
    )


def attend_backward(flow, ends, pair, qkv, grads, wide, lse):
    chunk = qkv[0].shape[1]
    count = SEQLEN // chunk
    steps = SEQLEN // BQ
    per = chunk // BQ

    def body(
        scal_ref, ends_ref, near_ref, far_ref, grad_near, grad_far, wide_ref, lse_ref, out_ref, qh, kh, gh, kt, vt, qt, gt,
        gq, gk, gv,
    ):
        step = pl.program_id(0)

        @pl.when(step == 0)
        def _():
            blocks = chunks_of(scal_ref, near_ref, far_ref)
            grad_blocks = chunks_of(scal_ref, grad_near, grad_far)
            for (j, block), (_, grad_block) in zip(blocks, grad_blocks):
                rows = pl.ds(pl.multiple_of(j * chunk, chunk), chunk)
                queries = block[:, :PAIR] * BF16(HD**-0.5)
                keys = block[:, PAIR : 2 * PAIR]
                back = grad_block[...]
                for h in range(2):
                    cols = slice(h * HD, (h + 1) * HD)
                    qh[h, rows, :] = queries[:, cols]
                    kh[h, rows, :] = keys[:, cols]
                    gh[h, rows, :] = back[:, cols]
                kt[j] = keys.T
                vt[j] = block[:, 2 * PAIR :].T
                for s in range(per):
                    sub = slice(s * BQ, (s + 1) * BQ)
                    qt[j * per + s] = queries[sub, :].T
                    gt[j * per + s] = back[sub, :].T
            gk[...] = jnp.zeros(gk.shape, F32)
            gv[...] = jnp.zeros(gv.shape, F32)

        start = step * BQ
        rows = pl.ds(pl.multiple_of(start, BQ), BQ)
        gq[...] = jnp.zeros(gq.shape, F32)
        sums = lse_ref[0].T
        inner, logs = [], []
        for h in range(2):
            product = gh[h, rows, :].astype(F32) * wide_ref[0, :, h * HD : (h + 1) * HD]
            inner.append(jnp.sum(product, 1, keepdims=True))
            logs.append(sums[:, 2 * pair + h : 2 * pair + h + 1])

        def block(b, allowed):
            keys = pl.ds(pl.multiple_of(b * chunk, chunk), chunk)
            for h in range(2):
                part = slice(h * HD, (h + 1) * HD)
                score = mm(qh[h, rows, :], kt[b, part, :])
                grad_weight = mm(gh[h, rows, :], vt[b, part, :])
                if allowed is not None:
                    score = jnp.where(allowed, score, FILL)
                weight = jnp.exp(score - logs[h])
                grad_score = (weight * (grad_weight - inner[h])).astype(BF16)
                gv[b, part, :] += mm(gt[step, part, :], weight.astype(BF16))
                gk[b, part, :] += mm(qt[step, part, :], grad_score)
                gq[h] += mm(grad_score, kh[h, keys, :])

        over_keys(ends_ref, start, chunk, False, block)
        place = pl.ds(pl.multiple_of((step % per) * BQ, BQ), BQ)
        for h in range(2):
            out_ref[step // per, place, h * HD : (h + 1) * HD] = (gq[h] * HD**-0.5).astype(BF16)

        @pl.when(step == steps - 1)
        def _():
            for j in range(count):
                out_ref[j, :, PAIR : 2 * PAIR] = gk[j].T.astype(BF16)
                out_ref[j, :, 2 * PAIR :] = gv[j].T.astype(BF16)

    out = (count, chunk, 3 * PAIR)
    return call(
        flow, body, (steps,),
        [pl.BlockSpec((2, chunk, 3 * PAIR), lambda i, *_: (0, 0, pair))] * 2
        + [pl.BlockSpec((2, chunk, PAIR), lambda i, *_: (0, 0, pair))] * 2
        + [pl.BlockSpec((1, BQ, PAIR), lambda i, *_: (i // per, i % per, pair)),
           pl.BlockSpec((1, 8, BQ), lambda i, *_: (i, 0, 0))],
        full(out), sds(out, BF16),
        [pltpu.VMEM((2, SEQLEN, HD), BF16)] * 3
        + [pltpu.VMEM((count, PAIR, chunk), BF16)] * 2
        + [pltpu.VMEM((steps, PAIR, BQ), BF16)] * 2
        + [pltpu.VMEM((2, BQ, HD), F32)]
        + [pltpu.VMEM((count, PAIR, chunk), F32)] * 2,
        [*qkv, *grads, wide, lse], 0, 0, "attend_backward", (flow.scal, ends),
    )


def flip(values_in, axes, mask):
    return lax.ppermute(values_in, axes, [(a, a ^ mask) for a in range(lax.axis_size(axes))])


def turn(values_in):
    return lax.ppermute(values_in, ("c", "zh"), [(2 * a + b, 2 * b + a) for a in range(2) for b in range(2)])


def uncross(values_in):
    return lax.ppermute(values_in, ("c", "zh"), [(2 * b + 1 - a, 2 * a + b) for a in range(2) for b in range(2)])


def from_members(values_in, axes):
    return [values_in] + [flip(values_in, axes, r) for r in range(1, lax.axis_size(axes))]


def to_members(parts, axes):
    return [parts[0]] + [flip(part, axes, r) for r, part in enumerate(parts) if r > 0]


def add(*parts):
    total = parts[0].astype(F32)
    for part in parts[1:]:
        total = total + part.astype(F32)
    return total


def is_small():
    return lax.axis_size("q") == 4


def order_by(values_in, axis, position, count):
    bit = 1
    while bit < count:
        shape = values_in.shape
        split = shape[:axis] + (count // (2 * bit), 2, bit) + shape[axis + 1 :]
        cut = values_in.reshape(split)
        values_in = jnp.where((position & bit) != 0, jnp.flip(cut, axis + 1), cut).reshape(shape)
        bit *= 2
    return values_in


def gather_group(values_in):
    across, sibling = flip(values_in, GROUP, 1), flip(values_in, GROUP, 2)
    return [values_in, across, sibling]


def forward(flow, members, *before):
    flow.wait(*before)
    flow.hold(across=members[1])
    gate(flow)
    members[1] = flow.free("across")
    members.append(flip(members[1], GROUP, 2))


def sum_group(keep, send):
    got = flip(send, GROUP, 2)
    passed = add(keep[1], got[1]).astype(BF16)
    return [keep[0], got, flip(passed, GROUP, 1)], passed


EXTRA = 16


def heads_shard_of(qkv, out, bias):
    rows = out.shape[0]
    paired = qkv.reshape(3, rows, -1, PAIR).transpose(1, 2, 0, 3).reshape(rows, -1)
    weights = jnp.concatenate([paired, out], axis=1)
    below = jnp.pad(bias.reshape(1, -1), ((0, EXTRA - 1), (0, weights.shape[1] - bias.size)))
    return jnp.concatenate([weights, below])


def heads_bias(rows, heads):
    bias = rows.reshape(rows.shape[0], 2, heads, -1).transpose(1, 2, 0, 3).reshape(2, -1).astype(F32)
    bias = jnp.stack([bias[0], jnp.zeros_like(bias[0]), bias[1]])
    return bias.reshape(3, -1, PAIR).transpose(1, 0, 2).reshape(1, -1)


def with_sibling(shard):
    return jnp.stack([shard, flip(shard, "c", 1)])


def heads_along_x(pair):
    return jnp.stack([pair, flip(pair, "q", 1)])


def heads_along_y(near, size, heads, where, zh):
    far = flip(near, "q", 2)
    rows = jnp.concatenate([near[:, :, ROWS, :size], far[:, :, ROWS, :size]])
    return [near, far], heads_bias(order_by(order_by(rows, 0, where[0], 4), 1, zh, 2).reshape(8, size), heads)


def all_heads_weight(shard, size, heads, zh):
    pair = turn(with_sibling(shard))
    every = order_by(lax.all_gather(pair, "q"), 1, zh, 2)
    count = shard.shape[0] - EXTRA
    weights = every[:, :, :count].reshape(4, 2, ROWS, -1)
    return [weights[:2], weights[2:]], heads_bias(every[:, :, count, :size].reshape(-1, size), heads)


class HeadsGrad:
    def __init__(self, keep, send):
        self.keep, self.send = keep, send

    def along_x(self):
        self.got = flip(self.send, "q", 1)
        return self.got

    def along_y(self):
        self.got_x = self.got
        self.got = flip(add(self.keep[1], self.got[1]).astype(BF16), "q", 2)
        return self.got

    def halves(self, zh):
        if is_small():
            return tuple(add(self.keep[0, k], self.got_x[0, k], self.got[k]).astype(BF16) for k in range(2))
        buckets = [self.keep[0], self.send[0], self.keep[1], self.send[1]]
        every = jnp.stack(buckets).reshape(lax.axis_size("q"), 2, -1, buckets[0].shape[-1])
        rows = order_by(lax.psum_scatter(every, "q", scatter_dimension=0, tiled=False), 0, zh, 2)
        return rows[0], rows[1]


SLOTS = (0, 2, 1, 3)


def all_units_weight(shard):
    matrices, _, width = shard.shape
    members = lax.axis_size(MODEL)
    every = lax.all_gather(shard, ALL).reshape(members, -1, matrices, shard.shape[1], width).transpose(0, 2, 1, 3, 4)
    every = every.reshape(members, matrices, 4, 2, ROWS, width)
    every = jnp.stack([every[slot] for slot in SLOTS])
    pieces = []
    for k in range(2):
        pieces += [every[:, :, r, k] for r in range(3)] + [every[:2, :, 3, k], every[2:, :, 3, k]]
    return pieces


class UnitsWeight:
    def __init__(self, shard):
        self.shard, self.theirs = shard, {}

    def start_far_z(self):
        self.other = flip(self.shard, "zh", 1)

    def join_far_z(self, shard):
        self.two = jnp.stack([shard, self.other])

    def far_z(self):
        self.start_far_z()
        self.join_far_z(self.shard)

    def start_z(self):
        self.other = flip(self.two, "zl", 1)

    def join_z(self, two):
        self.own = jnp.concatenate([two, self.other])

    def near_z(self):
        self.start_z()
        self.join_z(self.two)

    def near(self):
        self.near_x, self.near_y = flip(self.own, "q", 1), flip(self.own, "q", 2)

    def corner(self):
        self.far_a, self.far_b = flip(self.near_y[:2], "q", 1), flip(self.near_x[2:], "q", 2)

    def swap(self, *names):
        for name in names:
            self.theirs[name] = flip(getattr(self, name), "c", 1)

    def pieces(self):
        names = ("own", "near_x", "near_y", "far_a", "far_b")
        return [getattr(self, name) for name in names] + [self.theirs[name] for name in names]


class UnitsGrads:
    def __init__(self, flow, down, up, count):
        self.flow, self.down, self.up, self.count = flow, down, up, count

    def compute_theirs(self):
        self.theirs = unit_grads(self.flow, self.down, self.up, None, self.count, True)

    def send_theirs(self):
        self.got = flip(self.theirs, "c", 1) if is_small() else None

    def sibling(self):
        self.compute_theirs()
        self.send_theirs()

    def mine(self):
        self.made = unit_grads(self.flow, self.down, self.up, self.got, self.count, False)
        self.own, self.to_x, self.to_y, self.rest_x, self.rest_y = self.made

    def near(self):
        self.from_x, self.from_y = flip(self.to_x, "q", 1), flip(self.to_y, "q", 2)
        return [self.from_x, self.from_y]

    def far(self):
        half = self.count
        self.late_x = flip(add(self.rest_x, self.from_y[half:]).astype(BF16), "q", 1)
        self.late_y = flip(add(self.rest_y, self.from_x[half:]).astype(BF16), "q", 2)
        return [self.late_x, self.late_y]

    def near_z(self):
        half = self.count
        self.there = flip(add(self.own[half:], self.late_x, self.from_y[:half]).astype(BF16), "zl", 1)
        return [self.there]

    def far_z(self):
        self.last = flip(self.near_sum(slice(self.count // 2, self.count)).astype(BF16), "zh", 1)
        return [self.last]

    def near_sum(self, blocks):
        return add(self.own[blocks], self.from_x[blocks], self.late_y[blocks], self.there[blocks])

    def total(self):
        if is_small():
            return self.near_sum(slice(0, self.count // 2)) + self.last.astype(F32)
        half = self.count
        mine = jnp.stack(
            [self.own, jnp.concatenate([self.to_x[:half], self.rest_x]), jnp.concatenate([self.rest_y, self.to_y[:half]]),
             jnp.concatenate([self.to_x[half:], self.to_y[half:]])]
        ).reshape(4, self.count, 2, ROWS, -1)
        theirs = self.theirs.reshape(4, 2, self.count, ROWS, -1).transpose(0, 2, 1, 3, 4)
        every = jnp.stack([mine, theirs], axis=1)
        every = every.transpose(2, 0, 1, 4, 3, 5)
        every = jnp.stack([every[slot] for slot in SLOTS]).reshape(-1, 2, mine.shape[-1])
        return lax.psum_scatter(every, ALL, scatter_dimension=0, tiled=True).astype(F32).transpose(1, 0, 2)


SMALL_AXES = ("q", MODEL, "c")
SMALL_STEPS = (("q", 1), ("q", 2), ("zl", 1), ("zh", 1), ("c", 1))
SMALL_SHAPE = (128, 256)


def spread_by_distance(values_in, where):
    every = values_in.reshape(4, 4, 2, -1).transpose(1, 0, 2, 3)
    for axis, position in enumerate(where):
        every = order_by(every, axis, position, every.shape[axis])
    return every.transpose(2, 1, 0, 3).reshape(32, -1)


def fold_small(every, first, last):
    for axis, mask in SMALL_STEPS[::-1][first:last]:
        half = every.shape[0] // 2
        every = every[:half] + flip(every[half:], axis, mask)
    return every


def sum_all(value):
    if not is_small():
        return lax.psum(value, ALL)
    for axes in SMALL_AXES:
        parts = jnp.stack(from_members(value, axes))
        value = jnp.sum(order_by(parts, 0, lax.axis_index(axes), parts.shape[0]), 0)
    return value[0, 0]


def on_device(
    tokens, doc_lengths, qkv_weight, qv_bias, out_weight, up_weight, up_bias, down_weight, gains, shifts, cotangent
):
    layers = qkv_weight.shape[0]
    tz, dp = lax.axis_size(MODEL), lax.axis_size(("q", "c"))
    place, zh = lax.axis_index(GROUP), lax.axis_index("zh")
    where = (lax.axis_index("q"), lax.axis_index(MODEL), lax.axis_index("c"))
    if is_small():
        spots = [place, where[0], where[2], zh, where[1]]
    else:
        spots = [place] + [jnp.zeros((), jnp.int32)] * 4
    scal = jnp.stack([spot.astype(jnp.int32) for spot in spots])

    flow = Flow(scal)
    small_slice = is_small()
    qkv_cols, out_cols = 3 * out_weight.shape[2], out_weight.shape[2]
    in_cols, out_cols = slice(0, qkv_cols), slice(qkv_cols, qkv_cols + out_cols)
    hz, bias_size = qv_bias.shape[2], qv_bias.size // layers
    heads_shard = [heads_shard_of(qkv_weight[l], out_weight[l], qv_bias[l]) for l in range(layers)]
    pieces = [up_bias, gains, shifts]
    sizes = [piece.size // layers for piece in pieces]
    cuts = [0]
    for size in sizes:
        cuts.append(cuts[-1] + size)
    small = jnp.concatenate([piece.reshape(layers, -1) for piece in pieces], axis=1).reshape(-1)
    padded = jnp.pad(small, (0, SMALL_SHAPE[0] * SMALL_SHAPE[1] - small.size)).reshape(SMALL_SHAPE)
    gathered = lax.all_gather(padded, ALL)
    small_all = gathered.reshape(tz * dp, -1)[:, : small.size]

    def spread_small():
        every = small_all.reshape(tz, dp, layers, -1).astype(F32)
        parts = [every[..., cuts[i] : cuts[i + 1]] for i in range(3)]
        biases = parts[0].reshape(tz, dp, layers, up_bias.shape[1], -1).transpose(2, 0, 3, 1, 4)
        gain = parts[1].reshape(tz, dp, layers, 2, -1).transpose(2, 3, 1, 0, 4).reshape(layers, 2, D)
        shift = parts[2].reshape(tz, dp, layers, 4, -1).transpose(2, 3, 1, 0, 4).reshape(layers, 4, D)
        table = jnp.concatenate([gain, shift], axis=1).reshape(layers * 6, D)
        head = jnp.concatenate([jnp.ones((1, D), F32), jnp.zeros((1, D), F32)])
        return biases.reshape(layers, tz, 1, -1), jnp.pad(jnp.concatenate([head, table]), ((0, TABLE - 2 - 6 * layers), (0, 0)))

    up_bias_full, table = spread_small()
    if small_slice:
        pair = turn(with_sibling(heads_shard[0]))
        x_low = turn(tokens)
        ends = jnp.cumsum(turn(doc_lengths)[0], dtype=jnp.int32)
        near = heads_along_x(pair)
        up0, down0 = UnitsWeight(up_weight[0][None]), UnitsWeight(down_weight[0][None])
        both1 = UnitsWeight(jnp.stack([up_weight[1], down_weight[1]]))
        flow.hold(
            up0=up0.shard, down0=down0.shard, down0_twin=down0.shard, both1=both1.shard,
            heads1=with_sibling(heads_shard[1]), low=x_low,
        )
        gate(flow)
        x_low, up0.shard = flow.free("low"), flow.free("up0")
        up0.far_z()
        weights_of = [heads_along_y(near, bias_size, hz, where, zh)]
    else:
        x_low = turn(tokens)
        ends = jnp.cumsum(turn(doc_lengths)[0], dtype=jnp.int32)
        weights_of = [all_heads_weight(shard, bias_size, hz, zh) for shard in heads_shard]
        every = [all_units_weight(jnp.stack([up_weight[l], down_weight[l]])) for l in range(layers)]
        top_grad = turn(cotangent)

    prev, prev_gain, prev_shift = x_low, ONE, ZERO
    kept = []
    for l in range(layers):
        first, last = small_slice and l == 0, small_slice and l == 1
        xs = gather_group(x_low)
        w_heads, bias = weights_of[l]
        if first:
            flow.wait(up0.two)
            flow.hold(two=up0.two, two_twin=up0.two)
        qkv_near = project_in(flow, (xs[0], xs[2]), False, w_heads, in_cols, bias, "project_qkv")
        if first:
            up0.two, down0.shard = flow.free("two"), flow.free("down0")
            up0.start_z()
            down0.start_far_z()
        if last:
            flow.hold(top=cotangent, own=both1.own)
        forward(flow, xs, qkv_near)
        if last:
            both1.own = flow.free("own")
            both1.near()
        qkv_far = project_in(flow, (xs[1], xs[3]), True, w_heads, in_cols, bias, "project_qkv")
        qkv = (qkv_near, qkv_far)
        if first:
            down0.join_far_z(flow.free("down0_twin"))
            up0.join_z(flow.free("two_twin"))
            up0.near()
            down0.near_z()
            both1.shard = flow.free("both1")
            both1.far_z()
            pair = turn(flow.free("heads1"))
        if last:
            top_grad = turn(flow.free("top"))
            both1.swap("own")
        ctx, wide, lse = attend_forward(flow, ends, qkv)
        if first:
            flow.wait(up0.near_x, up0.near_y)
            flow.hold(both1=both1.two, down0=down0.own, pair=pair, pair_twin=pair)
            up0.corner()
            up0.swap("own", "near_x", "near_y")
        if last:
            flow.wait(both1.near_x, both1.near_y, top_grad)
            both1.corner()
            both1.swap("near_x", "near_y")
        send = project_out(flow, [ctx], (2, 3), w_heads, out_cols, True, "project_attn")
        flow.wait(send)
        keep = project_out(flow, [ctx], (0, 1), w_heads, out_cols, False, "project_attn")
        attn, passed = sum_group(keep, send)
        if first:
            flow.wait(passed, up0.far_a, up0.far_b, gathered)
            gate(flow)
            down0.own = flow.free("down0")
            up0.swap("far_a", "far_b")
            down0.near()
            down0.swap("own")
            flow.wait(down0.near_x, down0.near_y)
            down0.corner()
            down0.swap("near_x", "near_y")
            beside = flip(flow.free("pair"), "q", 1)
            w_up = up0.pieces(), 0
        elif last:
            flow.wait(passed)
            flow.hold(ends=ends)
            gate(flow)
            ends = flow.free("ends")
            flow.hold(far_a=both1.far_a, far_b=both1.far_b)
            flow.wait(attn[2])
            gate(flow)
            both1.far_a, both1.far_b = flow.free("far_a"), flow.free("far_b")
            both1.swap("far_a", "far_b")
            w_up, w_down = (both1.pieces(), 0), (both1.pieces(), 1)
        else:
            w_up, w_down = (every[l], 0), (every[l], 1)
        used = (prev_gain, prev_shift, shift_row(l, 0), gain_row(l, 0), shift_row(l, 1))
        n1, hs, r1, act, slope = norm_up(flow, prev, attn, table, used, *w_up, up_bias_full[l], tz)
        if first:
            flow.wait(n1, beside)
            flow.hold(far_a=down0.far_a, far_b=down0.far_b)
            gate(flow)
            down0.far_a, down0.far_b = flow.free("far_a"), flow.free("far_b")
            down0.swap("far_a", "far_b")
            both1.two = flow.free("both1")
            both1.near_z()
            near = jnp.stack([flow.free("pair_twin"), beside])
            weights_of.append(heads_along_y(near, bias_size, hz, where, zh))
            w_down = down0.pieces(), 0
        used = (gain_row(l, 0), shift_row(l, 1), shift_row(l, 2), gain_row(l, 1), shift_row(l, 3))
        n2, y_low, r2 = down_norm(flow, act, *w_down, n1, table, used, tz)
        kept.append((xs, qkv, ctx, wide, lse, n1, hs, r1, act, slope, n2, r2, w_heads, w_up, w_down))
        x_low, prev, prev_gain, prev_shift = y_low, n2, gain_row(l, 1), shift_row(l, 3)
    layer_output = turn(x_low)

    g2, gf, sums2 = norm_back(flow, top_grad, kept[-1][10], kept[-1][11], table, gain_row(layers - 1, 1))
    small_grads = [None] * layers
    units_of, heads_of = [None] * layers, [None] * layers
    above = above_heads = None
    for l in reversed(range(layers)):
        top = l == layers - 1
        xs, qkv, ctx, wide, lse, n1, hs, r1, act, slope, n2, r2, w_heads, w_up, w_down = kept[l]
        beside = small_slice and not top
        gu, up_bias_sum = units_back(flow, gf, *w_down, slope, tz)
        units = UnitsGrads(flow, (gf, act), (hs, gu), tz)
        if top:
            flow.hold(output=layer_output)
        else:
            if beside:
                flow.wait(*above.near())
                flow.hold(heads=above_heads.send)
            units.sibling()
            flow.wait(units.theirs)
            if beside:
                above_heads.send = flow.free("heads")
                above_heads.along_x()
                late = above.far()
        g1, ga, sums1 = up_back(flow, gu, *w_up, g2, n1, r1, table, gain_row(l, 0), tz)
        gas = gather_group(ga)
        flow.wait(ga)
        if top:
            layer_output = flow.free("output")
            units.compute_theirs()
            forward(flow, gas, units.theirs)
        else:
            units.mine()
            if beside:
                flow.wait(*late, above_heads.got)
            forward(flow, gas, *units.made)
        gc_near = project_in(flow, (gas[0], gas[2]), False, w_heads, out_cols, None, "project_gc")
        flow.wait(gc_near)
        if top:
            flow.hold(theirs=units.theirs)
        gc_far = project_in(flow, (gas[1], gas[3]), True, w_heads, out_cols, None, "project_gc")
        if top:
            units.theirs = flow.free("theirs")
            units.send_theirs()
        gcs = (gc_near, gc_far)
        if beside:
            flow.hold(rest_x=units.rest_x, rest_y=units.rest_y)
        gqkv = [attend_backward(flow, ends, 0, qkv, gcs, wide, lse)]
        if beside:
            units.rest_x, units.rest_y = flow.free("rest_x"), flow.free("rest_y")
        flow.wait(gqkv[0])
        if beside:
            flow.wait(*units.near(), *above.near_z(), above_heads.along_y())
            above.far_z()
            units.far()
            above_halves = above_heads.halves(zh)
            done = turn(above_halves[0]), uncross(above_halves[1])
            flow.hold(own=units.own)
        gqkv.append(attend_backward(flow, ends, 1, qkv, gcs, wide, lse))
        if beside:
            units.own = flow.free("own")
            flow.wait(units.late_x, units.late_y, above.last, *done)
            units.near_z()
        send = project_out(flow, gqkv, (2, 3), w_heads, in_cols, True, "project_gx")
        flow.wait(send)
        if beside:
            flow.hold(own=units.own)
        keep = project_out(flow, gqkv, (0, 1), w_heads, in_cols, False, "project_gx")
        back, passed = sum_group(keep, send)
        flow.wait(passed)
        if top:
            units.mine()
            flow.wait(*units.made)
        elif small_slice:
            units.own = flow.free("own")
            units.far_z()
        *buckets, qkv_sums = heads_grad(flow, xs, gqkv, gas, ctx)
        heads = HeadsGrad(*buckets)
        units_of[l], heads_of[l] = units, heads
        qv_sums = qkv_sums.reshape(-1, 3, PAIR).transpose(1, 0, 2).reshape(3, hz, dp, -1)
        qv_sums = jnp.stack([qv_sums[0], qv_sums[2]]).transpose(2, 0, 1, 3).reshape(1, dp, -1)
        mine = (jnp.arange(tz) == place).astype(F32).reshape(tz, 1, 1)
        small_grads[l] = jnp.concatenate(
            [
                mine * qv_sums,
                up_bias_sum.reshape(tz, up_bias.shape[1], dp, -1).transpose(0, 2, 1, 3).reshape(tz, dp, -1),
                jnp.stack([sums1[0], sums2[0]]).reshape(2, dp, tz, -1).transpose(2, 1, 0, 3).reshape(tz, dp, -1),
                jnp.stack([sums1[2], sums1[1], sums2[2], sums2[1]])
                .reshape(4, dp, tz, -1).transpose(2, 1, 0, 3).reshape(tz, dp, -1),
            ],
            axis=-1,
        )
        if l > 0:
            above, above_heads = units, heads
            flow.wait(heads.send)
            g2, gf, sums2 = sum_norm_back(flow, g1, back, kept[l - 1][10], kept[l - 1][11], table, gain_row(l - 1, 1))
    small_sums = jnp.stack(small_grads, axis=2).reshape(tz, dp, -1)
    if small_slice:
        heads.along_x()
        small_sums = fold_small(spread_by_distance(small_sums, where), 0, 1)
        flow.wait(back[2])
        flow.hold(small=small_sums, got=heads.got, own=units.own)
        gate(flow)
        small_sums, heads.got, units.own = flow.free("small"), flow.free("got"), flow.free("own")
        input_grad = turn(add(g1, back[0], back[1][0], back[2]).astype(BF16))
        heads.along_y()
        small_sums = fold_small(small_sums, 1, 2)
        flow.wait(heads.got)
        flow.hold(small=small_sums, own=units.own)
        gate(flow)
        units.own = flow.free("own")
        small_sums = fold_small(flow.free("small"), 2, 3)
        halves = heads.halves(zh)
        d_heads = jnp.stack([add(turn(halves[0]), uncross(halves[1])), add(*done)])
        small_out = fold_small(small_sums, 3, 5).reshape(layers, -1)
    else:
        halves = [member.halves(zh) for member in heads_of]
        d_heads = jnp.stack([add(turn(half[0]), uncross(half[1])) for half in halves])
        input_grad = turn(add(g1, back[0], back[1][0], back[2]).astype(BF16))
        small_out = lax.psum_scatter(small_sums.reshape(tz * dp, -1), ALL, scatter_dimension=0, tiled=True)
        small_out = small_out.reshape(layers, -1)
    qkv_grad = d_heads[:, :, : in_cols.stop].reshape(layers, d_heads.shape[1], -1, 3, PAIR)
    qkv_grad = qkv_grad.transpose(0, 3, 1, 2, 4).reshape(qkv_weight.shape)
    out_grad = d_heads[:, :, in_cols.stop :]
    totals = [member.total() for member in units_of]
    down_grad, up_grad = (jnp.stack([total[i] for total in totals]) for i in range(2))

    rest = small_out[:, bias_size:]
    qv_bias_grad = small_out[:, :bias_size].reshape(qv_bias.shape)
    up_bias_grad = rest[:, cuts[0] : cuts[1]].reshape(up_bias.shape)
    gains_grad = rest[:, cuts[1] : cuts[2]].reshape(gains.shape)
    shifts_grad = rest[:, cuts[2] : cuts[3]].reshape(shifts.shape)
    all_grads = (qkv_grad, qv_bias_grad, out_grad, up_grad, up_bias_grad, down_grad, gains_grad, shifts_grad)
    local_squares = sum(jnp.sum(member * member) for member in all_grads)
    entry_count = LAYERS * (4 * D * D + 2 * D * FF + FF + 8 * D)
    if small_slice:
        flow.hold(squares=jnp.broadcast_to(local_squares, (8, 128)), grad=input_grad, output=layer_output)
        flow.hold(**{f"out{i}": member for i, member in enumerate(all_grads)})
        gate(flow)
        local_squares, input_grad, layer_output = flow.free("squares"), flow.free("grad"), flow.free("output")
        all_grads = [flow.free(f"out{i}") for i in range(len(all_grads))]
    grad_rms = jnp.sqrt(sum_all(local_squares) / entry_count)
    return (layer_output, input_grad, *all_grads, grad_rms)


def solution(mesh):
    dp, tensor = mesh.shape["dp"], mesh.shape["tensor"]
    fine = Mesh(mesh.devices.reshape(dp // 2, 2, 2, tensor // 2), ("q", "c", "zh", "zl"))
    data, model = ("q", "c"), ("zh", "zl")
    both = data + model
    weight3, weight4 = P(None, data, model), P(None, None, data, model)
    in_specs = (
        P(both, None), P(data, None), weight4, P(None, None, model, data), weight3, weight3, P(None, model, data),
        weight3, P(None, None, both), P(None, None, both), P(both, None),
    )
    out_specs = (
        P(both, None), P(both, None), weight4, P(None, None, model, data), weight3, weight3, P(None, model, data),
        weight3, P(None, None, both), P(None, None, both), P(),
    )
    return jax.shard_map(on_device, mesh=fine, in_specs=in_specs, out_specs=out_specs, check_vma=False)
```

```python
import jax
import jax.numpy as jnp
from jax import lax
from jax.experimental import pallas as pl
from jax.experimental.pallas import tpu as pltpu
from jax.sharding import Mesh
from jax.sharding import PartitionSpec as P

D = 1024
HD = 64
HEADS = 16
FF = 4096
LAYERS = 2
SEQLEN = 2048
WINDOW = 1024
EPS = 1e-06
FILL = -1000000000.0

F32 = jnp.float32
BF16 = jnp.bfloat16
GROUP = ("c", "zl")
MODEL = ("zh", "zl")
ALL = ("zh", "zl", "q", "c")
VMEM_LIMIT = 56 * 1024 * 1024
TIMES = {
    "gate": 0.1, "norm_up": 20.0, "down_norm": 20.0, "units_back": 45.0, "up_back": 20.0, "norm_back": 6.0,
    "sum_norm_back": 20.0, "grads_theirs": 0.2, "grads_mine": 0.2, "project_qkv": 0.2, "project_gc": 0.2,
    "project_attn": 0.2, "project_gx": 0.2, "heads_grad": 0.2, "attend_forward": 40.0, "attend_backward": 30.0,
}
PEAK = 0.35e9
NT = (((1,), (1,)), ((), ()))
NN = (((1,), (0,)), ((), ()))
ROWS = 128
CHUNK = 64
BQ = 512
PAIR = 2 * HD


def mm(left, right, dims=NN):
    return lax.dot_general(left, right, dims, preferred_element_type=F32)


def full(shape):
    return pl.BlockSpec(shape, lambda *_: (0,) * len(shape))


ANY = pl.BlockSpec(memory_space=pl.ANY)


def sds(shape, kind):
    return jax.ShapeDtypeStruct(shape, kind)


class Flow:
    def __init__(self, scal):
        self.scal, self.before, self.held = scal, [], {}

    def wait(self, *arrays):
        self.before += arrays

    def hold(self, **arrays):
        self.held.update(arrays)

    def free(self, name):
        return self.held.pop(name)


def call(flow, body, grid, in_specs, out_specs, out_shape, scratch, args, flops, traffic, name, scalars=None):
    scalars = (flow.scal,) if scalars is None else scalars
    single = not isinstance(out_specs, (list, tuple))
    out_specs = [out_specs] if single else list(out_specs)
    out_shape = [out_shape] if single else list(out_shape)
    before, held = flow.before, list(flow.held.items())
    ns, nb, nh, no = len(scalars), len(before), len(held), len(out_specs)
    first, last = ns + nb + nh, ns + nb + nh + len(args) + no

    def wrapped(*refs):
        body(*refs[:ns], *refs[first:last], *refs[last + nh :])

    result = pl.pallas_call(
        wrapped,
        grid_spec=pltpu.PrefetchScalarGridSpec(
            num_scalar_prefetch=ns,
            grid=grid,
            in_specs=[ANY] * (nb + nh) + list(in_specs),
            out_specs=out_specs + [ANY] * nh,
            scratch_shapes=scratch,
        ),
        out_shape=out_shape + [sds(array.shape, array.dtype) for _, array in held],
        input_output_aliases={ns + nb + i: no + i for i in range(nh)},
        compiler_params=pltpu.CompilerParams(
            dimension_semantics=("arbitrary",) * len(grid), vmem_limit_bytes=VMEM_LIMIT
        ),
        cost_estimate=pl.CostEstimate(flops=int(TIMES[name] * PEAK), bytes_accessed=1024, transcendentals=0),
        name=name,
    )(*scalars, *before, *[array for _, array in held], *args)
    flow.before = []
    flow.held = {key: value for (key, _), value in zip(held, result[no:])}
    return result[0] if single else result[:no]


def gate(flow):
    if flow.held:
        call(flow, lambda *refs: None, (1,), [], [], [], [], [], 0, 0, "gate")


S_P, S_Q, S_C, S_ZH, S_Z = range(5)


def norm_rows(values_in):
    centred = values_in - jnp.mean(values_in, -1, keepdims=True)
    variance = jnp.mean(centred * centred, -1, keepdims=True)
    inverse = lax.rsqrt(variance + EPS)
    return centred * inverse, inverse


def norm_back_rows(grad, normed, inverse, gain):
    scaled = grad * gain
    centred = scaled - jnp.mean(scaled, -1, keepdims=True) - normed * jnp.mean(scaled * normed, -1, keepdims=True)
    return centred * inverse


def fold_rows(values_in):
    return jnp.sum(values_in.reshape(-1, 8, values_in.shape[-1]), 0)


def read(part, rows):
    return (part[0, rows, :] if len(part.shape) == 3 else part[rows, :]).astype(F32)


def part_spec(part):
    shape = part.shape
    return full(shape) if len(shape) == 2 else pl.BlockSpec((1,) + shape[1:], lambda *_: (0, 0, 0))


ONE, ZERO, TABLE = 0, 1, 16


def gain_row(layer, index):
    return 2 + 6 * layer + index


def shift_row(layer, index):
    return 4 + 6 * layer + index


def row_of(vec_ref, row):
    return vec_ref[row : row + 1, :]


def norm_forward(get_total, tokens, vec, gain, shift, n_ref, low_ref, inv_ref):

    def step(index, carry):
        rows = pl.ds(pl.multiple_of(index * CHUNK, CHUNK), CHUNK)
        normed, inverse = norm_rows(get_total(rows))
        n_ref[rows, :] = normed
        low_ref[rows, :] = (normed * row_of(vec, gain) + row_of(vec, shift)).astype(BF16)
        inv_ref[rows, :] = jnp.broadcast_to(inverse, (CHUNK, 128))
        return carry

    lax.fori_loop(0, tokens // CHUNK, step, 0)


def norm_backward(get_grad, tokens, n_ref, inv_ref, vec, gain, g_ref, low_ref, sums_ref):
    def step(index, carry):
        rows = pl.ds(pl.multiple_of(index * CHUNK, CHUNK), CHUNK)
        grad = get_grad(rows)
        normed = n_ref[rows, :]
        result = norm_back_rows(grad, normed, inv_ref[rows, 0:1], row_of(vec, gain))
        low = result.astype(BF16)
        g_ref[rows, :] = result
        low_ref[rows, :] = low
        return (
            carry[0] + fold_rows(grad * normed),
            carry[1] + fold_rows(grad),
            carry[2] + fold_rows(low.astype(F32)),
        )

    zero = jnp.zeros((8, D), F32)
    sums = lax.fori_loop(0, tokens // CHUNK, step, (zero, zero, zero))
    sums_ref[...] = jnp.zeros(sums_ref.shape, F32)
    for row, member in enumerate(sums):
        sums_ref[row : row + 1, :] = jnp.sum(member, 0, keepdims=True)


def away(s):
    return (s & 1) * 2 + s // 2


class Streamed:
    def __init__(self, refs, matrix, buffer, sems, scal):
        self.refs, self.matrix, self.buffer, self.sems, self.scal = refs, matrix, buffer, sems, scal

    def copies(self, s):
        slot = lax.rem(s, 2)
        plain, early, late = [], [], []
        for k in range(2):
            own, near_x, near_y, far_a, far_b = self.refs[5 * k : 5 * k + 5]

            def copy(source, r, k=k):
                row = ((self.scal[S_Q] ^ r) * 2 + (self.scal[S_C] ^ k)) * ROWS
                return pltpu.make_async_copy(
                    source, self.buffer.at[slot, pl.ds(pl.multiple_of(row, ROWS), ROWS), :], self.sems.at[slot, 4 * k + r]
                )

            for r, ref in enumerate((own, near_x, near_y)):
                plain.append(copy(ref.at[s, self.matrix], r))
            early.append(copy(far_a.at[jnp.minimum(s, 1), self.matrix], 3))
            late.append(copy(far_b.at[jnp.maximum(s - 2, 0), self.matrix], 3))
        return plain, early, late

    def each(self, s, act):
        plain, early, late = self.copies(s)
        for copy in plain:
            act(copy)

        @pl.when(s < 2)
        def _():
            for copy in early:
                act(copy)

        @pl.when(s >= 2)
        def _():
            for copy in late:
                act(copy)

    def start(self, s):
        self.each(s, lambda copy: copy.start())

    def wait(self, s):
        self.each(s, lambda copy: copy.wait())

    def turn(self, s, count):
        @pl.when(s == 0)
        def _():
            self.start(s)

        @pl.when(s + 1 < count)
        def _():
            self.start(s + 1)


def piece_shapes(width):
    return [pltpu.VMEM((2, D, width), BF16), pltpu.SemaphoreType.DMA((2, 8))]


def gelu_parts(u):
    size = jnp.abs(u)
    t = 1.0 / (1.0 + 0.2316419 * size)
    poly = t * (0.127414796 + t * (-0.142248368 + t * (0.7107068705 + t * (-0.7265760135 + t * 0.5307027145))))
    bell = jnp.exp(-0.5 * (u * u))
    tail = poly * bell
    cdf = jnp.where(u >= 0, 1.0 - tail, tail)
    return u * cdf, cdf + u * (0.3989422804014327 * bell)


def tiles(tokens, width):
    for i in range(2):
        for j in range(2):
            yield slice(i * tokens // 2, (i + 1) * tokens // 2), slice(j * width // 2, (j + 1) * width // 2)


def norm_up(flow, prev, parts, vec, rows_used, weight, matrix, bias, count):
    tokens = prev.shape[0]
    width = FF // count

    def body(scal_ref, prev_ref, *refs):
        part_refs, refs = refs[: len(parts)], refs[len(parts) :]
        vec_ref, bias_ref, refs = refs[0], refs[1], refs[2:]
        pieces, (n_ref, low_ref, inv_ref, act_ref, slope_ref, buffer, sems) = refs[:10], refs[10:]
        s = pl.program_id(0)
        stream = Streamed(pieces, matrix, buffer, sems, scal_ref)
        stream.turn(s, count)

        @pl.when(s == 0)
        def _():
            def total(rows):
                attn = read(part_refs[0], rows)
                for part in part_refs[1:]:
                    attn = attn + read(part, rows)
                before = read(prev_ref, rows) * row_of(vec_ref, rows_used[0]) + row_of(vec_ref, rows_used[1])
                return before + (attn + row_of(vec_ref, rows_used[2]))

            norm_forward(total, tokens, vec_ref, *rows_used[3:], n_ref, low_ref, inv_ref)

        stream.wait(s)
        slot = lax.rem(s, 2)
        for rows, cols in tiles(tokens, width):
            act, slope = gelu_parts(mm(low_ref[rows, :], buffer[slot, :, cols]) + bias_ref[0, :, cols])
            act_ref[rows, cols] = act.astype(BF16)
            slope_ref[rows, cols] = slope.astype(BF16)

    column = pl.BlockSpec((tokens, width), lambda s, _: (0, s))
    return call(
        flow, body, (count,),
        [full((tokens, D))] + [part_spec(part) for part in parts]
        + [full((TABLE, D)), pl.BlockSpec((1, 1, width), lambda s, scal_ref: (scal_ref[S_Z] ^ away(s), 0, 0))] + [ANY] * 10,
        [full((tokens, D)), full((tokens, D)), full((tokens, 128)), column, column],
        [sds((tokens, D), F32), sds((tokens, D), BF16), sds((tokens, 128), F32)] + [sds((tokens, FF), BF16)] * 2,
        piece_shapes(width), [prev, *parts, vec, bias, *weight], 2 * tokens * D * FF,
        2 * (D * FF + tokens * (10 * D + 2 * FF)), "norm_up",
    )


def down_norm(flow, act, weight, matrix, prev, vec, rows_used, count):
    tokens = prev.shape[0]
    width = FF // count

    def body(scal_ref, act_ref, prev_ref, vec_ref, *refs):
        pieces, (n_ref, low_ref, inv_ref, buffer, sems, acc) = refs[:10], refs[10:]
        s = pl.program_id(0)
        stream = Streamed(pieces, matrix, buffer, sems, scal_ref)
        stream.turn(s, count)
        stream.wait(s)
        value = mm(act_ref[...], buffer[lax.rem(s, 2)], NT)

        @pl.when(s == 0)
        def _():
            acc[...] = value

        @pl.when(s > 0)
        def _():
            acc[...] += value

        @pl.when(s == count - 1)
        def _():
            def total(rows):
                before = prev_ref[rows, :] * row_of(vec_ref, rows_used[0]) + row_of(vec_ref, rows_used[1])
                return before + (acc[rows, :] + row_of(vec_ref, rows_used[2]))

            norm_forward(total, tokens, vec_ref, *rows_used[3:], n_ref, low_ref, inv_ref)

    return call(
        flow, body, (count,),
        [pl.BlockSpec((tokens, width), lambda s, _: (0, s)), full((tokens, D)), full((TABLE, D))] + [ANY] * 10,
        [full((tokens, D)), full((tokens, D)), full((tokens, 128))],
        [sds((tokens, D), F32), sds((tokens, D), BF16), sds((tokens, 128), F32)],
        piece_shapes(width) + [pltpu.VMEM((tokens, D), F32)], [act, prev, vec, *weight], 2 * tokens * D * FF,
        2 * (D * FF + tokens * (5 * D + FF)), "down_norm",
    )


def units_back(flow, residual, parts, normed, inverse, vec, gain, weight, matrix, slope, count):
    tokens = residual.shape[0]
    width = FF // count

    def body(scal_ref, res_ref, *refs):
        part_refs, refs = refs[: len(parts)], refs[len(parts) :]
        n_ref, inv_ref, vec_ref, slope_ref, refs = refs[0], refs[1], refs[2], refs[3], refs[4:]
        pieces, (g_ref, low_ref, sums_ref, out_ref, sum_ref, buffer, sems) = refs[:10], refs[10:]
        s = pl.program_id(0)
        stream = Streamed(pieces, matrix, buffer, sems, scal_ref)
        stream.turn(s, count)

        @pl.when(s == 0)
        def _():
            def grad(rows):
                total = read(res_ref, rows)
                for part in part_refs:
                    total = total + read(part, rows)
                return total

            norm_backward(grad, tokens, n_ref, inv_ref, vec_ref, gain, g_ref, low_ref, sums_ref)

        stream.wait(s)
        slot = lax.rem(s, 2)
        sums = {}
        for rows, cols in tiles(tokens, width):
            low = (mm(low_ref[rows, :], buffer[slot, :, cols]) * slope_ref[rows, cols].astype(F32)).astype(BF16)
            out_ref[rows, cols] = low
            part = fold_rows(low.astype(F32))
            sums[cols.start] = sums[cols.start] + part if cols.start in sums else part
            if rows.start > 0:
                sum_ref[0, :, cols] = jnp.sum(sums[cols.start], 0, keepdims=True)

    column = pl.BlockSpec((tokens, width), lambda s, _: (0, s))
    return call(
        flow, body, (count,),
        [full((tokens, D))] + [part_spec(part) for part in parts]
        + [full((tokens, D)), full((tokens, 128)), full((TABLE, D)), column] + [ANY] * 10,
        [full((tokens, D)), full((tokens, D)), full((8, D)), column,
         pl.BlockSpec((1, 1, width), lambda s, scal_ref: (scal_ref[S_Z] ^ away(s), 0, 0))],
        [sds((tokens, D), F32), sds((tokens, D), BF16), sds((8, D), F32), sds((tokens, FF), BF16),
         sds((count, 1, width), F32)],
        piece_shapes(width), [residual, *parts, normed, inverse, vec, slope, *weight], 0, 0, "units_back",
    )


def up_back(flow, gu, weight, matrix, residual, normed, inverse, vec, gain, count):
    tokens = residual.shape[0]
    width = FF // count

    def body(scal_ref, gu_ref, res_ref, n_ref, inv_ref, vec_ref, *refs):
        pieces, (g_ref, low_ref, sums_ref, buffer, sems, acc) = refs[:10], refs[10:]
        s = pl.program_id(0)
        stream = Streamed(pieces, matrix, buffer, sems, scal_ref)
        stream.turn(s, count)
        stream.wait(s)
        value = mm(gu_ref[...], buffer[lax.rem(s, 2)], NT)

        @pl.when(s == 0)
        def _():
            acc[...] = value

        @pl.when(s > 0)
        def _():
            acc[...] += value

        @pl.when(s == count - 1)
        def _():
            norm_backward(
                lambda rows: res_ref[rows, :] + acc[rows, :], tokens, n_ref, inv_ref, vec_ref, gain, g_ref, low_ref,
                sums_ref,
            )

    return call(
        flow, body, (count,),
        [pl.BlockSpec((tokens, width), lambda s, _: (0, s)), full((tokens, D)), full((tokens, D)), full((tokens, 128)),
         full((TABLE, D))] + [ANY] * 10,
        [full((tokens, D)), full((tokens, D)), full((8, D))],
        [sds((tokens, D), F32), sds((tokens, D), BF16), sds((8, D), F32)],
        piece_shapes(width) + [pltpu.VMEM((tokens, D), F32)], [gu, residual, normed, inverse, vec, *weight],
        2 * tokens * D * FF, 2 * (D * FF + tokens * (8 * D + FF)), "up_back",
    )


def turn_rows(scal_ref, x_ref, turned, core):
    for r in range(4):
        row = ((scal_ref[S_Q] ^ r) * 2 + core) * ROWS
        turned[r * ROWS : (r + 1) * ROWS, :] = x_ref[:, pl.ds(pl.multiple_of(row, ROWS), ROWS)].T


def unit_grads(flow, down, up, received, count, sibling):
    tokens = down[0].shape[0]
    width = down[1].shape[1] // count
    half = count // 2
    steps = 2 * count

    def body(scal_ref, x0_ref, y0_ref, x1_ref, y1_ref, *refs):
        turned, t = refs[-1], pl.program_id(0)
        m, s = t // count, lax.rem(t, count)
        core = scal_ref[S_C] ^ 1 if sibling else scal_ref[S_C]

        @pl.when(t == 0)
        def _():
            turn_rows(scal_ref, x0_ref, turned, core)

        @pl.when(t == count)
        def _():
            turn_rows(scal_ref, x1_ref, turned, core)

        def store(y_ref):
            value = mm(turned[...], y_ref[...]).reshape(4, ROWS, width)
            if sibling:
                refs[0][:, 0] = value.astype(BF16)
                return
            if received is not None:
                value = value + refs[0][:, 0].astype(F32)
            value = value.astype(BF16)
            own, to_x, to_y, rest_x, rest_y = refs[-6:-1]
            spot = lax.rem(s, half) * 2 + m
            own[s // half * count + spot] = value[0]

            @pl.when(s < half)
            def _():
                to_x[spot] = value[1]
                to_x[count + spot] = value[3]
                rest_y[spot] = value[2]

            @pl.when(s >= half)
            def _():
                rest_x[spot] = value[1]
                to_y[spot] = value[2]
                to_y[count + spot] = value[3]

        @pl.when(m == 0)
        def _():
            store(y0_ref)

        @pl.when(m == 1)
        def _():
            store(y1_ref)

    left = full((tokens, D))
    pick_down = lambda t, _: (0, jnp.minimum(t, count - 1))
    pick_up = lambda t, _: (0, jnp.maximum(t - count, 0))
    specs = [left, pl.BlockSpec((tokens, width), pick_down), left, pl.BlockSpec((tokens, width), pick_up)]
    args = [*down, *up]
    one = pl.BlockSpec((4, 1, ROWS, width), lambda t, _: (0, t, 0, 0))
    if sibling:
        out_specs, out_shape = one, sds((4, steps, ROWS, width), BF16)
    else:
        if received is not None:
            specs.append(one)
            args.append(received)
        shapes = [(steps, ROWS, width)] * 3 + [(count, ROWS, width)] * 2
        out_specs, out_shape = [full(shape) for shape in shapes], [sds(shape, BF16) for shape in shapes]
    return call(
        flow, body, (steps,), specs, out_specs, out_shape, [pltpu.VMEM((4 * ROWS, tokens), BF16)], args,
        0, 0, "grads_theirs" if sibling else "grads_mine",
    )


def fetch_heads_weight(scal_ref, pieces, cols, buffer, sems):
    copies = []
    for r in range(4):
        for k in range(2):
            row = ((scal_ref[S_Q] ^ r) * 2 + (scal_ref[S_ZH] ^ k)) * ROWS
            copies.append(
                pltpu.make_async_copy(
                    pieces[r // 2].at[r % 2, k, pl.ds(0, ROWS), cols], buffer.at[pl.ds(pl.multiple_of(row, ROWS), ROWS), :],
                    sems.at[2 * r + k],
                )
            )
    for copy in copies:
        copy.start()
    for copy in copies:
        copy.wait()


def by_member(shape):
    return pl.BlockSpec((1,) + shape, lambda r, scal_ref: (scal_ref[S_P] ^ r, 0, 0))


def heads_weight_scratch(width):
    return [pltpu.VMEM((D, width), BF16), pltpu.SemaphoreType.DMA((8,))]


def project_in(flow, lefts, across, weight, cols, bias, name):
    tokens = lefts[0].shape[0]
    width = cols.stop - cols.start

    def body(scal_ref, left_ref, right_ref, *refs):
        if bias is not None:
            bias_ref, refs = refs[0], refs[1:]
        pieces, (out_ref, buffer, sems) = refs[:2], refs[2:]
        step = pl.program_id(0)

        @pl.when(step == 0)
        def _():
            fetch_heads_weight(scal_ref, pieces, cols, buffer, sems)

        for r, left in enumerate((left_ref, right_ref)):

            @pl.when(step == r)
            def _(left=left):
                value = mm(left[...], buffer[...])
                if bias is not None:
                    value = value + bias_ref[...]
                out_ref[0] = value.astype(BF16)

    extra, extra_specs = ([], []) if bias is None else ([bias], [full((1, width))])
    return call(
        flow, body, (2,), [full((tokens, D))] * 2 + extra_specs + [ANY] * 2,
        pl.BlockSpec((1, tokens, width), lambda r, scal_ref: ((scal_ref[S_P] >> 1) ^ r, 0, 0)),
        sds((2, tokens, width), BF16), heads_weight_scratch(width), [*lefts, *extra, *weight], 0, 0, name,
    )


def project_out(flow, blocks, members, weight, cols, stacked, name):
    count, tokens, width = blocks[0].shape

    def body(scal_ref, *refs):
        block_refs, refs = refs[: len(blocks)], refs[len(blocks) :]
        pieces, outs, (buffer, sems) = refs[:2], refs[2:-2], refs[-2:]
        step = pl.program_id(0)

        @pl.when(step == 0)
        def _():
            fetch_heads_weight(scal_ref, pieces, cols, buffer, sems)

        value = mm(block_refs[0][0], buffer[:, :width], NT)
        for index in range(1, len(blocks)):
            value = value + mm(block_refs[index][0], buffer[:, index * width : (index + 1) * width], NT)
        value = value.astype(BF16)
        if stacked:
            outs[0][0] = value
            return
        for r, out in enumerate(outs):

            @pl.when(step == r)
            def _(out=out):
                out[...] = value

    first, last = members
    pick = lambda r, scal_ref: (scal_ref[S_P] ^ (first + r * (last - first)), 0, 0)
    if stacked:
        out_specs, out_shape = pl.BlockSpec((1, tokens, D), lambda r, _: (r, 0, 0)), sds((2, tokens, D), BF16)
    else:
        out_specs, out_shape = [full((tokens, D))] * 2, [sds((tokens, D), BF16)] * 2
    return call(
        flow, body, (2,), [pl.BlockSpec((1, tokens, width), pick)] * len(blocks) + [ANY] * 2, out_specs, out_shape,
        heads_weight_scratch(width * len(blocks)), [*blocks, *weight], 0, 0, name,
    )


def heads_grad(flow, xs, parts, gas, ctx):
    count, tokens, width = parts[0].shape
    out_width = ctx.shape[2]
    cuts = [slice(i * width, (i + 1) * width) for i in range(len(parts))]
    total = width * len(parts)

    def body(scal_ref, *refs):
        x_refs, refs = refs[:count], refs[count:]
        ga_refs, refs = refs[:count], refs[count:]
        part_refs, refs = refs[: len(parts)], refs[len(parts) :]
        ctx_ref, outs, (sum_ref, acc, acc_out) = refs[0], refs[1:3], refs[3:]
        step = pl.program_id(0)
        for r in range(count):

            @pl.when(step == r)
            def _(r=r):
                turned = x_refs[r][...].T
                value_out = mm(ga_refs[r][...].T, ctx_ref[0])
                for cut, part in zip(cuts, part_refs):
                    value = mm(turned, part[0])
                    sums = jnp.sum(part[0].astype(F32), 0, keepdims=True)
                    acc[:, cut] = value if r == 0 else acc[:, cut] + value
                    sum_ref[:, cut] = sums if r == 0 else sum_ref[:, cut] + sums
                acc_out[...] = value_out if r == 0 else acc_out[...] + value_out

        @pl.when(step == count - 1)
        def _():
            for r in range(4):
                for k in range(2):
                    row = ((scal_ref[S_Q] ^ r) * 2 + (scal_ref[S_ZH] ^ k)) * ROWS
                    rows = pl.ds(pl.multiple_of(row, ROWS), ROWS)
                    outs[r % 2][r // 2, k, :, :total] = acc[rows, :].astype(BF16)
                    outs[r % 2][r // 2, k, :, total:] = acc_out[rows, :].astype(BF16)

    shape = (2, 2, ROWS, total + out_width)
    return call(
        flow, body, (count,),
        [full((tokens, D))] * (2 * count) + [by_member((tokens, width))] * len(parts) + [by_member((tokens, out_width))],
        [full(shape)] * 2 + [full((1, total))], [sds(shape, BF16)] * 2 + [sds((1, total), F32)],
        [pltpu.VMEM((D, total), F32), pltpu.VMEM((D, out_width), F32)], [*xs, *gas, *parts, ctx], 0, 0, "heads_grad",
    )


def reach(ends_ref, row):
    first = jnp.zeros_like(row)
    for index in range(3):
        first = jnp.where(row >= ends_ref[index], ends_ref[index], first)
    last = jnp.full_like(row, SEQLEN)
    for index in (2, 1, 0):
        last = jnp.where(row < ends_ref[index], ends_ref[index], last)
    return jnp.maximum(first, row - (WINDOW - 1)), jnp.minimum(last, row + WINDOW)


def chunks_of(scal_ref, near_ref, far_ref):
    here = scal_ref[S_P] & 1
    for core in range(2):
        yield 2 * core + here, near_ref.at[core]
        yield 2 * core + 1 - here, far_ref.at[core]


def over_keys(ends_ref, start, chunk, keys_first, block):
    low_first, high_first = reach(ends_ref, start)
    low_last, high_last = reach(ends_ref, start + BQ - 1)
    axis = 1 if keys_first else 0
    low_row, high_row = reach(ends_ref, start + lax.broadcasted_iota(jnp.int32, (1, BQ) if keys_first else (BQ, 1), axis))
    shape = (chunk, BQ) if keys_first else (BQ, chunk)

    def one(b, carry):
        open_all = (b * chunk >= low_last) & ((b + 1) * chunk <= high_first)

        @pl.when(open_all)
        def _():
            block(b, None)

        @pl.when(jnp.logical_not(open_all))
        def _():
            key = b * chunk + lax.broadcasted_iota(jnp.int32, shape, 1 - axis)
            block(b, (key >= low_row) & (key < high_row))

        return carry

    lax.fori_loop(low_first // chunk, (high_last + chunk - 1) // chunk, one, 0)


def attend_forward(flow, ends, qkv):
    _, chunk, width3 = qkv[0].shape
    count = SEQLEN // chunk
    width = width3 // 3
    heads = width // HD
    steps = SEQLEN // BQ
    per = chunk // BQ

    def body(scal_ref, ends_ref, near_ref, far_ref, ctx_ref, wide_ref, lse_ref, qt, kh, vt, acc, tops, sums, scores):
        step = pl.program_id(0)

        @pl.when(step == 0)
        def _():
            for j, block in chunks_of(scal_ref, near_ref, far_ref):
                rows = pl.ds(pl.multiple_of(j * chunk, chunk), chunk)
                for pair in range(heads // 2):
                    base = 3 * PAIR * pair
                    part = slice(pair * PAIR, (pair + 1) * PAIR)
                    vt[j, part, :] = block[:, base + 2 * PAIR : base + 3 * PAIR].T
                    for s in range(per):
                        queries = block[s * BQ : (s + 1) * BQ, base : base + PAIR] * BF16(HD**-0.5)
                        qt[j * per + s, part, :] = queries.T
                    for h in range(2):
                        kh[2 * pair + h, rows, :] = block[:, base + PAIR + h * HD : base + PAIR + (h + 1) * HD]

        start = step * BQ
        acc[...] = jnp.zeros(acc.shape, F32)
        tops[...] = jnp.full(tops.shape, -3.0e38, F32)
        sums[...] = jnp.zeros(sums.shape, F32)

        def score(b, allowed):
            keys = pl.ds(pl.multiple_of(b * chunk, chunk), chunk)
            for h in range(heads):
                value = mm(kh[h, keys, :], qt[step, h * HD : (h + 1) * HD, :])
                if allowed is not None:
                    value = jnp.where(allowed, value, FILL)
                scores[h, b] = value
                tops[h] = jnp.maximum(tops[h], jnp.max(value.reshape(-1, 8, BQ), 0))

        over_keys(ends_ref, start, chunk, True, score)
        top = [jnp.max(tops[h], 0, keepdims=True) for h in range(heads)]

        def weigh(b, carry):
            for h in range(heads):
                part = slice(h * HD, (h + 1) * HD)
                weight = jnp.exp(scores[h, b] - top[h])
                sums[h] += fold_rows(weight)
                acc[part, :] += mm(vt[b, part, :], weight.astype(BF16))
            return carry

        low_first, _ = reach(ends_ref, start)
        _, high_last = reach(ends_ref, start + BQ - 1)
        lax.fori_loop(low_first // chunk, (high_last + chunk - 1) // chunk, weigh, 0)
        lse_ref[...] = jnp.zeros(lse_ref.shape, F32)
        for h in range(heads):
            part = slice(h * HD, (h + 1) * HD)
            total = jnp.sum(sums[h], 0, keepdims=True)
            acc[part, :] = acc[part, :] / total
            lse_ref[0, h : h + 1, :] = top[h] + jnp.log(total)
        wide = acc[...].T
        wide_ref[0] = wide
        ctx_ref[0] = wide.astype(BF16)

    row_block = lambda i, *_: (i // per, i % per, 0)
    return call(
        flow, body, (steps,), [full((2, chunk, width3))] * 2,
        [pl.BlockSpec((1, BQ, width), row_block), pl.BlockSpec((1, BQ, width), row_block),
         pl.BlockSpec((1, 8, BQ), lambda i, *_: (i, 0, 0))],
        [sds((count, chunk, width), BF16), sds((count, chunk, width), F32), sds((steps, 8, BQ), F32)],
        [
            pltpu.VMEM((steps, width, BQ), BF16),
            pltpu.VMEM((heads, SEQLEN, HD), BF16),
            pltpu.VMEM((count, width, chunk), BF16),
            pltpu.VMEM((width, BQ), F32),
            pltpu.VMEM((heads, 8, BQ), F32),
            pltpu.VMEM((heads, 8, BQ), F32),
            pltpu.VMEM((heads, count, chunk, BQ), F32),
        ],
        [*qkv], 0, 0, "attend_forward", (flow.scal, ends),
    )


def attend_backward(flow, ends, pair, qkv, grads, wide, lse):
    chunk = qkv[0].shape[1]
    count = SEQLEN // chunk
    steps = SEQLEN // BQ
    per = chunk // BQ

    def body(
        scal_ref, ends_ref, near_ref, far_ref, grad_near, grad_far, wide_ref, lse_ref, out_ref, qh, gh, kt, vt, qt, gt,
        gq, gk, gv,
    ):
        step = pl.program_id(0)

        @pl.when(step == 0)
        def _():
            blocks = chunks_of(scal_ref, near_ref, far_ref)
            grad_blocks = chunks_of(scal_ref, grad_near, grad_far)
            for (j, block), (_, grad_block) in zip(blocks, grad_blocks):
                rows = pl.ds(pl.multiple_of(j * chunk, chunk), chunk)
                queries = block[:, :PAIR] * BF16(HD**-0.5)
                keys = block[:, PAIR : 2 * PAIR]
                back = grad_block[...]
                for h in range(2):
                    cols = slice(h * HD, (h + 1) * HD)
                    qh[h, rows, :] = queries[:, cols]
                    gh[h, rows, :] = back[:, cols]
                kt[j] = keys.T
                vt[j] = block[:, 2 * PAIR :].T
                for s in range(per):
                    sub = slice(s * BQ, (s + 1) * BQ)
                    qt[j * per + s] = queries[sub, :].T
                    gt[j * per + s] = back[sub, :].T
            gk[...] = jnp.zeros(gk.shape, F32)
            gv[...] = jnp.zeros(gv.shape, F32)

        start = step * BQ
        rows = pl.ds(pl.multiple_of(start, BQ), BQ)
        gq[...] = jnp.zeros(gq.shape, F32)
        sums = lse_ref[0].T
        inner, logs = [], []
        for h in range(2):
            product = gh[h, rows, :].astype(F32) * wide_ref[0, :, h * HD : (h + 1) * HD]
            inner.append(jnp.sum(product, 1, keepdims=True))
            logs.append(sums[:, 2 * pair + h : 2 * pair + h + 1])

        def block(b, allowed):
            for h in range(2):
                part = slice(h * HD, (h + 1) * HD)
                score = mm(qh[h, rows, :], kt[b, part, :])
                grad_weight = mm(gh[h, rows, :], vt[b, part, :])
                if allowed is not None:
                    score = jnp.where(allowed, score, FILL)
                weight = jnp.exp(score - logs[h])
                grad_score = (weight * (grad_weight - inner[h])).astype(BF16)
                gv[b, part, :] += mm(gt[step, part, :], weight.astype(BF16))
                gk[b, part, :] += mm(qt[step, part, :], grad_score)
                gq[part, :] += mm(kt[b, part, :], grad_score, NT)

        over_keys(ends_ref, start, chunk, False, block)
        place = pl.ds(pl.multiple_of((step % per) * BQ, BQ), BQ)
        out_ref[step // per, place, :PAIR] = (gq[...] * HD**-0.5).T.astype(BF16)

        @pl.when(step == steps - 1)
        def _():
            for j in range(count):
                out_ref[j, :, PAIR : 2 * PAIR] = gk[j].T.astype(BF16)
                out_ref[j, :, 2 * PAIR :] = gv[j].T.astype(BF16)

    out = (count, chunk, 3 * PAIR)
    return call(
        flow, body, (steps,),
        [pl.BlockSpec((2, chunk, 3 * PAIR), lambda i, *_: (0, 0, pair))] * 2
        + [pl.BlockSpec((2, chunk, PAIR), lambda i, *_: (0, 0, pair))] * 2
        + [pl.BlockSpec((1, BQ, PAIR), lambda i, *_: (i // per, i % per, pair)),
           pl.BlockSpec((1, 8, BQ), lambda i, *_: (i, 0, 0))],
        full(out), sds(out, BF16),
        [pltpu.VMEM((2, SEQLEN, HD), BF16)] * 2
        + [pltpu.VMEM((count, PAIR, chunk), BF16)] * 2
        + [pltpu.VMEM((steps, PAIR, BQ), BF16)] * 2
        + [pltpu.VMEM((PAIR, BQ), F32)]
        + [pltpu.VMEM((count, PAIR, chunk), F32)] * 2,
        [*qkv, *grads, wide, lse], 0, 0, "attend_backward", (flow.scal, ends),
    )


def flip(values_in, axes, mask):
    return lax.ppermute(values_in, axes, [(a, a ^ mask) for a in range(lax.axis_size(axes))])


def turn(values_in):
    return lax.ppermute(values_in, ("c", "zh"), [(2 * a + b, 2 * b + a) for a in range(2) for b in range(2)])


def uncross(values_in):
    return lax.ppermute(values_in, ("c", "zh"), [(2 * b + 1 - a, 2 * a + b) for a in range(2) for b in range(2)])


def from_members(values_in, axes):
    return [values_in] + [flip(values_in, axes, r) for r in range(1, lax.axis_size(axes))]


def to_members(parts, axes):
    return [parts[0]] + [flip(part, axes, r) for r, part in enumerate(parts) if r > 0]


def add(*parts):
    total = parts[0].astype(F32)
    for part in parts[1:]:
        total = total + part.astype(F32)
    return total


def is_small():
    return lax.axis_size("q") == 4


def order_by(values_in, axis, position, count):
    bit = 1
    while bit < count:
        shape = values_in.shape
        split = shape[:axis] + (count // (2 * bit), 2, bit) + shape[axis + 1 :]
        cut = values_in.reshape(split)
        values_in = jnp.where((position & bit) != 0, jnp.flip(cut, axis + 1), cut).reshape(shape)
        bit *= 2
    return values_in


def gather_group(values_in):
    across, sibling = flip(values_in, GROUP, 1), flip(values_in, GROUP, 2)
    return [values_in, across, sibling]


def forward(flow, members, *before):
    flow.wait(*before)
    flow.hold(across=members[1])
    gate(flow)
    members[1] = flow.free("across")
    members.append(flip(members[1], GROUP, 2))


def sum_group(keep, send):
    got = flip(send, GROUP, 2)
    passed = add(keep[1], got[1]).astype(BF16)
    return [keep[0], got, flip(passed, GROUP, 1)], passed


EXTRA = 16


def heads_shard_of(qkv, out, bias):
    rows = out.shape[0]
    paired = qkv.reshape(3, rows, -1, PAIR).transpose(1, 2, 0, 3).reshape(rows, -1)
    weights = jnp.concatenate([paired, out], axis=1)
    below = jnp.pad(bias.reshape(1, -1), ((0, EXTRA - 1), (0, weights.shape[1] - bias.size)))
    return jnp.concatenate([weights, below])


def heads_bias(rows, heads):
    bias = rows.reshape(rows.shape[0], 2, heads, -1).transpose(1, 2, 0, 3).reshape(2, -1).astype(F32)
    bias = jnp.stack([bias[0], jnp.zeros_like(bias[0]), bias[1]])
    return bias.reshape(3, -1, PAIR).transpose(1, 0, 2).reshape(1, -1)


def with_sibling(shard):
    return jnp.stack([shard, flip(shard, "c", 1)])


def heads_along_x(pair):
    return jnp.stack([pair, flip(pair, "q", 1)])


def heads_along_y(near, size, heads, where, zh):
    far = flip(near, "q", 2)
    rows = jnp.concatenate([near[:, :, ROWS, :size], far[:, :, ROWS, :size]])
    return [near, far], heads_bias(order_by(order_by(rows, 0, where[0], 4), 1, zh, 2).reshape(8, size), heads)


def all_heads_weight(shard, size, heads, zh):
    pair = turn(with_sibling(shard))
    every = order_by(lax.all_gather(pair, "q"), 1, zh, 2)
    count = shard.shape[0] - EXTRA
    weights = every[:, :, :count].reshape(4, 2, ROWS, -1)
    return [weights[:2], weights[2:]], heads_bias(every[:, :, count, :size].reshape(-1, size), heads)


class HeadsGrad:
    def __init__(self, keep, send):
        self.keep, self.send = keep, send

    def along_x(self):
        self.got = flip(self.send, "q", 1)
        return self.got

    def along_y(self):
        self.got_x = self.got
        self.got = flip(add(self.keep[1], self.got[1]).astype(BF16), "q", 2)
        return self.got

    def halves(self, zh):
        if is_small():
            return tuple(add(self.keep[0, k], self.got_x[0, k], self.got[k]).astype(BF16) for k in range(2))
        buckets = [self.keep[0], self.send[0], self.keep[1], self.send[1]]
        every = jnp.stack(buckets).reshape(lax.axis_size("q"), 2, -1, buckets[0].shape[-1])
        rows = order_by(lax.psum_scatter(every, "q", scatter_dimension=0, tiled=False), 0, zh, 2)
        return rows[0], rows[1]


SLOTS = (0, 2, 1, 3)


def all_units_weight(shard):
    matrices, _, width = shard.shape
    members = lax.axis_size(MODEL)
    every = lax.all_gather(shard, ALL).reshape(members, -1, matrices, shard.shape[1], width).transpose(0, 2, 1, 3, 4)
    every = every.reshape(members, matrices, 4, 2, ROWS, width)
    every = jnp.stack([every[slot] for slot in SLOTS])
    pieces = []
    for k in range(2):
        pieces += [every[:, :, r, k] for r in range(3)] + [every[:2, :, 3, k], every[2:, :, 3, k]]
    return pieces


class UnitsWeight:
    def __init__(self, shard):
        self.shard, self.theirs = shard, {}

    def start_far_z(self):
        self.other = flip(self.shard, "zh", 1)

    def join_far_z(self, shard):
        self.two = jnp.stack([shard, self.other])

    def far_z(self):
        self.start_far_z()
        self.join_far_z(self.shard)

    def start_z(self):
        self.other = flip(self.two, "zl", 1)

    def join_z(self, two):
        self.own = jnp.concatenate([two, self.other])

    def near_z(self):
        self.start_z()
        self.join_z(self.two)

    def near(self):
        self.near_x, self.near_y = flip(self.own, "q", 1), flip(self.own, "q", 2)

    def corner(self):
        self.far_a, self.far_b = flip(self.near_y[:2], "q", 1), flip(self.near_x[2:], "q", 2)

    def swap(self, *names):
        for name in names:
            self.theirs[name] = flip(getattr(self, name), "c", 1)

    def pieces(self):
        names = ("own", "near_x", "near_y", "far_a", "far_b")
        return [getattr(self, name) for name in names] + [self.theirs[name] for name in names]


class UnitsGrads:
    def __init__(self, flow, down, up, count):
        self.flow, self.down, self.up, self.count = flow, down, up, count

    def compute_theirs(self):
        self.theirs = unit_grads(self.flow, self.down, self.up, None, self.count, True)

    def send_theirs(self):
        self.got = flip(self.theirs, "c", 1) if is_small() else None

    def sibling(self):
        self.compute_theirs()
        self.send_theirs()

    def mine(self):
        self.made = unit_grads(self.flow, self.down, self.up, self.got, self.count, False)
        self.own, self.to_x, self.to_y, self.rest_x, self.rest_y = self.made

    def near(self):
        self.from_x, self.from_y = flip(self.to_x, "q", 1), flip(self.to_y, "q", 2)
        return [self.from_x, self.from_y]

    def far(self):
        half = self.count
        self.late_x = flip(add(self.rest_x, self.from_y[half:]).astype(BF16), "q", 1)
        self.late_y = flip(add(self.rest_y, self.from_x[half:]).astype(BF16), "q", 2)
        return [self.late_x, self.late_y]

    def near_z(self):
        half = self.count
        self.passing = add(self.own[half:], self.late_x, self.from_y[:half]).astype(BF16)
        self.there = flip(self.passing, "zl", 1)
        return [self.there]

    def far_z(self):
        self.last = flip(self.near_sum(slice(self.count // 2, self.count)).astype(BF16), "zh", 1)
        return [self.last]

    def near_sum(self, blocks):
        return add(self.own[blocks], self.from_x[blocks], self.late_y[blocks], self.there[blocks])

    def total(self):
        if is_small():
            return self.near_sum(slice(0, self.count // 2)) + self.last.astype(F32)
        half = self.count
        mine = jnp.stack(
            [self.own, jnp.concatenate([self.to_x[:half], self.rest_x]), jnp.concatenate([self.rest_y, self.to_y[:half]]),
             jnp.concatenate([self.to_x[half:], self.to_y[half:]])]
        ).reshape(4, self.count, 2, ROWS, -1)
        theirs = self.theirs.reshape(4, 2, self.count, ROWS, -1).transpose(0, 2, 1, 3, 4)
        every = jnp.stack([mine, theirs], axis=1)
        every = every.transpose(2, 0, 1, 4, 3, 5)
        every = jnp.stack([every[slot] for slot in SLOTS]).reshape(-1, 2, mine.shape[-1])
        return lax.psum_scatter(every, ALL, scatter_dimension=0, tiled=True).astype(F32).transpose(1, 0, 2)


SMALL_AXES = ("q", MODEL, "c")
SMALL_STEPS = (("q", 1), ("q", 2), ("zl", 1), ("zh", 1), ("c", 1))
SMALL_SHAPE = (128, 256)


def spread_by_distance(values_in, where):
    every = values_in.reshape(4, 4, 2, -1).transpose(1, 0, 2, 3)
    for axis, position in enumerate(where):
        every = order_by(every, axis, position, every.shape[axis])
    return every.transpose(2, 1, 0, 3).reshape(32, -1)


def fold_small(every, first, last):
    for axis, mask in SMALL_STEPS[::-1][first:last]:
        half = every.shape[0] // 2
        every = every[:half] + flip(every[half:], axis, mask)
    return every


def sum_all(value):
    if not is_small():
        return lax.psum(value, ALL)
    for axes in SMALL_AXES:
        parts = jnp.stack(from_members(value, axes))
        value = jnp.sum(order_by(parts, 0, lax.axis_index(axes), parts.shape[0]), 0)
    return value[0, 0]


def on_device(
    tokens, doc_lengths, qkv_weight, qv_bias, out_weight, up_weight, up_bias, down_weight, gains, shifts, cotangent
):
    layers = qkv_weight.shape[0]
    tz, dp = lax.axis_size(MODEL), lax.axis_size(("q", "c"))
    place, zh = lax.axis_index(GROUP), lax.axis_index("zh")
    where = (lax.axis_index("q"), lax.axis_index(MODEL), lax.axis_index("c"))
    if is_small():
        spots = [place, where[0], where[2], zh, where[1]]
    else:
        spots = [place] + [jnp.zeros((), jnp.int32)] * 4
    scal = jnp.stack([spot.astype(jnp.int32) for spot in spots])

    flow = Flow(scal)
    small_slice = is_small()
    qkv_cols, out_cols = 3 * out_weight.shape[2], out_weight.shape[2]
    in_cols, out_cols = slice(0, qkv_cols), slice(qkv_cols, qkv_cols + out_cols)
    hz, bias_size = qv_bias.shape[2], qv_bias.size // layers
    heads_shard = [heads_shard_of(qkv_weight[l], out_weight[l], qv_bias[l]) for l in range(layers)]
    pieces = [up_bias, gains, shifts]
    sizes = [piece.size // layers for piece in pieces]
    cuts = [0]
    for size in sizes:
        cuts.append(cuts[-1] + size)
    small = jnp.concatenate([piece.reshape(layers, -1) for piece in pieces], axis=1).reshape(-1)
    padded = jnp.pad(small, (0, SMALL_SHAPE[0] * SMALL_SHAPE[1] - small.size)).reshape(SMALL_SHAPE)
    gathered = lax.all_gather(padded, ALL)
    small_all = gathered.reshape(tz * dp, -1)[:, : small.size]

    def spread_small():
        every = small_all.reshape(tz, dp, layers, -1).astype(F32)
        parts = [every[..., cuts[i] : cuts[i + 1]] for i in range(3)]
        biases = parts[0].reshape(tz, dp, layers, up_bias.shape[1], -1).transpose(2, 0, 3, 1, 4)
        gain = parts[1].reshape(tz, dp, layers, 2, -1).transpose(2, 3, 1, 0, 4).reshape(layers, 2, D)
        shift = parts[2].reshape(tz, dp, layers, 4, -1).transpose(2, 3, 1, 0, 4).reshape(layers, 4, D)
        table = jnp.concatenate([gain, shift], axis=1).reshape(layers * 6, D)
        head = jnp.concatenate([jnp.ones((1, D), F32), jnp.zeros((1, D), F32)])
        return biases.reshape(layers, tz, 1, -1), jnp.pad(jnp.concatenate([head, table]), ((0, TABLE - 2 - 6 * layers), (0, 0)))

    up_bias_full, table = spread_small()
    if small_slice:
        pair = turn(with_sibling(heads_shard[0]))
        x_low = turn(tokens)
        ends = jnp.cumsum(turn(doc_lengths)[0], dtype=jnp.int32)
        near = heads_along_x(pair)
        up0, down0 = UnitsWeight(up_weight[0][None]), UnitsWeight(down_weight[0][None])
        both1 = UnitsWeight(jnp.stack([up_weight[1], down_weight[1]]))
        flow.hold(
            up0=up0.shard, down0=down0.shard, down0_twin=down0.shard, both1=both1.shard,
            heads1=heads_shard[1], low=x_low,
        )
        gate(flow)
        x_low, up0.shard = flow.free("low"), flow.free("up0")
        up0.far_z()
        weights_of = [heads_along_y(near, bias_size, hz, where, zh)]
    else:
        x_low = turn(tokens)
        ends = jnp.cumsum(turn(doc_lengths)[0], dtype=jnp.int32)
        weights_of = [all_heads_weight(shard, bias_size, hz, zh) for shard in heads_shard]
        every = [all_units_weight(jnp.stack([up_weight[l], down_weight[l]])) for l in range(layers)]
        top_grad = turn(cotangent)

    prev, prev_gain, prev_shift = x_low, ONE, ZERO
    kept = []
    for l in range(layers):
        first, last = small_slice and l == 0, small_slice and l == 1
        xs = gather_group(x_low)
        w_heads, bias = weights_of[l]
        if first:
            flow.wait(up0.two)
            flow.hold(two=up0.two, two_twin=up0.two)
        qkv_near = project_in(flow, (xs[0], xs[2]), False, w_heads, in_cols, bias, "project_qkv")
        if first:
            up0.two, down0.shard = flow.free("two"), flow.free("down0")
            up0.start_z()
            down0.start_far_z()
        if last:
            flow.hold(top=cotangent, own=both1.own)
        forward(flow, xs, qkv_near)
        if first:
            pair = with_sibling(flow.free("heads1"))
        if last:
            both1.own = flow.free("own")
            both1.near()
        qkv_far = project_in(flow, (xs[1], xs[3]), True, w_heads, in_cols, bias, "project_qkv")
        qkv = (qkv_near, qkv_far)
        if first:
            down0.join_far_z(flow.free("down0_twin"))
            up0.join_z(flow.free("two_twin"))
            up0.near()
            down0.near_z()
            both1.shard = flow.free("both1")
            both1.far_z()
            pair = turn(pair)
        if last:
            top_grad = turn(flow.free("top"))
            both1.swap("own")
        ctx, wide, lse = attend_forward(flow, ends, qkv)
        if first:
            flow.wait(up0.near_x, up0.near_y)
            flow.hold(both1=both1.two, down0=down0.own, pair_twin=pair)
            flow.wait(pair)
            beside = flip(pair, "q", 1)
            up0.corner()
            up0.swap("own")
        if last:
            flow.wait(both1.near_x, both1.near_y, top_grad)
            both1.corner()
            both1.swap("near_x", "near_y")
        send = project_out(flow, [ctx], (2, 3), w_heads, out_cols, True, "project_attn")
        flow.wait(send)
        keep = project_out(flow, [ctx], (0, 1), w_heads, out_cols, False, "project_attn")
        attn, passed = sum_group(keep, send)
        if first:
            flow.wait(passed, gathered)
            flow.hold(near_x=up0.near_x, near_y=up0.near_y)
            gate(flow)
            down0.own, up0.near_x, up0.near_y = flow.free("down0"), flow.free("near_x"), flow.free("near_y")
            up0.swap("near_x", "near_y", "far_a", "far_b")
            down0.near()
            down0.swap("own")
            flow.wait(down0.near_x, down0.near_y)
            down0.corner()
            down0.swap("near_x", "near_y")
            w_up = up0.pieces(), 0
        elif last:
            flow.wait(passed)
            flow.hold(ends=ends)
            gate(flow)
            ends = flow.free("ends")
            flow.hold(far_a=both1.far_a, far_b=both1.far_b)
            flow.wait(attn[2])
            gate(flow)
            both1.far_a, both1.far_b = flow.free("far_a"), flow.free("far_b")
            both1.swap("far_a", "far_b")
            w_up, w_down = (both1.pieces(), 0), (both1.pieces(), 1)
        else:
            w_up, w_down = (every[l], 0), (every[l], 1)
        used = (prev_gain, prev_shift, shift_row(l, 0), gain_row(l, 0), shift_row(l, 1))
        n1, hs, r1, act, slope = norm_up(flow, prev, attn, table, used, *w_up, up_bias_full[l], tz)
        if first:
            flow.wait(n1, beside)
            flow.hold(far_a=down0.far_a, far_b=down0.far_b)
            gate(flow)
            down0.far_a, down0.far_b = flow.free("far_a"), flow.free("far_b")
            down0.swap("far_a", "far_b")
            both1.two = flow.free("both1")
            both1.near_z()
            near = jnp.stack([flow.free("pair_twin"), beside])
            weights_of.append(heads_along_y(near, bias_size, hz, where, zh))
            w_down = down0.pieces(), 0
        used = (gain_row(l, 0), shift_row(l, 1), shift_row(l, 2), gain_row(l, 1), shift_row(l, 3))
        n2, y_low, r2 = down_norm(flow, act, *w_down, n1, table, used, tz)
        kept.append((xs, qkv, ctx, wide, lse, n1, hs, r1, act, slope, n2, r2, w_heads, w_up, w_down))
        x_low, prev, prev_gain, prev_shift = y_low, n2, gain_row(l, 1), shift_row(l, 3)
    layer_output = turn(x_low)

    residual, back = top_grad, []
    small_grads = [None] * layers
    units_of, heads_of = [None] * layers, [None] * layers
    above = above_heads = None
    for l in reversed(range(layers)):
        top = l == layers - 1
        xs, qkv, ctx, wide, lse, n1, hs, r1, act, slope, n2, r2, w_heads, w_up, w_down = kept[l]
        beside = small_slice and not top
        g2, gf, sums2, gu, up_bias_sum = units_back(
            flow, residual, back, n2, r2, table, gain_row(l, 1), *w_down, slope, tz
        )
        units = UnitsGrads(flow, (gf, act), (hs, gu), tz)
        if top:
            flow.hold(output=layer_output)
        else:
            if beside:
                flow.wait(*above.near())
                flow.hold(heads=above_heads.send)
            units.sibling()
            flow.wait(units.theirs)
            if beside:
                above_heads.send = flow.free("heads")
                above_heads.along_x()
                late = above.far()
        g1, ga, sums1 = up_back(flow, gu, *w_up, g2, n1, r1, table, gain_row(l, 0), tz)
        gas = gather_group(ga)
        flow.wait(ga)
        if top:
            layer_output = flow.free("output")
            units.compute_theirs()
            forward(flow, gas, units.theirs)
        else:
            units.mine()
            if beside:
                flow.wait(*late, above_heads.got)
            forward(flow, gas, *units.made)
        gc_near = project_in(flow, (gas[0], gas[2]), False, w_heads, out_cols, None, "project_gc")
        flow.wait(gc_near)
        if top:
            flow.hold(theirs=units.theirs)
        gc_far = project_in(flow, (gas[1], gas[3]), True, w_heads, out_cols, None, "project_gc")
        if top:
            units.theirs = flow.free("theirs")
            units.send_theirs()
        gcs = (gc_near, gc_far)
        if beside:
            flow.hold(rest_x=units.rest_x, rest_y=units.rest_y)
        gqkv = [attend_backward(flow, ends, 0, qkv, gcs, wide, lse)]
        if beside:
            units.rest_x, units.rest_y = flow.free("rest_x"), flow.free("rest_y")
        flow.wait(gqkv[0])
        if beside:
            flow.wait(*units.near(), *above.near_z(), above_heads.along_y())
            above.far_z()
            units.far()
            above_halves = above_heads.halves(zh)
            done = turn(above_halves[0]), uncross(above_halves[1])
            flow.hold(own=units.own)
        gqkv.append(attend_backward(flow, ends, 1, qkv, gcs, wide, lse))
        if beside:
            units.own = flow.free("own")
            units.near_z()
            flow.wait(units.passing, units.late_y, above.last, *done)
        send = project_out(flow, gqkv, (2, 3), w_heads, in_cols, True, "project_gx")
        flow.wait(send)
        if beside:
            flow.hold(own=units.own)
        keep = project_out(flow, gqkv, (0, 1), w_heads, in_cols, False, "project_gx")
        back, passed = sum_group(keep, send)
        flow.wait(passed)
        if top:
            units.mine()
            flow.wait(*units.made)
        elif small_slice:
            units.own = flow.free("own")
            flow.wait(units.there)
            units.far_z()
        *buckets, qkv_sums = heads_grad(flow, xs, gqkv, gas, ctx)
        heads = HeadsGrad(*buckets)
        units_of[l], heads_of[l] = units, heads
        qv_sums = qkv_sums.reshape(-1, 3, PAIR).transpose(1, 0, 2).reshape(3, hz, dp, -1)
        qv_sums = jnp.stack([qv_sums[0], qv_sums[2]]).transpose(2, 0, 1, 3).reshape(1, dp, -1)
        mine = (jnp.arange(tz) == place).astype(F32).reshape(tz, 1, 1)
        small_grads[l] = jnp.concatenate(
            [
                mine * qv_sums,
                up_bias_sum.reshape(tz, up_bias.shape[1], dp, -1).transpose(0, 2, 1, 3).reshape(tz, dp, -1),
                jnp.stack([sums1[0], sums2[0]]).reshape(2, dp, tz, -1).transpose(2, 1, 0, 3).reshape(tz, dp, -1),
                jnp.stack([sums1[2], sums1[1], sums2[2], sums2[1]])
                .reshape(4, dp, tz, -1).transpose(2, 1, 0, 3).reshape(tz, dp, -1),
            ],
            axis=-1,
        )
        if l > 0:
            above, above_heads = units, heads
            flow.wait(heads.send)
            residual = g1
    small_sums = jnp.stack(small_grads, axis=2).reshape(tz, dp, -1)
    if small_slice:
        heads.along_x()
        small_sums = fold_small(spread_by_distance(small_sums, where), 0, 1)
        flow.wait(back[2])
        flow.hold(small=small_sums, got=heads.got, own=units.own)
        gate(flow)
        small_sums, heads.got, units.own = flow.free("small"), flow.free("got"), flow.free("own")
        input_grad = turn(add(g1, back[0], back[1][0], back[2]).astype(BF16))
        heads.along_y()
        small_sums = fold_small(small_sums, 1, 2)
        flow.wait(heads.got)
        flow.hold(small=small_sums, own=units.own)
        gate(flow)
        units.own = flow.free("own")
        small_sums = fold_small(flow.free("small"), 2, 3)
        halves = heads.halves(zh)
        d_heads = jnp.stack([add(turn(halves[0]), uncross(halves[1])), add(*done)])
        small_out = fold_small(small_sums, 3, 5).reshape(layers, -1)
    else:
        halves = [member.halves(zh) for member in heads_of]
        d_heads = jnp.stack([add(turn(half[0]), uncross(half[1])) for half in halves])
        input_grad = turn(add(g1, back[0], back[1][0], back[2]).astype(BF16))
        small_out = lax.psum_scatter(small_sums.reshape(tz * dp, -1), ALL, scatter_dimension=0, tiled=True)
        small_out = small_out.reshape(layers, -1)
    qkv_grad = d_heads[:, :, : in_cols.stop].reshape(layers, d_heads.shape[1], -1, 3, PAIR)
    qkv_grad = qkv_grad.transpose(0, 3, 1, 2, 4).reshape(qkv_weight.shape)
    out_grad = d_heads[:, :, in_cols.stop :]
    totals = [member.total() for member in units_of]
    down_grad, up_grad = (jnp.stack([total[i] for total in totals]) for i in range(2))

    rest = small_out[:, bias_size:]
    qv_bias_grad = small_out[:, :bias_size].reshape(qv_bias.shape)
    up_bias_grad = rest[:, cuts[0] : cuts[1]].reshape(up_bias.shape)
    gains_grad = rest[:, cuts[1] : cuts[2]].reshape(gains.shape)
    shifts_grad = rest[:, cuts[2] : cuts[3]].reshape(shifts.shape)
    all_grads = (qkv_grad, qv_bias_grad, out_grad, up_grad, up_bias_grad, down_grad, gains_grad, shifts_grad)
    local_squares = sum(jnp.sum(member * member) for member in all_grads)
    entry_count = LAYERS * (4 * D * D + 2 * D * FF + FF + 8 * D)
    if small_slice:
        flow.hold(squares=jnp.broadcast_to(local_squares, (8, 128)), grad=input_grad, output=layer_output)
        flow.hold(**{f"out{i}": member for i, member in enumerate(all_grads)})
        gate(flow)
        local_squares, input_grad, layer_output = flow.free("squares"), flow.free("grad"), flow.free("output")
        all_grads = [flow.free(f"out{i}") for i in range(len(all_grads))]
    grad_rms = jnp.sqrt(sum_all(local_squares) / entry_count)
    return (layer_output, input_grad, *all_grads, grad_rms)


def solution(mesh):
    dp, tensor = mesh.shape["dp"], mesh.shape["tensor"]
    fine = Mesh(mesh.devices.reshape(dp // 2, 2, 2, tensor // 2), ("q", "c", "zh", "zl"))
    data, model = ("q", "c"), ("zh", "zl")
    both = data + model
    weight3, weight4 = P(None, data, model), P(None, None, data, model)
    in_specs = (
        P(both, None), P(data, None), weight4, P(None, None, model, data), weight3, weight3, P(None, model, data),
        weight3, P(None, None, both), P(None, None, both), P(both, None),
    )
    out_specs = (
        P(both, None), P(both, None), weight4, P(None, None, model, data), weight3, weight3, P(None, model, data),
        weight3, P(None, None, both), P(None, None, both), P(),
    )
    return jax.shard_map(on_device, mesh=fine, in_specs=in_specs, out_specs=out_specs, check_vma=False)
```

```python
import jax
import jax.numpy as jnp
from jax import lax
from jax.experimental import pallas as pl
from jax.experimental.pallas import tpu as pltpu
from jax.sharding import Mesh
from jax.sharding import PartitionSpec as P

D = 1024
HD = 64
HEADS = 16
FF = 4096
LAYERS = 2
SEQLEN = 2048
WINDOW = 1024
EPS = 1e-06
FILL = -1000000000.0

F32 = jnp.float32
BF16 = jnp.bfloat16
GROUP = ("c", "zl")
MODEL = ("zh", "zl")
ALL = ("zh", "zl", "q", "c")
VMEM_LIMIT = 56 * 1024 * 1024
TIMES = {
    "gate": 0.1, "finish": 0.2, "norm_up": 20.0, "down_norm": 20.0, "units_back": 45.0, "up_back": 20.0, "norm_back": 6.0,
    "sum_norm_back": 20.0, "grads_theirs": 0.2, "grads_mine": 0.2, "project_qkv": 0.2, "project_gc": 0.2,
    "project_attn": 0.2, "project_gx": 0.2, "heads_grad": 0.2, "attend_forward": 40.0, "attend_backward": 30.0,
}
PEAK = 0.35e9
NT = (((1,), (1,)), ((), ()))
NN = (((1,), (0,)), ((), ()))
ROWS = 128
CHUNK = 64
BQ = 512
PAIR = 2 * HD


def mm(left, right, dims=NN):
    return lax.dot_general(left, right, dims, preferred_element_type=F32)


def full(shape):
    return pl.BlockSpec(shape, lambda *_: (0,) * len(shape))


ANY = pl.BlockSpec(memory_space=pl.ANY)


def sds(shape, kind):
    return jax.ShapeDtypeStruct(shape, kind)


class Flow:
    def __init__(self, scal):
        self.scal, self.before, self.held = scal, [], {}

    def wait(self, *arrays):
        self.before += arrays

    def hold(self, **arrays):
        self.held.update(arrays)

    def free(self, name):
        return self.held.pop(name)


def call(flow, body, grid, in_specs, out_specs, out_shape, scratch, args, flops, traffic, name, scalars=None):
    scalars = (flow.scal,) if scalars is None else scalars
    single = not isinstance(out_specs, (list, tuple))
    out_specs = [out_specs] if single else list(out_specs)
    out_shape = [out_shape] if single else list(out_shape)
    before, held = flow.before, list(flow.held.items())
    ns, nb, nh, no = len(scalars), len(before), len(held), len(out_specs)
    first, last = ns + nb + nh, ns + nb + nh + len(args) + no

    def wrapped(*refs):
        body(*refs[:ns], *refs[first:last], *refs[last + nh :])

    result = pl.pallas_call(
        wrapped,
        grid_spec=pltpu.PrefetchScalarGridSpec(
            num_scalar_prefetch=ns,
            grid=grid,
            in_specs=[ANY] * (nb + nh) + list(in_specs),
            out_specs=out_specs + [ANY] * nh,
            scratch_shapes=scratch,
        ),
        out_shape=out_shape + [sds(array.shape, array.dtype) for _, array in held],
        input_output_aliases={ns + nb + i: no + i for i in range(nh)},
        compiler_params=pltpu.CompilerParams(
            dimension_semantics=("arbitrary",) * len(grid), vmem_limit_bytes=VMEM_LIMIT
        ),
        cost_estimate=pl.CostEstimate(flops=int(TIMES[name] * PEAK), bytes_accessed=1024, transcendentals=0),
        name=name,
    )(*scalars, *before, *[array for _, array in held], *args)
    flow.before = []
    flow.held = {key: value for (key, _), value in zip(held, result[no:])}
    return result[0] if single else result[:no]


def gate(flow):
    if flow.held:
        call(flow, lambda *refs: None, (1,), [], [], [], [], [], 0, 0, "gate")


S_P, S_Q, S_C, S_ZH, S_Z = range(5)


def norm_rows(values_in):
    centred = values_in - jnp.mean(values_in, -1, keepdims=True)
    variance = jnp.mean(centred * centred, -1, keepdims=True)
    inverse = lax.rsqrt(variance + EPS)
    return centred * inverse, inverse


def norm_back_rows(grad, normed, inverse, gain):
    scaled = grad * gain
    centred = scaled - jnp.mean(scaled, -1, keepdims=True) - normed * jnp.mean(scaled * normed, -1, keepdims=True)
    return centred * inverse


def fold_rows(values_in):
    return jnp.sum(values_in.reshape(-1, 8, values_in.shape[-1]), 0)


def read(part, rows):
    return (part[0, rows, :] if len(part.shape) == 3 else part[rows, :]).astype(F32)


def part_spec(part):
    shape = part.shape
    return full(shape) if len(shape) == 2 else pl.BlockSpec((1,) + shape[1:], lambda *_: (0, 0, 0))


ONE, ZERO, TABLE = 0, 1, 16


def gain_row(layer, index):
    return 2 + 6 * layer + index


def shift_row(layer, index):
    return 4 + 6 * layer + index


def row_of(vec_ref, row):
    return vec_ref[row : row + 1, :]


def norm_forward(get_total, tokens, vec, gain, shift, n_ref, low_ref, inv_ref):

    def step(index, carry):
        rows = pl.ds(pl.multiple_of(index * CHUNK, CHUNK), CHUNK)
        normed, inverse = norm_rows(get_total(rows))
        n_ref[rows, :] = normed
        low_ref[rows, :] = (normed * row_of(vec, gain) + row_of(vec, shift)).astype(BF16)
        inv_ref[rows, :] = jnp.broadcast_to(inverse, (CHUNK, 128))
        return carry

    lax.fori_loop(0, tokens // CHUNK, step, 0)


def norm_backward(get_grad, tokens, n_ref, inv_ref, vec, gain, g_ref, low_ref, sums_ref):
    def step(index, carry):
        rows = pl.ds(pl.multiple_of(index * CHUNK, CHUNK), CHUNK)
        grad = get_grad(rows)
        normed = n_ref[rows, :]
        result = norm_back_rows(grad, normed, inv_ref[rows, 0:1], row_of(vec, gain))
        low = result.astype(BF16)
        g_ref[rows, :] = result
        low_ref[rows, :] = low
        return (
            carry[0] + fold_rows(grad * normed),
            carry[1] + fold_rows(grad),
            carry[2] + fold_rows(low.astype(F32)),
        )

    zero = jnp.zeros((8, D), F32)
    sums = lax.fori_loop(0, tokens // CHUNK, step, (zero, zero, zero))
    sums_ref[...] = jnp.zeros(sums_ref.shape, F32)
    for row, member in enumerate(sums):
        sums_ref[row : row + 1, :] = jnp.sum(member, 0, keepdims=True)


def away(s):
    return (s & 1) * 2 + s // 2


class Streamed:
    def __init__(self, refs, matrix, buffer, sems, scal):
        self.refs, self.matrix, self.buffer, self.sems, self.scal = refs, matrix, buffer, sems, scal

    def copies(self, s):
        slot = lax.rem(s, 2)
        plain, early, late = [], [], []
        for k in range(2):
            own, near_x, near_y, far_a, far_b = self.refs[5 * k : 5 * k + 5]

            def copy(source, r, k=k):
                row = ((self.scal[S_Q] ^ r) * 2 + (self.scal[S_C] ^ k)) * ROWS
                return pltpu.make_async_copy(
                    source, self.buffer.at[slot, pl.ds(pl.multiple_of(row, ROWS), ROWS), :], self.sems.at[slot, 4 * k + r]
                )

            for r, ref in enumerate((own, near_x, near_y)):
                plain.append(copy(ref.at[s, self.matrix], r))
            early.append(copy(far_a.at[jnp.minimum(s, 1), self.matrix], 3))
            late.append(copy(far_b.at[jnp.maximum(s - 2, 0), self.matrix], 3))
        return plain, early, late

    def each(self, s, act):
        plain, early, late = self.copies(s)
        for copy in plain:
            act(copy)

        @pl.when(s < 2)
        def _():
            for copy in early:
                act(copy)

        @pl.when(s >= 2)
        def _():
            for copy in late:
                act(copy)

    def start(self, s):
        self.each(s, lambda copy: copy.start())

    def wait(self, s):
        self.each(s, lambda copy: copy.wait())

    def turn(self, s, count):
        @pl.when(s == 0)
        def _():
            self.start(s)

        @pl.when(s + 1 < count)
        def _():
            self.start(s + 1)


def piece_shapes(width):
    return [pltpu.VMEM((2, D, width), BF16), pltpu.SemaphoreType.DMA((2, 8))]


def gelu_parts(u):
    size = jnp.abs(u)
    t = 1.0 / (1.0 + 0.2316419 * size)
    poly = t * (0.127414796 + t * (-0.142248368 + t * (0.7107068705 + t * (-0.7265760135 + t * 0.5307027145))))
    bell = jnp.exp(-0.5 * (u * u))
    tail = poly * bell
    cdf = jnp.where(u >= 0, 1.0 - tail, tail)
    return u * cdf, cdf + u * (0.3989422804014327 * bell)


def tiles(tokens, width):
    for i in range(2):
        for j in range(2):
            yield slice(i * tokens // 2, (i + 1) * tokens // 2), slice(j * width // 2, (j + 1) * width // 2)


def norm_up(flow, prev, parts, vec, rows_used, weight, matrix, bias, count):
    tokens = prev.shape[0]
    width = FF // count

    def body(scal_ref, prev_ref, *refs):
        part_refs, refs = refs[: len(parts)], refs[len(parts) :]
        vec_ref, bias_ref, refs = refs[0], refs[1], refs[2:]
        pieces, (n_ref, low_ref, inv_ref, act_ref, slope_ref, buffer, sems) = refs[:10], refs[10:]
        s = pl.program_id(0)
        stream = Streamed(pieces, matrix, buffer, sems, scal_ref)
        stream.turn(s, count)

        @pl.when(s == 0)
        def _():
            def total(rows):
                attn = read(part_refs[0], rows)
                for part in part_refs[1:]:
                    attn = attn + read(part, rows)
                before = read(prev_ref, rows) * row_of(vec_ref, rows_used[0]) + row_of(vec_ref, rows_used[1])
                return before + (attn + row_of(vec_ref, rows_used[2]))

            norm_forward(total, tokens, vec_ref, *rows_used[3:], n_ref, low_ref, inv_ref)

        stream.wait(s)
        slot = lax.rem(s, 2)
        for rows, cols in tiles(tokens, width):
            act, slope = gelu_parts(mm(low_ref[rows, :], buffer[slot, :, cols]) + bias_ref[0, :, cols])
            act_ref[rows, cols] = act.astype(BF16)
            slope_ref[rows, cols] = slope.astype(BF16)

    column = pl.BlockSpec((tokens, width), lambda s, _: (0, s))
    return call(
        flow, body, (count,),
        [full((tokens, D))] + [part_spec(part) for part in parts]
        + [full((TABLE, D)), pl.BlockSpec((1, 1, width), lambda s, scal_ref: (scal_ref[S_Z] ^ away(s), 0, 0))] + [ANY] * 10,
        [full((tokens, D)), full((tokens, D)), full((tokens, 128)), column, column],
        [sds((tokens, D), F32), sds((tokens, D), BF16), sds((tokens, 128), F32)] + [sds((tokens, FF), BF16)] * 2,
        piece_shapes(width), [prev, *parts, vec, bias, *weight], 2 * tokens * D * FF,
        2 * (D * FF + tokens * (10 * D + 2 * FF)), "norm_up",
    )


def down_norm(flow, act, weight, matrix, prev, vec, rows_used, count):
    tokens = prev.shape[0]
    width = FF // count

    def body(scal_ref, act_ref, prev_ref, vec_ref, *refs):
        pieces, (n_ref, low_ref, inv_ref, buffer, sems, acc) = refs[:10], refs[10:]
        s = pl.program_id(0)
        stream = Streamed(pieces, matrix, buffer, sems, scal_ref)
        stream.turn(s, count)
        stream.wait(s)
        value = mm(act_ref[...], buffer[lax.rem(s, 2)], NT)

        @pl.when(s == 0)
        def _():
            acc[...] = value

        @pl.when(s > 0)
        def _():
            acc[...] += value

        @pl.when(s == count - 1)
        def _():
            def total(rows):
                before = prev_ref[rows, :] * row_of(vec_ref, rows_used[0]) + row_of(vec_ref, rows_used[1])
                return before + (acc[rows, :] + row_of(vec_ref, rows_used[2]))

            norm_forward(total, tokens, vec_ref, *rows_used[3:], n_ref, low_ref, inv_ref)

    return call(
        flow, body, (count,),
        [pl.BlockSpec((tokens, width), lambda s, _: (0, s)), full((tokens, D)), full((TABLE, D))] + [ANY] * 10,
        [full((tokens, D)), full((tokens, D)), full((tokens, 128))],
        [sds((tokens, D), F32), sds((tokens, D), BF16), sds((tokens, 128), F32)],
        piece_shapes(width) + [pltpu.VMEM((tokens, D), F32)], [act, prev, vec, *weight], 2 * tokens * D * FF,
        2 * (D * FF + tokens * (5 * D + FF)), "down_norm",
    )


def units_back(flow, residual, parts, normed, inverse, vec, gain, weight, matrix, slope, count):
    tokens = residual.shape[0]
    width = FF // count

    def body(scal_ref, res_ref, *refs):
        part_refs, refs = refs[: len(parts)], refs[len(parts) :]
        n_ref, inv_ref, vec_ref, slope_ref, refs = refs[0], refs[1], refs[2], refs[3], refs[4:]
        pieces, (g_ref, low_ref, sums_ref, out_ref, sum_ref, buffer, sems) = refs[:10], refs[10:]
        s = pl.program_id(0)
        stream = Streamed(pieces, matrix, buffer, sems, scal_ref)
        stream.turn(s, count)

        @pl.when(s == 0)
        def _():
            def grad(rows):
                total = read(res_ref, rows)
                for part in part_refs:
                    total = total + read(part, rows)
                return total

            norm_backward(grad, tokens, n_ref, inv_ref, vec_ref, gain, g_ref, low_ref, sums_ref)

        stream.wait(s)
        slot = lax.rem(s, 2)
        sums = {}
        for rows, cols in tiles(tokens, width):
            low = (mm(low_ref[rows, :], buffer[slot, :, cols]) * slope_ref[rows, cols].astype(F32)).astype(BF16)
            out_ref[rows, cols] = low
            part = fold_rows(low.astype(F32))
            sums[cols.start] = sums[cols.start] + part if cols.start in sums else part
            if rows.start > 0:
                sum_ref[0, :, cols] = jnp.sum(sums[cols.start], 0, keepdims=True)

    column = pl.BlockSpec((tokens, width), lambda s, _: (0, s))
    return call(
        flow, body, (count,),
        [full((tokens, D))] + [part_spec(part) for part in parts]
        + [full((tokens, D)), full((tokens, 128)), full((TABLE, D)), column] + [ANY] * 10,
        [full((tokens, D)), full((tokens, D)), full((8, D)), column,
         pl.BlockSpec((1, 1, width), lambda s, scal_ref: (scal_ref[S_Z] ^ away(s), 0, 0))],
        [sds((tokens, D), F32), sds((tokens, D), BF16), sds((8, D), F32), sds((tokens, FF), BF16),
         sds((count, 1, width), F32)],
        piece_shapes(width), [residual, *parts, normed, inverse, vec, slope, *weight], 0, 0, "units_back",
    )


def up_back(flow, gu, weight, matrix, residual, normed, inverse, vec, gain, count):
    tokens = residual.shape[0]
    width = FF // count

    def body(scal_ref, gu_ref, res_ref, n_ref, inv_ref, vec_ref, *refs):
        pieces, (g_ref, low_ref, sums_ref, buffer, sems, acc) = refs[:10], refs[10:]
        s = pl.program_id(0)
        stream = Streamed(pieces, matrix, buffer, sems, scal_ref)
        stream.turn(s, count)
        stream.wait(s)
        value = mm(gu_ref[...], buffer[lax.rem(s, 2)], NT)

        @pl.when(s == 0)
        def _():
            acc[...] = value

        @pl.when(s > 0)
        def _():
            acc[...] += value

        @pl.when(s == count - 1)
        def _():
            norm_backward(
                lambda rows: res_ref[rows, :] + acc[rows, :], tokens, n_ref, inv_ref, vec_ref, gain, g_ref, low_ref,
                sums_ref,
            )

    return call(
        flow, body, (count,),
        [pl.BlockSpec((tokens, width), lambda s, _: (0, s)), full((tokens, D)), full((tokens, D)), full((tokens, 128)),
         full((TABLE, D))] + [ANY] * 10,
        [full((tokens, D)), full((tokens, D)), full((8, D))],
        [sds((tokens, D), F32), sds((tokens, D), BF16), sds((8, D), F32)],
        piece_shapes(width) + [pltpu.VMEM((tokens, D), F32)], [gu, residual, normed, inverse, vec, *weight],
        2 * tokens * D * FF, 2 * (D * FF + tokens * (8 * D + FF)), "up_back",
    )


def turn_rows(scal_ref, x_ref, turned, core):
    for r in range(4):
        row = ((scal_ref[S_Q] ^ r) * 2 + core) * ROWS
        turned[r * ROWS : (r + 1) * ROWS, :] = x_ref[:, pl.ds(pl.multiple_of(row, ROWS), ROWS)].T


def unit_grads(flow, down, up, received, count, sibling):
    tokens = down[0].shape[0]
    width = down[1].shape[1] // count
    half = count // 2
    steps = 2 * count

    def body(scal_ref, x0_ref, y0_ref, x1_ref, y1_ref, *refs):
        turned, t = refs[-1], pl.program_id(0)
        m, s = t // count, lax.rem(t, count)
        core = scal_ref[S_C] ^ 1 if sibling else scal_ref[S_C]

        @pl.when(t == 0)
        def _():
            turn_rows(scal_ref, x0_ref, turned, core)

        @pl.when(t == count)
        def _():
            turn_rows(scal_ref, x1_ref, turned, core)

        def store(y_ref):
            value = mm(turned[...], y_ref[...]).reshape(4, ROWS, width)
            if sibling:
                refs[0][:, 0] = value.astype(BF16)
                return
            if received is not None:
                value = value + refs[0][:, 0].astype(F32)
            value = value.astype(BF16)
            own, to_x, to_y, rest_x, rest_y = refs[-6:-1]
            spot = lax.rem(s, half) * 2 + m
            own[s // half * count + spot] = value[0]

            @pl.when(s < half)
            def _():
                to_x[spot] = value[1]
                to_x[count + spot] = value[3]
                rest_y[spot] = value[2]

            @pl.when(s >= half)
            def _():
                rest_x[spot] = value[1]
                to_y[spot] = value[2]
                to_y[count + spot] = value[3]

        @pl.when(m == 0)
        def _():
            store(y0_ref)

        @pl.when(m == 1)
        def _():
            store(y1_ref)

    left = full((tokens, D))
    pick_down = lambda t, _: (0, jnp.minimum(t, count - 1))
    pick_up = lambda t, _: (0, jnp.maximum(t - count, 0))
    specs = [left, pl.BlockSpec((tokens, width), pick_down), left, pl.BlockSpec((tokens, width), pick_up)]
    args = [*down, *up]
    one = pl.BlockSpec((4, 1, ROWS, width), lambda t, _: (0, t, 0, 0))
    if sibling:
        out_specs, out_shape = one, sds((4, steps, ROWS, width), BF16)
    else:
        if received is not None:
            specs.append(one)
            args.append(received)
        shapes = [(steps, ROWS, width)] * 3 + [(count, ROWS, width)] * 2
        out_specs, out_shape = [full(shape) for shape in shapes], [sds(shape, BF16) for shape in shapes]
    return call(
        flow, body, (steps,), specs, out_specs, out_shape, [pltpu.VMEM((4 * ROWS, tokens), BF16)], args,
        0, 0, "grads_theirs" if sibling else "grads_mine",
    )


def finish(flow, units, heads, small):
    layers = len(units)
    rows, cols = heads[0][0].shape
    in_width = cols * 3 // 4
    pairs = in_width // (3 * PAIR)
    width = units[0][0].shape[2]

    def body(scal_ref, *refs):
        qkv_ref, out_ref, up_ref, down_ref, square_ref = refs[-5:]
        small_ref, refs = refs[-6], refs[:-6]
        squares = jnp.sum(small_ref[...] * small_ref[...], keepdims=True)
        for l in range(layers):
            unit_refs, (first, second) = refs[7 * l : 7 * l + 5], refs[7 * l + 5 : 7 * l + 7]
            for m, target in enumerate((down_ref, up_ref)):
                total = unit_refs[0][m].astype(F32)
                for part in unit_refs[1:]:
                    total = total + part[m].astype(F32)
                target[l] = total
                squares = squares + jnp.sum(jnp.sum(total * total, 0, keepdims=True), 1, keepdims=True)
            total = first[...].astype(F32) + second[...].astype(F32)
            squares = squares + jnp.sum(jnp.sum(total * total, 0, keepdims=True), 1, keepdims=True)
            out_ref[l] = total[:, in_width:]
            for pair in range(pairs):
                for which in range(3):
                    base = (3 * pair + which) * PAIR
                    qkv_ref[l, which, :, pair * PAIR : (pair + 1) * PAIR] = total[:, base : base + PAIR]
        square_ref[...] = jnp.broadcast_to(squares, (8, 128))

    specs, args = [], []
    for l in range(layers):
        specs += [pl.BlockSpec((2, rows, width), lambda *_: (0, 0, 0))] * 5 + [full((rows, cols))] * 2
        args += [*units[l], *heads[l]]
    shapes = [(layers, 3, rows, in_width // 3), (layers, rows, cols - in_width), (layers, rows, width), (layers, rows, width),
              (8, 128)]
    return call(
        flow, body, (1,), specs + [full(small.shape)], [full(shape) for shape in shapes],
        [sds(shape, F32) for shape in shapes], [], args + [small], 0, 0, "finish",
    )


def place_heads_weight(scal_ref, pieces, buffer):
    for r in range(4):
        for k in range(2):
            row = ((scal_ref[S_Q] ^ r) * 2 + (scal_ref[S_ZH] ^ k)) * ROWS
            buffer[pl.ds(pl.multiple_of(row, ROWS), ROWS), :] = pieces[r // 2][r % 2, k, :ROWS, :]


def heads_weight_specs(weight, cols):
    width = cols.stop - cols.start
    return [pl.BlockSpec((2, 2, piece.shape[2], width), lambda *_: (0, 0, 0, cols.start // width)) for piece in weight]


def by_member(shape):
    return pl.BlockSpec((1,) + shape, lambda r, scal_ref: (scal_ref[S_P] ^ r, 0, 0))


def heads_weight_scratch(width):
    return [pltpu.VMEM((D, width), BF16)]


def project_in(flow, lefts, across, weight, cols, bias, name):
    tokens = lefts[0].shape[0]
    width = cols.stop - cols.start

    def body(scal_ref, left_ref, right_ref, *refs):
        if bias is not None:
            bias_ref, refs = refs[0], refs[1:]
        pieces, (out_ref, buffer) = refs[:2], refs[2:]
        step = pl.program_id(0)

        @pl.when(step == 0)
        def _():
            place_heads_weight(scal_ref, pieces, buffer)

        for r, left in enumerate((left_ref, right_ref)):

            @pl.when(step == r)
            def _(left=left):
                value = mm(left[...], buffer[...])
                if bias is not None:
                    value = value + bias_ref[...]
                out_ref[0] = value.astype(BF16)

    extra, extra_specs = ([], []) if bias is None else ([bias], [full((1, width))])
    return call(
        flow, body, (2,), [full((tokens, D))] * 2 + extra_specs + heads_weight_specs(weight, cols),
        pl.BlockSpec((1, tokens, width), lambda r, scal_ref: ((scal_ref[S_P] >> 1) ^ r, 0, 0)),
        sds((2, tokens, width), BF16), heads_weight_scratch(width), [*lefts, *extra, *weight], 0, 0, name,
    )


def project_out(flow, blocks, members, weight, cols, stacked, name):
    count, tokens, width = blocks[0].shape

    def body(scal_ref, *refs):
        block_refs, refs = refs[: len(blocks)], refs[len(blocks) :]
        pieces, outs, buffer = refs[:2], refs[2:-1], refs[-1]
        step = pl.program_id(0)

        @pl.when(step == 0)
        def _():
            place_heads_weight(scal_ref, pieces, buffer)

        value = mm(block_refs[0][0], buffer[:, :width], NT)
        for index in range(1, len(blocks)):
            value = value + mm(block_refs[index][0], buffer[:, index * width : (index + 1) * width], NT)
        value = value.astype(BF16)
        if stacked:
            outs[0][0] = value
            return
        for r, out in enumerate(outs):

            @pl.when(step == r)
            def _(out=out):
                out[...] = value

    first, last = members
    pick = lambda r, scal_ref: (scal_ref[S_P] ^ (first + r * (last - first)), 0, 0)
    if stacked:
        out_specs, out_shape = pl.BlockSpec((1, tokens, D), lambda r, _: (r, 0, 0)), sds((2, tokens, D), BF16)
    else:
        out_specs, out_shape = [full((tokens, D))] * 2, [sds((tokens, D), BF16)] * 2
    return call(
        flow, body, (2,), [pl.BlockSpec((1, tokens, width), pick)] * len(blocks) + heads_weight_specs(weight, cols), out_specs,
        out_shape,
        heads_weight_scratch(width * len(blocks)), [*blocks, *weight], 0, 0, name,
    )


def heads_grad(flow, xs, parts, gas, ctx):
    count, tokens, width = parts[0].shape
    out_width = ctx.shape[2]
    cuts = [slice(i * width, (i + 1) * width) for i in range(len(parts))]
    total = width * len(parts)

    def body(scal_ref, *refs):
        x_refs, refs = refs[:count], refs[count:]
        ga_refs, refs = refs[:count], refs[count:]
        part_refs, refs = refs[: len(parts)], refs[len(parts) :]
        ctx_ref, outs, (sum_ref, acc, acc_out) = refs[0], refs[1:3], refs[3:]
        step = pl.program_id(0)
        for r in range(count):

            @pl.when(step == r)
            def _(r=r):
                turned = x_refs[r][...].T
                value_out = mm(ga_refs[r][...].T, ctx_ref[0])
                for cut, part in zip(cuts, part_refs):
                    value = mm(turned, part[0])
                    sums = jnp.sum(part[0].astype(F32), 0, keepdims=True)
                    acc[:, cut] = value if r == 0 else acc[:, cut] + value
                    sum_ref[:, cut] = sums if r == 0 else sum_ref[:, cut] + sums
                acc_out[...] = value_out if r == 0 else acc_out[...] + value_out

        @pl.when(step == count - 1)
        def _():
            for r in range(4):
                for k in range(2):
                    row = ((scal_ref[S_Q] ^ r) * 2 + (scal_ref[S_ZH] ^ k)) * ROWS
                    rows = pl.ds(pl.multiple_of(row, ROWS), ROWS)
                    outs[r % 2][r // 2, k, :, :total] = acc[rows, :].astype(BF16)
                    outs[r % 2][r // 2, k, :, total:] = acc_out[rows, :].astype(BF16)

    shape = (2, 2, ROWS, total + out_width)
    return call(
        flow, body, (count,),
        [full((tokens, D))] * (2 * count) + [by_member((tokens, width))] * len(parts) + [by_member((tokens, out_width))],
        [full(shape)] * 2 + [full((1, total))], [sds(shape, BF16)] * 2 + [sds((1, total), F32)],
        [pltpu.VMEM((D, total), F32), pltpu.VMEM((D, out_width), F32)], [*xs, *gas, *parts, ctx], 0, 0, "heads_grad",
    )


def reach(ends_ref, row):
    first = jnp.zeros_like(row)
    for index in range(3):
        first = jnp.where(row >= ends_ref[index], ends_ref[index], first)
    last = jnp.full_like(row, SEQLEN)
    for index in (2, 1, 0):
        last = jnp.where(row < ends_ref[index], ends_ref[index], last)
    return jnp.maximum(first, row - (WINDOW - 1)), jnp.minimum(last, row + WINDOW)


def chunks_of(scal_ref, near_ref, far_ref):
    here = scal_ref[S_P] & 1
    for core in range(2):
        yield 2 * core + here, near_ref.at[core]
        yield 2 * core + 1 - here, far_ref.at[core]


def over_keys(ends_ref, start, chunk, keys_first, block):
    low_first, high_first = reach(ends_ref, start)
    low_last, high_last = reach(ends_ref, start + BQ - 1)
    axis = 1 if keys_first else 0
    low_row, high_row = reach(ends_ref, start + lax.broadcasted_iota(jnp.int32, (1, BQ) if keys_first else (BQ, 1), axis))
    shape = (chunk, BQ) if keys_first else (BQ, chunk)

    def one(b, carry):
        open_all = (b * chunk >= low_last) & ((b + 1) * chunk <= high_first)

        @pl.when(open_all)
        def _():
            block(b, None)

        @pl.when(jnp.logical_not(open_all))
        def _():
            key = b * chunk + lax.broadcasted_iota(jnp.int32, shape, 1 - axis)
            block(b, (key >= low_row) & (key < high_row))

        return carry

    lax.fori_loop(low_first // chunk, (high_last + chunk - 1) // chunk, one, 0)


def attend_forward(flow, ends, qkv):
    _, chunk, width3 = qkv[0].shape
    count = SEQLEN // chunk
    width = width3 // 3
    heads = width // HD
    steps = SEQLEN // BQ
    per = chunk // BQ

    def body(scal_ref, ends_ref, near_ref, far_ref, ctx_ref, wide_ref, lse_ref, qt, kh, vt, acc, tops, sums, scores):
        step = pl.program_id(0)

        @pl.when(step == 0)
        def _():
            for j, block in chunks_of(scal_ref, near_ref, far_ref):
                rows = pl.ds(pl.multiple_of(j * chunk, chunk), chunk)
                for pair in range(heads // 2):
                    base = 3 * PAIR * pair
                    part = slice(pair * PAIR, (pair + 1) * PAIR)
                    vt[j, part, :] = block[:, base + 2 * PAIR : base + 3 * PAIR].T
                    for s in range(per):
                        queries = block[s * BQ : (s + 1) * BQ, base : base + PAIR] * BF16(HD**-0.5)
                        qt[j * per + s, part, :] = queries.T
                    for h in range(2):
                        kh[2 * pair + h, rows, :] = block[:, base + PAIR + h * HD : base + PAIR + (h + 1) * HD]

        start = step * BQ
        acc[...] = jnp.zeros(acc.shape, F32)
        tops[...] = jnp.full(tops.shape, -3.0e38, F32)
        sums[...] = jnp.zeros(sums.shape, F32)

        def score(b, allowed):
            keys = pl.ds(pl.multiple_of(b * chunk, chunk), chunk)
            for h in range(heads):
                value = mm(kh[h, keys, :], qt[step, h * HD : (h + 1) * HD, :])
                if allowed is not None:
                    value = jnp.where(allowed, value, FILL)
                scores[h, b] = value
                tops[h] = jnp.maximum(tops[h], jnp.max(value.reshape(-1, 8, BQ), 0))

        over_keys(ends_ref, start, chunk, True, score)
        top = [jnp.max(tops[h], 0, keepdims=True) for h in range(heads)]

        def weigh(b, carry):
            for h in range(heads):
                part = slice(h * HD, (h + 1) * HD)
                weight = jnp.exp(scores[h, b] - top[h])
                sums[h] += fold_rows(weight)
                acc[part, :] += mm(vt[b, part, :], weight.astype(BF16))
            return carry

        low_first, _ = reach(ends_ref, start)
        _, high_last = reach(ends_ref, start + BQ - 1)
        lax.fori_loop(low_first // chunk, (high_last + chunk - 1) // chunk, weigh, 0)
        lse_ref[...] = jnp.zeros(lse_ref.shape, F32)
        for h in range(heads):
            part = slice(h * HD, (h + 1) * HD)
            total = jnp.sum(sums[h], 0, keepdims=True)
            acc[part, :] = acc[part, :] / total
            lse_ref[0, h : h + 1, :] = top[h] + jnp.log(total)
        wide = acc[...].T
        wide_ref[0] = wide
        ctx_ref[0] = wide.astype(BF16)

    row_block = lambda i, *_: (i // per, i % per, 0)
    return call(
        flow, body, (steps,), [full((2, chunk, width3))] * 2,
        [pl.BlockSpec((1, BQ, width), row_block), pl.BlockSpec((1, BQ, width), row_block),
         pl.BlockSpec((1, 8, BQ), lambda i, *_: (i, 0, 0))],
        [sds((count, chunk, width), BF16), sds((count, chunk, width), F32), sds((steps, 8, BQ), F32)],
        [
            pltpu.VMEM((steps, width, BQ), BF16),
            pltpu.VMEM((heads, SEQLEN, HD), BF16),
            pltpu.VMEM((count, width, chunk), BF16),
            pltpu.VMEM((width, BQ), F32),
            pltpu.VMEM((heads, 8, BQ), F32),
            pltpu.VMEM((heads, 8, BQ), F32),
            pltpu.VMEM((heads, count, chunk, BQ), F32),
        ],
        [*qkv], 0, 0, "attend_forward", (flow.scal, ends),
    )


def attend_backward(flow, ends, pair, qkv, grads, wide, lse):
    chunk = qkv[0].shape[1]
    count = SEQLEN // chunk
    steps = SEQLEN // BQ
    per = chunk // BQ

    def body(
        scal_ref, ends_ref, near_ref, far_ref, grad_near, grad_far, wide_ref, lse_ref, out_ref, qh, gh, kt, vt, qt, gt,
        gq, gk, gv,
    ):
        step = pl.program_id(0)

        @pl.when(step == 0)
        def _():
            blocks = chunks_of(scal_ref, near_ref, far_ref)
            grad_blocks = chunks_of(scal_ref, grad_near, grad_far)
            for (j, block), (_, grad_block) in zip(blocks, grad_blocks):
                rows = pl.ds(pl.multiple_of(j * chunk, chunk), chunk)
                queries = block[:, :PAIR] * BF16(HD**-0.5)
                keys = block[:, PAIR : 2 * PAIR]
                back = grad_block[...]
                for h in range(2):
                    cols = slice(h * HD, (h + 1) * HD)
                    qh[h, rows, :] = queries[:, cols]
                    gh[h, rows, :] = back[:, cols]
                kt[j] = keys.T
                vt[j] = block[:, 2 * PAIR :].T
                for s in range(per):
                    sub = slice(s * BQ, (s + 1) * BQ)
                    qt[j * per + s] = queries[sub, :].T
                    gt[j * per + s] = back[sub, :].T
            gk[...] = jnp.zeros(gk.shape, F32)
            gv[...] = jnp.zeros(gv.shape, F32)

        start = step * BQ
        rows = pl.ds(pl.multiple_of(start, BQ), BQ)
        gq[...] = jnp.zeros(gq.shape, F32)
        sums = lse_ref[0].T
        inner, logs = [], []
        for h in range(2):
            product = gh[h, rows, :].astype(F32) * wide_ref[0, :, h * HD : (h + 1) * HD]
            inner.append(jnp.sum(product, 1, keepdims=True))
            logs.append(sums[:, 2 * pair + h : 2 * pair + h + 1])

        def block(b, allowed):
            for h in range(2):
                part = slice(h * HD, (h + 1) * HD)
                score = mm(qh[h, rows, :], kt[b, part, :])
                grad_weight = mm(gh[h, rows, :], vt[b, part, :])
                if allowed is not None:
                    score = jnp.where(allowed, score, FILL)
                weight = jnp.exp(score - logs[h])
                grad_score = (weight * (grad_weight - inner[h])).astype(BF16)
                gv[b, part, :] += mm(gt[step, part, :], weight.astype(BF16))
                gk[b, part, :] += mm(qt[step, part, :], grad_score)
                gq[part, :] += mm(kt[b, part, :], grad_score, NT)

        over_keys(ends_ref, start, chunk, False, block)
        place = pl.ds(pl.multiple_of((step % per) * BQ, BQ), BQ)
        out_ref[step // per, place, :PAIR] = (gq[...] * HD**-0.5).T.astype(BF16)

        @pl.when(step == steps - 1)
        def _():
            for j in range(count):
                out_ref[j, :, PAIR : 2 * PAIR] = gk[j].T.astype(BF16)
                out_ref[j, :, 2 * PAIR :] = gv[j].T.astype(BF16)

    out = (count, chunk, 3 * PAIR)
    return call(
        flow, body, (steps,),
        [pl.BlockSpec((2, chunk, 3 * PAIR), lambda i, *_: (0, 0, pair))] * 2
        + [pl.BlockSpec((2, chunk, PAIR), lambda i, *_: (0, 0, pair))] * 2
        + [pl.BlockSpec((1, BQ, PAIR), lambda i, *_: (i // per, i % per, pair)),
           pl.BlockSpec((1, 8, BQ), lambda i, *_: (i, 0, 0))],
        full(out), sds(out, BF16),
        [pltpu.VMEM((2, SEQLEN, HD), BF16)] * 2
        + [pltpu.VMEM((count, PAIR, chunk), BF16)] * 2
        + [pltpu.VMEM((steps, PAIR, BQ), BF16)] * 2
        + [pltpu.VMEM((PAIR, BQ), F32)]
        + [pltpu.VMEM((count, PAIR, chunk), F32)] * 2,
        [*qkv, *grads, wide, lse], 0, 0, "attend_backward", (flow.scal, ends),
    )


def flip(values_in, axes, mask):
    return lax.ppermute(values_in, axes, [(a, a ^ mask) for a in range(lax.axis_size(axes))])


def turn(values_in):
    return lax.ppermute(values_in, ("c", "zh"), [(2 * a + b, 2 * b + a) for a in range(2) for b in range(2)])


def uncross(values_in):
    return lax.ppermute(values_in, ("c", "zh"), [(2 * b + 1 - a, 2 * a + b) for a in range(2) for b in range(2)])


def from_members(values_in, axes):
    return [values_in] + [flip(values_in, axes, r) for r in range(1, lax.axis_size(axes))]


def to_members(parts, axes):
    return [parts[0]] + [flip(part, axes, r) for r, part in enumerate(parts) if r > 0]


def add(*parts):
    total = parts[0].astype(F32)
    for part in parts[1:]:
        total = total + part.astype(F32)
    return total


def is_small():
    return lax.axis_size("q") == 4


def order_by(values_in, axis, position, count):
    bit = 1
    while bit < count:
        shape = values_in.shape
        split = shape[:axis] + (count // (2 * bit), 2, bit) + shape[axis + 1 :]
        cut = values_in.reshape(split)
        values_in = jnp.where((position & bit) != 0, jnp.flip(cut, axis + 1), cut).reshape(shape)
        bit *= 2
    return values_in


def gather_group(values_in):
    across, sibling = flip(values_in, GROUP, 1), flip(values_in, GROUP, 2)
    return [values_in, across, sibling]


def forward(flow, members, *before):
    flow.wait(*before)
    flow.hold(across=members[1])
    gate(flow)
    members[1] = flow.free("across")
    members.append(flip(members[1], GROUP, 2))


def sum_group(keep, send):
    got = flip(send, GROUP, 2)
    passed = add(keep[1], got[1]).astype(BF16)
    return [keep[0], got, flip(passed, GROUP, 1)], passed


EXTRA = 16


def heads_shard_of(qkv, out, bias):
    rows = out.shape[0]
    paired = qkv.reshape(3, rows, -1, PAIR).transpose(1, 2, 0, 3).reshape(rows, -1)
    weights = jnp.concatenate([paired, out], axis=1)
    below = jnp.pad(bias.reshape(1, -1), ((0, EXTRA - 1), (0, weights.shape[1] - bias.size)))
    return jnp.concatenate([weights, below])


def heads_bias(rows, heads):
    bias = rows.reshape(rows.shape[0], 2, heads, -1).transpose(1, 2, 0, 3).reshape(2, -1).astype(F32)
    bias = jnp.stack([bias[0], jnp.zeros_like(bias[0]), bias[1]])
    return bias.reshape(3, -1, PAIR).transpose(1, 0, 2).reshape(1, -1)


def with_sibling(shard):
    return jnp.stack([shard, flip(shard, "c", 1)])


def heads_along_x(pair):
    return jnp.stack([pair, flip(pair, "q", 1)])


def heads_along_y(near, size, heads, where, zh):
    return heads_pieces(near, flip(near, "q", 2), size, heads, where, zh)


def heads_pieces(near, far, size, heads, where, zh):
    rows = jnp.concatenate([near[:, :, ROWS, :size], far[:, :, ROWS, :size]])
    return [near, far], heads_bias(order_by(order_by(rows, 0, where[0], 4), 1, zh, 2).reshape(8, size), heads)


def all_heads_weight(shard, size, heads, zh):
    pair = turn(with_sibling(shard))
    every = order_by(lax.all_gather(pair, "q"), 1, zh, 2)
    count = shard.shape[0] - EXTRA
    weights = every[:, :, :count].reshape(4, 2, ROWS, -1)
    return [weights[:2], weights[2:]], heads_bias(every[:, :, count, :size].reshape(-1, size), heads)


class HeadsGrad:
    def __init__(self, keep, send):
        self.keep, self.send = keep, send

    def along_x(self):
        self.got = flip(self.send, "q", 1)
        return self.got

    def along_y(self):
        self.got_x = self.got
        self.got = flip(add(self.keep[1], self.got[1]).astype(BF16), "q", 2)
        return self.got

    def halves(self, zh):
        if is_small():
            return tuple(add(self.keep[0, k], self.got_x[0, k], self.got[k]).astype(BF16) for k in range(2))
        buckets = [self.keep[0], self.send[0], self.keep[1], self.send[1]]
        every = jnp.stack(buckets).reshape(lax.axis_size("q"), 2, -1, buckets[0].shape[-1])
        rows = order_by(lax.psum_scatter(every, "q", scatter_dimension=0, tiled=False), 0, zh, 2)
        return rows[0], rows[1]


SLOTS = (0, 2, 1, 3)


def all_units_weight(shard):
    matrices, _, width = shard.shape
    members = lax.axis_size(MODEL)
    every = lax.all_gather(shard, ALL).reshape(members, -1, matrices, shard.shape[1], width).transpose(0, 2, 1, 3, 4)
    every = every.reshape(members, matrices, 4, 2, ROWS, width)
    every = jnp.stack([every[slot] for slot in SLOTS])
    pieces = []
    for k in range(2):
        pieces += [every[:, :, r, k] for r in range(3)] + [every[:2, :, 3, k], every[2:, :, 3, k]]
    return pieces


class UnitsWeight:
    def __init__(self, shard):
        self.shard, self.theirs = shard, {}

    def start_far_z(self):
        self.other = flip(self.shard, "zh", 1)

    def join_far_z(self, shard):
        self.two = jnp.stack([shard, self.other])

    def far_z(self):
        self.start_far_z()
        self.join_far_z(self.shard)

    def start_z(self):
        self.other = flip(self.two, "zl", 1)

    def join_z(self, two):
        self.own = jnp.concatenate([two, self.other])

    def near_z(self):
        self.start_z()
        self.join_z(self.two)

    def near(self):
        self.near_x, self.near_y = flip(self.own, "q", 1), flip(self.own, "q", 2)

    def corner(self):
        self.far_a, self.far_b = flip(self.near_y[:2], "q", 1), flip(self.near_x[2:], "q", 2)

    def swap(self, *names):
        for name in names:
            self.theirs[name] = flip(getattr(self, name), "c", 1)

    def pieces(self):
        names = ("own", "near_x", "near_y", "far_a", "far_b")
        return [getattr(self, name) for name in names] + [self.theirs[name] for name in names]


class UnitsGrads:
    def __init__(self, flow, down, up, count):
        self.flow, self.down, self.up, self.count = flow, down, up, count

    def compute_theirs(self):
        self.theirs = unit_grads(self.flow, self.down, self.up, None, self.count, True)

    def send_theirs(self):
        self.got = flip(self.theirs, "c", 1) if is_small() else None

    def sibling(self):
        self.compute_theirs()
        self.send_theirs()

    def mine(self):
        self.made = unit_grads(self.flow, self.down, self.up, self.got, self.count, False)
        self.own, self.to_x, self.to_y, self.rest_x, self.rest_y = self.made

    def near(self):
        self.from_x, self.from_y = flip(self.to_x, "q", 1), flip(self.to_y, "q", 2)
        return [self.from_x, self.from_y]

    def far(self):
        half = self.count
        self.late_x = flip(add(self.rest_x, self.from_y[half:]).astype(BF16), "q", 1)
        self.late_y = flip(add(self.rest_y, self.from_x[half:]).astype(BF16), "q", 2)
        return [self.late_x, self.late_y]

    def near_z(self):
        half = self.count
        self.passing = add(self.own[half:], self.late_x, self.from_y[:half]).astype(BF16)
        self.there = flip(self.passing, "zl", 1)
        return [self.there]

    def far_z(self):
        self.last = flip(self.near_sum(slice(self.count // 2, self.count)).astype(BF16), "zh", 1)
        return [self.last]

    def near_sum(self, blocks):
        return add(self.own[blocks], self.from_x[blocks], self.late_y[blocks], self.there[blocks])

    def parts(self):
        return self.own, self.from_x, self.late_y, self.there, self.last

    def total(self):
        half = self.count
        mine = jnp.stack(
            [self.own, jnp.concatenate([self.to_x[:half], self.rest_x]), jnp.concatenate([self.rest_y, self.to_y[:half]]),
             jnp.concatenate([self.to_x[half:], self.to_y[half:]])]
        ).reshape(4, self.count, 2, ROWS, -1)
        theirs = self.theirs.reshape(4, 2, self.count, ROWS, -1).transpose(0, 2, 1, 3, 4)
        every = jnp.stack([mine, theirs], axis=1)
        every = every.transpose(2, 0, 1, 4, 3, 5)
        every = jnp.stack([every[slot] for slot in SLOTS]).reshape(-1, 2, mine.shape[-1])
        return lax.psum_scatter(every, ALL, scatter_dimension=0, tiled=True).astype(F32).transpose(1, 0, 2)


SMALL_AXES = ("q", MODEL, "c")
SMALL_STEPS = (("q", 1), ("q", 2), ("zl", 1), ("zh", 1), ("c", 1))
SMALL_SHAPE = (128, 256)


def spread_by_distance(values_in, where):
    every = values_in.reshape(4, 4, 2, -1).transpose(1, 0, 2, 3)
    for axis, position in enumerate(where):
        every = order_by(every, axis, position, every.shape[axis])
    return every.transpose(2, 1, 0, 3).reshape(32, -1)


def fold_small(every, first, last):
    for axis, mask in SMALL_STEPS[::-1][first:last]:
        half = every.shape[0] // 2
        every = every[:half] + flip(every[half:], axis, mask)
    return every


def sum_all(value):
    if not is_small():
        return lax.psum(value, ALL)
    for axes in SMALL_AXES:
        parts = jnp.stack(from_members(value, axes))
        value = jnp.sum(order_by(parts, 0, lax.axis_index(axes), parts.shape[0]), 0)
    return value[0, 0]


def on_device(
    tokens, doc_lengths, qkv_weight, qv_bias, out_weight, up_weight, up_bias, down_weight, gains, shifts, cotangent
):
    layers = qkv_weight.shape[0]
    tz, dp = lax.axis_size(MODEL), lax.axis_size(("q", "c"))
    place, zh = lax.axis_index(GROUP), lax.axis_index("zh")
    where = (lax.axis_index("q"), lax.axis_index(MODEL), lax.axis_index("c"))
    if is_small():
        spots = [place, where[0], where[2], zh, where[1]]
    else:
        spots = [place] + [jnp.zeros((), jnp.int32)] * 4
    scal = jnp.stack([spot.astype(jnp.int32) for spot in spots])

    flow = Flow(scal)
    small_slice = is_small()
    qkv_cols, out_cols = 3 * out_weight.shape[2], out_weight.shape[2]
    in_cols, out_cols = slice(0, qkv_cols), slice(qkv_cols, qkv_cols + out_cols)
    hz, bias_size = qv_bias.shape[2], qv_bias.size // layers
    heads_shard = [heads_shard_of(qkv_weight[l], out_weight[l], qv_bias[l]) for l in range(layers)]
    pieces = [up_bias, gains, shifts]
    sizes = [piece.size // layers for piece in pieces]
    cuts = [0]
    for size in sizes:
        cuts.append(cuts[-1] + size)
    small = jnp.concatenate([piece.reshape(layers, -1) for piece in pieces], axis=1).reshape(-1)
    padded = jnp.pad(small, (0, SMALL_SHAPE[0] * SMALL_SHAPE[1] - small.size)).reshape(SMALL_SHAPE)
    gathered = lax.all_gather(padded, ALL)
    small_all = gathered.reshape(tz * dp, -1)[:, : small.size]

    def spread_small():
        every = small_all.reshape(tz, dp, layers, -1).astype(F32)
        parts = [every[..., cuts[i] : cuts[i + 1]] for i in range(3)]
        biases = parts[0].reshape(tz, dp, layers, up_bias.shape[1], -1).transpose(2, 0, 3, 1, 4)
        gain = parts[1].reshape(tz, dp, layers, 2, -1).transpose(2, 3, 1, 0, 4).reshape(layers, 2, D)
        shift = parts[2].reshape(tz, dp, layers, 4, -1).transpose(2, 3, 1, 0, 4).reshape(layers, 4, D)
        table = jnp.concatenate([gain, shift], axis=1).reshape(layers * 6, D)
        head = jnp.concatenate([jnp.ones((1, D), F32), jnp.zeros((1, D), F32)])
        return biases.reshape(layers, tz, 1, -1), jnp.pad(jnp.concatenate([head, table]), ((0, TABLE - 2 - 6 * layers), (0, 0)))

    up_bias_full, table = spread_small()
    if small_slice:
        pair = with_sibling(heads_shard[0])
        bundle = turn(jnp.concatenate([tokens, pair.reshape(-1, D)]))
        x_low, pair = bundle[: tokens.shape[0]], bundle[tokens.shape[0] :].reshape(pair.shape)
        ends = jnp.cumsum(turn(doc_lengths)[0], dtype=jnp.int32)
        members = from_members(pair, "q")
        weights_of = [heads_pieces(jnp.stack(members[:2]), jnp.stack(members[2:]), bias_size, hz, where, zh)]
        up0, down0 = UnitsWeight(up_weight[0][None]), UnitsWeight(down_weight[0][None])
        both1 = UnitsWeight(jnp.stack([up_weight[1], down_weight[1]]))
        flow.hold(
            up0=up0.shard, down0=down0.shard, down0_twin=down0.shard, both1=both1.shard, heads1=heads_shard[1], low=x_low
        )
        gate(flow)
        x_low = flow.free("low")
    else:
        x_low = turn(tokens)
        ends = jnp.cumsum(turn(doc_lengths)[0], dtype=jnp.int32)
        weights_of = [all_heads_weight(shard, bias_size, hz, zh) for shard in heads_shard]
        every = [all_units_weight(jnp.stack([up_weight[l], down_weight[l]])) for l in range(layers)]
        top_grad = turn(cotangent)

    prev, prev_gain, prev_shift = x_low, ONE, ZERO
    kept = []
    for l in range(layers):
        first, last = small_slice and l == 0, small_slice and l == 1
        xs = gather_group(x_low)
        w_heads, bias = weights_of[l]
        qkv_near = project_in(flow, (xs[0], xs[2]), False, w_heads, in_cols, bias, "project_qkv")
        if first:
            up0.shard = flow.free("up0")
            up0.far_z()
            flow.hold(two=up0.two, two_twin=up0.two)
        if last:
            flow.hold(top=cotangent, own=both1.own)
        forward(flow, xs, qkv_near)
        if first:
            up0.two, down0.shard = flow.free("two"), flow.free("down0")
            up0.start_z()
            down0.start_far_z()
            pair = with_sibling(flow.free("heads1"))
        if last:
            both1.own = flow.free("own")
            both1.near()
        qkv_far = project_in(flow, (xs[1], xs[3]), True, w_heads, in_cols, bias, "project_qkv")
        qkv = (qkv_near, qkv_far)
        if first:
            down0.join_far_z(flow.free("down0_twin"))
            up0.join_z(flow.free("two_twin"))
            up0.near()
            down0.near_z()
            both1.shard = flow.free("both1")
            both1.far_z()
            pair = turn(pair)
        if last:
            top_grad = turn(flow.free("top"))
            both1.swap("own")
        ctx, wide, lse = attend_forward(flow, ends, qkv)
        if first:
            flow.wait(up0.near_x, up0.near_y)
            flow.hold(both1=both1.two, down0=down0.own, pair_twin=pair)
            flow.wait(pair)
            beside = flip(pair, "q", 1)
            up0.corner()
            up0.swap("own")
        if last:
            flow.wait(both1.near_x, both1.near_y, top_grad)
            both1.corner()
            both1.swap("near_x", "near_y")
        send = project_out(flow, [ctx], (2, 3), w_heads, out_cols, True, "project_attn")
        flow.wait(send)
        keep = project_out(flow, [ctx], (0, 1), w_heads, out_cols, False, "project_attn")
        attn, passed = sum_group(keep, send)
        if first:
            flow.wait(passed, gathered)
            flow.hold(near_x=up0.near_x, near_y=up0.near_y)
            gate(flow)
            down0.own, up0.near_x, up0.near_y = flow.free("down0"), flow.free("near_x"), flow.free("near_y")
            up0.swap("near_x", "near_y", "far_a", "far_b")
            down0.near()
            down0.swap("own")
            flow.wait(down0.near_x, down0.near_y)
            down0.corner()
            down0.swap("near_x", "near_y")
            w_up = up0.pieces(), 0
        elif last:
            flow.wait(passed)
            flow.hold(ends=ends)
            gate(flow)
            ends = flow.free("ends")
            flow.hold(far_a=both1.far_a, far_b=both1.far_b)
            flow.wait(attn[2])
            gate(flow)
            both1.far_a, both1.far_b = flow.free("far_a"), flow.free("far_b")
            both1.swap("far_a", "far_b")
            w_up, w_down = (both1.pieces(), 0), (both1.pieces(), 1)
        else:
            w_up, w_down = (every[l], 0), (every[l], 1)
        used = (prev_gain, prev_shift, shift_row(l, 0), gain_row(l, 0), shift_row(l, 1))
        n1, hs, r1, act, slope = norm_up(flow, prev, attn, table, used, *w_up, up_bias_full[l], tz)
        if first:
            flow.wait(n1, beside)
            flow.hold(far_a=down0.far_a, far_b=down0.far_b)
            gate(flow)
            down0.far_a, down0.far_b = flow.free("far_a"), flow.free("far_b")
            down0.swap("far_a", "far_b")
            both1.two = flow.free("both1")
            both1.near_z()
            near = jnp.stack([flow.free("pair_twin"), beside])
            weights_of.append(heads_along_y(near, bias_size, hz, where, zh))
            w_down = down0.pieces(), 0
        used = (gain_row(l, 0), shift_row(l, 1), shift_row(l, 2), gain_row(l, 1), shift_row(l, 3))
        n2, y_low, r2 = down_norm(flow, act, *w_down, n1, table, used, tz)
        kept.append((xs, qkv, ctx, wide, lse, n1, hs, r1, act, slope, n2, r2, w_heads, w_up, w_down))
        x_low, prev, prev_gain, prev_shift = y_low, n2, gain_row(l, 1), shift_row(l, 3)
    layer_output = turn(x_low)

    residual, back = top_grad, []
    small_grads = [None] * layers
    units_of, heads_of = [None] * layers, [None] * layers
    above = above_heads = None
    for l in reversed(range(layers)):
        top = l == layers - 1
        xs, qkv, ctx, wide, lse, n1, hs, r1, act, slope, n2, r2, w_heads, w_up, w_down = kept[l]
        beside = small_slice and not top
        g2, gf, sums2, gu, up_bias_sum = units_back(
            flow, residual, back, n2, r2, table, gain_row(l, 1), *w_down, slope, tz
        )
        units = UnitsGrads(flow, (gf, act), (hs, gu), tz)
        if top:
            flow.hold(output=layer_output)
        else:
            if beside:
                flow.wait(*above.near())
                flow.hold(heads=above_heads.send)
            units.sibling()
            flow.wait(units.theirs)
            if beside:
                above_heads.send = flow.free("heads")
                above_heads.along_x()
                late = above.far()
        g1, ga, sums1 = up_back(flow, gu, *w_up, g2, n1, r1, table, gain_row(l, 0), tz)
        gas = gather_group(ga)
        flow.wait(ga)
        if top:
            layer_output = flow.free("output")
            units.compute_theirs()
            forward(flow, gas, units.theirs)
        else:
            units.mine()
            if beside:
                flow.wait(*late, above_heads.got)
            forward(flow, gas, *units.made)
        gc_near = project_in(flow, (gas[0], gas[2]), False, w_heads, out_cols, None, "project_gc")
        flow.wait(gc_near)
        if top:
            flow.hold(theirs=units.theirs)
        gc_far = project_in(flow, (gas[1], gas[3]), True, w_heads, out_cols, None, "project_gc")
        if top:
            units.theirs = flow.free("theirs")
            units.send_theirs()
        gcs = (gc_near, gc_far)
        if beside:
            early = [above_heads.along_y(), *above.near_z()]
            flow.hold(rest_x=units.rest_x, rest_y=units.rest_y, keep=above_heads.keep, above=above.own)
        gqkv = [attend_backward(flow, ends, 0, qkv, gcs, wide, lse)]
        if beside:
            units.rest_x, units.rest_y = flow.free("rest_x"), flow.free("rest_y")
            above_heads.keep, above.own = flow.free("keep"), flow.free("above")
        flow.wait(gqkv[0])
        if beside:
            flow.wait(*units.near(), *early)
            above.far_z()
            units.far()
            above_halves = above_heads.halves(zh)
            done = turn(above_halves[0]), uncross(above_halves[1])
            flow.hold(own=units.own)
        gqkv.append(attend_backward(flow, ends, 1, qkv, gcs, wide, lse))
        if beside:
            units.own = flow.free("own")
            units.near_z()
            flow.wait(units.passing, units.late_y, above.last, *done)
        send = project_out(flow, gqkv, (2, 3), w_heads, in_cols, True, "project_gx")
        flow.wait(send)
        if beside:
            flow.hold(own=units.own)
        keep = project_out(flow, gqkv, (0, 1), w_heads, in_cols, False, "project_gx")
        back, passed = sum_group(keep, send)
        flow.wait(passed)
        if top:
            units.mine()
            flow.wait(*units.made)
        elif small_slice:
            units.own = flow.free("own")
            units.far_z()
        *buckets, qkv_sums = heads_grad(flow, xs, gqkv, gas, ctx)
        heads = HeadsGrad(*buckets)
        units_of[l], heads_of[l] = units, heads
        qv_sums = qkv_sums.reshape(-1, 3, PAIR).transpose(1, 0, 2).reshape(3, hz, dp, -1)
        qv_sums = jnp.stack([qv_sums[0], qv_sums[2]]).transpose(2, 0, 1, 3).reshape(1, dp, -1)
        mine = (jnp.arange(tz) == place).astype(F32).reshape(tz, 1, 1)
        small_grads[l] = jnp.concatenate(
            [
                mine * qv_sums,
                up_bias_sum.reshape(tz, up_bias.shape[1], dp, -1).transpose(0, 2, 1, 3).reshape(tz, dp, -1),
                jnp.stack([sums1[0], sums2[0]]).reshape(2, dp, tz, -1).transpose(2, 1, 0, 3).reshape(tz, dp, -1),
                jnp.stack([sums1[2], sums1[1], sums2[2], sums2[1]])
                .reshape(4, dp, tz, -1).transpose(2, 1, 0, 3).reshape(tz, dp, -1),
            ],
            axis=-1,
        )
        if l > 0:
            above, above_heads = units, heads
            flow.wait(heads.send)
            residual = g1
    small_sums = jnp.stack(small_grads, axis=2).reshape(tz, dp, -1)
    if small_slice:
        heads.along_x()
        small_sums = fold_small(spread_by_distance(small_sums, where), 0, 1)
        flow.wait(back[2])
        flow.hold(small=small_sums, got=heads.got)
        gate(flow)
        small_sums, heads.got = flow.free("small"), flow.free("got")
        input_grad = turn(add(g1, back[0], back[1][0], back[2]).astype(BF16))
        heads.along_y()
        small_sums = fold_small(small_sums, 1, 2)
        flow.wait(heads.got, units.last)
        flow.hold(small=small_sums)
        gate(flow)
        small_sums = fold_small(flow.free("small"), 2, 3)
        halves = heads.halves(zh)
        small_out = fold_small(small_sums, 3, 5).reshape(layers, -1)
        parts = [(turn(halves[0]), uncross(halves[1])), done]
        flow.hold(grad=input_grad, output=layer_output)
        qkv_grad, out_grad, up_grad, down_grad, squares = finish(
            flow, [member.parts() for member in units_of], parts, small_out
        )
        input_grad, layer_output = flow.free("grad"), flow.free("output")
    else:
        halves = [member.halves(zh) for member in heads_of]
        d_heads = jnp.stack([add(turn(half[0]), uncross(half[1])) for half in halves])
        input_grad = turn(add(g1, back[0], back[1][0], back[2]).astype(BF16))
        small_out = lax.psum_scatter(small_sums.reshape(tz * dp, -1), ALL, scatter_dimension=0, tiled=True)
        small_out = small_out.reshape(layers, -1)
        qkv_grad = d_heads[:, :, : in_cols.stop].reshape(layers, d_heads.shape[1], -1, 3, PAIR)
        qkv_grad = qkv_grad.transpose(0, 3, 1, 2, 4).reshape(qkv_weight.shape)
        out_grad = d_heads[:, :, in_cols.stop :]
        totals = [member.total() for member in units_of]
        down_grad, up_grad = (jnp.stack([total[i] for total in totals]) for i in range(2))
        squares = sum(jnp.sum(member * member) for member in (qkv_grad, out_grad, up_grad, down_grad, small_out))

    rest = small_out[:, bias_size:]
    qv_bias_grad = small_out[:, :bias_size].reshape(qv_bias.shape)
    up_bias_grad = rest[:, cuts[0] : cuts[1]].reshape(up_bias.shape)
    gains_grad = rest[:, cuts[1] : cuts[2]].reshape(gains.shape)
    shifts_grad = rest[:, cuts[2] : cuts[3]].reshape(shifts.shape)
    entry_count = LAYERS * (4 * D * D + 2 * D * FF + FF + 8 * D)
    grad_rms = jnp.sqrt(sum_all(squares) / entry_count)
    return (
        layer_output, input_grad, qkv_grad, qv_bias_grad, out_grad, up_grad, up_bias_grad, down_grad, gains_grad,
        shifts_grad, grad_rms,
    )


def solution(mesh):
    dp, tensor = mesh.shape["dp"], mesh.shape["tensor"]
    fine = Mesh(mesh.devices.reshape(dp // 2, 2, 2, tensor // 2), ("q", "c", "zh", "zl"))
    data, model = ("q", "c"), ("zh", "zl")
    both = data + model
    weight3, weight4 = P(None, data, model), P(None, None, data, model)
    in_specs = (
        P(both, None), P(data, None), weight4, P(None, None, model, data), weight3, weight3, P(None, model, data),
        weight3, P(None, None, both), P(None, None, both), P(both, None),
    )
    out_specs = (
        P(both, None), P(both, None), weight4, P(None, None, model, data), weight3, weight3, P(None, model, data),
        weight3, P(None, None, both), P(None, None, both), P(),
    )
    return jax.shard_map(on_device, mesh=fine, in_specs=in_specs, out_specs=out_specs, check_vma=False)
```

```python
import jax
import jax.numpy as jnp
from jax import lax
from jax.experimental import pallas as pl
from jax.experimental.pallas import tpu as pltpu
from jax.sharding import Mesh
from jax.sharding import PartitionSpec as P

D = 1024
HD = 64
HEADS = 16
FF = 4096
LAYERS = 2
SEQLEN = 2048
WINDOW = 1024
EPS = 1e-06
FILL = -1000000000.0

F32 = jnp.float32
BF16 = jnp.bfloat16
GROUP = ("c", "zl")
MODEL = ("zh", "zl")
ALL = ("zh", "zl", "q", "c")
VMEM_LIMIT = 56 * 1024 * 1024
TIMES = {
    "gate": 0.1, "finish": 0.2, "norm_up": 20.0, "down_norm": 20.0, "units_back": 45.0, "up_back": 20.0, "norm_back": 6.0,
    "sum_norm_back": 20.0, "grads_theirs": 0.2, "grads_mine": 0.2, "project_qkv": 0.2, "project_gc": 0.2,
    "project_attn": 0.2, "project_gx": 0.2, "heads_grad": 0.2, "attend_forward": 40.0, "attend_backward": 30.0,
}
PEAK = 0.35e9
NT = (((1,), (1,)), ((), ()))
NN = (((1,), (0,)), ((), ()))
ROWS = 128
CHUNK = 64
BQ = 512
PAIR = 2 * HD


def mm(left, right, dims=NN):
    return lax.dot_general(left, right, dims, preferred_element_type=F32)


def full(shape):
    return pl.BlockSpec(shape, lambda *_: (0,) * len(shape))


ANY = pl.BlockSpec(memory_space=pl.ANY)


def sds(shape, kind):
    return jax.ShapeDtypeStruct(shape, kind)


class Flow:
    def __init__(self, scal):
        self.scal, self.before, self.held = scal, [], {}

    def wait(self, *arrays):
        self.before += arrays

    def hold(self, **arrays):
        self.held.update(arrays)

    def free(self, name):
        return self.held.pop(name)


def call(flow, body, grid, in_specs, out_specs, out_shape, scratch, args, flops, traffic, name, scalars=None):
    scalars = (flow.scal,) if scalars is None else scalars
    single = not isinstance(out_specs, (list, tuple))
    out_specs = [out_specs] if single else list(out_specs)
    out_shape = [out_shape] if single else list(out_shape)
    before, held = flow.before, list(flow.held.items())
    ns, nb, nh, no = len(scalars), len(before), len(held), len(out_specs)
    first, last = ns + nb + nh, ns + nb + nh + len(args) + no

    def wrapped(*refs):
        body(*refs[:ns], *refs[first:last], *refs[last + nh :])

    result = pl.pallas_call(
        wrapped,
        grid_spec=pltpu.PrefetchScalarGridSpec(
            num_scalar_prefetch=ns,
            grid=grid,
            in_specs=[ANY] * (nb + nh) + list(in_specs),
            out_specs=out_specs + [ANY] * nh,
            scratch_shapes=scratch,
        ),
        out_shape=out_shape + [sds(array.shape, array.dtype) for _, array in held],
        input_output_aliases={ns + nb + i: no + i for i in range(nh)},
        compiler_params=pltpu.CompilerParams(
            dimension_semantics=("arbitrary",) * len(grid), vmem_limit_bytes=VMEM_LIMIT
        ),
        cost_estimate=pl.CostEstimate(flops=int(TIMES[name] * PEAK), bytes_accessed=1024, transcendentals=0),
        name=name,
    )(*scalars, *before, *[array for _, array in held], *args)
    flow.before = []
    flow.held = {key: value for (key, _), value in zip(held, result[no:])}
    return result[0] if single else result[:no]


def gate(flow):
    if flow.held:
        call(flow, lambda *refs: None, (1,), [], [], [], [], [], 0, 0, "gate")


S_P, S_Q, S_C, S_ZH, S_Z = range(5)


def norm_rows(values_in):
    centred = values_in - jnp.mean(values_in, -1, keepdims=True)
    variance = jnp.mean(centred * centred, -1, keepdims=True)
    inverse = lax.rsqrt(variance + EPS)
    return centred * inverse, inverse


def norm_back_rows(grad, normed, inverse, gain):
    scaled = grad * gain
    centred = scaled - jnp.mean(scaled, -1, keepdims=True) - normed * jnp.mean(scaled * normed, -1, keepdims=True)
    return centred * inverse


def fold_rows(values_in):
    return jnp.sum(values_in.reshape(-1, 8, values_in.shape[-1]), 0)


def read(part, rows):
    return (part[0, rows, :] if len(part.shape) == 3 else part[rows, :]).astype(F32)


def part_spec(part):
    shape = part.shape
    return full(shape) if len(shape) == 2 else pl.BlockSpec((1,) + shape[1:], lambda *_: (0, 0, 0))


ONE, ZERO, TABLE = 0, 1, 16


def gain_row(layer, index):
    return 2 + 6 * layer + index


def shift_row(layer, index):
    return 4 + 6 * layer + index


def row_of(vec_ref, row):
    return vec_ref[row : row + 1, :]


def norm_forward(get_total, tokens, vec, gain, shift, n_ref, low_ref, inv_ref):

    def step(index, carry):
        rows = pl.ds(pl.multiple_of(index * CHUNK, CHUNK), CHUNK)
        normed, inverse = norm_rows(get_total(rows))
        n_ref[rows, :] = normed
        low_ref[rows, :] = (normed * row_of(vec, gain) + row_of(vec, shift)).astype(BF16)
        inv_ref[rows, :] = jnp.broadcast_to(inverse, (CHUNK, 128))
        return carry

    lax.fori_loop(0, tokens // CHUNK, step, 0)


def norm_backward(get_grad, tokens, n_ref, inv_ref, vec, gain, g_ref, low_ref, sums_ref):
    def step(index, carry):
        rows = pl.ds(pl.multiple_of(index * CHUNK, CHUNK), CHUNK)
        grad = get_grad(rows)
        normed = n_ref[rows, :]
        result = norm_back_rows(grad, normed, inv_ref[rows, 0:1], row_of(vec, gain))
        low = result.astype(BF16)
        g_ref[rows, :] = result
        low_ref[rows, :] = low
        return (
            carry[0] + fold_rows(grad * normed),
            carry[1] + fold_rows(grad),
            carry[2] + fold_rows(low.astype(F32)),
        )

    zero = jnp.zeros((8, D), F32)
    sums = lax.fori_loop(0, tokens // CHUNK, step, (zero, zero, zero))
    sums_ref[...] = jnp.zeros(sums_ref.shape, F32)
    for row, member in enumerate(sums):
        sums_ref[row : row + 1, :] = jnp.sum(member, 0, keepdims=True)


def away(s):
    return (s & 1) * 2 + s // 2


class Streamed:
    def __init__(self, refs, matrix, buffer, sems, scal):
        self.refs, self.matrix, self.buffer, self.sems, self.scal = refs, matrix, buffer, sems, scal

    def copies(self, s):
        slot = lax.rem(s, 2)
        plain, early, late = [], [], []
        for k in range(2):
            own, near_x, near_y, far_a, far_b = self.refs[5 * k : 5 * k + 5]

            def copy(source, r, k=k):
                row = ((self.scal[S_Q] ^ r) * 2 + (self.scal[S_C] ^ k)) * ROWS
                return pltpu.make_async_copy(
                    source, self.buffer.at[slot, pl.ds(pl.multiple_of(row, ROWS), ROWS), :], self.sems.at[slot, 4 * k + r]
                )

            for r, ref in enumerate((own, near_x, near_y)):
                plain.append(copy(ref.at[s, self.matrix], r))
            early.append(copy(far_a.at[jnp.minimum(s, 1), self.matrix], 3))
            late.append(copy(far_b.at[jnp.maximum(s - 2, 0), self.matrix], 3))
        return plain, early, late

    def each(self, s, act):
        plain, early, late = self.copies(s)
        for copy in plain:
            act(copy)

        @pl.when(s < 2)
        def _():
            for copy in early:
                act(copy)

        @pl.when(s >= 2)
        def _():
            for copy in late:
                act(copy)

    def start(self, s):
        self.each(s, lambda copy: copy.start())

    def wait(self, s):
        self.each(s, lambda copy: copy.wait())

    def turn(self, s, count):
        @pl.when(s == 0)
        def _():
            self.start(s)

        @pl.when(s + 1 < count)
        def _():
            self.start(s + 1)


def piece_shapes(width):
    return [pltpu.VMEM((2, D, width), BF16), pltpu.SemaphoreType.DMA((2, 8))]


def gelu_parts(u):
    size = jnp.abs(u)
    t = 1.0 / (1.0 + 0.2316419 * size)
    poly = t * (0.127414796 + t * (-0.142248368 + t * (0.7107068705 + t * (-0.7265760135 + t * 0.5307027145))))
    bell = jnp.exp(-0.5 * (u * u))
    tail = poly * bell
    cdf = jnp.where(u >= 0, 1.0 - tail, tail)
    return u * cdf, cdf + u * (0.3989422804014327 * bell)


def tiles(tokens, width):
    for i in range(2):
        for j in range(2):
            yield slice(i * tokens // 2, (i + 1) * tokens // 2), slice(j * width // 2, (j + 1) * width // 2)


def norm_up(flow, prev, parts, vec, rows_used, weight, matrix, bias, count):
    tokens = prev.shape[0]
    width = FF // count

    def body(scal_ref, prev_ref, *refs):
        part_refs, refs = refs[: len(parts)], refs[len(parts) :]
        vec_ref, bias_ref, refs = refs[0], refs[1], refs[2:]
        pieces, (n_ref, low_ref, inv_ref, act_ref, slope_ref, buffer, sems) = refs[:10], refs[10:]
        s = pl.program_id(0)
        stream = Streamed(pieces, matrix, buffer, sems, scal_ref)
        stream.turn(s, count)

        @pl.when(s == 0)
        def _():
            def total(rows):
                attn = read(part_refs[0], rows)
                for part in part_refs[1:]:
                    attn = attn + read(part, rows)
                before = read(prev_ref, rows) * row_of(vec_ref, rows_used[0]) + row_of(vec_ref, rows_used[1])
                return before + (attn + row_of(vec_ref, rows_used[2]))

            norm_forward(total, tokens, vec_ref, *rows_used[3:], n_ref, low_ref, inv_ref)

        stream.wait(s)
        slot = lax.rem(s, 2)
        for rows, cols in tiles(tokens, width):
            act, slope = gelu_parts(mm(low_ref[rows, :], buffer[slot, :, cols]) + bias_ref[0, :, cols])
            act_ref[rows, cols] = act.astype(BF16)
            slope_ref[rows, cols] = slope.astype(BF16)

    column = pl.BlockSpec((tokens, width), lambda s, _: (0, s))
    return call(
        flow, body, (count,),
        [full((tokens, D))] + [part_spec(part) for part in parts]
        + [full((TABLE, D)), pl.BlockSpec((1, 1, width), lambda s, scal_ref: (scal_ref[S_Z] ^ away(s), 0, 0))] + [ANY] * 10,
        [full((tokens, D)), full((tokens, D)), full((tokens, 128)), column, column],
        [sds((tokens, D), F32), sds((tokens, D), BF16), sds((tokens, 128), F32)] + [sds((tokens, FF), BF16)] * 2,
        piece_shapes(width), [prev, *parts, vec, bias, *weight], 2 * tokens * D * FF,
        2 * (D * FF + tokens * (10 * D + 2 * FF)), "norm_up",
    )


def down_norm(flow, act, weight, matrix, prev, vec, rows_used, count):
    tokens = prev.shape[0]
    width = FF // count

    def body(scal_ref, act_ref, prev_ref, vec_ref, *refs):
        pieces, (n_ref, low_ref, inv_ref, buffer, sems, acc) = refs[:10], refs[10:]
        s = pl.program_id(0)
        stream = Streamed(pieces, matrix, buffer, sems, scal_ref)
        stream.turn(s, count)
        stream.wait(s)
        value = mm(act_ref[...], buffer[lax.rem(s, 2)], NT)

        @pl.when(s == 0)
        def _():
            acc[...] = value

        @pl.when(s > 0)
        def _():
            acc[...] += value

        @pl.when(s == count - 1)
        def _():
            def total(rows):
                before = prev_ref[rows, :] * row_of(vec_ref, rows_used[0]) + row_of(vec_ref, rows_used[1])
                return before + (acc[rows, :] + row_of(vec_ref, rows_used[2]))

            norm_forward(total, tokens, vec_ref, *rows_used[3:], n_ref, low_ref, inv_ref)

    return call(
        flow, body, (count,),
        [pl.BlockSpec((tokens, width), lambda s, _: (0, s)), full((tokens, D)), full((TABLE, D))] + [ANY] * 10,
        [full((tokens, D)), full((tokens, D)), full((tokens, 128))],
        [sds((tokens, D), F32), sds((tokens, D), BF16), sds((tokens, 128), F32)],
        piece_shapes(width) + [pltpu.VMEM((tokens, D), F32)], [act, prev, vec, *weight], 2 * tokens * D * FF,
        2 * (D * FF + tokens * (5 * D + FF)), "down_norm",
    )


def units_back(flow, residual, parts, normed, inverse, vec, gain, weight, matrix, slope, count):
    tokens = residual.shape[0]
    width = FF // count

    def body(scal_ref, res_ref, *refs):
        part_refs, refs = refs[: len(parts)], refs[len(parts) :]
        n_ref, inv_ref, vec_ref, slope_ref, refs = refs[0], refs[1], refs[2], refs[3], refs[4:]
        pieces, (g_ref, low_ref, sums_ref, out_ref, sum_ref, buffer, sems) = refs[:10], refs[10:]
        s = pl.program_id(0)
        stream = Streamed(pieces, matrix, buffer, sems, scal_ref)
        stream.turn(s, count)

        @pl.when(s == 0)
        def _():
            def grad(rows):
                total = read(res_ref, rows)
                for part in part_refs:
                    total = total + read(part, rows)
                return total

            norm_backward(grad, tokens, n_ref, inv_ref, vec_ref, gain, g_ref, low_ref, sums_ref)

        stream.wait(s)
        slot = lax.rem(s, 2)
        sums = {}
        for rows, cols in tiles(tokens, width):
            low = (mm(low_ref[rows, :], buffer[slot, :, cols]) * slope_ref[rows, cols].astype(F32)).astype(BF16)
            out_ref[rows, cols] = low
            part = fold_rows(low.astype(F32))
            sums[cols.start] = sums[cols.start] + part if cols.start in sums else part
            if rows.start > 0:
                sum_ref[0, :, cols] = jnp.sum(sums[cols.start], 0, keepdims=True)

    column = pl.BlockSpec((tokens, width), lambda s, _: (0, s))
    return call(
        flow, body, (count,),
        [full((tokens, D))] + [part_spec(part) for part in parts]
        + [full((tokens, D)), full((tokens, 128)), full((TABLE, D)), column] + [ANY] * 10,
        [full((tokens, D)), full((tokens, D)), full((8, D)), column,
         pl.BlockSpec((1, 1, width), lambda s, scal_ref: (scal_ref[S_Z] ^ away(s), 0, 0))],
        [sds((tokens, D), F32), sds((tokens, D), BF16), sds((8, D), F32), sds((tokens, FF), BF16),
         sds((count, 1, width), F32)],
        piece_shapes(width), [residual, *parts, normed, inverse, vec, slope, *weight], 0, 0, "units_back",
    )


def up_back(flow, gu, weight, matrix, residual, normed, inverse, vec, gain, count):
    tokens = residual.shape[0]
    width = FF // count

    def body(scal_ref, gu_ref, res_ref, n_ref, inv_ref, vec_ref, *refs):
        pieces, (g_ref, low_ref, sums_ref, buffer, sems, acc) = refs[:10], refs[10:]
        s = pl.program_id(0)
        stream = Streamed(pieces, matrix, buffer, sems, scal_ref)
        stream.turn(s, count)
        stream.wait(s)
        value = mm(gu_ref[...], buffer[lax.rem(s, 2)], NT)

        @pl.when(s == 0)
        def _():
            acc[...] = value

        @pl.when(s > 0)
        def _():
            acc[...] += value

        @pl.when(s == count - 1)
        def _():
            norm_backward(
                lambda rows: res_ref[rows, :] + acc[rows, :], tokens, n_ref, inv_ref, vec_ref, gain, g_ref, low_ref,
                sums_ref,
            )

    return call(
        flow, body, (count,),
        [pl.BlockSpec((tokens, width), lambda s, _: (0, s)), full((tokens, D)), full((tokens, D)), full((tokens, 128)),
         full((TABLE, D))] + [ANY] * 10,
        [full((tokens, D)), full((tokens, D)), full((8, D))],
        [sds((tokens, D), F32), sds((tokens, D), BF16), sds((8, D), F32)],
        piece_shapes(width) + [pltpu.VMEM((tokens, D), F32)], [gu, residual, normed, inverse, vec, *weight],
        2 * tokens * D * FF, 2 * (D * FF + tokens * (8 * D + FF)), "up_back",
    )


def turn_rows(scal_ref, x_ref, turned, core):
    for r in range(4):
        row = ((scal_ref[S_Q] ^ r) * 2 + core) * ROWS
        turned[r * ROWS : (r + 1) * ROWS, :] = x_ref[:, pl.ds(pl.multiple_of(row, ROWS), ROWS)].T


def unit_grads(flow, down, up, received, count, sibling):
    tokens = down[0].shape[0]
    width = down[1].shape[1] // count
    half = count // 2
    steps = 2 * count

    def body(scal_ref, x0_ref, y0_ref, x1_ref, y1_ref, *refs):
        turned, t = refs[-1], pl.program_id(0)
        m, s = t // count, lax.rem(t, count)
        core = scal_ref[S_C] ^ 1 if sibling else scal_ref[S_C]

        @pl.when(t == 0)
        def _():
            turn_rows(scal_ref, x0_ref, turned, core)

        @pl.when(t == count)
        def _():
            turn_rows(scal_ref, x1_ref, turned, core)

        def store(y_ref):
            value = mm(turned[...], y_ref[...]).reshape(4, ROWS, width)
            if sibling:
                refs[0][:, 0] = value.astype(BF16)
                return
            if received is not None:
                value = value + refs[0][:, 0].astype(F32)
            value = value.astype(BF16)
            own, to_x, to_y, rest_x, rest_y = refs[-6:-1]
            spot = lax.rem(s, half) * 2 + m
            own[s // half * count + spot] = value[0]

            @pl.when(s < half)
            def _():
                to_x[spot] = value[1]
                to_x[count + spot] = value[3]
                rest_y[spot] = value[2]

            @pl.when(s >= half)
            def _():
                rest_x[spot] = value[1]
                to_y[spot] = value[2]
                to_y[count + spot] = value[3]

        @pl.when(m == 0)
        def _():
            store(y0_ref)

        @pl.when(m == 1)
        def _():
            store(y1_ref)

    left = full((tokens, D))
    pick_down = lambda t, _: (0, jnp.minimum(t, count - 1))
    pick_up = lambda t, _: (0, jnp.maximum(t - count, 0))
    specs = [left, pl.BlockSpec((tokens, width), pick_down), left, pl.BlockSpec((tokens, width), pick_up)]
    args = [*down, *up]
    one = pl.BlockSpec((4, 1, ROWS, width), lambda t, _: (0, t, 0, 0))
    if sibling:
        out_specs, out_shape = one, sds((4, steps, ROWS, width), BF16)
    else:
        if received is not None:
            specs.append(one)
            args.append(received)
        shapes = [(steps, ROWS, width)] * 3 + [(count, ROWS, width)] * 2
        out_specs, out_shape = [full(shape) for shape in shapes], [sds(shape, BF16) for shape in shapes]
    return call(
        flow, body, (steps,), specs, out_specs, out_shape, [pltpu.VMEM((4 * ROWS, tokens), BF16)], args,
        0, 0, "grads_theirs" if sibling else "grads_mine",
    )


def finish(flow, units, heads, small):
    layers, rows, cols = heads[0].shape
    in_width = cols * 3 // 4
    pairs = in_width // (3 * PAIR)
    width = units[0][0].shape[2]

    def body(scal_ref, *refs):
        qkv_ref, out_ref, up_ref, down_ref, square_ref = refs[-5:]
        small_ref, refs = refs[-6], refs[:-6]
        first, second, refs = refs[0], refs[1], refs[2:]
        squares = jnp.sum(small_ref[...] * small_ref[...], keepdims=True)
        for l in range(layers):
            unit_refs = refs[5 * l : 5 * l + 5]
            for m, target in enumerate((down_ref, up_ref)):
                total = unit_refs[0][m].astype(F32)
                for part in unit_refs[1:]:
                    total = total + part[m].astype(F32)
                target[l] = total
                squares = squares + jnp.sum(jnp.sum(total * total, 0, keepdims=True), 1, keepdims=True)
            total = first[l].astype(F32) + second[l].astype(F32)
            squares = squares + jnp.sum(jnp.sum(total * total, 0, keepdims=True), 1, keepdims=True)
            out_ref[l] = total[:, in_width:]
            for pair in range(pairs):
                for which in range(3):
                    base = (3 * pair + which) * PAIR
                    qkv_ref[l, which, :, pair * PAIR : (pair + 1) * PAIR] = total[:, base : base + PAIR]
        square_ref[...] = jnp.broadcast_to(squares, (8, 128))

    specs, args = [full((layers, rows, cols))] * 2, list(heads)
    for l in range(layers):
        specs += [pl.BlockSpec((2, rows, width), lambda *_: (0, 0, 0))] * 5
        args += units[l]
    shapes = [(layers, 3, rows, in_width // 3), (layers, rows, cols - in_width), (layers, rows, width), (layers, rows, width),
              (8, 128)]
    return call(
        flow, body, (1,), specs + [full(small.shape)], [full(shape) for shape in shapes],
        [sds(shape, F32) for shape in shapes], [], args + [small], 0, 0, "finish",
    )


def place_heads_weight(scal_ref, pieces, buffer):
    for r in range(4):
        for k in range(2):
            row = ((scal_ref[S_Q] ^ r) * 2 + (scal_ref[S_ZH] ^ k)) * ROWS
            buffer[pl.ds(pl.multiple_of(row, ROWS), ROWS), :] = pieces[r // 2][r % 2, k, :ROWS, :]


def heads_weight_specs(weight, cols):
    width = cols.stop - cols.start
    return [pl.BlockSpec((2, 2, piece.shape[2], width), lambda *_: (0, 0, 0, cols.start // width)) for piece in weight]


def by_member(shape):
    return pl.BlockSpec((1,) + shape, lambda r, scal_ref: (scal_ref[S_P] ^ r, 0, 0))


def heads_weight_scratch(width):
    return [pltpu.VMEM((D, width), BF16)]


def project_in(flow, lefts, across, weight, cols, bias, name):
    tokens = lefts[0].shape[0]
    width = cols.stop - cols.start

    def body(scal_ref, left_ref, right_ref, *refs):
        if bias is not None:
            bias_ref, refs = refs[0], refs[1:]
        pieces, (out_ref, buffer) = refs[:2], refs[2:]
        step = pl.program_id(0)

        @pl.when(step == 0)
        def _():
            place_heads_weight(scal_ref, pieces, buffer)

        for r, left in enumerate((left_ref, right_ref)):

            @pl.when(step == r)
            def _(left=left):
                value = mm(left[...], buffer[...])
                if bias is not None:
                    value = value + bias_ref[...]
                out_ref[0] = value.astype(BF16)

    extra, extra_specs = ([], []) if bias is None else ([bias], [full((1, width))])
    return call(
        flow, body, (2,), [full((tokens, D))] * 2 + extra_specs + heads_weight_specs(weight, cols),
        pl.BlockSpec((1, tokens, width), lambda r, scal_ref: ((scal_ref[S_P] >> 1) ^ r, 0, 0)),
        sds((2, tokens, width), BF16), heads_weight_scratch(width), [*lefts, *extra, *weight], 0, 0, name,
    )


def project_out(flow, blocks, members, weight, cols, stacked, name):
    count, tokens, width = blocks[0].shape

    def body(scal_ref, *refs):
        block_refs, refs = refs[: len(blocks)], refs[len(blocks) :]
        pieces, outs, buffer = refs[:2], refs[2:-1], refs[-1]
        step = pl.program_id(0)

        @pl.when(step == 0)
        def _():
            place_heads_weight(scal_ref, pieces, buffer)

        value = mm(block_refs[0][0], buffer[:, :width], NT)
        for index in range(1, len(blocks)):
            value = value + mm(block_refs[index][0], buffer[:, index * width : (index + 1) * width], NT)
        value = value.astype(BF16)
        if stacked:
            outs[0][0] = value
            return
        for r, out in enumerate(outs):

            @pl.when(step == r)
            def _(out=out):
                out[...] = value

    first, last = members
    pick = lambda r, scal_ref: (scal_ref[S_P] ^ (first + r * (last - first)), 0, 0)
    if stacked:
        out_specs, out_shape = pl.BlockSpec((1, tokens, D), lambda r, _: (r, 0, 0)), sds((2, tokens, D), BF16)
    else:
        out_specs, out_shape = [full((tokens, D))] * 2, [sds((tokens, D), BF16)] * 2
    return call(
        flow, body, (2,), [pl.BlockSpec((1, tokens, width), pick)] * len(blocks) + heads_weight_specs(weight, cols), out_specs,
        out_shape,
        heads_weight_scratch(width * len(blocks)), [*blocks, *weight], 0, 0, name,
    )


def heads_grad(flow, xs, parts, gas, ctx):
    count, tokens, width = parts[0].shape
    out_width = ctx.shape[2]
    cuts = [slice(i * width, (i + 1) * width) for i in range(len(parts))]
    total = width * len(parts)

    def body(scal_ref, *refs):
        x_refs, refs = refs[:count], refs[count:]
        ga_refs, refs = refs[:count], refs[count:]
        part_refs, refs = refs[: len(parts)], refs[len(parts) :]
        ctx_ref, outs, (sum_ref, acc, acc_out) = refs[0], refs[1:3], refs[3:]
        step = pl.program_id(0)
        for r in range(count):

            @pl.when(step == r)
            def _(r=r):
                turned = x_refs[r][...].T
                value_out = mm(ga_refs[r][...].T, ctx_ref[0])
                for cut, part in zip(cuts, part_refs):
                    value = mm(turned, part[0])
                    sums = jnp.sum(part[0].astype(F32), 0, keepdims=True)
                    acc[:, cut] = value if r == 0 else acc[:, cut] + value
                    sum_ref[:, cut] = sums if r == 0 else sum_ref[:, cut] + sums
                acc_out[...] = value_out if r == 0 else acc_out[...] + value_out

        @pl.when(step == count - 1)
        def _():
            for r in range(4):
                for k in range(2):
                    row = ((scal_ref[S_Q] ^ r) * 2 + (scal_ref[S_ZH] ^ k)) * ROWS
                    rows = pl.ds(pl.multiple_of(row, ROWS), ROWS)
                    outs[r % 2][r // 2, k, :, :total] = acc[rows, :].astype(BF16)
                    outs[r % 2][r // 2, k, :, total:] = acc_out[rows, :].astype(BF16)

    shape = (2, 2, ROWS, total + out_width)
    return call(
        flow, body, (count,),
        [full((tokens, D))] * (2 * count) + [by_member((tokens, width))] * len(parts) + [by_member((tokens, out_width))],
        [full(shape)] * 2 + [full((1, total))], [sds(shape, BF16)] * 2 + [sds((1, total), F32)],
        [pltpu.VMEM((D, total), F32), pltpu.VMEM((D, out_width), F32)], [*xs, *gas, *parts, ctx], 0, 0, "heads_grad",
    )


def reach(ends_ref, row):
    first = jnp.zeros_like(row)
    for index in range(3):
        first = jnp.where(row >= ends_ref[index], ends_ref[index], first)
    last = jnp.full_like(row, SEQLEN)
    for index in (2, 1, 0):
        last = jnp.where(row < ends_ref[index], ends_ref[index], last)
    return jnp.maximum(first, row - (WINDOW - 1)), jnp.minimum(last, row + WINDOW)


def chunks_of(scal_ref, near_ref, far_ref):
    here = scal_ref[S_P] & 1
    for core in range(2):
        yield 2 * core + here, near_ref.at[core]
        yield 2 * core + 1 - here, far_ref.at[core]


def over_keys(ends_ref, start, chunk, keys_first, block):
    low_first, high_first = reach(ends_ref, start)
    low_last, high_last = reach(ends_ref, start + BQ - 1)
    axis = 1 if keys_first else 0
    low_row, high_row = reach(ends_ref, start + lax.broadcasted_iota(jnp.int32, (1, BQ) if keys_first else (BQ, 1), axis))
    shape = (chunk, BQ) if keys_first else (BQ, chunk)

    def one(b, carry):
        open_all = (b * chunk >= low_last) & ((b + 1) * chunk <= high_first)

        @pl.when(open_all)
        def _():
            block(b, None)

        @pl.when(jnp.logical_not(open_all))
        def _():
            key = b * chunk + lax.broadcasted_iota(jnp.int32, shape, 1 - axis)
            block(b, (key >= low_row) & (key < high_row))

        return carry

    lax.fori_loop(low_first // chunk, (high_last + chunk - 1) // chunk, one, 0)


def attend_forward(flow, ends, qkv):
    _, chunk, width3 = qkv[0].shape
    count = SEQLEN // chunk
    width = width3 // 3
    heads = width // HD
    steps = SEQLEN // BQ
    per = chunk // BQ

    def body(scal_ref, ends_ref, near_ref, far_ref, ctx_ref, wide_ref, lse_ref, qt, kh, vt, acc, tops, sums, scores):
        step = pl.program_id(0)

        @pl.when(step == 0)
        def _():
            for j, block in chunks_of(scal_ref, near_ref, far_ref):
                rows = pl.ds(pl.multiple_of(j * chunk, chunk), chunk)
                for pair in range(heads // 2):
                    base = 3 * PAIR * pair
                    part = slice(pair * PAIR, (pair + 1) * PAIR)
                    vt[j, part, :] = block[:, base + 2 * PAIR : base + 3 * PAIR].T
                    for s in range(per):
                        queries = block[s * BQ : (s + 1) * BQ, base : base + PAIR] * BF16(HD**-0.5)
                        qt[j * per + s, part, :] = queries.T
                    for h in range(2):
                        kh[2 * pair + h, rows, :] = block[:, base + PAIR + h * HD : base + PAIR + (h + 1) * HD]

        start = step * BQ
        acc[...] = jnp.zeros(acc.shape, F32)
        tops[...] = jnp.full(tops.shape, -3.0e38, F32)
        sums[...] = jnp.zeros(sums.shape, F32)

        def score(b, allowed):
            keys = pl.ds(pl.multiple_of(b * chunk, chunk), chunk)
            for h in range(heads):
                value = mm(kh[h, keys, :], qt[step, h * HD : (h + 1) * HD, :])
                if allowed is not None:
                    value = jnp.where(allowed, value, FILL)
                scores[h, b] = value
                tops[h] = jnp.maximum(tops[h], jnp.max(value.reshape(-1, 8, BQ), 0))

        over_keys(ends_ref, start, chunk, True, score)
        top = [jnp.max(tops[h], 0, keepdims=True) for h in range(heads)]

        def weigh(b, carry):
            for h in range(heads):
                part = slice(h * HD, (h + 1) * HD)
                weight = jnp.exp(scores[h, b] - top[h])
                sums[h] += fold_rows(weight)
                acc[part, :] += mm(vt[b, part, :], weight.astype(BF16))
            return carry

        low_first, _ = reach(ends_ref, start)
        _, high_last = reach(ends_ref, start + BQ - 1)
        lax.fori_loop(low_first // chunk, (high_last + chunk - 1) // chunk, weigh, 0)
        lse_ref[...] = jnp.zeros(lse_ref.shape, F32)
        for h in range(heads):
            part = slice(h * HD, (h + 1) * HD)
            total = jnp.sum(sums[h], 0, keepdims=True)
            acc[part, :] = acc[part, :] / total
            lse_ref[0, h : h + 1, :] = top[h] + jnp.log(total)
        wide = acc[...].T
        wide_ref[0] = wide
        ctx_ref[0] = wide.astype(BF16)

    row_block = lambda i, *_: (i // per, i % per, 0)
    return call(
        flow, body, (steps,), [full((2, chunk, width3))] * 2,
        [pl.BlockSpec((1, BQ, width), row_block), pl.BlockSpec((1, BQ, width), row_block),
         pl.BlockSpec((1, 8, BQ), lambda i, *_: (i, 0, 0))],
        [sds((count, chunk, width), BF16), sds((count, chunk, width), F32), sds((steps, 8, BQ), F32)],
        [
            pltpu.VMEM((steps, width, BQ), BF16),
            pltpu.VMEM((heads, SEQLEN, HD), BF16),
            pltpu.VMEM((count, width, chunk), BF16),
            pltpu.VMEM((width, BQ), F32),
            pltpu.VMEM((heads, 8, BQ), F32),
            pltpu.VMEM((heads, 8, BQ), F32),
            pltpu.VMEM((heads, count, chunk, BQ), F32),
        ],
        [*qkv], 0, 0, "attend_forward", (flow.scal, ends),
    )


def attend_backward(flow, ends, pair, qkv, grads, wide, lse):
    chunk = qkv[0].shape[1]
    count = SEQLEN // chunk
    steps = SEQLEN // BQ
    per = chunk // BQ

    def body(
        scal_ref, ends_ref, near_ref, far_ref, grad_near, grad_far, wide_ref, lse_ref, out_ref, qh, gh, kt, vt, qt, gt,
        gq, gk, gv,
    ):
        step = pl.program_id(0)

        @pl.when(step == 0)
        def _():
            blocks = chunks_of(scal_ref, near_ref, far_ref)
            grad_blocks = chunks_of(scal_ref, grad_near, grad_far)
            for (j, block), (_, grad_block) in zip(blocks, grad_blocks):
                rows = pl.ds(pl.multiple_of(j * chunk, chunk), chunk)
                queries = block[:, :PAIR] * BF16(HD**-0.5)
                keys = block[:, PAIR : 2 * PAIR]
                back = grad_block[...]
                for h in range(2):
                    cols = slice(h * HD, (h + 1) * HD)
                    qh[h, rows, :] = queries[:, cols]
                    gh[h, rows, :] = back[:, cols]
                kt[j] = keys.T
                vt[j] = block[:, 2 * PAIR :].T
                for s in range(per):
                    sub = slice(s * BQ, (s + 1) * BQ)
                    qt[j * per + s] = queries[sub, :].T
                    gt[j * per + s] = back[sub, :].T
            gk[...] = jnp.zeros(gk.shape, F32)
            gv[...] = jnp.zeros(gv.shape, F32)

        start = step * BQ
        rows = pl.ds(pl.multiple_of(start, BQ), BQ)
        gq[...] = jnp.zeros(gq.shape, F32)
        sums = lse_ref[0].T
        inner, logs = [], []
        for h in range(2):
            product = gh[h, rows, :].astype(F32) * wide_ref[0, :, h * HD : (h + 1) * HD]
            inner.append(jnp.sum(product, 1, keepdims=True))
            logs.append(sums[:, 2 * pair + h : 2 * pair + h + 1])

        def block(b, allowed):
            for h in range(2):
                part = slice(h * HD, (h + 1) * HD)
                score = mm(qh[h, rows, :], kt[b, part, :])
                grad_weight = mm(gh[h, rows, :], vt[b, part, :])
                if allowed is not None:
                    score = jnp.where(allowed, score, FILL)
                weight = jnp.exp(score - logs[h])
                grad_score = (weight * (grad_weight - inner[h])).astype(BF16)
                gv[b, part, :] += mm(gt[step, part, :], weight.astype(BF16))
                gk[b, part, :] += mm(qt[step, part, :], grad_score)
                gq[part, :] += mm(kt[b, part, :], grad_score, NT)

        over_keys(ends_ref, start, chunk, False, block)
        place = pl.ds(pl.multiple_of((step % per) * BQ, BQ), BQ)
        out_ref[step // per, place, :PAIR] = (gq[...] * HD**-0.5).T.astype(BF16)

        @pl.when(step == steps - 1)
        def _():
            for j in range(count):
                out_ref[j, :, PAIR : 2 * PAIR] = gk[j].T.astype(BF16)
                out_ref[j, :, 2 * PAIR :] = gv[j].T.astype(BF16)

    out = (count, chunk, 3 * PAIR)
    return call(
        flow, body, (steps,),
        [pl.BlockSpec((2, chunk, 3 * PAIR), lambda i, *_: (0, 0, pair))] * 2
        + [pl.BlockSpec((2, chunk, PAIR), lambda i, *_: (0, 0, pair))] * 2
        + [pl.BlockSpec((1, BQ, PAIR), lambda i, *_: (i // per, i % per, pair)),
           pl.BlockSpec((1, 8, BQ), lambda i, *_: (i, 0, 0))],
        full(out), sds(out, BF16),
        [pltpu.VMEM((2, SEQLEN, HD), BF16)] * 2
        + [pltpu.VMEM((count, PAIR, chunk), BF16)] * 2
        + [pltpu.VMEM((steps, PAIR, BQ), BF16)] * 2
        + [pltpu.VMEM((PAIR, BQ), F32)]
        + [pltpu.VMEM((count, PAIR, chunk), F32)] * 2,
        [*qkv, *grads, wide, lse], 0, 0, "attend_backward", (flow.scal, ends),
    )


def flip(values_in, axes, mask):
    return lax.ppermute(values_in, axes, [(a, a ^ mask) for a in range(lax.axis_size(axes))])


def turn(values_in):
    return lax.ppermute(values_in, ("c", "zh"), [(2 * a + b, 2 * b + a) for a in range(2) for b in range(2)])


def uncross(values_in):
    return lax.ppermute(values_in, ("c", "zh"), [(2 * b + 1 - a, 2 * a + b) for a in range(2) for b in range(2)])


def from_members(values_in, axes):
    return [values_in] + [flip(values_in, axes, r) for r in range(1, lax.axis_size(axes))]


def to_members(parts, axes):
    return [parts[0]] + [flip(part, axes, r) for r, part in enumerate(parts) if r > 0]


def add(*parts):
    total = parts[0].astype(F32)
    for part in parts[1:]:
        total = total + part.astype(F32)
    return total


def is_small():
    return lax.axis_size("q") == 4


def order_by(values_in, axis, position, count):
    bit = 1
    while bit < count:
        shape = values_in.shape
        split = shape[:axis] + (count // (2 * bit), 2, bit) + shape[axis + 1 :]
        cut = values_in.reshape(split)
        values_in = jnp.where((position & bit) != 0, jnp.flip(cut, axis + 1), cut).reshape(shape)
        bit *= 2
    return values_in


def gather_group(values_in):
    across, sibling = flip(values_in, GROUP, 1), flip(values_in, GROUP, 2)
    return [values_in, across, sibling]


def forward(flow, members, *before):
    flow.wait(*before)
    flow.hold(across=members[1])
    gate(flow)
    members[1] = flow.free("across")
    members.append(flip(members[1], GROUP, 2))


def sum_group(keep, send):
    got = flip(send, GROUP, 2)
    passed = add(keep[1], got[1]).astype(BF16)
    return [keep[0], got, flip(passed, GROUP, 1)], passed


EXTRA = 16


def heads_shard_of(qkv, out, bias):
    rows = out.shape[0]
    paired = qkv.reshape(3, rows, -1, PAIR).transpose(1, 2, 0, 3).reshape(rows, -1)
    weights = jnp.concatenate([paired, out], axis=1)
    below = jnp.pad(bias.reshape(1, -1), ((0, EXTRA - 1), (0, weights.shape[1] - bias.size)))
    return jnp.concatenate([weights, below])


def heads_bias(rows, heads):
    bias = rows.reshape(rows.shape[0], 2, heads, -1).transpose(1, 2, 0, 3).reshape(2, -1).astype(F32)
    bias = jnp.stack([bias[0], jnp.zeros_like(bias[0]), bias[1]])
    return bias.reshape(3, -1, PAIR).transpose(1, 0, 2).reshape(1, -1)


def with_sibling(shard):
    return jnp.stack([shard, flip(shard, "c", 1)])


def heads_along_x(pair):
    return jnp.stack([pair, flip(pair, "q", 1)])


def heads_along_y(near, size, heads, where, zh):
    return heads_pieces(near, flip(near, "q", 2), size, heads, where, zh)


def heads_pieces(near, far, size, heads, where, zh):
    rows = jnp.concatenate([near[:, :, ROWS, :size], far[:, :, ROWS, :size]])
    return [near, far], heads_bias(order_by(order_by(rows, 0, where[0], 4), 1, zh, 2).reshape(8, size), heads)


def all_heads_weight(shard, size, heads, zh):
    pair = turn(with_sibling(shard))
    every = order_by(lax.all_gather(pair, "q"), 1, zh, 2)
    count = shard.shape[0] - EXTRA
    weights = every[:, :, :count].reshape(4, 2, ROWS, -1)
    return [weights[:2], weights[2:]], heads_bias(every[:, :, count, :size].reshape(-1, size), heads)


class HeadsGrad:
    def __init__(self, keep, send):
        self.keep, self.send = keep, send

    def along_x(self):
        self.got = flip(self.send, "q", 1)
        return self.got

    def along_y(self):
        self.got_x = self.got
        self.got = flip(add(self.keep[1], self.got[1]).astype(BF16), "q", 2)
        return self.got

    def halves(self, zh):
        if is_small():
            return tuple(add(self.keep[0, k], self.got_x[0, k], self.got[k]).astype(BF16) for k in range(2))
        buckets = [self.keep[0], self.send[0], self.keep[1], self.send[1]]
        every = jnp.stack(buckets).reshape(lax.axis_size("q"), 2, -1, buckets[0].shape[-1])
        rows = order_by(lax.psum_scatter(every, "q", scatter_dimension=0, tiled=False), 0, zh, 2)
        return rows[0], rows[1]


SLOTS = (0, 2, 1, 3)


def all_units_weight(shard):
    matrices, _, width = shard.shape
    members = lax.axis_size(MODEL)
    every = lax.all_gather(shard, ALL).reshape(members, -1, matrices, shard.shape[1], width).transpose(0, 2, 1, 3, 4)
    every = every.reshape(members, matrices, 4, 2, ROWS, width)
    every = jnp.stack([every[slot] for slot in SLOTS])
    pieces = []
    for k in range(2):
        pieces += [every[:, :, r, k] for r in range(3)] + [every[:2, :, 3, k], every[2:, :, 3, k]]
    return pieces


class UnitsWeight:
    def __init__(self, shard):
        self.shard, self.theirs = shard, {}

    def start_far_z(self):
        self.other = flip(self.shard, "zh", 1)

    def join_far_z(self, shard):
        self.two = jnp.stack([shard, self.other])

    def far_z(self):
        self.start_far_z()
        self.join_far_z(self.shard)

    def start_z(self):
        self.other = flip(self.two, "zl", 1)

    def join_z(self, two):
        self.own = jnp.concatenate([two, self.other])

    def near_z(self):
        self.start_z()
        self.join_z(self.two)

    def near(self):
        self.near_x, self.near_y = flip(self.own, "q", 1), flip(self.own, "q", 2)

    def corner(self):
        self.far_a, self.far_b = flip(self.near_y[:2], "q", 1), flip(self.near_x[2:], "q", 2)

    def swap(self, *names):
        for name in names:
            self.theirs[name] = flip(getattr(self, name), "c", 1)

    def pieces(self):
        names = ("own", "near_x", "near_y", "far_a", "far_b")
        return [getattr(self, name) for name in names] + [self.theirs[name] for name in names]


class UnitsGrads:
    def __init__(self, flow, down, up, count):
        self.flow, self.down, self.up, self.count = flow, down, up, count

    def compute_theirs(self):
        self.theirs = unit_grads(self.flow, self.down, self.up, None, self.count, True)

    def send_theirs(self):
        self.got = flip(self.theirs, "c", 1) if is_small() else None

    def sibling(self):
        self.compute_theirs()
        self.send_theirs()

    def mine(self):
        self.made = unit_grads(self.flow, self.down, self.up, self.got, self.count, False)
        self.own, self.to_x, self.to_y, self.rest_x, self.rest_y = self.made

    def near(self):
        self.from_x, self.from_y = flip(self.to_x, "q", 1), flip(self.to_y, "q", 2)
        return [self.from_x, self.from_y]

    def far(self):
        half = self.count
        self.late_x = flip(add(self.rest_x, self.from_y[half:]).astype(BF16), "q", 1)
        self.late_y = flip(add(self.rest_y, self.from_x[half:]).astype(BF16), "q", 2)
        return [self.late_x, self.late_y]

    def near_z(self):
        half = self.count
        self.passing = add(self.own[half:], self.late_x, self.from_y[:half]).astype(BF16)
        self.there = flip(self.passing, "zl", 1)
        return [self.there]

    def far_z(self):
        self.last = flip(self.near_sum(slice(self.count // 2, self.count)).astype(BF16), "zh", 1)
        return [self.last]

    def near_sum(self, blocks):
        return add(self.own[blocks], self.from_x[blocks], self.late_y[blocks], self.there[blocks])

    def parts(self):
        return self.own, self.from_x, self.late_y, self.there, self.last

    def total(self):
        half = self.count
        mine = jnp.stack(
            [self.own, jnp.concatenate([self.to_x[:half], self.rest_x]), jnp.concatenate([self.rest_y, self.to_y[:half]]),
             jnp.concatenate([self.to_x[half:], self.to_y[half:]])]
        ).reshape(4, self.count, 2, ROWS, -1)
        theirs = self.theirs.reshape(4, 2, self.count, ROWS, -1).transpose(0, 2, 1, 3, 4)
        every = jnp.stack([mine, theirs], axis=1)
        every = every.transpose(2, 0, 1, 4, 3, 5)
        every = jnp.stack([every[slot] for slot in SLOTS]).reshape(-1, 2, mine.shape[-1])
        return lax.psum_scatter(every, ALL, scatter_dimension=0, tiled=True).astype(F32).transpose(1, 0, 2)


SMALL_AXES = ("q", MODEL, "c")
SMALL_STEPS = (("q", 1), ("q", 2), ("zl", 1), ("zh", 1), ("c", 1))
SMALL_SHAPE = (128, 256)


def spread_by_distance(values_in, where):
    every = values_in.reshape(4, 4, 2, -1).transpose(1, 0, 2, 3)
    for axis, position in enumerate(where):
        every = order_by(every, axis, position, every.shape[axis])
    return every.transpose(2, 1, 0, 3).reshape(32, -1)


def fold_small(every, first, last):
    for axis, mask in SMALL_STEPS[::-1][first:last]:
        half = every.shape[0] // 2
        every = every[:half] + flip(every[half:], axis, mask)
    return every


def sum_all(value):
    if not is_small():
        return lax.psum(value, ALL)
    for axes in SMALL_AXES:
        parts = jnp.stack(from_members(value, axes))
        value = jnp.sum(order_by(parts, 0, lax.axis_index(axes), parts.shape[0]), 0)
    return value[0, 0]


def on_device(
    tokens, doc_lengths, qkv_weight, qv_bias, out_weight, up_weight, up_bias, down_weight, gains, shifts, cotangent
):
    layers = qkv_weight.shape[0]
    tz, dp = lax.axis_size(MODEL), lax.axis_size(("q", "c"))
    place, zh = lax.axis_index(GROUP), lax.axis_index("zh")
    where = (lax.axis_index("q"), lax.axis_index(MODEL), lax.axis_index("c"))
    if is_small():
        spots = [place, where[0], where[2], zh, where[1]]
    else:
        spots = [place] + [jnp.zeros((), jnp.int32)] * 4
    scal = jnp.stack([spot.astype(jnp.int32) for spot in spots])

    flow = Flow(scal)
    small_slice = is_small()
    qkv_cols, out_cols = 3 * out_weight.shape[2], out_weight.shape[2]
    in_cols, out_cols = slice(0, qkv_cols), slice(qkv_cols, qkv_cols + out_cols)
    hz, bias_size = qv_bias.shape[2], qv_bias.size // layers
    heads_shard = [heads_shard_of(qkv_weight[l], out_weight[l], qv_bias[l]) for l in range(layers)]
    pieces = [up_bias, gains, shifts]
    sizes = [piece.size // layers for piece in pieces]
    cuts = [0]
    for size in sizes:
        cuts.append(cuts[-1] + size)
    small = jnp.concatenate([piece.reshape(layers, -1) for piece in pieces], axis=1).reshape(-1)
    padded = jnp.pad(small, (0, SMALL_SHAPE[0] * SMALL_SHAPE[1] - small.size)).reshape(SMALL_SHAPE)
    gathered = lax.all_gather(padded, ALL)
    small_all = gathered.reshape(tz * dp, -1)[:, : small.size]

    def spread_small():
        every = small_all.reshape(tz, dp, layers, -1).astype(F32)
        parts = [every[..., cuts[i] : cuts[i + 1]] for i in range(3)]
        biases = parts[0].reshape(tz, dp, layers, up_bias.shape[1], -1).transpose(2, 0, 3, 1, 4)
        gain = parts[1].reshape(tz, dp, layers, 2, -1).transpose(2, 3, 1, 0, 4).reshape(layers, 2, D)
        shift = parts[2].reshape(tz, dp, layers, 4, -1).transpose(2, 3, 1, 0, 4).reshape(layers, 4, D)
        table = jnp.concatenate([gain, shift], axis=1).reshape(layers * 6, D)
        head = jnp.concatenate([jnp.ones((1, D), F32), jnp.zeros((1, D), F32)])
        return biases.reshape(layers, tz, 1, -1), jnp.pad(jnp.concatenate([head, table]), ((0, TABLE - 2 - 6 * layers), (0, 0)))

    up_bias_full, table = spread_small()
    if small_slice:
        pair = with_sibling(heads_shard[0])
        bundle = turn(jnp.concatenate([tokens, pair.reshape(-1, D)]))
        x_low, pair = bundle[: tokens.shape[0]], bundle[tokens.shape[0] :].reshape(pair.shape)
        ends = jnp.cumsum(turn(doc_lengths)[0], dtype=jnp.int32)
        members = from_members(pair, "q")
        weights_of = [heads_pieces(jnp.stack(members[:2]), jnp.stack(members[2:]), bias_size, hz, where, zh)]
        up0, down0 = UnitsWeight(up_weight[0][None]), UnitsWeight(down_weight[0][None])
        both1 = UnitsWeight(jnp.stack([up_weight[1], down_weight[1]]))
        flow.hold(
            up0=up0.shard, up0_twin=up0.shard, up0_last=up0.shard, down0=down0.shard, down0_twin=down0.shard, both1=both1.shard,
            heads1=heads_shard[1], low=x_low,
        )
        gate(flow)
        x_low = flow.free("low")
    else:
        x_low = turn(tokens)
        ends = jnp.cumsum(turn(doc_lengths)[0], dtype=jnp.int32)
        weights_of = [all_heads_weight(shard, bias_size, hz, zh) for shard in heads_shard]
        every = [all_units_weight(jnp.stack([up_weight[l], down_weight[l]])) for l in range(layers)]
        top_grad = turn(cotangent)

    prev, prev_gain, prev_shift = x_low, ONE, ZERO
    kept = []
    for l in range(layers):
        first, last = small_slice and l == 0, small_slice and l == 1
        xs = gather_group(x_low)
        w_heads, bias = weights_of[l]
        qkv_near = project_in(flow, (xs[0], xs[2]), False, w_heads, in_cols, bias, "project_qkv")
        if first:
            up0.shard = flow.free("up0")
            up0.start_far_z()
            flow.wait(up0.other)
        if last:
            flow.hold(top=cotangent, own=both1.own)
        forward(flow, xs, qkv_near)
        if first:
            twin, down0.shard = flow.free("up0_twin"), flow.free("down0")
            up0.join_far_z(twin)
            across = up0.other
            up0.start_z()
            down0.start_far_z()
        if last:
            both1.own = flow.free("own")
            both1.near()
        qkv_far = project_in(flow, (xs[1], xs[3]), True, w_heads, in_cols, bias, "project_qkv")
        qkv = (qkv_near, qkv_far)
        if first:
            down0.join_far_z(flow.free("down0_twin"))
            up0.join_z(jnp.stack([flow.free("up0_last"), across]))
            up0.near()
            down0.near_z()
            both1.shard = flow.free("both1")
            both1.far_z()
        if last:
            top_grad = turn(flow.free("top"))
            both1.swap("own")
        ctx, wide, lse = attend_forward(flow, ends, qkv)
        if first:
            flow.wait(up0.near_x, up0.near_y)
            flow.hold(both1=both1.two, down0=down0.own)
            up0.corner()
            up0.swap("own")
        if last:
            flow.wait(both1.near_x, both1.near_y, top_grad)
            both1.corner()
            both1.swap("near_x", "near_y")
        send = project_out(flow, [ctx], (2, 3), w_heads, out_cols, True, "project_attn")
        flow.wait(send)
        keep = project_out(flow, [ctx], (0, 1), w_heads, out_cols, False, "project_attn")
        attn, passed = sum_group(keep, send)
        if first:
            flow.wait(passed, gathered)
            flow.hold(near_x=up0.near_x, near_y=up0.near_y)
            gate(flow)
            down0.own, up0.near_x, up0.near_y = flow.free("down0"), flow.free("near_x"), flow.free("near_y")
            up0.swap("near_x", "near_y", "far_a", "far_b")
            down0.near()
            down0.swap("own")
            flow.wait(down0.near_x, down0.near_y)
            down0.corner()
            down0.swap("near_x", "near_y")
            pair = with_sibling(flow.free("heads1"))
            flow.hold(pair=pair)
            w_up = up0.pieces(), 0
        elif last:
            flow.wait(passed)
            flow.hold(ends=ends)
            gate(flow)
            ends = flow.free("ends")
            flow.hold(far_a=both1.far_a, far_b=both1.far_b)
            flow.wait(attn[2])
            gate(flow)
            both1.far_a, both1.far_b = flow.free("far_a"), flow.free("far_b")
            both1.swap("far_a", "far_b")
            w_up, w_down = (both1.pieces(), 0), (both1.pieces(), 1)
        else:
            w_up, w_down = (every[l], 0), (every[l], 1)
        used = (prev_gain, prev_shift, shift_row(l, 0), gain_row(l, 0), shift_row(l, 1))
        n1, hs, r1, act, slope = norm_up(flow, prev, attn, table, used, *w_up, up_bias_full[l], tz)
        if first:
            pair = turn(flow.free("pair"))
            flow.wait(n1)
            flow.hold(far_a=down0.far_a, far_b=down0.far_b)
            gate(flow)
            down0.far_a, down0.far_b = flow.free("far_a"), flow.free("far_b")
            down0.swap("far_a", "far_b")
            both1.two = flow.free("both1")
            both1.near_z()
            flow.wait(pair)
            w_down = down0.pieces(), 0
        used = (gain_row(l, 0), shift_row(l, 1), shift_row(l, 2), gain_row(l, 1), shift_row(l, 3))
        n2, y_low, r2 = down_norm(flow, act, *w_down, n1, table, used, tz)
        if first:
            members = from_members(pair, "q")
            weights_of.append(heads_pieces(jnp.stack(members[:2]), jnp.stack(members[2:]), bias_size, hz, where, zh))
        kept.append((xs, qkv, ctx, wide, lse, n1, hs, r1, act, slope, n2, r2, w_heads, w_up, w_down))
        x_low, prev, prev_gain, prev_shift = y_low, n2, gain_row(l, 1), shift_row(l, 3)
    layer_output = turn(x_low)

    residual, back = top_grad, []
    small_grads = [None] * layers
    units_of, heads_of = [None] * layers, [None] * layers
    above = above_heads = None
    for l in reversed(range(layers)):
        top = l == layers - 1
        xs, qkv, ctx, wide, lse, n1, hs, r1, act, slope, n2, r2, w_heads, w_up, w_down = kept[l]
        beside = small_slice and not top
        g2, gf, sums2, gu, up_bias_sum = units_back(
            flow, residual, back, n2, r2, table, gain_row(l, 1), *w_down, slope, tz
        )
        units = UnitsGrads(flow, (gf, act), (hs, gu), tz)
        if top:
            flow.hold(output=layer_output)
        else:
            if beside:
                flow.wait(*above.near())
                flow.hold(heads=above_heads.send)
            units.sibling()
            flow.wait(units.theirs)
            if beside:
                above_heads.send = flow.free("heads")
                above_heads.along_x()
                late = above.far()
        g1, ga, sums1 = up_back(flow, gu, *w_up, g2, n1, r1, table, gain_row(l, 0), tz)
        gas = gather_group(ga)
        flow.wait(ga)
        if top:
            layer_output = flow.free("output")
            units.compute_theirs()
            forward(flow, gas, units.theirs)
        else:
            units.mine()
            if beside:
                flow.wait(*late)
            forward(flow, gas, *units.made)
        gc_near = project_in(flow, (gas[0], gas[2]), False, w_heads, out_cols, None, "project_gc")
        flow.wait(gc_near)
        if top:
            flow.hold(theirs=units.theirs)
        gc_far = project_in(flow, (gas[1], gas[3]), True, w_heads, out_cols, None, "project_gc")
        if top:
            units.theirs = flow.free("theirs")
            units.send_theirs()
        gcs = (gc_near, gc_far)
        if beside:
            early = above.near_z()
            flow.hold(rest_x=units.rest_x, rest_y=units.rest_y, keep=above_heads.keep, above=above.own)
        gqkv = [attend_backward(flow, ends, 0, qkv, gcs, wide, lse)]
        if beside:
            units.rest_x, units.rest_y = flow.free("rest_x"), flow.free("rest_y")
            above_heads.keep, above.own = flow.free("keep"), flow.free("above")
        flow.wait(gqkv[0])
        if beside:
            flow.wait(*units.near(), *early, above_heads.got)
            above.far_z()
            units.far()
            above_heads.along_y()
            flow.hold(own=units.own, keep=above_heads.keep)
        gqkv.append(attend_backward(flow, ends, 1, qkv, gcs, wide, lse))
        if beside:
            units.own, above_heads.keep = flow.free("own"), flow.free("keep")
            units.near_z()
            flow.wait(units.passing, units.late_y, above.last, above_heads.got)
            above_halves = above_heads.halves(zh)
        send = project_out(flow, gqkv, (2, 3), w_heads, in_cols, True, "project_gx")
        flow.wait(send)
        if beside:
            flow.hold(own=units.own)
        keep = project_out(flow, gqkv, (0, 1), w_heads, in_cols, False, "project_gx")
        back, passed = sum_group(keep, send)
        flow.wait(passed)
        if top:
            units.mine()
            flow.wait(*units.made)
        elif small_slice:
            units.own = flow.free("own")
            units.far_z()
        *buckets, qkv_sums = heads_grad(flow, xs, gqkv, gas, ctx)
        heads = HeadsGrad(*buckets)
        units_of[l], heads_of[l] = units, heads
        qv_sums = qkv_sums.reshape(-1, 3, PAIR).transpose(1, 0, 2).reshape(3, hz, dp, -1)
        qv_sums = jnp.stack([qv_sums[0], qv_sums[2]]).transpose(2, 0, 1, 3).reshape(1, dp, -1)
        mine = (jnp.arange(tz) == place).astype(F32).reshape(tz, 1, 1)
        small_grads[l] = jnp.concatenate(
            [
                mine * qv_sums,
                up_bias_sum.reshape(tz, up_bias.shape[1], dp, -1).transpose(0, 2, 1, 3).reshape(tz, dp, -1),
                jnp.stack([sums1[0], sums2[0]]).reshape(2, dp, tz, -1).transpose(2, 1, 0, 3).reshape(tz, dp, -1),
                jnp.stack([sums1[2], sums1[1], sums2[2], sums2[1]])
                .reshape(4, dp, tz, -1).transpose(2, 1, 0, 3).reshape(tz, dp, -1),
            ],
            axis=-1,
        )
        if l > 0:
            above, above_heads = units, heads
            flow.wait(heads.send)
            residual = g1
    small_sums = jnp.stack(small_grads, axis=2).reshape(tz, dp, -1)
    if small_slice:
        heads.along_x()
        small_sums = fold_small(spread_by_distance(small_sums, where), 0, 1)
        flow.wait(back[2])
        flow.hold(small=small_sums, got=heads.got)
        gate(flow)
        small_sums, heads.got = flow.free("small"), flow.free("got")
        input_grad = turn(add(g1, back[0], back[1][0], back[2]).astype(BF16))
        heads.along_y()
        small_sums = fold_small(small_sums, 1, 2)
        flow.wait(heads.got, units.last)
        flow.hold(small=small_sums)
        gate(flow)
        small_sums = fold_small(flow.free("small"), 2, 3)
        halves = heads.halves(zh)
        small_out = fold_small(small_sums, 3, 5).reshape(layers, -1)
        stacked = [jnp.stack([half, above_half]) for half, above_half in zip(halves, above_halves)]
        arrived = turn(stacked[0]), uncross(stacked[1])
        flow.hold(grad=input_grad, output=layer_output)
        qkv_grad, out_grad, up_grad, down_grad, squares = finish(
            flow, [member.parts() for member in units_of], arrived, small_out
        )
        input_grad, layer_output = flow.free("grad"), flow.free("output")
    else:
        halves = [member.halves(zh) for member in heads_of]
        d_heads = jnp.stack([add(turn(half[0]), uncross(half[1])) for half in halves])
        input_grad = turn(add(g1, back[0], back[1][0], back[2]).astype(BF16))
        small_out = lax.psum_scatter(small_sums.reshape(tz * dp, -1), ALL, scatter_dimension=0, tiled=True)
        small_out = small_out.reshape(layers, -1)
        qkv_grad = d_heads[:, :, : in_cols.stop].reshape(layers, d_heads.shape[1], -1, 3, PAIR)
        qkv_grad = qkv_grad.transpose(0, 3, 1, 2, 4).reshape(qkv_weight.shape)
        out_grad = d_heads[:, :, in_cols.stop :]
        totals = [member.total() for member in units_of]
        down_grad, up_grad = (jnp.stack([total[i] for total in totals]) for i in range(2))
        squares = sum(jnp.sum(member * member) for member in (qkv_grad, out_grad, up_grad, down_grad, small_out))

    rest = small_out[:, bias_size:]
    qv_bias_grad = small_out[:, :bias_size].reshape(qv_bias.shape)
    up_bias_grad = rest[:, cuts[0] : cuts[1]].reshape(up_bias.shape)
    gains_grad = rest[:, cuts[1] : cuts[2]].reshape(gains.shape)
    shifts_grad = rest[:, cuts[2] : cuts[3]].reshape(shifts.shape)
    entry_count = LAYERS * (4 * D * D + 2 * D * FF + FF + 8 * D)
    grad_rms = jnp.sqrt(sum_all(squares) / entry_count)
    return (
        layer_output, input_grad, qkv_grad, qv_bias_grad, out_grad, up_grad, up_bias_grad, down_grad, gains_grad,
        shifts_grad, grad_rms,
    )


def solution(mesh):
    dp, tensor = mesh.shape["dp"], mesh.shape["tensor"]
    fine = Mesh(mesh.devices.reshape(dp // 2, 2, 2, tensor // 2), ("q", "c", "zh", "zl"))
    data, model = ("q", "c"), ("zh", "zl")
    both = data + model
    weight3, weight4 = P(None, data, model), P(None, None, data, model)
    in_specs = (
        P(both, None), P(data, None), weight4, P(None, None, model, data), weight3, weight3, P(None, model, data),
        weight3, P(None, None, both), P(None, None, both), P(both, None),
    )
    out_specs = (
        P(both, None), P(both, None), weight4, P(None, None, model, data), weight3, weight3, P(None, model, data),
        weight3, P(None, None, both), P(None, None, both), P(),
    )
    return jax.shard_map(on_device, mesh=fine, in_specs=in_specs, out_specs=out_specs, check_vma=False)
```

```python
import jax
import jax.numpy as jnp
from jax import lax
from jax.experimental import pallas as pl
from jax.experimental.pallas import tpu as pltpu
from jax.sharding import Mesh
from jax.sharding import PartitionSpec as P

D = 1024
HD = 64
HEADS = 16
FF = 4096
LAYERS = 2
SEQLEN = 2048
WINDOW = 1024
EPS = 1e-06
FILL = -1000000000.0

F32 = jnp.float32
BF16 = jnp.bfloat16
GROUP = ("c", "zl")
MODEL = ("zh", "zl")
ALL = ("zh", "zl", "q", "c")
VMEM_LIMIT = 56 * 1024 * 1024
TIMES = {
    "gate": 0.1, "finish": 0.2, "norm_up": 20.0, "down_norm": 20.0, "units_back": 45.0, "up_back": 20.0, "norm_back": 6.0,
    "sum_norm_back": 20.0, "grads_theirs": 0.2, "grads_mine": 0.2, "project_qkv": 0.2, "project_gc": 0.2,
    "project_attn": 0.2, "project_gx": 0.2, "heads_grad": 0.2, "attend_forward": 40.0, "attend_backward": 30.0,
}
PEAK = 0.35e9
NT = (((1,), (1,)), ((), ()))
NN = (((1,), (0,)), ((), ()))
ROWS = 128
CHUNK = 64
BQ = 512
PAIR = 2 * HD


def mm(left, right, dims=NN):
    return lax.dot_general(left, right, dims, preferred_element_type=F32)


def full(shape):
    return pl.BlockSpec(shape, lambda *_: (0,) * len(shape))


ANY = pl.BlockSpec(memory_space=pl.ANY)


def sds(shape, kind):
    return jax.ShapeDtypeStruct(shape, kind)


class Flow:
    def __init__(self, scal):
        self.scal, self.before, self.held = scal, [], {}

    def wait(self, *arrays):
        self.before += arrays

    def hold(self, **arrays):
        self.held.update(arrays)

    def free(self, name):
        return self.held.pop(name)


def call(flow, body, grid, in_specs, out_specs, out_shape, scratch, args, flops, traffic, name, scalars=None):
    scalars = (flow.scal,) if scalars is None else scalars
    single = not isinstance(out_specs, (list, tuple))
    out_specs = [out_specs] if single else list(out_specs)
    out_shape = [out_shape] if single else list(out_shape)
    before, held = flow.before, list(flow.held.items())
    ns, nb, nh, no = len(scalars), len(before), len(held), len(out_specs)
    first, last = ns + nb + nh, ns + nb + nh + len(args) + no

    def wrapped(*refs):
        body(*refs[:ns], *refs[first:last], *refs[last + nh :])

    result = pl.pallas_call(
        wrapped,
        grid_spec=pltpu.PrefetchScalarGridSpec(
            num_scalar_prefetch=ns,
            grid=grid,
            in_specs=[ANY] * (nb + nh) + list(in_specs),
            out_specs=out_specs + [ANY] * nh,
            scratch_shapes=scratch,
        ),
        out_shape=out_shape + [sds(array.shape, array.dtype) for _, array in held],
        input_output_aliases={ns + nb + i: no + i for i in range(nh)},
        compiler_params=pltpu.CompilerParams(
            dimension_semantics=("arbitrary",) * len(grid), vmem_limit_bytes=VMEM_LIMIT
        ),
        cost_estimate=pl.CostEstimate(flops=int(TIMES[name] * PEAK), bytes_accessed=1024, transcendentals=0),
        name=name,
    )(*scalars, *before, *[array for _, array in held], *args)
    flow.before = []
    flow.held = {key: value for (key, _), value in zip(held, result[no:])}
    return result[0] if single else result[:no]


def gate(flow):
    if flow.held:
        call(flow, lambda *refs: None, (1,), [], [], [], [], [], 0, 0, "gate")


S_P, S_Q, S_C, S_ZH, S_Z = range(5)


def norm_rows(values_in):
    centred = values_in - jnp.mean(values_in, -1, keepdims=True)
    variance = jnp.mean(centred * centred, -1, keepdims=True)
    inverse = lax.rsqrt(variance + EPS)
    return centred * inverse, inverse


def norm_back_rows(grad, normed, inverse, gain):
    scaled = grad * gain
    centred = scaled - jnp.mean(scaled, -1, keepdims=True) - normed * jnp.mean(scaled * normed, -1, keepdims=True)
    return centred * inverse


def fold_rows(values_in):
    return jnp.sum(values_in.reshape(-1, 8, values_in.shape[-1]), 0)


def read(part, rows):
    return (part[0, rows, :] if len(part.shape) == 3 else part[rows, :]).astype(F32)


def part_spec(part):
    shape = part.shape
    return full(shape) if len(shape) == 2 else pl.BlockSpec((1,) + shape[1:], lambda *_: (0, 0, 0))


ONE, ZERO, TABLE = 0, 1, 16


def gain_row(layer, index):
    return 2 + 6 * layer + index


def shift_row(layer, index):
    return 4 + 6 * layer + index


def row_of(vec_ref, row):
    return vec_ref[row : row + 1, :]


def norm_forward(get_total, tokens, vec, gain, shift, n_ref, low_ref, inv_ref):

    def step(index, carry):
        rows = pl.ds(pl.multiple_of(index * CHUNK, CHUNK), CHUNK)
        normed, inverse = norm_rows(get_total(rows))
        n_ref[rows, :] = normed
        low_ref[rows, :] = (normed * row_of(vec, gain) + row_of(vec, shift)).astype(BF16)
        inv_ref[rows, :] = jnp.broadcast_to(inverse, (CHUNK, 128))
        return carry

    lax.fori_loop(0, tokens // CHUNK, step, 0)


def norm_backward(get_grad, tokens, n_ref, inv_ref, vec, gain, g_ref, low_ref, sums_ref):
    def step(index, carry):
        rows = pl.ds(pl.multiple_of(index * CHUNK, CHUNK), CHUNK)
        grad = get_grad(rows)
        normed = n_ref[rows, :]
        result = norm_back_rows(grad, normed, inv_ref[rows, 0:1], row_of(vec, gain))
        low = result.astype(BF16)
        g_ref[rows, :] = result
        low_ref[rows, :] = low
        return (
            carry[0] + fold_rows(grad * normed),
            carry[1] + fold_rows(grad),
            carry[2] + fold_rows(low.astype(F32)),
        )

    zero = jnp.zeros((8, D), F32)
    sums = lax.fori_loop(0, tokens // CHUNK, step, (zero, zero, zero))
    sums_ref[...] = jnp.zeros(sums_ref.shape, F32)
    for row, member in enumerate(sums):
        sums_ref[row : row + 1, :] = jnp.sum(member, 0, keepdims=True)


def away(s):
    return (s & 1) * 2 + s // 2


class Streamed:
    def __init__(self, refs, matrix, buffer, sems, scal):
        self.refs, self.matrix, self.buffer, self.sems, self.scal = refs, matrix, buffer, sems, scal

    def copies(self, s):
        slot = lax.rem(s, 2)
        plain, early, late = [], [], []
        for k in range(2):
            own, near_x, near_y, far_a, far_b = self.refs[5 * k : 5 * k + 5]

            def copy(source, r, k=k):
                row = ((self.scal[S_Q] ^ r) * 2 + (self.scal[S_C] ^ k)) * ROWS
                return pltpu.make_async_copy(
                    source, self.buffer.at[slot, pl.ds(pl.multiple_of(row, ROWS), ROWS), :], self.sems.at[slot, 4 * k + r]
                )

            for r, ref in enumerate((own, near_x, near_y)):
                plain.append(copy(ref.at[s, self.matrix], r))
            early.append(copy(far_a.at[jnp.minimum(s, 1), self.matrix], 3))
            late.append(copy(far_b.at[jnp.maximum(s - 2, 0), self.matrix], 3))
        return plain, early, late

    def each(self, s, act):
        plain, early, late = self.copies(s)
        for copy in plain:
            act(copy)

        @pl.when(s < 2)
        def _():
            for copy in early:
                act(copy)

        @pl.when(s >= 2)
        def _():
            for copy in late:
                act(copy)

    def start(self, s):
        self.each(s, lambda copy: copy.start())

    def wait(self, s):
        self.each(s, lambda copy: copy.wait())

    def turn(self, s, count):
        @pl.when(s == 0)
        def _():
            self.start(s)

        @pl.when(s + 1 < count)
        def _():
            self.start(s + 1)


def piece_shapes(width):
    return [pltpu.VMEM((2, D, width), BF16), pltpu.SemaphoreType.DMA((2, 8))]


def gelu_parts(u):
    size = jnp.abs(u)
    t = 1.0 / (1.0 + 0.2316419 * size)
    poly = t * (0.127414796 + t * (-0.142248368 + t * (0.7107068705 + t * (-0.7265760135 + t * 0.5307027145))))
    bell = jnp.exp(-0.5 * (u * u))
    tail = poly * bell
    cdf = jnp.where(u >= 0, 1.0 - tail, tail)
    return u * cdf, cdf + u * (0.3989422804014327 * bell)


def tiles(tokens, width):
    for i in range(2):
        for j in range(2):
            yield slice(i * tokens // 2, (i + 1) * tokens // 2), slice(j * width // 2, (j + 1) * width // 2)


def norm_up(flow, prev, parts, vec, rows_used, weight, matrix, bias, count):
    tokens = prev.shape[0]
    width = FF // count

    def body(scal_ref, prev_ref, *refs):
        part_refs, refs = refs[: len(parts)], refs[len(parts) :]
        vec_ref, bias_ref, refs = refs[0], refs[1], refs[2:]
        pieces, (n_ref, low_ref, inv_ref, act_ref, slope_ref, buffer, sems) = refs[:10], refs[10:]
        s = pl.program_id(0)
        stream = Streamed(pieces, matrix, buffer, sems, scal_ref)
        stream.turn(s, count)

        @pl.when(s == 0)
        def _():
            def total(rows):
                attn = read(part_refs[0], rows)
                for part in part_refs[1:]:
                    attn = attn + read(part, rows)
                before = read(prev_ref, rows) * row_of(vec_ref, rows_used[0]) + row_of(vec_ref, rows_used[1])
                return before + (attn + row_of(vec_ref, rows_used[2]))

            norm_forward(total, tokens, vec_ref, *rows_used[3:], n_ref, low_ref, inv_ref)

        stream.wait(s)
        slot = lax.rem(s, 2)
        for rows, cols in tiles(tokens, width):
            act, slope = gelu_parts(mm(low_ref[rows, :], buffer[slot, :, cols]) + bias_ref[0, :, cols])
            act_ref[rows, cols] = act.astype(BF16)
            slope_ref[rows, cols] = slope.astype(BF16)

    column = pl.BlockSpec((tokens, width), lambda s, _: (0, s))
    return call(
        flow, body, (count,),
        [full((tokens, D))] + [part_spec(part) for part in parts]
        + [full((TABLE, D)), pl.BlockSpec((1, 1, width), lambda s, scal_ref: (scal_ref[S_Z] ^ away(s), 0, 0))] + [ANY] * 10,
        [full((tokens, D)), full((tokens, D)), full((tokens, 128)), column, column],
        [sds((tokens, D), F32), sds((tokens, D), BF16), sds((tokens, 128), F32)] + [sds((tokens, FF), BF16)] * 2,
        piece_shapes(width), [prev, *parts, vec, bias, *weight], 2 * tokens * D * FF,
        2 * (D * FF + tokens * (10 * D + 2 * FF)), "norm_up",
    )


def down_norm(flow, act, weight, matrix, prev, vec, rows_used, count):
    tokens = prev.shape[0]
    width = FF // count

    def body(scal_ref, act_ref, prev_ref, vec_ref, *refs):
        pieces, (n_ref, low_ref, inv_ref, buffer, sems, acc) = refs[:10], refs[10:]
        s = pl.program_id(0)
        stream = Streamed(pieces, matrix, buffer, sems, scal_ref)
        stream.turn(s, count)
        stream.wait(s)
        value = mm(act_ref[...], buffer[lax.rem(s, 2)], NT)

        @pl.when(s == 0)
        def _():
            acc[...] = value

        @pl.when(s > 0)
        def _():
            acc[...] += value

        @pl.when(s == count - 1)
        def _():
            def total(rows):
                before = prev_ref[rows, :] * row_of(vec_ref, rows_used[0]) + row_of(vec_ref, rows_used[1])
                return before + (acc[rows, :] + row_of(vec_ref, rows_used[2]))

            norm_forward(total, tokens, vec_ref, *rows_used[3:], n_ref, low_ref, inv_ref)

    return call(
        flow, body, (count,),
        [pl.BlockSpec((tokens, width), lambda s, _: (0, s)), full((tokens, D)), full((TABLE, D))] + [ANY] * 10,
        [full((tokens, D)), full((tokens, D)), full((tokens, 128))],
        [sds((tokens, D), F32), sds((tokens, D), BF16), sds((tokens, 128), F32)],
        piece_shapes(width) + [pltpu.VMEM((tokens, D), F32)], [act, prev, vec, *weight], 2 * tokens * D * FF,
        2 * (D * FF + tokens * (5 * D + FF)), "down_norm",
    )


def units_back(flow, residual, parts, normed, inverse, vec, gain, weight, matrix, slope, count):
    tokens = residual.shape[0]
    width = FF // count

    def body(scal_ref, res_ref, *refs):
        part_refs, refs = refs[: len(parts)], refs[len(parts) :]
        n_ref, inv_ref, vec_ref, slope_ref, refs = refs[0], refs[1], refs[2], refs[3], refs[4:]
        pieces, (g_ref, low_ref, sums_ref, out_ref, sum_ref, buffer, sems) = refs[:10], refs[10:]
        s = pl.program_id(0)
        stream = Streamed(pieces, matrix, buffer, sems, scal_ref)
        stream.turn(s, count)

        @pl.when(s == 0)
        def _():
            def grad(rows):
                total = read(res_ref, rows)
                for part in part_refs:
                    total = total + read(part, rows)
                return total

            norm_backward(grad, tokens, n_ref, inv_ref, vec_ref, gain, g_ref, low_ref, sums_ref)

        stream.wait(s)
        slot = lax.rem(s, 2)
        sums = {}
        for rows, cols in tiles(tokens, width):
            low = (mm(low_ref[rows, :], buffer[slot, :, cols]) * slope_ref[rows, cols].astype(F32)).astype(BF16)
            out_ref[rows, cols] = low
            part = fold_rows(low.astype(F32))
            sums[cols.start] = sums[cols.start] + part if cols.start in sums else part
            if rows.start > 0:
                sum_ref[0, :, cols] = jnp.sum(sums[cols.start], 0, keepdims=True)

    column = pl.BlockSpec((tokens, width), lambda s, _: (0, s))
    return call(
        flow, body, (count,),
        [full((tokens, D))] + [part_spec(part) for part in parts]
        + [full((tokens, D)), full((tokens, 128)), full((TABLE, D)), column] + [ANY] * 10,
        [full((tokens, D)), full((tokens, D)), full((8, D)), column,
         pl.BlockSpec((1, 1, width), lambda s, scal_ref: (scal_ref[S_Z] ^ away(s), 0, 0))],
        [sds((tokens, D), F32), sds((tokens, D), BF16), sds((8, D), F32), sds((tokens, FF), BF16),
         sds((count, 1, width), F32)],
        piece_shapes(width), [residual, *parts, normed, inverse, vec, slope, *weight], 0, 0, "units_back",
    )


def up_back(flow, gu, weight, matrix, residual, normed, inverse, vec, gain, count):
    tokens = residual.shape[0]
    width = FF // count

    def body(scal_ref, gu_ref, res_ref, n_ref, inv_ref, vec_ref, *refs):
        pieces, (g_ref, low_ref, sums_ref, buffer, sems, acc) = refs[:10], refs[10:]
        s = pl.program_id(0)
        stream = Streamed(pieces, matrix, buffer, sems, scal_ref)
        stream.turn(s, count)
        stream.wait(s)
        value = mm(gu_ref[...], buffer[lax.rem(s, 2)], NT)

        @pl.when(s == 0)
        def _():
            acc[...] = value

        @pl.when(s > 0)
        def _():
            acc[...] += value

        @pl.when(s == count - 1)
        def _():
            norm_backward(
                lambda rows: res_ref[rows, :] + acc[rows, :], tokens, n_ref, inv_ref, vec_ref, gain, g_ref, low_ref,
                sums_ref,
            )

    return call(
        flow, body, (count,),
        [pl.BlockSpec((tokens, width), lambda s, _: (0, s)), full((tokens, D)), full((tokens, D)), full((tokens, 128)),
         full((TABLE, D))] + [ANY] * 10,
        [full((tokens, D)), full((tokens, D)), full((8, D))],
        [sds((tokens, D), F32), sds((tokens, D), BF16), sds((8, D), F32)],
        piece_shapes(width) + [pltpu.VMEM((tokens, D), F32)], [gu, residual, normed, inverse, vec, *weight],
        2 * tokens * D * FF, 2 * (D * FF + tokens * (8 * D + FF)), "up_back",
    )


def turn_rows(scal_ref, x_ref, turned, core):
    for r in range(4):
        row = ((scal_ref[S_Q] ^ r) * 2 + core) * ROWS
        turned[r * ROWS : (r + 1) * ROWS, :] = x_ref[:, pl.ds(pl.multiple_of(row, ROWS), ROWS)].T


def unit_grads(flow, down, up, received, count, sibling):
    tokens = down[0].shape[0]
    width = down[1].shape[1] // count
    half = count // 2
    steps = 2 * count

    def body(scal_ref, x0_ref, y0_ref, x1_ref, y1_ref, *refs):
        turned, t = refs[-1], pl.program_id(0)
        m, s = t // count, lax.rem(t, count)
        core = scal_ref[S_C] ^ 1 if sibling else scal_ref[S_C]

        @pl.when(t == 0)
        def _():
            turn_rows(scal_ref, x0_ref, turned, core)

        @pl.when(t == count)
        def _():
            turn_rows(scal_ref, x1_ref, turned, core)

        def store(y_ref):
            value = mm(turned[...], y_ref[...]).reshape(4, ROWS, width)
            if sibling:
                refs[0][:, 0] = value.astype(BF16)
                return
            if received is not None:
                value = value + refs[0][:, 0].astype(F32)
            value = value.astype(BF16)
            own, to_x, to_y, rest_x, rest_y = refs[-6:-1]
            spot = lax.rem(s, half) * 2 + m
            own[s // half * count + spot] = value[0]

            @pl.when(s < half)
            def _():
                to_x[spot] = value[1]
                to_x[count + spot] = value[3]
                rest_y[spot] = value[2]

            @pl.when(s >= half)
            def _():
                rest_x[spot] = value[1]
                to_y[spot] = value[2]
                to_y[count + spot] = value[3]

        @pl.when(m == 0)
        def _():
            store(y0_ref)

        @pl.when(m == 1)
        def _():
            store(y1_ref)

    left = full((tokens, D))
    pick_down = lambda t, _: (0, jnp.minimum(t, count - 1))
    pick_up = lambda t, _: (0, jnp.maximum(t - count, 0))
    specs = [left, pl.BlockSpec((tokens, width), pick_down), left, pl.BlockSpec((tokens, width), pick_up)]
    args = [*down, *up]
    one = pl.BlockSpec((4, 1, ROWS, width), lambda t, _: (0, t, 0, 0))
    if sibling:
        out_specs, out_shape = one, sds((4, steps, ROWS, width), BF16)
    else:
        if received is not None:
            specs.append(one)
            args.append(received)
        shapes = [(steps, ROWS, width)] * 3 + [(count, ROWS, width)] * 2
        out_specs, out_shape = [full(shape) for shape in shapes], [sds(shape, BF16) for shape in shapes]
    return call(
        flow, body, (steps,), specs, out_specs, out_shape, [pltpu.VMEM((4 * ROWS, tokens), BF16)], args,
        0, 0, "grads_theirs" if sibling else "grads_mine",
    )


def finish(flow, units, heads, small):
    layers = len(units)
    rows, cols = heads[0][0].shape
    in_width = cols * 3 // 4
    pairs = in_width // (3 * PAIR)
    width = units[0][0].shape[2]

    def body(scal_ref, *refs):
        qkv_ref, out_ref, up_ref, down_ref, square_ref = refs[-5:]
        small_ref, refs = refs[-6], refs[:-6]
        squares = jnp.sum(small_ref[...] * small_ref[...], keepdims=True)
        for l in range(layers):
            unit_refs, (first, second) = refs[7 * l : 7 * l + 5], refs[7 * l + 5 : 7 * l + 7]
            for m, target in enumerate((down_ref, up_ref)):
                total = unit_refs[0][m].astype(F32)
                for part in unit_refs[1:]:
                    total = total + part[m].astype(F32)
                target[l] = total
                squares = squares + jnp.sum(jnp.sum(total * total, 0, keepdims=True), 1, keepdims=True)
            total = first[...].astype(F32) + second[...].astype(F32)
            squares = squares + jnp.sum(jnp.sum(total * total, 0, keepdims=True), 1, keepdims=True)
            out_ref[l] = total[:, in_width:]
            for pair in range(pairs):
                for which in range(3):
                    base = (3 * pair + which) * PAIR
                    qkv_ref[l, which, :, pair * PAIR : (pair + 1) * PAIR] = total[:, base : base + PAIR]
        square_ref[...] = jnp.broadcast_to(squares, (8, 128))

    specs, args = [], []
    for l in range(layers):
        specs += [pl.BlockSpec((2, rows, width), lambda *_: (0, 0, 0))] * 5 + [full((rows, cols))] * 2
        args += [*units[l], *heads[l]]
    shapes = [(layers, 3, rows, in_width // 3), (layers, rows, cols - in_width), (layers, rows, width), (layers, rows, width),
              (8, 128)]
    return call(
        flow, body, (1,), specs + [full(small.shape)], [full(shape) for shape in shapes],
        [sds(shape, F32) for shape in shapes], [], args + [small], 0, 0, "finish",
    )


def place_heads_weight(scal_ref, pieces, buffer):
    for r in range(4):
        for k in range(2):
            row = ((scal_ref[S_Q] ^ r) * 2 + (scal_ref[S_ZH] ^ k)) * ROWS
            buffer[pl.ds(pl.multiple_of(row, ROWS), ROWS), :] = pieces[r // 2][r % 2, k, :ROWS, :]


def heads_weight_specs(weight, cols):
    width = cols.stop - cols.start
    return [pl.BlockSpec((2, 2, piece.shape[2], width), lambda *_: (0, 0, 0, cols.start // width)) for piece in weight]


def by_member(shape):
    return pl.BlockSpec((1,) + shape, lambda r, scal_ref: (scal_ref[S_P] ^ r, 0, 0))


def heads_weight_scratch(width):
    return [pltpu.VMEM((D, width), BF16)]


def project_in(flow, lefts, across, weight, cols, bias, name):
    tokens = lefts[0].shape[0]
    width = cols.stop - cols.start

    def body(scal_ref, left_ref, right_ref, *refs):
        if bias is not None:
            bias_ref, refs = refs[0], refs[1:]
        pieces, (out_ref, buffer) = refs[:2], refs[2:]
        step = pl.program_id(0)

        @pl.when(step == 0)
        def _():
            place_heads_weight(scal_ref, pieces, buffer)

        for r, left in enumerate((left_ref, right_ref)):

            @pl.when(step == r)
            def _(left=left):
                value = mm(left[...], buffer[...])
                if bias is not None:
                    value = value + bias_ref[...]
                out_ref[0] = value.astype(BF16)

    extra, extra_specs = ([], []) if bias is None else ([bias], [full((1, width))])
    return call(
        flow, body, (2,), [full((tokens, D))] * 2 + extra_specs + heads_weight_specs(weight, cols),
        pl.BlockSpec((1, tokens, width), lambda r, scal_ref: ((scal_ref[S_P] >> 1) ^ r, 0, 0)),
        sds((2, tokens, width), BF16), heads_weight_scratch(width), [*lefts, *extra, *weight], 0, 0, name,
    )


def project_out(flow, blocks, members, weight, cols, stacked, name):
    count, tokens, width = blocks[0].shape

    def body(scal_ref, *refs):
        block_refs, refs = refs[: len(blocks)], refs[len(blocks) :]
        pieces, outs, buffer = refs[:2], refs[2:-1], refs[-1]
        step = pl.program_id(0)

        @pl.when(step == 0)
        def _():
            place_heads_weight(scal_ref, pieces, buffer)

        value = mm(block_refs[0][0], buffer[:, :width], NT)
        for index in range(1, len(blocks)):
            value = value + mm(block_refs[index][0], buffer[:, index * width : (index + 1) * width], NT)
        value = value.astype(BF16)
        if stacked:
            outs[0][0] = value
            return
        for r, out in enumerate(outs):

            @pl.when(step == r)
            def _(out=out):
                out[...] = value

    first, last = members
    pick = lambda r, scal_ref: (scal_ref[S_P] ^ (first + r * (last - first)), 0, 0)
    if stacked:
        out_specs, out_shape = pl.BlockSpec((1, tokens, D), lambda r, _: (r, 0, 0)), sds((2, tokens, D), BF16)
    else:
        out_specs, out_shape = [full((tokens, D))] * 2, [sds((tokens, D), BF16)] * 2
    return call(
        flow, body, (2,), [pl.BlockSpec((1, tokens, width), pick)] * len(blocks) + heads_weight_specs(weight, cols), out_specs,
        out_shape,
        heads_weight_scratch(width * len(blocks)), [*blocks, *weight], 0, 0, name,
    )


def heads_grad(flow, xs, parts, gas, ctx):
    count, tokens, width = parts[0].shape
    out_width = ctx.shape[2]
    cuts = [slice(i * width, (i + 1) * width) for i in range(len(parts))]
    total = width * len(parts)

    def body(scal_ref, *refs):
        x_refs, refs = refs[:count], refs[count:]
        ga_refs, refs = refs[:count], refs[count:]
        part_refs, refs = refs[: len(parts)], refs[len(parts) :]
        ctx_ref, outs, (sum_ref, acc, acc_out) = refs[0], refs[1:3], refs[3:]
        step = pl.program_id(0)
        for r in range(count):

            @pl.when(step == r)
            def _(r=r):
                turned = x_refs[r][...].T
                value_out = mm(ga_refs[r][...].T, ctx_ref[0])
                for cut, part in zip(cuts, part_refs):
                    value = mm(turned, part[0])
                    sums = jnp.sum(part[0].astype(F32), 0, keepdims=True)
                    acc[:, cut] = value if r == 0 else acc[:, cut] + value
                    sum_ref[:, cut] = sums if r == 0 else sum_ref[:, cut] + sums
                acc_out[...] = value_out if r == 0 else acc_out[...] + value_out

        @pl.when(step == count - 1)
        def _():
            for r in range(4):
                for k in range(2):
                    row = ((scal_ref[S_Q] ^ r) * 2 + (scal_ref[S_ZH] ^ k)) * ROWS
                    rows = pl.ds(pl.multiple_of(row, ROWS), ROWS)
                    outs[r % 2][r // 2, k, :, :total] = acc[rows, :].astype(BF16)
                    outs[r % 2][r // 2, k, :, total:] = acc_out[rows, :].astype(BF16)

    shape = (2, 2, ROWS, total + out_width)
    return call(
        flow, body, (count,),
        [full((tokens, D))] * (2 * count) + [by_member((tokens, width))] * len(parts) + [by_member((tokens, out_width))],
        [full(shape)] * 2 + [full((1, total))], [sds(shape, BF16)] * 2 + [sds((1, total), F32)],
        [pltpu.VMEM((D, total), F32), pltpu.VMEM((D, out_width), F32)], [*xs, *gas, *parts, ctx], 0, 0, "heads_grad",
    )


def reach(ends_ref, row):
    first = jnp.zeros_like(row)
    for index in range(3):
        first = jnp.where(row >= ends_ref[index], ends_ref[index], first)
    last = jnp.full_like(row, SEQLEN)
    for index in (2, 1, 0):
        last = jnp.where(row < ends_ref[index], ends_ref[index], last)
    return jnp.maximum(first, row - (WINDOW - 1)), jnp.minimum(last, row + WINDOW)


def chunks_of(scal_ref, near_ref, far_ref):
    here = scal_ref[S_P] & 1
    for core in range(2):
        yield 2 * core + here, near_ref.at[core]
        yield 2 * core + 1 - here, far_ref.at[core]


def over_keys(ends_ref, start, chunk, keys_first, block):
    low_first, high_first = reach(ends_ref, start)
    low_last, high_last = reach(ends_ref, start + BQ - 1)
    axis = 1 if keys_first else 0
    low_row, high_row = reach(ends_ref, start + lax.broadcasted_iota(jnp.int32, (1, BQ) if keys_first else (BQ, 1), axis))
    shape = (chunk, BQ) if keys_first else (BQ, chunk)

    def one(b, carry):
        open_all = (b * chunk >= low_last) & ((b + 1) * chunk <= high_first)

        @pl.when(open_all)
        def _():
            block(b, None)

        @pl.when(jnp.logical_not(open_all))
        def _():
            key = b * chunk + lax.broadcasted_iota(jnp.int32, shape, 1 - axis)
            block(b, (key >= low_row) & (key < high_row))

        return carry

    lax.fori_loop(low_first // chunk, (high_last + chunk - 1) // chunk, one, 0)


def attend_forward(flow, ends, qkv):
    _, chunk, width3 = qkv[0].shape
    count = SEQLEN // chunk
    width = width3 // 3
    heads = width // HD
    steps = SEQLEN // BQ
    per = chunk // BQ

    def body(scal_ref, ends_ref, near_ref, far_ref, ctx_ref, wide_ref, lse_ref, qt, kh, vt, acc, tops, sums, scores):
        step = pl.program_id(0)

        @pl.when(step == 0)
        def _():
            for j, block in chunks_of(scal_ref, near_ref, far_ref):
                rows = pl.ds(pl.multiple_of(j * chunk, chunk), chunk)
                for pair in range(heads // 2):
                    base = 3 * PAIR * pair
                    part = slice(pair * PAIR, (pair + 1) * PAIR)
                    vt[j, part, :] = block[:, base + 2 * PAIR : base + 3 * PAIR].T
                    for s in range(per):
                        queries = block[s * BQ : (s + 1) * BQ, base : base + PAIR] * BF16(HD**-0.5)
                        qt[j * per + s, part, :] = queries.T
                    for h in range(2):
                        kh[2 * pair + h, rows, :] = block[:, base + PAIR + h * HD : base + PAIR + (h + 1) * HD]

        start = step * BQ
        acc[...] = jnp.zeros(acc.shape, F32)
        tops[...] = jnp.full(tops.shape, -3.0e38, F32)
        sums[...] = jnp.zeros(sums.shape, F32)

        def score(b, allowed):
            keys = pl.ds(pl.multiple_of(b * chunk, chunk), chunk)
            for h in range(heads):
                value = mm(kh[h, keys, :], qt[step, h * HD : (h + 1) * HD, :])
                if allowed is not None:
                    value = jnp.where(allowed, value, FILL)
                scores[h, b] = value
                tops[h] = jnp.maximum(tops[h], jnp.max(value.reshape(-1, 8, BQ), 0))

        over_keys(ends_ref, start, chunk, True, score)
        top = [jnp.max(tops[h], 0, keepdims=True) for h in range(heads)]

        def weigh(b, carry):
            for h in range(heads):
                part = slice(h * HD, (h + 1) * HD)
                weight = jnp.exp(scores[h, b] - top[h])
                sums[h] += fold_rows(weight)
                acc[part, :] += mm(vt[b, part, :], weight.astype(BF16))
            return carry

        low_first, _ = reach(ends_ref, start)
        _, high_last = reach(ends_ref, start + BQ - 1)
        lax.fori_loop(low_first // chunk, (high_last + chunk - 1) // chunk, weigh, 0)
        lse_ref[...] = jnp.zeros(lse_ref.shape, F32)
        for h in range(heads):
            part = slice(h * HD, (h + 1) * HD)
            total = jnp.sum(sums[h], 0, keepdims=True)
            acc[part, :] = acc[part, :] / total
            lse_ref[0, h : h + 1, :] = top[h] + jnp.log(total)
        wide = acc[...].T
        wide_ref[0] = wide
        ctx_ref[0] = wide.astype(BF16)

    row_block = lambda i, *_: (i // per, i % per, 0)
    return call(
        flow, body, (steps,), [full((2, chunk, width3))] * 2,
        [pl.BlockSpec((1, BQ, width), row_block), pl.BlockSpec((1, BQ, width), row_block),
         pl.BlockSpec((1, 8, BQ), lambda i, *_: (i, 0, 0))],
        [sds((count, chunk, width), BF16), sds((count, chunk, width), F32), sds((steps, 8, BQ), F32)],
        [
            pltpu.VMEM((steps, width, BQ), BF16),
            pltpu.VMEM((heads, SEQLEN, HD), BF16),
            pltpu.VMEM((count, width, chunk), BF16),
            pltpu.VMEM((width, BQ), F32),
            pltpu.VMEM((heads, 8, BQ), F32),
            pltpu.VMEM((heads, 8, BQ), F32),
            pltpu.VMEM((heads, count, chunk, BQ), F32),
        ],
        [*qkv], 0, 0, "attend_forward", (flow.scal, ends),
    )


def attend_backward(flow, ends, pair, qkv, grads, wide, lse):
    chunk = qkv[0].shape[1]
    count = SEQLEN // chunk
    steps = SEQLEN // BQ
    per = chunk // BQ

    def body(
        scal_ref, ends_ref, near_ref, far_ref, grad_near, grad_far, wide_ref, lse_ref, out_ref, qh, gh, kt, vt, qt, gt,
        gq, gk, gv,
    ):
        step = pl.program_id(0)

        @pl.when(step == 0)
        def _():
            blocks = chunks_of(scal_ref, near_ref, far_ref)
            grad_blocks = chunks_of(scal_ref, grad_near, grad_far)
            for (j, block), (_, grad_block) in zip(blocks, grad_blocks):
                rows = pl.ds(pl.multiple_of(j * chunk, chunk), chunk)
                queries = block[:, :PAIR] * BF16(HD**-0.5)
                keys = block[:, PAIR : 2 * PAIR]
                back = grad_block[...]
                for h in range(2):
                    cols = slice(h * HD, (h + 1) * HD)
                    qh[h, rows, :] = queries[:, cols]
                    gh[h, rows, :] = back[:, cols]
                kt[j] = keys.T
                vt[j] = block[:, 2 * PAIR :].T
                for s in range(per):
                    sub = slice(s * BQ, (s + 1) * BQ)
                    qt[j * per + s] = queries[sub, :].T
                    gt[j * per + s] = back[sub, :].T
            gk[...] = jnp.zeros(gk.shape, F32)
            gv[...] = jnp.zeros(gv.shape, F32)

        start = step * BQ
        rows = pl.ds(pl.multiple_of(start, BQ), BQ)
        gq[...] = jnp.zeros(gq.shape, F32)
        sums = lse_ref[0].T
        inner, logs = [], []
        for h in range(2):
            product = gh[h, rows, :].astype(F32) * wide_ref[0, :, h * HD : (h + 1) * HD]
            inner.append(jnp.sum(product, 1, keepdims=True))
            logs.append(sums[:, 2 * pair + h : 2 * pair + h + 1])

        def block(b, allowed):
            for h in range(2):
                part = slice(h * HD, (h + 1) * HD)
                score = mm(qh[h, rows, :], kt[b, part, :])
                grad_weight = mm(gh[h, rows, :], vt[b, part, :])
                if allowed is not None:
                    score = jnp.where(allowed, score, FILL)
                weight = jnp.exp(score - logs[h])
                grad_score = (weight * (grad_weight - inner[h])).astype(BF16)
                gv[b, part, :] += mm(gt[step, part, :], weight.astype(BF16))
                gk[b, part, :] += mm(qt[step, part, :], grad_score)
                gq[part, :] += mm(kt[b, part, :], grad_score, NT)

        over_keys(ends_ref, start, chunk, False, block)
        place = pl.ds(pl.multiple_of((step % per) * BQ, BQ), BQ)
        out_ref[step // per, place, :PAIR] = (gq[...] * HD**-0.5).T.astype(BF16)

        @pl.when(step == steps - 1)
        def _():
            for j in range(count):
                out_ref[j, :, PAIR : 2 * PAIR] = gk[j].T.astype(BF16)
                out_ref[j, :, 2 * PAIR :] = gv[j].T.astype(BF16)

    out = (count, chunk, 3 * PAIR)
    return call(
        flow, body, (steps,),
        [pl.BlockSpec((2, chunk, 3 * PAIR), lambda i, *_: (0, 0, pair))] * 2
        + [pl.BlockSpec((2, chunk, PAIR), lambda i, *_: (0, 0, pair))] * 2
        + [pl.BlockSpec((1, BQ, PAIR), lambda i, *_: (i // per, i % per, pair)),
           pl.BlockSpec((1, 8, BQ), lambda i, *_: (i, 0, 0))],
        full(out), sds(out, BF16),
        [pltpu.VMEM((2, SEQLEN, HD), BF16)] * 2
        + [pltpu.VMEM((count, PAIR, chunk), BF16)] * 2
        + [pltpu.VMEM((steps, PAIR, BQ), BF16)] * 2
        + [pltpu.VMEM((PAIR, BQ), F32)]
        + [pltpu.VMEM((count, PAIR, chunk), F32)] * 2,
        [*qkv, *grads, wide, lse], 0, 0, "attend_backward", (flow.scal, ends),
    )


def flip(values_in, axes, mask):
    return lax.ppermute(values_in, axes, [(a, a ^ mask) for a in range(lax.axis_size(axes))])


def turn(values_in):
    return lax.ppermute(values_in, ("c", "zh"), [(2 * a + b, 2 * b + a) for a in range(2) for b in range(2)])


def uncross(values_in):
    return lax.ppermute(values_in, ("c", "zh"), [(2 * b + 1 - a, 2 * a + b) for a in range(2) for b in range(2)])


def from_members(values_in, axes):
    return [values_in] + [flip(values_in, axes, r) for r in range(1, lax.axis_size(axes))]


def to_members(parts, axes):
    return [parts[0]] + [flip(part, axes, r) for r, part in enumerate(parts) if r > 0]


def add(*parts):
    total = parts[0].astype(F32)
    for part in parts[1:]:
        total = total + part.astype(F32)
    return total


def is_small():
    return lax.axis_size("q") == 4


def order_by(values_in, axis, position, count):
    bit = 1
    while bit < count:
        shape = values_in.shape
        split = shape[:axis] + (count // (2 * bit), 2, bit) + shape[axis + 1 :]
        cut = values_in.reshape(split)
        values_in = jnp.where((position & bit) != 0, jnp.flip(cut, axis + 1), cut).reshape(shape)
        bit *= 2
    return values_in


def gather_group(values_in):
    across, sibling = flip(values_in, GROUP, 1), flip(values_in, GROUP, 2)
    return [values_in, across, sibling]


def forward(flow, members, *before):
    flow.wait(*before)
    flow.hold(across=members[1])
    gate(flow)
    members[1] = flow.free("across")
    members.append(flip(members[1], GROUP, 2))


def sum_group(keep, send):
    got = flip(send, GROUP, 2)
    passed = add(keep[1], got[1]).astype(BF16)
    return [keep[0], got, flip(passed, GROUP, 1)], passed


EXTRA = 16


def heads_shard_of(qkv, out, bias):
    rows = out.shape[0]
    paired = qkv.reshape(3, rows, -1, PAIR).transpose(1, 2, 0, 3).reshape(rows, -1)
    weights = jnp.concatenate([paired, out], axis=1)
    below = jnp.pad(bias.reshape(1, -1), ((0, EXTRA - 1), (0, weights.shape[1] - bias.size)))
    return jnp.concatenate([weights, below])


def heads_bias(rows, heads):
    bias = rows.reshape(rows.shape[0], 2, heads, -1).transpose(1, 2, 0, 3).reshape(2, -1).astype(F32)
    bias = jnp.stack([bias[0], jnp.zeros_like(bias[0]), bias[1]])
    return bias.reshape(3, -1, PAIR).transpose(1, 0, 2).reshape(1, -1)


def with_sibling(shard):
    return jnp.stack([shard, flip(shard, "c", 1)])


def heads_along_x(pair):
    return jnp.stack([pair, flip(pair, "q", 1)])


def heads_along_y(near, size, heads, where, zh):
    return heads_pieces(near, flip(near, "q", 2), size, heads, where, zh)


def heads_pieces(near, far, size, heads, where, zh):
    rows = jnp.concatenate([near[:, :, ROWS, :size], far[:, :, ROWS, :size]])
    return [near, far], heads_bias(order_by(order_by(rows, 0, where[0], 4), 1, zh, 2).reshape(8, size), heads)


def all_heads_weight(shard, size, heads, zh):
    pair = turn(with_sibling(shard))
    every = order_by(lax.all_gather(pair, "q"), 1, zh, 2)
    count = shard.shape[0] - EXTRA
    weights = every[:, :, :count].reshape(4, 2, ROWS, -1)
    return [weights[:2], weights[2:]], heads_bias(every[:, :, count, :size].reshape(-1, size), heads)


class HeadsGrad:
    def __init__(self, keep, send):
        self.keep, self.send = keep, send

    def along_x(self):
        self.got = flip(self.send, "q", 1)
        return self.got

    def along_y(self):
        self.got_x = self.got
        self.got = flip(add(self.keep[1], self.got[1]).astype(BF16), "q", 2)
        return self.got

    def halves(self, zh):
        if is_small():
            return tuple(add(self.keep[0, k], self.got_x[0, k], self.got[k]).astype(BF16) for k in range(2))
        buckets = [self.keep[0], self.send[0], self.keep[1], self.send[1]]
        every = jnp.stack(buckets).reshape(lax.axis_size("q"), 2, -1, buckets[0].shape[-1])
        rows = order_by(lax.psum_scatter(every, "q", scatter_dimension=0, tiled=False), 0, zh, 2)
        return rows[0], rows[1]


SLOTS = (0, 2, 1, 3)


def all_units_weight(shard):
    matrices, _, width = shard.shape
    members = lax.axis_size(MODEL)
    every = lax.all_gather(shard, ALL).reshape(members, -1, matrices, shard.shape[1], width).transpose(0, 2, 1, 3, 4)
    every = every.reshape(members, matrices, 4, 2, ROWS, width)
    every = jnp.stack([every[slot] for slot in SLOTS])
    pieces = []
    for k in range(2):
        pieces += [every[:, :, r, k] for r in range(3)] + [every[:2, :, 3, k], every[2:, :, 3, k]]
    return pieces


class UnitsWeight:
    def __init__(self, shard):
        self.shard, self.theirs = shard, {}

    def start_far_z(self):
        self.other = flip(self.shard, "zh", 1)

    def join_far_z(self, shard):
        self.two = jnp.stack([shard, self.other])

    def far_z(self):
        self.start_far_z()
        self.join_far_z(self.shard)

    def start_z(self):
        self.other = flip(self.two, "zl", 1)

    def join_z(self, two):
        self.own = jnp.concatenate([two, self.other])

    def near_z(self):
        self.start_z()
        self.join_z(self.two)

    def near(self):
        self.near_x, self.near_y = flip(self.own, "q", 1), flip(self.own, "q", 2)

    def corner(self):
        self.far_a, self.far_b = flip(self.near_y[:2], "q", 1), flip(self.near_x[2:], "q", 2)

    def swap(self, *names):
        for name in names:
            self.theirs[name] = flip(getattr(self, name), "c", 1)

    def pieces(self):
        names = ("own", "near_x", "near_y", "far_a", "far_b")
        return [getattr(self, name) for name in names] + [self.theirs[name] for name in names]


class UnitsGrads:
    def __init__(self, flow, down, up, count):
        self.flow, self.down, self.up, self.count = flow, down, up, count

    def compute_theirs(self):
        self.theirs = unit_grads(self.flow, self.down, self.up, None, self.count, True)

    def send_theirs(self):
        self.got = flip(self.theirs, "c", 1) if is_small() else None

    def sibling(self):
        self.compute_theirs()
        self.send_theirs()

    def mine(self):
        self.made = unit_grads(self.flow, self.down, self.up, self.got, self.count, False)
        self.own, self.to_x, self.to_y, self.rest_x, self.rest_y = self.made

    def near(self):
        self.from_x, self.from_y = flip(self.to_x, "q", 1), flip(self.to_y, "q", 2)
        return [self.from_x, self.from_y]

    def far(self):
        half = self.count
        self.late_x = flip(add(self.rest_x, self.from_y[half:]).astype(BF16), "q", 1)
        self.late_y = flip(add(self.rest_y, self.from_x[half:]).astype(BF16), "q", 2)
        return [self.late_x, self.late_y]

    def near_z(self):
        half = self.count
        self.passing = add(self.own[half:], self.late_x, self.from_y[:half]).astype(BF16)
        self.there = flip(self.passing, "zl", 1)
        return [self.there]

    def far_z(self):
        self.last = flip(self.near_sum(slice(self.count // 2, self.count)).astype(BF16), "zh", 1)
        return [self.last]

    def near_sum(self, blocks):
        return add(self.own[blocks], self.from_x[blocks], self.late_y[blocks], self.there[blocks])

    def parts(self):
        return self.own, self.from_x, self.late_y, self.there, self.last

    def total(self):
        half = self.count
        mine = jnp.stack(
            [self.own, jnp.concatenate([self.to_x[:half], self.rest_x]), jnp.concatenate([self.rest_y, self.to_y[:half]]),
             jnp.concatenate([self.to_x[half:], self.to_y[half:]])]
        ).reshape(4, self.count, 2, ROWS, -1)
        theirs = self.theirs.reshape(4, 2, self.count, ROWS, -1).transpose(0, 2, 1, 3, 4)
        every = jnp.stack([mine, theirs], axis=1)
        every = every.transpose(2, 0, 1, 4, 3, 5)
        every = jnp.stack([every[slot] for slot in SLOTS]).reshape(-1, 2, mine.shape[-1])
        return lax.psum_scatter(every, ALL, scatter_dimension=0, tiled=True).astype(F32).transpose(1, 0, 2)


SMALL_AXES = ("q", MODEL, "c")
SMALL_STEPS = (("q", 1), ("q", 2), ("zl", 1), ("zh", 1), ("c", 1))
SMALL_SHAPE = (128, 256)


def spread_by_distance(values_in, where):
    every = values_in.reshape(4, 4, 2, -1).transpose(1, 0, 2, 3)
    for axis, position in enumerate(where):
        every = order_by(every, axis, position, every.shape[axis])
    return every.transpose(2, 1, 0, 3).reshape(32, -1)


def fold_small(every, first, last):
    for axis, mask in SMALL_STEPS[::-1][first:last]:
        half = every.shape[0] // 2
        every = every[:half] + flip(every[half:], axis, mask)
    return every


def sum_all(value):
    if not is_small():
        return lax.psum(value, ALL)
    for axes in SMALL_AXES:
        parts = jnp.stack(from_members(value, axes))
        value = jnp.sum(order_by(parts, 0, lax.axis_index(axes), parts.shape[0]), 0)
    return value[0, 0]


def on_device(
    tokens, doc_lengths, qkv_weight, qv_bias, out_weight, up_weight, up_bias, down_weight, gains, shifts, cotangent
):
    layers = qkv_weight.shape[0]
    tz, dp = lax.axis_size(MODEL), lax.axis_size(("q", "c"))
    place, zh = lax.axis_index(GROUP), lax.axis_index("zh")
    where = (lax.axis_index("q"), lax.axis_index(MODEL), lax.axis_index("c"))
    if is_small():
        spots = [place, where[0], where[2], zh, where[1]]
    else:
        spots = [place] + [jnp.zeros((), jnp.int32)] * 4
    scal = jnp.stack([spot.astype(jnp.int32) for spot in spots])

    flow = Flow(scal)
    small_slice = is_small()
    qkv_cols, out_cols = 3 * out_weight.shape[2], out_weight.shape[2]
    in_cols, out_cols = slice(0, qkv_cols), slice(qkv_cols, qkv_cols + out_cols)
    hz, bias_size = qv_bias.shape[2], qv_bias.size // layers
    heads_shard = [heads_shard_of(qkv_weight[l], out_weight[l], qv_bias[l]) for l in range(layers)]
    pieces = [up_bias, gains, shifts]
    sizes = [piece.size // layers for piece in pieces]
    cuts = [0]
    for size in sizes:
        cuts.append(cuts[-1] + size)
    small = jnp.concatenate([piece.reshape(layers, -1) for piece in pieces], axis=1).reshape(-1)
    padded = jnp.pad(small, (0, SMALL_SHAPE[0] * SMALL_SHAPE[1] - small.size)).reshape(SMALL_SHAPE)
    gathered = lax.all_gather(padded, ALL)
    small_all = gathered.reshape(tz * dp, -1)[:, : small.size]

    def spread_small():
        every = small_all.reshape(tz, dp, layers, -1).astype(F32)
        parts = [every[..., cuts[i] : cuts[i + 1]] for i in range(3)]
        biases = parts[0].reshape(tz, dp, layers, up_bias.shape[1], -1).transpose(2, 0, 3, 1, 4)
        gain = parts[1].reshape(tz, dp, layers, 2, -1).transpose(2, 3, 1, 0, 4).reshape(layers, 2, D)
        shift = parts[2].reshape(tz, dp, layers, 4, -1).transpose(2, 3, 1, 0, 4).reshape(layers, 4, D)
        table = jnp.concatenate([gain, shift], axis=1).reshape(layers * 6, D)
        head = jnp.concatenate([jnp.ones((1, D), F32), jnp.zeros((1, D), F32)])
        return biases.reshape(layers, tz, 1, -1), jnp.pad(jnp.concatenate([head, table]), ((0, TABLE - 2 - 6 * layers), (0, 0)))

    up_bias_full, table = spread_small()
    if small_slice:
        pair = with_sibling(heads_shard[0])
        bundle = turn(jnp.concatenate([tokens, pair.reshape(-1, D)]))
        x_low, pair = bundle[: tokens.shape[0]], bundle[tokens.shape[0] :].reshape(pair.shape)
        ends = jnp.cumsum(turn(doc_lengths)[0], dtype=jnp.int32)
        members = from_members(pair, "q")
        weights_of = [heads_pieces(jnp.stack(members[:2]), jnp.stack(members[2:]), bias_size, hz, where, zh)]
        up0, down0 = UnitsWeight(up_weight[0][None]), UnitsWeight(down_weight[0][None])
        both1 = UnitsWeight(jnp.stack([up_weight[1], down_weight[1]]))
        flow.hold(
            up0=up0.shard, up0_twin=up0.shard, up0_last=up0.shard, down0=down0.shard, down0_twin=down0.shard, both1=both1.shard,
            heads1=heads_shard[1], low=x_low,
        )
        gate(flow)
        x_low = flow.free("low")
    else:
        x_low = turn(tokens)
        ends = jnp.cumsum(turn(doc_lengths)[0], dtype=jnp.int32)
        weights_of = [all_heads_weight(shard, bias_size, hz, zh) for shard in heads_shard]
        every = [all_units_weight(jnp.stack([up_weight[l], down_weight[l]])) for l in range(layers)]
        top_grad = turn(cotangent)

    prev, prev_gain, prev_shift = x_low, ONE, ZERO
    kept = []
    for l in range(layers):
        first, last = small_slice and l == 0, small_slice and l == 1
        xs = gather_group(x_low)
        w_heads, bias = weights_of[l]
        qkv_near = project_in(flow, (xs[0], xs[2]), False, w_heads, in_cols, bias, "project_qkv")
        if first:
            up0.shard = flow.free("up0")
            up0.start_far_z()
            flow.wait(up0.other)
        if last:
            flow.hold(top=cotangent, own=both1.own)
        forward(flow, xs, qkv_near)
        if first:
            twin, down0.shard = flow.free("up0_twin"), flow.free("down0")
            up0.join_far_z(twin)
            across = up0.other
            up0.start_z()
            down0.start_far_z()
        if last:
            both1.own = flow.free("own")
            both1.near()
        qkv_far = project_in(flow, (xs[1], xs[3]), True, w_heads, in_cols, bias, "project_qkv")
        qkv = (qkv_near, qkv_far)
        if first:
            down0.join_far_z(flow.free("down0_twin"))
            up0.join_z(jnp.stack([flow.free("up0_last"), across]))
            up0.near()
            down0.near_z()
            both1.shard = flow.free("both1")
            both1.far_z()
        if last:
            top_grad = turn(flow.free("top"))
            both1.swap("own")
        ctx, wide, lse = attend_forward(flow, ends, qkv)
        if first:
            flow.wait(up0.near_x, up0.near_y)
            flow.hold(both1=both1.two, down0=down0.own)
            up0.swap("own", "near_x", "near_y")
        if last:
            flow.wait(both1.near_x, both1.near_y, top_grad)
            both1.corner()
            both1.swap("near_x", "near_y")
        send = project_out(flow, [ctx], (2, 3), w_heads, out_cols, True, "project_attn")
        flow.wait(send)
        if first:
            pair = with_sibling(flow.free("heads1"))
        keep = project_out(flow, [ctx], (0, 1), w_heads, out_cols, False, "project_attn")
        attn, passed = sum_group(keep, send)
        if first:
            flow.wait(passed, gathered, pair, *up0.theirs.values())
            flow.hold(near_x=up0.near_x, near_y=up0.near_y)
            gate(flow)
            down0.own, up0.near_x, up0.near_y = flow.free("down0"), flow.free("near_x"), flow.free("near_y")
            up0.corner()
            up0.swap("far_a", "far_b")
            down0.near()
            down0.swap("own")
            flow.wait(down0.near_x, down0.near_y)
            down0.corner()
            down0.swap("near_x", "near_y")
            flow.hold(pair=pair)
            w_up = up0.pieces(), 0
        elif last:
            flow.wait(passed)
            flow.hold(ends=ends)
            gate(flow)
            ends = flow.free("ends")
            flow.hold(far_a=both1.far_a, far_b=both1.far_b)
            flow.wait(attn[2])
            gate(flow)
            both1.far_a, both1.far_b = flow.free("far_a"), flow.free("far_b")
            both1.swap("far_a", "far_b")
            w_up, w_down = (both1.pieces(), 0), (both1.pieces(), 1)
        else:
            w_up, w_down = (every[l], 0), (every[l], 1)
        used = (prev_gain, prev_shift, shift_row(l, 0), gain_row(l, 0), shift_row(l, 1))
        n1, hs, r1, act, slope = norm_up(flow, prev, attn, table, used, *w_up, up_bias_full[l], tz)
        if first:
            pair = turn(flow.free("pair"))
            flow.wait(n1, *down0.theirs.values())
            flow.hold(far_a=down0.far_a, far_b=down0.far_b)
            gate(flow)
            down0.far_a, down0.far_b = flow.free("far_a"), flow.free("far_b")
            down0.swap("far_a", "far_b")
            both1.two = flow.free("both1")
            both1.near_z()
            flow.hold(pair=pair, pair_twin=pair)
            gate(flow)
            across = flip(flow.free("pair"), "q", 1)
            w_down = down0.pieces(), 0
        used = (gain_row(l, 0), shift_row(l, 1), shift_row(l, 2), gain_row(l, 1), shift_row(l, 3))
        n2, y_low, r2 = down_norm(flow, act, *w_down, n1, table, used, tz)
        if first:
            near = jnp.stack([flow.free("pair_twin"), across])
            weights_of.append(heads_along_y(near, bias_size, hz, where, zh))
        kept.append((xs, qkv, ctx, wide, lse, n1, hs, r1, act, slope, n2, r2, w_heads, w_up, w_down))
        x_low, prev, prev_gain, prev_shift = y_low, n2, gain_row(l, 1), shift_row(l, 3)
    layer_output = turn(x_low)

    residual, back = top_grad, []
    small_grads = [None] * layers
    units_of, heads_of = [None] * layers, [None] * layers
    above = above_heads = None
    for l in reversed(range(layers)):
        top = l == layers - 1
        xs, qkv, ctx, wide, lse, n1, hs, r1, act, slope, n2, r2, w_heads, w_up, w_down = kept[l]
        beside = small_slice and not top
        g2, gf, sums2, gu, up_bias_sum = units_back(
            flow, residual, back, n2, r2, table, gain_row(l, 1), *w_down, slope, tz
        )
        units = UnitsGrads(flow, (gf, act), (hs, gu), tz)
        if top:
            flow.hold(output=layer_output)
        else:
            if beside:
                flow.wait(*above.near())
                flow.hold(heads=above_heads.send)
            units.sibling()
            flow.wait(units.theirs)
            if beside:
                above_heads.send = flow.free("heads")
                above_heads.along_x()
                late = above.far()
        g1, ga, sums1 = up_back(flow, gu, *w_up, g2, n1, r1, table, gain_row(l, 0), tz)
        gas = gather_group(ga)
        flow.wait(ga)
        if top:
            layer_output = flow.free("output")
            units.compute_theirs()
            forward(flow, gas, units.theirs)
        else:
            units.mine()
            if beside:
                flow.wait(*late, above_heads.got)
            forward(flow, gas, *units.made)
        gc_near = project_in(flow, (gas[0], gas[2]), False, w_heads, out_cols, None, "project_gc")
        flow.wait(gc_near)
        if top:
            flow.hold(theirs=units.theirs)
        gc_far = project_in(flow, (gas[1], gas[3]), True, w_heads, out_cols, None, "project_gc")
        if top:
            units.theirs = flow.free("theirs")
            units.send_theirs()
        gcs = (gc_near, gc_far)
        if beside:
            early = above.near_z()
            flow.hold(rest_x=units.rest_x, rest_y=units.rest_y, keep=above_heads.keep, above=above.own)
        gqkv = [attend_backward(flow, ends, 0, qkv, gcs, wide, lse)]
        if beside:
            units.rest_x, units.rest_y = flow.free("rest_x"), flow.free("rest_y")
            above_heads.keep, above.own = flow.free("keep"), flow.free("above")
        flow.wait(gqkv[0])
        if beside:
            flow.wait(*units.near(), *early)
            above.far_z()
            units.far()
            above_heads.along_y()
            flow.hold(own=units.own, keep=above_heads.keep)
        gqkv.append(attend_backward(flow, ends, 1, qkv, gcs, wide, lse))
        if beside:
            units.own, above_heads.keep = flow.free("own"), flow.free("keep")
            units.near_z()
            flow.wait(units.passing, units.late_y, above.last, above_heads.got)
            above_halves = above_heads.halves(zh)
            done = turn(above_halves[0]), uncross(above_halves[1])
        send = project_out(flow, gqkv, (2, 3), w_heads, in_cols, True, "project_gx")
        flow.wait(send)
        if beside:
            flow.hold(own=units.own)
        keep = project_out(flow, gqkv, (0, 1), w_heads, in_cols, False, "project_gx")
        back, passed = sum_group(keep, send)
        flow.wait(passed)
        if top:
            units.mine()
            flow.wait(*units.made)
        elif small_slice:
            units.own = flow.free("own")
            units.far_z()
            flow.wait(*done)
        *buckets, qkv_sums = heads_grad(flow, xs, gqkv, gas, ctx)
        heads = HeadsGrad(*buckets)
        units_of[l], heads_of[l] = units, heads
        qv_sums = qkv_sums.reshape(-1, 3, PAIR).transpose(1, 0, 2).reshape(3, hz, dp, -1)
        qv_sums = jnp.stack([qv_sums[0], qv_sums[2]]).transpose(2, 0, 1, 3).reshape(1, dp, -1)
        mine = (jnp.arange(tz) == place).astype(F32).reshape(tz, 1, 1)
        small_grads[l] = jnp.concatenate(
            [
                mine * qv_sums,
                up_bias_sum.reshape(tz, up_bias.shape[1], dp, -1).transpose(0, 2, 1, 3).reshape(tz, dp, -1),
                jnp.stack([sums1[0], sums2[0]]).reshape(2, dp, tz, -1).transpose(2, 1, 0, 3).reshape(tz, dp, -1),
                jnp.stack([sums1[2], sums1[1], sums2[2], sums2[1]])
                .reshape(4, dp, tz, -1).transpose(2, 1, 0, 3).reshape(tz, dp, -1),
            ],
            axis=-1,
        )
        if l > 0:
            above, above_heads = units, heads
            flow.wait(heads.send)
            residual = g1
    small_sums = jnp.stack(small_grads, axis=2).reshape(tz, dp, -1)
    if small_slice:
        heads.along_x()
        small_sums = fold_small(spread_by_distance(small_sums, where), 0, 1)
        flow.wait(back[2])
        flow.hold(small=small_sums, got=heads.got)
        gate(flow)
        small_sums, heads.got = flow.free("small"), flow.free("got")
        input_grad = turn(add(g1, back[0], back[1][0], back[2]).astype(BF16))
        heads.along_y()
        small_sums = fold_small(small_sums, 1, 2)
        flow.wait(heads.got, units.last)
        flow.hold(small=small_sums)
        gate(flow)
        small_sums = fold_small(flow.free("small"), 2, 3)
        halves = heads.halves(zh)
        small_out = fold_small(small_sums, 3, 5).reshape(layers, -1)
        arrived = [(turn(halves[0]), uncross(halves[1])), done]
        flow.hold(grad=input_grad, output=layer_output)
        qkv_grad, out_grad, up_grad, down_grad, squares = finish(
            flow, [member.parts() for member in units_of], arrived, small_out
        )
        input_grad, layer_output = flow.free("grad"), flow.free("output")
    else:
        halves = [member.halves(zh) for member in heads_of]
        d_heads = jnp.stack([add(turn(half[0]), uncross(half[1])) for half in halves])
        input_grad = turn(add(g1, back[0], back[1][0], back[2]).astype(BF16))
        small_out = lax.psum_scatter(small_sums.reshape(tz * dp, -1), ALL, scatter_dimension=0, tiled=True)
        small_out = small_out.reshape(layers, -1)
        qkv_grad = d_heads[:, :, : in_cols.stop].reshape(layers, d_heads.shape[1], -1, 3, PAIR)
        qkv_grad = qkv_grad.transpose(0, 3, 1, 2, 4).reshape(qkv_weight.shape)
        out_grad = d_heads[:, :, in_cols.stop :]
        totals = [member.total() for member in units_of]
        down_grad, up_grad = (jnp.stack([total[i] for total in totals]) for i in range(2))
        squares = sum(jnp.sum(member * member) for member in (qkv_grad, out_grad, up_grad, down_grad, small_out))

    rest = small_out[:, bias_size:]
    qv_bias_grad = small_out[:, :bias_size].reshape(qv_bias.shape)
    up_bias_grad = rest[:, cuts[0] : cuts[1]].reshape(up_bias.shape)
    gains_grad = rest[:, cuts[1] : cuts[2]].reshape(gains.shape)
    shifts_grad = rest[:, cuts[2] : cuts[3]].reshape(shifts.shape)
    entry_count = LAYERS * (4 * D * D + 2 * D * FF + FF + 8 * D)
    grad_rms = jnp.sqrt(sum_all(squares) / entry_count)
    return (
        layer_output, input_grad, qkv_grad, qv_bias_grad, out_grad, up_grad, up_bias_grad, down_grad, gains_grad,
        shifts_grad, grad_rms,
    )


def solution(mesh):
    dp, tensor = mesh.shape["dp"], mesh.shape["tensor"]
    fine = Mesh(mesh.devices.reshape(dp // 2, 2, 2, tensor // 2), ("q", "c", "zh", "zl"))
    data, model = ("q", "c"), ("zh", "zl")
    both = data + model
    weight3, weight4 = P(None, data, model), P(None, None, data, model)
    in_specs = (
        P(both, None), P(data, None), weight4, P(None, None, model, data), weight3, weight3, P(None, model, data),
        weight3, P(None, None, both), P(None, None, both), P(both, None),
    )
    out_specs = (
        P(both, None), P(both, None), weight4, P(None, None, model, data), weight3, weight3, P(None, model, data),
        weight3, P(None, None, both), P(None, None, both), P(),
    )
    return jax.shard_map(on_device, mesh=fine, in_specs=in_specs, out_specs=out_specs, check_vma=False)
```

```python
import jax
import jax.numpy as jnp
from jax import lax
from jax.experimental import pallas as pl
from jax.experimental.pallas import tpu as pltpu
from jax.sharding import Mesh
from jax.sharding import PartitionSpec as P

D = 1024
HD = 64
HEADS = 16
FF = 4096
LAYERS = 2
SEQLEN = 2048
WINDOW = 1024
EPS = 1e-06
FILL = -1000000000.0

F32 = jnp.float32
BF16 = jnp.bfloat16
GROUP = ("c", "zl")
MODEL = ("zh", "zl")
ALL = ("zh", "zl", "q", "c")
VMEM_LIMIT = 56 * 1024 * 1024
TIMES = {
    "gate": 0.1, "finish": 0.2, "norm_up": 20.0, "down_norm": 20.0, "units_back": 45.0, "up_back": 20.0, "norm_back": 6.0,
    "sum_norm_back": 20.0, "grads_theirs": 0.2, "grads_mine": 0.2, "project_qkv": 0.2, "project_gc": 0.2,
    "project_attn": 0.2, "project_gx": 0.2, "heads_grad": 0.2, "attend_forward": 40.0, "attend_backward": 30.0,
}
PEAK = 0.35e9
NT = (((1,), (1,)), ((), ()))
NN = (((1,), (0,)), ((), ()))
ROWS = 128
CHUNK = 64
BQ = 512
PAIR = 2 * HD


def mm(left, right, dims=NN):
    return lax.dot_general(left, right, dims, preferred_element_type=F32)


def full(shape):
    return pl.BlockSpec(shape, lambda *_: (0,) * len(shape))


ANY = pl.BlockSpec(memory_space=pl.ANY)


def sds(shape, kind):
    return jax.ShapeDtypeStruct(shape, kind)


class Flow:
    def __init__(self, scal):
        self.scal, self.before, self.held = scal, [], {}

    def wait(self, *arrays):
        self.before += arrays

    def hold(self, **arrays):
        self.held.update(arrays)

    def free(self, name):
        return self.held.pop(name)


def call(flow, body, grid, in_specs, out_specs, out_shape, scratch, args, flops, traffic, name, scalars=None):
    scalars = (flow.scal,) if scalars is None else scalars
    single = not isinstance(out_specs, (list, tuple))
    out_specs = [out_specs] if single else list(out_specs)
    out_shape = [out_shape] if single else list(out_shape)
    before, held = flow.before, list(flow.held.items())
    ns, nb, nh, no = len(scalars), len(before), len(held), len(out_specs)
    first, last = ns + nb + nh, ns + nb + nh + len(args) + no

    def wrapped(*refs):
        body(*refs[:ns], *refs[first:last], *refs[last + nh :])

    result = pl.pallas_call(
        wrapped,
        grid_spec=pltpu.PrefetchScalarGridSpec(
            num_scalar_prefetch=ns,
            grid=grid,
            in_specs=[ANY] * (nb + nh) + list(in_specs),
            out_specs=out_specs + [ANY] * nh,
            scratch_shapes=scratch,
        ),
        out_shape=out_shape + [sds(array.shape, array.dtype) for _, array in held],
        input_output_aliases={ns + nb + i: no + i for i in range(nh)},
        compiler_params=pltpu.CompilerParams(
            dimension_semantics=("arbitrary",) * len(grid), vmem_limit_bytes=VMEM_LIMIT
        ),
        cost_estimate=pl.CostEstimate(flops=int(TIMES[name] * PEAK), bytes_accessed=1024, transcendentals=0),
        name=name,
    )(*scalars, *before, *[array for _, array in held], *args)
    flow.before = []
    flow.held = {key: value for (key, _), value in zip(held, result[no:])}
    return result[0] if single else result[:no]


def gate(flow):
    if flow.held:
        call(flow, lambda *refs: None, (1,), [], [], [], [], [], 0, 0, "gate")


S_P, S_Q, S_C, S_ZH, S_Z = range(5)


def norm_rows(values_in):
    centred = values_in - jnp.mean(values_in, -1, keepdims=True)
    variance = jnp.mean(centred * centred, -1, keepdims=True)
    inverse = lax.rsqrt(variance + EPS)
    return centred * inverse, inverse


def norm_back_rows(grad, normed, inverse, gain):
    scaled = grad * gain
    centred = scaled - jnp.mean(scaled, -1, keepdims=True) - normed * jnp.mean(scaled * normed, -1, keepdims=True)
    return centred * inverse


def fold_rows(values_in):
    return jnp.sum(values_in.reshape(-1, 8, values_in.shape[-1]), 0)


def read(part, rows):
    return (part[0, rows, :] if len(part.shape) == 3 else part[rows, :]).astype(F32)


def part_spec(part):
    shape = part.shape
    return full(shape) if len(shape) == 2 else pl.BlockSpec((1,) + shape[1:], lambda *_: (0, 0, 0))


ONE, ZERO, TABLE = 0, 1, 16


def gain_row(layer, index):
    return 2 + 6 * layer + index


def shift_row(layer, index):
    return 4 + 6 * layer + index


def row_of(vec_ref, row):
    return vec_ref[row : row + 1, :]


def norm_forward(get_total, tokens, vec, gain, shift, n_ref, low_ref, inv_ref):

    def step(index, carry):
        rows = pl.ds(pl.multiple_of(index * CHUNK, CHUNK), CHUNK)
        normed, inverse = norm_rows(get_total(rows))
        n_ref[rows, :] = normed
        low_ref[rows, :] = (normed * row_of(vec, gain) + row_of(vec, shift)).astype(BF16)
        inv_ref[rows, :] = jnp.broadcast_to(inverse, (CHUNK, 128))
        return carry

    lax.fori_loop(0, tokens // CHUNK, step, 0)


def norm_backward(get_grad, tokens, n_ref, inv_ref, vec, gain, g_ref, low_ref, sums_ref):
    def step(index, carry):
        rows = pl.ds(pl.multiple_of(index * CHUNK, CHUNK), CHUNK)
        grad = get_grad(rows)
        normed = n_ref[rows, :]
        result = norm_back_rows(grad, normed, inv_ref[rows, 0:1], row_of(vec, gain))
        low = result.astype(BF16)
        g_ref[rows, :] = result
        low_ref[rows, :] = low
        return (
            carry[0] + fold_rows(grad * normed),
            carry[1] + fold_rows(grad),
            carry[2] + fold_rows(low.astype(F32)),
        )

    zero = jnp.zeros((8, D), F32)
    sums = lax.fori_loop(0, tokens // CHUNK, step, (zero, zero, zero))
    sums_ref[...] = jnp.zeros(sums_ref.shape, F32)
    for row, member in enumerate(sums):
        sums_ref[row : row + 1, :] = jnp.sum(member, 0, keepdims=True)


def away(s):
    return (s & 1) * 2 + s // 2


class Streamed:
    def __init__(self, refs, matrix, buffer, sems, scal):
        self.refs, self.matrix, self.buffer, self.sems, self.scal = refs, matrix, buffer, sems, scal

    def copies(self, s):
        slot = lax.rem(s, 2)
        plain, early, late = [], [], []
        for k in range(2):
            own, near_x, near_y, far_a, far_b = self.refs[5 * k : 5 * k + 5]

            def copy(source, r, k=k):
                row = ((self.scal[S_Q] ^ r) * 2 + (self.scal[S_C] ^ k)) * ROWS
                return pltpu.make_async_copy(
                    source, self.buffer.at[slot, pl.ds(pl.multiple_of(row, ROWS), ROWS), :], self.sems.at[slot, 4 * k + r]
                )

            for r, ref in enumerate((own, near_x, near_y)):
                plain.append(copy(ref.at[s, self.matrix], r))
            early.append(copy(far_a.at[jnp.minimum(s, 1), self.matrix], 3))
            late.append(copy(far_b.at[jnp.maximum(s - 2, 0), self.matrix], 3))
        return plain, early, late

    def each(self, s, act):
        plain, early, late = self.copies(s)
        for copy in plain:
            act(copy)

        @pl.when(s < 2)
        def _():
            for copy in early:
                act(copy)

        @pl.when(s >= 2)
        def _():
            for copy in late:
                act(copy)

    def start(self, s):
        self.each(s, lambda copy: copy.start())

    def wait(self, s):
        self.each(s, lambda copy: copy.wait())

    def turn(self, s, count):
        @pl.when(s == 0)
        def _():
            self.start(s)

        @pl.when(s + 1 < count)
        def _():
            self.start(s + 1)


def piece_shapes(width):
    return [pltpu.VMEM((2, D, width), BF16), pltpu.SemaphoreType.DMA((2, 8))]


def gelu_parts(u):
    size = jnp.abs(u)
    t = 1.0 / (1.0 + 0.2316419 * size)
    poly = t * (0.127414796 + t * (-0.142248368 + t * (0.7107068705 + t * (-0.7265760135 + t * 0.5307027145))))
    bell = jnp.exp(-0.5 * (u * u))
    tail = poly * bell
    cdf = jnp.where(u >= 0, 1.0 - tail, tail)
    return u * cdf, cdf + u * (0.3989422804014327 * bell)


def tiles(tokens, width):
    for i in range(2):
        for j in range(2):
            yield slice(i * tokens // 2, (i + 1) * tokens // 2), slice(j * width // 2, (j + 1) * width // 2)


def norm_up(flow, prev, parts, vec, rows_used, weight, matrix, bias, count):
    tokens = prev.shape[0]
    width = FF // count

    def body(scal_ref, prev_ref, *refs):
        part_refs, refs = refs[: len(parts)], refs[len(parts) :]
        vec_ref, bias_ref, refs = refs[0], refs[1], refs[2:]
        pieces, (n_ref, low_ref, inv_ref, act_ref, slope_ref, buffer, sems) = refs[:10], refs[10:]
        s = pl.program_id(0)
        stream = Streamed(pieces, matrix, buffer, sems, scal_ref)
        stream.turn(s, count)

        @pl.when(s == 0)
        def _():
            def total(rows):
                attn = read(part_refs[0], rows)
                for part in part_refs[1:]:
                    attn = attn + read(part, rows)
                before = read(prev_ref, rows) * row_of(vec_ref, rows_used[0]) + row_of(vec_ref, rows_used[1])
                return before + (attn + row_of(vec_ref, rows_used[2]))

            norm_forward(total, tokens, vec_ref, *rows_used[3:], n_ref, low_ref, inv_ref)

        stream.wait(s)
        slot = lax.rem(s, 2)
        for rows, cols in tiles(tokens, width):
            act, slope = gelu_parts(mm(low_ref[rows, :], buffer[slot, :, cols]) + bias_ref[0, :, cols])
            act_ref[rows, cols] = act.astype(BF16)
            slope_ref[rows, cols] = slope.astype(BF16)

    column = pl.BlockSpec((tokens, width), lambda s, _: (0, s))
    return call(
        flow, body, (count,),
        [full((tokens, D))] + [part_spec(part) for part in parts]
        + [full((TABLE, D)), pl.BlockSpec((1, 1, width), lambda s, scal_ref: (scal_ref[S_Z] ^ away(s), 0, 0))] + [ANY] * 10,
        [full((tokens, D)), full((tokens, D)), full((tokens, 128)), column, column],
        [sds((tokens, D), F32), sds((tokens, D), BF16), sds((tokens, 128), F32)] + [sds((tokens, FF), BF16)] * 2,
        piece_shapes(width), [prev, *parts, vec, bias, *weight], 2 * tokens * D * FF,
        2 * (D * FF + tokens * (10 * D + 2 * FF)), "norm_up",
    )


def down_norm(flow, act, weight, matrix, prev, vec, rows_used, count):
    tokens = prev.shape[0]
    width = FF // count

    def body(scal_ref, act_ref, prev_ref, vec_ref, *refs):
        pieces, (n_ref, low_ref, inv_ref, buffer, sems, acc) = refs[:10], refs[10:]
        s = pl.program_id(0)
        stream = Streamed(pieces, matrix, buffer, sems, scal_ref)
        stream.turn(s, count)
        stream.wait(s)
        value = mm(act_ref[...], buffer[lax.rem(s, 2)], NT)

        @pl.when(s == 0)
        def _():
            acc[...] = value

        @pl.when(s > 0)
        def _():
            acc[...] += value

        @pl.when(s == count - 1)
        def _():
            def total(rows):
                before = prev_ref[rows, :] * row_of(vec_ref, rows_used[0]) + row_of(vec_ref, rows_used[1])
                return before + (acc[rows, :] + row_of(vec_ref, rows_used[2]))

            norm_forward(total, tokens, vec_ref, *rows_used[3:], n_ref, low_ref, inv_ref)

    return call(
        flow, body, (count,),
        [pl.BlockSpec((tokens, width), lambda s, _: (0, s)), full((tokens, D)), full((TABLE, D))] + [ANY] * 10,
        [full((tokens, D)), full((tokens, D)), full((tokens, 128))],
        [sds((tokens, D), F32), sds((tokens, D), BF16), sds((tokens, 128), F32)],
        piece_shapes(width) + [pltpu.VMEM((tokens, D), F32)], [act, prev, vec, *weight], 2 * tokens * D * FF,
        2 * (D * FF + tokens * (5 * D + FF)), "down_norm",
    )


def units_back(flow, residual, parts, normed, inverse, vec, gain, weight, matrix, slope, count):
    tokens = residual.shape[0]
    width = FF // count

    def body(scal_ref, res_ref, *refs):
        part_refs, refs = refs[: len(parts)], refs[len(parts) :]
        n_ref, inv_ref, vec_ref, slope_ref, refs = refs[0], refs[1], refs[2], refs[3], refs[4:]
        pieces, (g_ref, low_ref, sums_ref, out_ref, sum_ref, buffer, sems) = refs[:10], refs[10:]
        s = pl.program_id(0)
        stream = Streamed(pieces, matrix, buffer, sems, scal_ref)
        stream.turn(s, count)

        @pl.when(s == 0)
        def _():
            def grad(rows):
                total = read(res_ref, rows)
                for part in part_refs:
                    total = total + read(part, rows)
                return total

            norm_backward(grad, tokens, n_ref, inv_ref, vec_ref, gain, g_ref, low_ref, sums_ref)

        stream.wait(s)
        slot = lax.rem(s, 2)
        sums = {}
        for rows, cols in tiles(tokens, width):
            low = (mm(low_ref[rows, :], buffer[slot, :, cols]) * slope_ref[rows, cols].astype(F32)).astype(BF16)
            out_ref[rows, cols] = low
            part = fold_rows(low.astype(F32))
            sums[cols.start] = sums[cols.start] + part if cols.start in sums else part
            if rows.start > 0:
                sum_ref[0, :, cols] = jnp.sum(sums[cols.start], 0, keepdims=True)

    column = pl.BlockSpec((tokens, width), lambda s, _: (0, s))
    return call(
        flow, body, (count,),
        [full((tokens, D))] + [part_spec(part) for part in parts]
        + [full((tokens, D)), full((tokens, 128)), full((TABLE, D)), column] + [ANY] * 10,
        [full((tokens, D)), full((tokens, D)), full((8, D)), column,
         pl.BlockSpec((1, 1, width), lambda s, scal_ref: (scal_ref[S_Z] ^ away(s), 0, 0))],
        [sds((tokens, D), F32), sds((tokens, D), BF16), sds((8, D), F32), sds((tokens, FF), BF16),
         sds((count, 1, width), F32)],
        piece_shapes(width), [residual, *parts, normed, inverse, vec, slope, *weight], 0, 0, "units_back",
    )


def up_back(flow, gu, weight, matrix, residual, normed, inverse, vec, gain, count):
    tokens = residual.shape[0]
    width = FF // count

    def body(scal_ref, gu_ref, res_ref, n_ref, inv_ref, vec_ref, *refs):
        pieces, (g_ref, low_ref, sums_ref, buffer, sems, acc) = refs[:10], refs[10:]
        s = pl.program_id(0)
        stream = Streamed(pieces, matrix, buffer, sems, scal_ref)
        stream.turn(s, count)
        stream.wait(s)
        value = mm(gu_ref[...], buffer[lax.rem(s, 2)], NT)

        @pl.when(s == 0)
        def _():
            acc[...] = value

        @pl.when(s > 0)
        def _():
            acc[...] += value

        @pl.when(s == count - 1)
        def _():
            norm_backward(
                lambda rows: res_ref[rows, :] + acc[rows, :], tokens, n_ref, inv_ref, vec_ref, gain, g_ref, low_ref,
                sums_ref,
            )

    return call(
        flow, body, (count,),
        [pl.BlockSpec((tokens, width), lambda s, _: (0, s)), full((tokens, D)), full((tokens, D)), full((tokens, 128)),
         full((TABLE, D))] + [ANY] * 10,
        [full((tokens, D)), full((tokens, D)), full((8, D))],
        [sds((tokens, D), F32), sds((tokens, D), BF16), sds((8, D), F32)],
        piece_shapes(width) + [pltpu.VMEM((tokens, D), F32)], [gu, residual, normed, inverse, vec, *weight],
        2 * tokens * D * FF, 2 * (D * FF + tokens * (8 * D + FF)), "up_back",
    )


def turn_rows(scal_ref, x_ref, turned, core):
    for r in range(4):
        row = ((scal_ref[S_Q] ^ r) * 2 + core) * ROWS
        turned[r * ROWS : (r + 1) * ROWS, :] = x_ref[:, pl.ds(pl.multiple_of(row, ROWS), ROWS)].T


def unit_grads(flow, down, up, received, count, sibling):
    tokens = down[0].shape[0]
    width = down[1].shape[1] // count
    half = count // 2
    steps = 2 * count

    def body(scal_ref, x0_ref, y0_ref, x1_ref, y1_ref, *refs):
        turned, t = refs[-1], pl.program_id(0)
        m, s = t // count, lax.rem(t, count)
        core = scal_ref[S_C] ^ 1 if sibling else scal_ref[S_C]

        @pl.when(t == 0)
        def _():
            turn_rows(scal_ref, x0_ref, turned, core)

        @pl.when(t == count)
        def _():
            turn_rows(scal_ref, x1_ref, turned, core)

        def store(y_ref):
            value = mm(turned[...], y_ref[...]).reshape(4, ROWS, width)
            if sibling:
                refs[0][:, 0] = value.astype(BF16)
                return
            if received is not None:
                value = value + refs[0][:, 0].astype(F32)
            value = value.astype(BF16)
            own, to_x, to_y, rest_x, rest_y = refs[-6:-1]
            spot = lax.rem(s, half) * 2 + m
            own[s // half * count + spot] = value[0]

            @pl.when(s < half)
            def _():
                to_x[spot] = value[1]
                to_x[count + spot] = value[3]
                rest_y[spot] = value[2]

            @pl.when(s >= half)
            def _():
                rest_x[spot] = value[1]
                to_y[spot] = value[2]
                to_y[count + spot] = value[3]

        @pl.when(m == 0)
        def _():
            store(y0_ref)

        @pl.when(m == 1)
        def _():
            store(y1_ref)

    left = full((tokens, D))
    pick_down = lambda t, _: (0, jnp.minimum(t, count - 1))
    pick_up = lambda t, _: (0, jnp.maximum(t - count, 0))
    specs = [left, pl.BlockSpec((tokens, width), pick_down), left, pl.BlockSpec((tokens, width), pick_up)]
    args = [*down, *up]
    one = pl.BlockSpec((4, 1, ROWS, width), lambda t, _: (0, t, 0, 0))
    if sibling:
        out_specs, out_shape = one, sds((4, steps, ROWS, width), BF16)
    else:
        if received is not None:
            specs.append(one)
            args.append(received)
        shapes = [(steps, ROWS, width)] * 3 + [(count, ROWS, width)] * 2
        out_specs, out_shape = [full(shape) for shape in shapes], [sds(shape, BF16) for shape in shapes]
    return call(
        flow, body, (steps,), specs, out_specs, out_shape, [pltpu.VMEM((4 * ROWS, tokens), BF16)], args,
        0, 0, "grads_theirs" if sibling else "grads_mine",
    )


def finish(flow, units, heads, small):
    layers = len(units)
    rows, cols = heads[0][0].shape
    in_width = cols * 3 // 4
    pairs = in_width // (3 * PAIR)
    width = units[0][0].shape[2]

    def body(scal_ref, *refs):
        qkv_ref, out_ref, up_ref, down_ref, square_ref = refs[-5:]
        small_ref, refs = refs[-6], refs[:-6]
        squares = jnp.sum(small_ref[...] * small_ref[...], keepdims=True)
        for l in range(layers):
            unit_refs, (first, second) = refs[7 * l : 7 * l + 5], refs[7 * l + 5 : 7 * l + 7]
            for m, target in enumerate((down_ref, up_ref)):
                total = unit_refs[0][m].astype(F32)
                for part in unit_refs[1:]:
                    total = total + part[m].astype(F32)
                target[l] = total
                squares = squares + jnp.sum(jnp.sum(total * total, 0, keepdims=True), 1, keepdims=True)
            total = first[...].astype(F32) + second[...].astype(F32)
            squares = squares + jnp.sum(jnp.sum(total * total, 0, keepdims=True), 1, keepdims=True)
            out_ref[l] = total[:, in_width:]
            for pair in range(pairs):
                for which in range(3):
                    base = (3 * pair + which) * PAIR
                    qkv_ref[l, which, :, pair * PAIR : (pair + 1) * PAIR] = total[:, base : base + PAIR]
        square_ref[...] = jnp.broadcast_to(squares, (8, 128))

    specs, args = [], []
    for l in range(layers):
        specs += [pl.BlockSpec((2, rows, width), lambda *_: (0, 0, 0))] * 5 + [full((rows, cols))] * 2
        args += [*units[l], *heads[l]]
    shapes = [(layers, 3, rows, in_width // 3), (layers, rows, cols - in_width), (layers, rows, width), (layers, rows, width),
              (8, 128)]
    return call(
        flow, body, (1,), specs + [full(small.shape)], [full(shape) for shape in shapes],
        [sds(shape, F32) for shape in shapes], [], args + [small], 0, 0, "finish",
    )


def place_heads_weight(scal_ref, pieces, buffer):
    for r in range(4):
        for k in range(2):
            row = ((scal_ref[S_Q] ^ r) * 2 + (scal_ref[S_ZH] ^ k)) * ROWS
            buffer[pl.ds(pl.multiple_of(row, ROWS), ROWS), :] = pieces[r // 2][r % 2, k, :ROWS, :]


def heads_weight_specs(weight, cols):
    width = cols.stop - cols.start
    return [pl.BlockSpec((2, 2, piece.shape[2], width), lambda *_: (0, 0, 0, cols.start // width)) for piece in weight]


def by_member(shape):
    return pl.BlockSpec((1,) + shape, lambda r, scal_ref: (scal_ref[S_P] ^ r, 0, 0))


def heads_weight_scratch(width):
    return [pltpu.VMEM((D, width), BF16)]


def project_in(flow, lefts, across, weight, cols, bias, name):
    tokens = lefts[0].shape[0]
    width = cols.stop - cols.start

    def body(scal_ref, left_ref, right_ref, *refs):
        if bias is not None:
            bias_ref, refs = refs[0], refs[1:]
        pieces, (out_ref, buffer) = refs[:2], refs[2:]
        step = pl.program_id(0)

        @pl.when(step == 0)
        def _():
            place_heads_weight(scal_ref, pieces, buffer)

        for r, left in enumerate((left_ref, right_ref)):

            @pl.when(step == r)
            def _(left=left):
                value = mm(left[...], buffer[...])
                if bias is not None:
                    value = value + bias_ref[...]
                out_ref[0] = value.astype(BF16)

    extra, extra_specs = ([], []) if bias is None else ([bias], [full((1, width))])
    return call(
        flow, body, (2,), [full((tokens, D))] * 2 + extra_specs + heads_weight_specs(weight, cols),
        pl.BlockSpec((1, tokens, width), lambda r, scal_ref: ((scal_ref[S_P] >> 1) ^ r, 0, 0)),
        sds((2, tokens, width), BF16), heads_weight_scratch(width), [*lefts, *extra, *weight], 0, 0, name,
    )


def project_out(flow, blocks, members, weight, cols, stacked, name):
    count, tokens, width = blocks[0].shape

    def body(scal_ref, *refs):
        block_refs, refs = refs[: len(blocks)], refs[len(blocks) :]
        pieces, outs, buffer = refs[:2], refs[2:-1], refs[-1]
        step = pl.program_id(0)

        @pl.when(step == 0)
        def _():
            place_heads_weight(scal_ref, pieces, buffer)

        value = mm(block_refs[0][0], buffer[:, :width], NT)
        for index in range(1, len(blocks)):
            value = value + mm(block_refs[index][0], buffer[:, index * width : (index + 1) * width], NT)
        value = value.astype(BF16)
        if stacked:
            outs[0][0] = value
            return
        for r, out in enumerate(outs):

            @pl.when(step == r)
            def _(out=out):
                out[...] = value

    first, last = members
    pick = lambda r, scal_ref: (scal_ref[S_P] ^ (first + r * (last - first)), 0, 0)
    if stacked:
        out_specs, out_shape = pl.BlockSpec((1, tokens, D), lambda r, _: (r, 0, 0)), sds((2, tokens, D), BF16)
    else:
        out_specs, out_shape = [full((tokens, D))] * 2, [sds((tokens, D), BF16)] * 2
    return call(
        flow, body, (2,), [pl.BlockSpec((1, tokens, width), pick)] * len(blocks) + heads_weight_specs(weight, cols), out_specs,
        out_shape,
        heads_weight_scratch(width * len(blocks)), [*blocks, *weight], 0, 0, name,
    )


def heads_grad(flow, xs, parts, gas, ctx):
    count, tokens, width = parts[0].shape
    out_width = ctx.shape[2]
    cuts = [slice(i * width, (i + 1) * width) for i in range(len(parts))]
    total = width * len(parts)

    def body(scal_ref, *refs):
        x_refs, refs = refs[:count], refs[count:]
        ga_refs, refs = refs[:count], refs[count:]
        part_refs, refs = refs[: len(parts)], refs[len(parts) :]
        ctx_ref, outs, (sum_ref, acc, acc_out) = refs[0], refs[1:3], refs[3:]
        step = pl.program_id(0)
        for r in range(count):

            @pl.when(step == r)
            def _(r=r):
                turned = x_refs[r][...].T
                value_out = mm(ga_refs[r][...].T, ctx_ref[0])
                for cut, part in zip(cuts, part_refs):
                    value = mm(turned, part[0])
                    sums = jnp.sum(part[0].astype(F32), 0, keepdims=True)
                    acc[:, cut] = value if r == 0 else acc[:, cut] + value
                    sum_ref[:, cut] = sums if r == 0 else sum_ref[:, cut] + sums
                acc_out[...] = value_out if r == 0 else acc_out[...] + value_out

        @pl.when(step == count - 1)
        def _():
            for r in range(4):
                for k in range(2):
                    row = ((scal_ref[S_Q] ^ r) * 2 + (scal_ref[S_ZH] ^ k)) * ROWS
                    rows = pl.ds(pl.multiple_of(row, ROWS), ROWS)
                    outs[r % 2][r // 2, k, :, :total] = acc[rows, :].astype(BF16)
                    outs[r % 2][r // 2, k, :, total:] = acc_out[rows, :].astype(BF16)

    shape = (2, 2, ROWS, total + out_width)
    return call(
        flow, body, (count,),
        [full((tokens, D))] * (2 * count) + [by_member((tokens, width))] * len(parts) + [by_member((tokens, out_width))],
        [full(shape)] * 2 + [full((1, total))], [sds(shape, BF16)] * 2 + [sds((1, total), F32)],
        [pltpu.VMEM((D, total), F32), pltpu.VMEM((D, out_width), F32)], [*xs, *gas, *parts, ctx], 0, 0, "heads_grad",
    )


def reach(ends_ref, row):
    first = jnp.zeros_like(row)
    for index in range(3):
        first = jnp.where(row >= ends_ref[index], ends_ref[index], first)
    last = jnp.full_like(row, SEQLEN)
    for index in (2, 1, 0):
        last = jnp.where(row < ends_ref[index], ends_ref[index], last)
    return jnp.maximum(first, row - (WINDOW - 1)), jnp.minimum(last, row + WINDOW)


def chunks_of(scal_ref, near_ref, far_ref):
    here = scal_ref[S_P] & 1
    for core in range(2):
        yield 2 * core + here, near_ref.at[core]
        yield 2 * core + 1 - here, far_ref.at[core]


def over_keys(ends_ref, start, chunk, keys_first, block):
    low_first, high_first = reach(ends_ref, start)
    low_last, high_last = reach(ends_ref, start + BQ - 1)
    axis = 1 if keys_first else 0
    low_row, high_row = reach(ends_ref, start + lax.broadcasted_iota(jnp.int32, (1, BQ) if keys_first else (BQ, 1), axis))
    shape = (chunk, BQ) if keys_first else (BQ, chunk)

    def one(b, carry):
        open_all = (b * chunk >= low_last) & ((b + 1) * chunk <= high_first)

        @pl.when(open_all)
        def _():
            block(b, None)

        @pl.when(jnp.logical_not(open_all))
        def _():
            key = b * chunk + lax.broadcasted_iota(jnp.int32, shape, 1 - axis)
            block(b, (key >= low_row) & (key < high_row))

        return carry

    lax.fori_loop(low_first // chunk, (high_last + chunk - 1) // chunk, one, 0)


def attend_forward(flow, ends, qkv):
    _, chunk, width3 = qkv[0].shape
    count = SEQLEN // chunk
    width = width3 // 3
    heads = width // HD
    steps = SEQLEN // BQ
    per = chunk // BQ

    def body(scal_ref, ends_ref, near_ref, far_ref, ctx_ref, wide_ref, lse_ref, qt, kh, vt, acc, tops, sums, scores):
        step = pl.program_id(0)

        @pl.when(step == 0)
        def _():
            for j, block in chunks_of(scal_ref, near_ref, far_ref):
                rows = pl.ds(pl.multiple_of(j * chunk, chunk), chunk)
                for pair in range(heads // 2):
                    base = 3 * PAIR * pair
                    part = slice(pair * PAIR, (pair + 1) * PAIR)
                    vt[j, part, :] = block[:, base + 2 * PAIR : base + 3 * PAIR].T
                    for s in range(per):
                        queries = block[s * BQ : (s + 1) * BQ, base : base + PAIR] * BF16(HD**-0.5)
                        qt[j * per + s, part, :] = queries.T
                    for h in range(2):
                        kh[2 * pair + h, rows, :] = block[:, base + PAIR + h * HD : base + PAIR + (h + 1) * HD]

        start = step * BQ
        acc[...] = jnp.zeros(acc.shape, F32)
        tops[...] = jnp.full(tops.shape, -3.0e38, F32)
        sums[...] = jnp.zeros(sums.shape, F32)

        def score(b, allowed):
            keys = pl.ds(pl.multiple_of(b * chunk, chunk), chunk)
            for h in range(heads):
                value = mm(kh[h, keys, :], qt[step, h * HD : (h + 1) * HD, :])
                if allowed is not None:
                    value = jnp.where(allowed, value, FILL)
                scores[h, b] = value
                tops[h] = jnp.maximum(tops[h], jnp.max(value.reshape(-1, 8, BQ), 0))

        over_keys(ends_ref, start, chunk, True, score)
        top = [jnp.max(tops[h], 0, keepdims=True) for h in range(heads)]

        def weigh(b, carry):
            for h in range(heads):
                part = slice(h * HD, (h + 1) * HD)
                weight = jnp.exp(scores[h, b] - top[h])
                sums[h] += fold_rows(weight)
                acc[part, :] += mm(vt[b, part, :], weight.astype(BF16))
            return carry

        low_first, _ = reach(ends_ref, start)
        _, high_last = reach(ends_ref, start + BQ - 1)
        lax.fori_loop(low_first // chunk, (high_last + chunk - 1) // chunk, weigh, 0)
        lse_ref[...] = jnp.zeros(lse_ref.shape, F32)
        for h in range(heads):
            part = slice(h * HD, (h + 1) * HD)
            total = jnp.sum(sums[h], 0, keepdims=True)
            acc[part, :] = acc[part, :] / total
            lse_ref[0, h : h + 1, :] = top[h] + jnp.log(total)
        wide = acc[...].T
        wide_ref[0] = wide
        ctx_ref[0] = wide.astype(BF16)

    row_block = lambda i, *_: (i // per, i % per, 0)
    return call(
        flow, body, (steps,), [full((2, chunk, width3))] * 2,
        [pl.BlockSpec((1, BQ, width), row_block), pl.BlockSpec((1, BQ, width), row_block),
         pl.BlockSpec((1, 8, BQ), lambda i, *_: (i, 0, 0))],
        [sds((count, chunk, width), BF16), sds((count, chunk, width), F32), sds((steps, 8, BQ), F32)],
        [
            pltpu.VMEM((steps, width, BQ), BF16),
            pltpu.VMEM((heads, SEQLEN, HD), BF16),
            pltpu.VMEM((count, width, chunk), BF16),
            pltpu.VMEM((width, BQ), F32),
            pltpu.VMEM((heads, 8, BQ), F32),
            pltpu.VMEM((heads, 8, BQ), F32),
            pltpu.VMEM((heads, count, chunk, BQ), F32),
        ],
        [*qkv], 0, 0, "attend_forward", (flow.scal, ends),
    )


def attend_backward(flow, ends, pair, qkv, grads, wide, lse):
    chunk = qkv[0].shape[1]
    count = SEQLEN // chunk
    steps = SEQLEN // BQ
    per = chunk // BQ

    def body(
        scal_ref, ends_ref, near_ref, far_ref, grad_near, grad_far, wide_ref, lse_ref, out_ref, qh, gh, kt, vt, qt, gt,
        gq, gk, gv,
    ):
        step = pl.program_id(0)

        @pl.when(step == 0)
        def _():
            blocks = chunks_of(scal_ref, near_ref, far_ref)
            grad_blocks = chunks_of(scal_ref, grad_near, grad_far)
            for (j, block), (_, grad_block) in zip(blocks, grad_blocks):
                rows = pl.ds(pl.multiple_of(j * chunk, chunk), chunk)
                queries = block[:, :PAIR] * BF16(HD**-0.5)
                keys = block[:, PAIR : 2 * PAIR]
                back = grad_block[...]
                for h in range(2):
                    cols = slice(h * HD, (h + 1) * HD)
                    qh[h, rows, :] = queries[:, cols]
                    gh[h, rows, :] = back[:, cols]
                kt[j] = keys.T
                vt[j] = block[:, 2 * PAIR :].T
                for s in range(per):
                    sub = slice(s * BQ, (s + 1) * BQ)
                    qt[j * per + s] = queries[sub, :].T
                    gt[j * per + s] = back[sub, :].T
            gk[...] = jnp.zeros(gk.shape, F32)
            gv[...] = jnp.zeros(gv.shape, F32)

        start = step * BQ
        rows = pl.ds(pl.multiple_of(start, BQ), BQ)
        gq[...] = jnp.zeros(gq.shape, F32)
        sums = lse_ref[0].T
        inner, logs = [], []
        for h in range(2):
            product = gh[h, rows, :].astype(F32) * wide_ref[0, :, h * HD : (h + 1) * HD]
            inner.append(jnp.sum(product, 1, keepdims=True))
            logs.append(sums[:, 2 * pair + h : 2 * pair + h + 1])

        def block(b, allowed):
            for h in range(2):
                part = slice(h * HD, (h + 1) * HD)
                score = mm(qh[h, rows, :], kt[b, part, :])
                grad_weight = mm(gh[h, rows, :], vt[b, part, :])
                if allowed is not None:
                    score = jnp.where(allowed, score, FILL)
                weight = jnp.exp(score - logs[h])
                grad_score = (weight * (grad_weight - inner[h])).astype(BF16)
                gv[b, part, :] += mm(gt[step, part, :], weight.astype(BF16))
                gk[b, part, :] += mm(qt[step, part, :], grad_score)
                gq[part, :] += mm(kt[b, part, :], grad_score, NT)

        over_keys(ends_ref, start, chunk, False, block)
        place = pl.ds(pl.multiple_of((step % per) * BQ, BQ), BQ)
        out_ref[step // per, place, :PAIR] = (gq[...] * HD**-0.5).T.astype(BF16)

        @pl.when(step == steps - 1)
        def _():
            for j in range(count):
                out_ref[j, :, PAIR : 2 * PAIR] = gk[j].T.astype(BF16)
                out_ref[j, :, 2 * PAIR :] = gv[j].T.astype(BF16)

    out = (count, chunk, 3 * PAIR)
    return call(
        flow, body, (steps,),
        [pl.BlockSpec((2, chunk, 3 * PAIR), lambda i, *_: (0, 0, pair))] * 2
        + [pl.BlockSpec((2, chunk, PAIR), lambda i, *_: (0, 0, pair))] * 2
        + [pl.BlockSpec((1, BQ, PAIR), lambda i, *_: (i // per, i % per, pair)),
           pl.BlockSpec((1, 8, BQ), lambda i, *_: (i, 0, 0))],
        full(out), sds(out, BF16),
        [pltpu.VMEM((2, SEQLEN, HD), BF16)] * 2
        + [pltpu.VMEM((count, PAIR, chunk), BF16)] * 2
        + [pltpu.VMEM((steps, PAIR, BQ), BF16)] * 2
        + [pltpu.VMEM((PAIR, BQ), F32)]
        + [pltpu.VMEM((count, PAIR, chunk), F32)] * 2,
        [*qkv, *grads, wide, lse], 0, 0, "attend_backward", (flow.scal, ends),
    )


def flip(values_in, axes, mask):
    return lax.ppermute(values_in, axes, [(a, a ^ mask) for a in range(lax.axis_size(axes))])


def turn(values_in):
    return lax.ppermute(values_in, ("c", "zh"), [(2 * a + b, 2 * b + a) for a in range(2) for b in range(2)])


def uncross(values_in):
    return lax.ppermute(values_in, ("c", "zh"), [(2 * b + 1 - a, 2 * a + b) for a in range(2) for b in range(2)])


def from_members(values_in, axes):
    return [values_in] + [flip(values_in, axes, r) for r in range(1, lax.axis_size(axes))]


def to_members(parts, axes):
    return [parts[0]] + [flip(part, axes, r) for r, part in enumerate(parts) if r > 0]


def add(*parts):
    total = parts[0].astype(F32)
    for part in parts[1:]:
        total = total + part.astype(F32)
    return total


def is_small():
    return lax.axis_size("q") == 4


def order_by(values_in, axis, position, count):
    bit = 1
    while bit < count:
        shape = values_in.shape
        split = shape[:axis] + (count // (2 * bit), 2, bit) + shape[axis + 1 :]
        cut = values_in.reshape(split)
        values_in = jnp.where((position & bit) != 0, jnp.flip(cut, axis + 1), cut).reshape(shape)
        bit *= 2
    return values_in


def gather_group(values_in):
    across, sibling = flip(values_in, GROUP, 1), flip(values_in, GROUP, 2)
    return [values_in, across, sibling]


def forward(flow, members, *before):
    flow.wait(*before)
    flow.hold(across=members[1])
    gate(flow)
    members[1] = flow.free("across")
    members.append(flip(members[1], GROUP, 2))


def sum_group(keep, send):
    got = flip(send, GROUP, 2)
    passed = add(keep[1], got[1]).astype(BF16)
    return [keep[0], got, flip(passed, GROUP, 1)], passed


EXTRA = 16


def heads_shard_of(qkv, out, bias):
    rows = out.shape[0]
    paired = qkv.reshape(3, rows, -1, PAIR).transpose(1, 2, 0, 3).reshape(rows, -1)
    weights = jnp.concatenate([paired, out], axis=1)
    below = jnp.pad(bias.reshape(1, -1), ((0, EXTRA - 1), (0, weights.shape[1] - bias.size)))
    return jnp.concatenate([weights, below])


def heads_bias(rows, heads):
    bias = rows.reshape(rows.shape[0], 2, heads, -1).transpose(1, 2, 0, 3).reshape(2, -1).astype(F32)
    bias = jnp.stack([bias[0], jnp.zeros_like(bias[0]), bias[1]])
    return bias.reshape(3, -1, PAIR).transpose(1, 0, 2).reshape(1, -1)


def with_sibling(shard):
    return jnp.stack([shard, flip(shard, "c", 1)])


def heads_along_x(pair):
    return jnp.stack([pair, flip(pair, "q", 1)])


def heads_along_y(near, size, heads, where, zh):
    return heads_pieces(near, flip(near, "q", 2), size, heads, where, zh)


def heads_pieces(near, far, size, heads, where, zh):
    rows = jnp.concatenate([near[:, :, ROWS, :size], far[:, :, ROWS, :size]])
    return [near, far], heads_bias(order_by(order_by(rows, 0, where[0], 4), 1, zh, 2).reshape(8, size), heads)


def all_heads_weight(shard, size, heads, zh):
    pair = turn(with_sibling(shard))
    every = order_by(lax.all_gather(pair, "q"), 1, zh, 2)
    count = shard.shape[0] - EXTRA
    weights = every[:, :, :count].reshape(4, 2, ROWS, -1)
    return [weights[:2], weights[2:]], heads_bias(every[:, :, count, :size].reshape(-1, size), heads)


class HeadsGrad:
    def __init__(self, keep, send):
        self.keep, self.send = keep, send

    def along_x(self):
        self.got = flip(self.send, "q", 1)
        return self.got

    def along_y(self):
        self.got_x = self.got
        self.got = flip(add(self.keep[1], self.got[1]).astype(BF16), "q", 2)
        return self.got

    def halves(self, zh):
        if is_small():
            return tuple(add(self.keep[0, k], self.got_x[0, k], self.got[k]).astype(BF16) for k in range(2))
        buckets = [self.keep[0], self.send[0], self.keep[1], self.send[1]]
        every = jnp.stack(buckets).reshape(lax.axis_size("q"), 2, -1, buckets[0].shape[-1])
        rows = order_by(lax.psum_scatter(every, "q", scatter_dimension=0, tiled=False), 0, zh, 2)
        return rows[0], rows[1]


SLOTS = (0, 2, 1, 3)


def all_units_weight(shard):
    matrices, _, width = shard.shape
    members = lax.axis_size(MODEL)
    every = lax.all_gather(shard, ALL).reshape(members, -1, matrices, shard.shape[1], width).transpose(0, 2, 1, 3, 4)
    every = every.reshape(members, matrices, 4, 2, ROWS, width)
    every = jnp.stack([every[slot] for slot in SLOTS])
    pieces = []
    for k in range(2):
        pieces += [every[:, :, r, k] for r in range(3)] + [every[:2, :, 3, k], every[2:, :, 3, k]]
    return pieces


class UnitsWeight:
    def __init__(self, shard):
        self.shard, self.theirs = shard, {}

    def start_far_z(self):
        self.other = flip(self.shard, "zh", 1)

    def join_far_z(self, shard):
        self.two = jnp.stack([shard, self.other])

    def far_z(self):
        self.start_far_z()
        self.join_far_z(self.shard)

    def start_z(self):
        self.other = flip(self.two, "zl", 1)

    def join_z(self, two):
        self.own = jnp.concatenate([two, self.other])

    def near_z(self):
        self.start_z()
        self.join_z(self.two)

    def near(self):
        self.near_x, self.near_y = flip(self.own, "q", 1), flip(self.own, "q", 2)

    def corner(self):
        self.far_a, self.far_b = flip(self.near_y[:2], "q", 1), flip(self.near_x[2:], "q", 2)

    def swap(self, *names):
        for name in names:
            self.theirs[name] = flip(getattr(self, name), "c", 1)

    def pieces(self):
        names = ("own", "near_x", "near_y", "far_a", "far_b")
        return [getattr(self, name) for name in names] + [self.theirs[name] for name in names]


class UnitsGrads:
    def __init__(self, flow, down, up, count):
        self.flow, self.down, self.up, self.count = flow, down, up, count

    def compute_theirs(self):
        self.theirs = unit_grads(self.flow, self.down, self.up, None, self.count, True)

    def send_theirs(self):
        self.got = flip(self.theirs, "c", 1) if is_small() else None

    def sibling(self):
        self.compute_theirs()
        self.send_theirs()

    def mine(self):
        self.made = unit_grads(self.flow, self.down, self.up, self.got, self.count, False)
        self.own, self.to_x, self.to_y, self.rest_x, self.rest_y = self.made

    def near(self):
        self.from_x, self.from_y = flip(self.to_x, "q", 1), flip(self.to_y, "q", 2)
        return [self.from_x, self.from_y]

    def far(self):
        half = self.count
        self.late_x = flip(add(self.rest_x, self.from_y[half:]).astype(BF16), "q", 1)
        self.late_y = flip(add(self.rest_y, self.from_x[half:]).astype(BF16), "q", 2)
        return [self.late_x, self.late_y]

    def near_z(self):
        half = self.count
        self.passing = add(self.own[half:], self.late_x, self.from_y[:half]).astype(BF16)
        self.there = flip(self.passing, "zl", 1)
        return [self.there]

    def far_z(self):
        self.last = flip(self.near_sum(slice(self.count // 2, self.count)).astype(BF16), "zh", 1)
        return [self.last]

    def near_sum(self, blocks):
        return add(self.own[blocks], self.from_x[blocks], self.late_y[blocks], self.there[blocks])

    def parts(self):
        return self.own, self.from_x, self.late_y, self.there, self.last

    def total(self):
        half = self.count
        mine = jnp.stack(
            [self.own, jnp.concatenate([self.to_x[:half], self.rest_x]), jnp.concatenate([self.rest_y, self.to_y[:half]]),
             jnp.concatenate([self.to_x[half:], self.to_y[half:]])]
        ).reshape(4, self.count, 2, ROWS, -1)
        theirs = self.theirs.reshape(4, 2, self.count, ROWS, -1).transpose(0, 2, 1, 3, 4)
        every = jnp.stack([mine, theirs], axis=1)
        every = every.transpose(2, 0, 1, 4, 3, 5)
        every = jnp.stack([every[slot] for slot in SLOTS]).reshape(-1, 2, mine.shape[-1])
        return lax.psum_scatter(every, ALL, scatter_dimension=0, tiled=True).astype(F32).transpose(1, 0, 2)


SMALL_AXES = ("q", MODEL, "c")
SMALL_STEPS = (("q", 1), ("q", 2), ("zl", 1), ("zh", 1), ("c", 1))
SMALL_SHAPE = (128, 256)


def spread_by_distance(values_in, where):
    every = values_in.reshape(4, 4, 2, -1).transpose(1, 0, 2, 3)
    for axis, position in enumerate(where):
        every = order_by(every, axis, position, every.shape[axis])
    return every.transpose(2, 1, 0, 3).reshape(32, -1)


def fold_small(every, first, last):
    for axis, mask in SMALL_STEPS[::-1][first:last]:
        half = every.shape[0] // 2
        every = every[:half] + flip(every[half:], axis, mask)
    return every


def sum_all(value):
    if not is_small():
        return lax.psum(value, ALL)
    for axes in SMALL_AXES:
        parts = jnp.stack(from_members(value, axes))
        value = jnp.sum(order_by(parts, 0, lax.axis_index(axes), parts.shape[0]), 0)
    return value[0, 0]


def on_device(
    tokens, doc_lengths, qkv_weight, qv_bias, out_weight, up_weight, up_bias, down_weight, gains, shifts, cotangent
):
    layers = qkv_weight.shape[0]
    tz, dp = lax.axis_size(MODEL), lax.axis_size(("q", "c"))
    place, zh = lax.axis_index(GROUP), lax.axis_index("zh")
    where = (lax.axis_index("q"), lax.axis_index(MODEL), lax.axis_index("c"))
    if is_small():
        spots = [place, where[0], where[2], zh, where[1]]
    else:
        spots = [place] + [jnp.zeros((), jnp.int32)] * 4
    scal = jnp.stack([spot.astype(jnp.int32) for spot in spots])

    flow = Flow(scal)
    small_slice = is_small()
    qkv_cols, out_cols = 3 * out_weight.shape[2], out_weight.shape[2]
    in_cols, out_cols = slice(0, qkv_cols), slice(qkv_cols, qkv_cols + out_cols)
    hz, bias_size = qv_bias.shape[2], qv_bias.size // layers
    heads_shard = [heads_shard_of(qkv_weight[l], out_weight[l], qv_bias[l]) for l in range(layers)]
    pieces = [up_bias, gains, shifts]
    sizes = [piece.size // layers for piece in pieces]
    cuts = [0]
    for size in sizes:
        cuts.append(cuts[-1] + size)
    small = jnp.concatenate([piece.reshape(layers, -1) for piece in pieces], axis=1).reshape(-1)
    padded = jnp.pad(small, (0, SMALL_SHAPE[0] * SMALL_SHAPE[1] - small.size)).reshape(SMALL_SHAPE)
    gathered = lax.all_gather(padded, ALL)
    small_all = gathered.reshape(tz * dp, -1)[:, : small.size]

    def spread_small():
        every = small_all.reshape(tz, dp, layers, -1).astype(F32)
        parts = [every[..., cuts[i] : cuts[i + 1]] for i in range(3)]
        biases = parts[0].reshape(tz, dp, layers, up_bias.shape[1], -1).transpose(2, 0, 3, 1, 4)
        gain = parts[1].reshape(tz, dp, layers, 2, -1).transpose(2, 3, 1, 0, 4).reshape(layers, 2, D)
        shift = parts[2].reshape(tz, dp, layers, 4, -1).transpose(2, 3, 1, 0, 4).reshape(layers, 4, D)
        table = jnp.concatenate([gain, shift], axis=1).reshape(layers * 6, D)
        head = jnp.concatenate([jnp.ones((1, D), F32), jnp.zeros((1, D), F32)])
        return biases.reshape(layers, tz, 1, -1), jnp.pad(jnp.concatenate([head, table]), ((0, TABLE - 2 - 6 * layers), (0, 0)))

    up_bias_full, table = spread_small()
    if small_slice:
        pair = with_sibling(heads_shard[0])
        bundle = turn(jnp.concatenate([tokens, pair.reshape(-1, D)]))
        x_low, pair = bundle[: tokens.shape[0]], bundle[tokens.shape[0] :].reshape(pair.shape)
        ends = jnp.cumsum(turn(doc_lengths)[0], dtype=jnp.int32)
        members = from_members(pair, "q")
        weights_of = [heads_pieces(jnp.stack(members[:2]), jnp.stack(members[2:]), bias_size, hz, where, zh)]
        up0, down0 = UnitsWeight(up_weight[0][None]), UnitsWeight(down_weight[0][None])
        both1 = UnitsWeight(jnp.stack([up_weight[1], down_weight[1]]))
        flow.hold(
            up0=up0.shard, up0_twin=up0.shard, up0_last=up0.shard, down0=down0.shard, down0_twin=down0.shard, both1=both1.shard,
            heads1=heads_shard[1], low=x_low,
        )
        gate(flow)
        x_low = flow.free("low")
    else:
        x_low = turn(tokens)
        ends = jnp.cumsum(turn(doc_lengths)[0], dtype=jnp.int32)
        weights_of = [all_heads_weight(shard, bias_size, hz, zh) for shard in heads_shard]
        every = [all_units_weight(jnp.stack([up_weight[l], down_weight[l]])) for l in range(layers)]
        top_grad = turn(cotangent)

    prev, prev_gain, prev_shift = x_low, ONE, ZERO
    kept = []
    for l in range(layers):
        first, last = small_slice and l == 0, small_slice and l == 1
        xs = gather_group(x_low)
        w_heads, bias = weights_of[l]
        qkv_near = project_in(flow, (xs[0], xs[2]), False, w_heads, in_cols, bias, "project_qkv")
        if first:
            up0.shard = flow.free("up0")
            up0.start_far_z()
            flow.wait(up0.other)
        if last:
            flow.hold(top=cotangent, own=both1.own)
        forward(flow, xs, qkv_near)
        if first:
            twin, down0.shard = flow.free("up0_twin"), flow.free("down0")
            up0.join_far_z(twin)
            across = up0.other
            up0.start_z()
            down0.start_far_z()
            flow.hold(pair=with_sibling(flow.free("heads1")))
        if last:
            both1.own = flow.free("own")
            both1.near()
        qkv_far = project_in(flow, (xs[1], xs[3]), True, w_heads, in_cols, bias, "project_qkv")
        qkv = (qkv_near, qkv_far)
        if first:
            down0.join_far_z(flow.free("down0_twin"))
            up0.join_z(jnp.stack([flow.free("up0_last"), across]))
            up0.near()
            down0.near_z()
            both1.shard = flow.free("both1")
            both1.far_z()
            pair = turn(flow.free("pair"))
        if last:
            top_grad = turn(flow.free("top"))
            both1.swap("own")
        ctx, wide, lse = attend_forward(flow, ends, qkv)
        if first:
            flow.wait(up0.near_x, up0.near_y)
            flow.hold(both1=both1.two, down0=down0.own, pair_twin=pair)
            flow.wait(pair)
            beside = flip(pair, "q", 1)
            up0.swap("own", "near_x", "near_y")
        if last:
            flow.wait(both1.near_x, both1.near_y, top_grad)
        send = project_out(flow, [ctx], (2, 3), w_heads, out_cols, True, "project_attn")
        flow.wait(send)
        if last:
            flow.hold(near_x=both1.near_x, near_y=both1.near_y)
        keep = project_out(flow, [ctx], (0, 1), w_heads, out_cols, False, "project_attn")
        if last:
            both1.near_x, both1.near_y = flow.free("near_x"), flow.free("near_y")
            both1.corner()
            both1.swap("near_x", "near_y")
        attn, passed = sum_group(keep, send)
        if first:
            flow.wait(passed, gathered, *up0.theirs.values())
            flow.hold(near_x=up0.near_x, near_y=up0.near_y)
            gate(flow)
            down0.own, up0.near_x, up0.near_y = flow.free("down0"), flow.free("near_x"), flow.free("near_y")
            up0.corner()
            up0.swap("far_a", "far_b")
            down0.near()
            down0.swap("own")
            flow.wait(down0.near_x, down0.near_y)
            down0.corner()
            down0.swap("near_x", "near_y")
            w_up = up0.pieces(), 0
        elif last:
            flow.wait(passed)
            flow.hold(ends=ends)
            gate(flow)
            ends = flow.free("ends")
            flow.hold(far_a=both1.far_a, far_b=both1.far_b)
            flow.wait(attn[2])
            gate(flow)
            both1.far_a, both1.far_b = flow.free("far_a"), flow.free("far_b")
            both1.swap("far_a", "far_b")
            w_up, w_down = (both1.pieces(), 0), (both1.pieces(), 1)
        else:
            w_up, w_down = (every[l], 0), (every[l], 1)
        used = (prev_gain, prev_shift, shift_row(l, 0), gain_row(l, 0), shift_row(l, 1))
        n1, hs, r1, act, slope = norm_up(flow, prev, attn, table, used, *w_up, up_bias_full[l], tz)
        if first:
            flow.wait(n1, beside, *down0.theirs.values())
            flow.hold(far_a=down0.far_a, far_b=down0.far_b)
            gate(flow)
            down0.far_a, down0.far_b = flow.free("far_a"), flow.free("far_b")
            down0.swap("far_a", "far_b")
            both1.two = flow.free("both1")
            both1.near_z()
            near = jnp.stack([flow.free("pair_twin"), beside])
            weights_of.append(heads_along_y(near, bias_size, hz, where, zh))
            w_down = down0.pieces(), 0
        used = (gain_row(l, 0), shift_row(l, 1), shift_row(l, 2), gain_row(l, 1), shift_row(l, 3))
        n2, y_low, r2 = down_norm(flow, act, *w_down, n1, table, used, tz)
        kept.append((xs, qkv, ctx, wide, lse, n1, hs, r1, act, slope, n2, r2, w_heads, w_up, w_down))
        x_low, prev, prev_gain, prev_shift = y_low, n2, gain_row(l, 1), shift_row(l, 3)
    layer_output = turn(x_low)

    residual, back = top_grad, []
    small_grads = [None] * layers
    units_of, heads_of = [None] * layers, [None] * layers
    above = above_heads = None
    for l in reversed(range(layers)):
        top = l == layers - 1
        xs, qkv, ctx, wide, lse, n1, hs, r1, act, slope, n2, r2, w_heads, w_up, w_down = kept[l]
        beside = small_slice and not top
        g2, gf, sums2, gu, up_bias_sum = units_back(
            flow, residual, back, n2, r2, table, gain_row(l, 1), *w_down, slope, tz
        )
        units = UnitsGrads(flow, (gf, act), (hs, gu), tz)
        if top:
            flow.hold(output=layer_output)
        else:
            if beside:
                flow.wait(*above.near())
                flow.hold(heads=above_heads.send)
            units.sibling()
            flow.wait(units.theirs)
            if beside:
                above_heads.send = flow.free("heads")
                above_heads.along_x()
                late = above.far()
        g1, ga, sums1 = up_back(flow, gu, *w_up, g2, n1, r1, table, gain_row(l, 0), tz)
        gas = gather_group(ga)
        flow.wait(ga)
        if top:
            layer_output = flow.free("output")
            units.compute_theirs()
            forward(flow, gas, units.theirs)
        else:
            units.mine()
            if beside:
                flow.wait(*late, above_heads.got)
            forward(flow, gas, *units.made)
        gc_near = project_in(flow, (gas[0], gas[2]), False, w_heads, out_cols, None, "project_gc")
        flow.wait(gc_near)
        if top:
            flow.hold(theirs=units.theirs)
        gc_far = project_in(flow, (gas[1], gas[3]), True, w_heads, out_cols, None, "project_gc")
        if top:
            units.theirs = flow.free("theirs")
            units.send_theirs()
        gcs = (gc_near, gc_far)
        if beside:
            early = above.near_z()
            flow.hold(rest_x=units.rest_x, rest_y=units.rest_y, keep=above_heads.keep, above=above.own)
        gqkv = [attend_backward(flow, ends, 0, qkv, gcs, wide, lse)]
        if beside:
            units.rest_x, units.rest_y = flow.free("rest_x"), flow.free("rest_y")
            above_heads.keep, above.own = flow.free("keep"), flow.free("above")
        flow.wait(gqkv[0])
        if beside:
            flow.wait(*units.near(), *early)
            above.far_z()
            units.far()
            above_heads.along_y()
            flow.hold(own=units.own, keep=above_heads.keep)
        gqkv.append(attend_backward(flow, ends, 1, qkv, gcs, wide, lse))
        if beside:
            units.own, above_heads.keep = flow.free("own"), flow.free("keep")
            flow.wait(units.late_x, units.late_y, above.last, above_heads.got)
            above_halves = above_heads.halves(zh)
            done = turn(above_halves[0]), uncross(above_halves[1])
        send = project_out(flow, gqkv, (2, 3), w_heads, in_cols, True, "project_gx")
        flow.wait(send)
        keep = project_out(flow, gqkv, (0, 1), w_heads, in_cols, False, "project_gx")
        back, passed = sum_group(keep, send)
        flow.wait(passed)
        if top:
            units.mine()
            flow.wait(*units.made)
        elif small_slice:
            flow.wait(*done)
        *buckets, qkv_sums = heads_grad(flow, xs, gqkv, gas, ctx)
        heads = HeadsGrad(*buckets)
        units_of[l], heads_of[l] = units, heads
        qv_sums = qkv_sums.reshape(-1, 3, PAIR).transpose(1, 0, 2).reshape(3, hz, dp, -1)
        qv_sums = jnp.stack([qv_sums[0], qv_sums[2]]).transpose(2, 0, 1, 3).reshape(1, dp, -1)
        mine = (jnp.arange(tz) == place).astype(F32).reshape(tz, 1, 1)
        small_grads[l] = jnp.concatenate(
            [
                mine * qv_sums,
                up_bias_sum.reshape(tz, up_bias.shape[1], dp, -1).transpose(0, 2, 1, 3).reshape(tz, dp, -1),
                jnp.stack([sums1[0], sums2[0]]).reshape(2, dp, tz, -1).transpose(2, 1, 0, 3).reshape(tz, dp, -1),
                jnp.stack([sums1[2], sums1[1], sums2[2], sums2[1]])
                .reshape(4, dp, tz, -1).transpose(2, 1, 0, 3).reshape(tz, dp, -1),
            ],
            axis=-1,
        )
        if l > 0:
            above, above_heads = units, heads
            flow.wait(heads.send)
            residual = g1
    small_sums = jnp.stack(small_grads, axis=2).reshape(tz, dp, -1)
    if small_slice:
        heads.along_x()
        small_sums = fold_small(spread_by_distance(small_sums, where), 0, 1)
        flow.wait(back[2])
        flow.hold(small=small_sums, got=heads.got, own=units.own)
        gate(flow)
        small_sums, heads.got, units.own = flow.free("small"), flow.free("got"), flow.free("own")
        input_grad = turn(add(g1, back[0], back[1][0], back[2]).astype(BF16))
        heads.along_y()
        units.near_z()
        small_sums = fold_small(small_sums, 1, 2)
        flow.wait(heads.got)
        flow.hold(small=small_sums, there=units.there)
        gate(flow)
        units.there = flow.free("there")
        units.far_z()
        small_sums = fold_small(flow.free("small"), 2, 3)
        halves = heads.halves(zh)
        small_out = fold_small(small_sums, 3, 5).reshape(layers, -1)
        arrived = [(turn(halves[0]), uncross(halves[1])), done]
        flow.hold(grad=input_grad, output=layer_output)
        qkv_grad, out_grad, up_grad, down_grad, squares = finish(
            flow, [member.parts() for member in units_of], arrived, small_out
        )
        input_grad, layer_output = flow.free("grad"), flow.free("output")
    else:
        halves = [member.halves(zh) for member in heads_of]
        d_heads = jnp.stack([add(turn(half[0]), uncross(half[1])) for half in halves])
        input_grad = turn(add(g1, back[0], back[1][0], back[2]).astype(BF16))
        small_out = lax.psum_scatter(small_sums.reshape(tz * dp, -1), ALL, scatter_dimension=0, tiled=True)
        small_out = small_out.reshape(layers, -1)
        qkv_grad = d_heads[:, :, : in_cols.stop].reshape(layers, d_heads.shape[1], -1, 3, PAIR)
        qkv_grad = qkv_grad.transpose(0, 3, 1, 2, 4).reshape(qkv_weight.shape)
        out_grad = d_heads[:, :, in_cols.stop :]
        totals = [member.total() for member in units_of]
        down_grad, up_grad = (jnp.stack([total[i] for total in totals]) for i in range(2))
        squares = sum(jnp.sum(member * member) for member in (qkv_grad, out_grad, up_grad, down_grad, small_out))

    rest = small_out[:, bias_size:]
    qv_bias_grad = small_out[:, :bias_size].reshape(qv_bias.shape)
    up_bias_grad = rest[:, cuts[0] : cuts[1]].reshape(up_bias.shape)
    gains_grad = rest[:, cuts[1] : cuts[2]].reshape(gains.shape)
    shifts_grad = rest[:, cuts[2] : cuts[3]].reshape(shifts.shape)
    entry_count = LAYERS * (4 * D * D + 2 * D * FF + FF + 8 * D)
    grad_rms = jnp.sqrt(sum_all(squares) / entry_count)
    return (
        layer_output, input_grad, qkv_grad, qv_bias_grad, out_grad, up_grad, up_bias_grad, down_grad, gains_grad,
        shifts_grad, grad_rms,
    )


def solution(mesh):
    dp, tensor = mesh.shape["dp"], mesh.shape["tensor"]
    fine = Mesh(mesh.devices.reshape(dp // 2, 2, 2, tensor // 2), ("q", "c", "zh", "zl"))
    data, model = ("q", "c"), ("zh", "zl")
    both = data + model
    weight3, weight4 = P(None, data, model), P(None, None, data, model)
    in_specs = (
        P(both, None), P(data, None), weight4, P(None, None, model, data), weight3, weight3, P(None, model, data),
        weight3, P(None, None, both), P(None, None, both), P(both, None),
    )
    out_specs = (
        P(both, None), P(both, None), weight4, P(None, None, model, data), weight3, weight3, P(None, model, data),
        weight3, P(None, None, both), P(None, None, both), P(),
    )
    return jax.shard_map(on_device, mesh=fine, in_specs=in_specs, out_specs=out_specs, check_vma=False)
```

```python
import jax
import jax.numpy as jnp
from jax import lax
from jax.experimental import pallas as pl
from jax.experimental.pallas import tpu as pltpu
from jax.sharding import Mesh
from jax.sharding import PartitionSpec as P

D = 1024
HD = 64
HEADS = 16
FF = 4096
LAYERS = 2
SEQLEN = 2048
WINDOW = 1024
EPS = 1e-06
FILL = -1000000000.0

F32 = jnp.float32
BF16 = jnp.bfloat16
GROUP = ("c", "zl")
MODEL = ("zh", "zl")
ALL = ("zh", "zl", "q", "c")
VMEM_LIMIT = 62 * 1024 * 1024
TIMES = {
    "gate": 0.1, "finish": 0.2, "norm_up": 20.0, "down_norm": 20.0, "units_back": 45.0, "up_back": 20.0, "norm_back": 6.0,
    "sum_norm_back": 20.0, "grads_theirs": 0.2, "grads_mine": 0.2, "project_qkv": 0.2, "project_gc": 0.2,
    "project_attn": 0.2, "project_gx": 0.2, "heads_grad": 0.2, "attend_forward": 40.0, "attend_backward": 30.0,
}
PEAK = 0.35e9
NT = (((1,), (1,)), ((), ()))
NN = (((1,), (0,)), ((), ()))
ROWS = 128
CHUNK = 64
BQ = 512
PAIR = 2 * HD


def mm(left, right, dims=NN):
    return lax.dot_general(left, right, dims, preferred_element_type=F32)


def full(shape):
    return pl.BlockSpec(shape, lambda *_: (0,) * len(shape))


ANY = pl.BlockSpec(memory_space=pl.ANY)


def sds(shape, kind):
    return jax.ShapeDtypeStruct(shape, kind)


class Flow:
    def __init__(self, scal):
        self.scal, self.before, self.held = scal, [], {}

    def wait(self, *arrays):
        self.before += arrays

    def hold(self, **arrays):
        self.held.update(arrays)

    def free(self, name):
        return self.held.pop(name)


def call(flow, body, grid, in_specs, out_specs, out_shape, scratch, args, flops, traffic, name, scalars=None):
    scalars = (flow.scal,) if scalars is None else scalars
    single = not isinstance(out_specs, (list, tuple))
    out_specs = [out_specs] if single else list(out_specs)
    out_shape = [out_shape] if single else list(out_shape)
    before, held = flow.before, list(flow.held.items())
    ns, nb, nh, no = len(scalars), len(before), len(held), len(out_specs)
    first, last = ns + nb + nh, ns + nb + nh + len(args) + no

    def wrapped(*refs):
        body(*refs[:ns], *refs[first:last], *refs[last + nh :])

    result = pl.pallas_call(
        wrapped,
        grid_spec=pltpu.PrefetchScalarGridSpec(
            num_scalar_prefetch=ns,
            grid=grid,
            in_specs=[ANY] * (nb + nh) + list(in_specs),
            out_specs=out_specs + [ANY] * nh,
            scratch_shapes=scratch,
        ),
        out_shape=out_shape + [sds(array.shape, array.dtype) for _, array in held],
        input_output_aliases={ns + nb + i: no + i for i in range(nh)},
        compiler_params=pltpu.CompilerParams(
            dimension_semantics=("arbitrary",) * len(grid), vmem_limit_bytes=VMEM_LIMIT
        ),
        cost_estimate=pl.CostEstimate(flops=int(TIMES[name] * PEAK), bytes_accessed=1024, transcendentals=0),
        name=name,
    )(*scalars, *before, *[array for _, array in held], *args)
    flow.before = []
    flow.held = {key: value for (key, _), value in zip(held, result[no:])}
    return result[0] if single else result[:no]


def gate(flow):
    if flow.held:
        call(flow, lambda *refs: None, (1,), [], [], [], [], [], 0, 0, "gate")


S_P, S_Q, S_C, S_ZH, S_Z = range(5)


def norm_rows(values_in):
    centred = values_in - jnp.mean(values_in, -1, keepdims=True)
    variance = jnp.mean(centred * centred, -1, keepdims=True)
    inverse = lax.rsqrt(variance + EPS)
    return centred * inverse, inverse


def norm_back_rows(grad, normed, inverse, gain):
    scaled = grad * gain
    centred = scaled - jnp.mean(scaled, -1, keepdims=True) - normed * jnp.mean(scaled * normed, -1, keepdims=True)
    return centred * inverse


def fold_rows(values_in):
    return jnp.sum(values_in.reshape(-1, 8, values_in.shape[-1]), 0)


def read(part, rows):
    return (part[0, rows, :] if len(part.shape) == 3 else part[rows, :]).astype(F32)


def part_spec(part):
    shape = part.shape
    return full(shape) if len(shape) == 2 else pl.BlockSpec((1,) + shape[1:], lambda *_: (0, 0, 0))


ONE, ZERO, TABLE = 0, 1, 16


def gain_row(layer, index):
    return 2 + 6 * layer + index


def shift_row(layer, index):
    return 4 + 6 * layer + index


def row_of(vec_ref, row):
    return vec_ref[row : row + 1, :]


def norm_forward(get_total, tokens, vec, gain, shift, n_ref, low_ref, inv_ref):

    def step(index, carry):
        rows = pl.ds(pl.multiple_of(index * CHUNK, CHUNK), CHUNK)
        normed, inverse = norm_rows(get_total(rows))
        n_ref[rows, :] = normed
        low_ref[rows, :] = (normed * row_of(vec, gain) + row_of(vec, shift)).astype(BF16)
        inv_ref[rows, :] = jnp.broadcast_to(inverse, (CHUNK, 128))
        return carry

    lax.fori_loop(0, tokens // CHUNK, step, 0)


def norm_backward(get_grad, tokens, n_ref, inv_ref, vec, gain, g_ref, low_ref, sums_ref):
    def step(index, carry):
        rows = pl.ds(pl.multiple_of(index * CHUNK, CHUNK), CHUNK)
        grad = get_grad(rows)
        normed = n_ref[rows, :]
        result = norm_back_rows(grad, normed, inv_ref[rows, 0:1], row_of(vec, gain))
        low = result.astype(BF16)
        g_ref[rows, :] = result
        low_ref[rows, :] = low
        return (
            carry[0] + fold_rows(grad * normed),
            carry[1] + fold_rows(grad),
            carry[2] + fold_rows(low.astype(F32)),
        )

    zero = jnp.zeros((8, D), F32)
    sums = lax.fori_loop(0, tokens // CHUNK, step, (zero, zero, zero))
    sums_ref[...] = jnp.zeros(sums_ref.shape, F32)
    for row, member in enumerate(sums):
        sums_ref[row : row + 1, :] = jnp.sum(member, 0, keepdims=True)


def away(s):
    return (s & 1) * 2 + s // 2


class Streamed:
    def __init__(self, refs, matrix, buffer, sems, scal):
        self.refs, self.matrix, self.buffer, self.sems, self.scal = refs, matrix, buffer, sems, scal

    def copies(self, s):
        slot = lax.rem(s, 2)
        plain, early, late = [], [], []
        for k in range(2):
            own, near_x, near_y, far_a, far_b = self.refs[5 * k : 5 * k + 5]

            def copy(source, r, k=k):
                row = ((self.scal[S_Q] ^ r) * 2 + (self.scal[S_C] ^ k)) * ROWS
                return pltpu.make_async_copy(
                    source, self.buffer.at[slot, pl.ds(pl.multiple_of(row, ROWS), ROWS), :], self.sems.at[slot, 4 * k + r]
                )

            for r, ref in enumerate((own, near_x, near_y)):
                plain.append(copy(ref.at[s, self.matrix], r))
            early.append(copy(far_a.at[jnp.minimum(s, 1), self.matrix], 3))
            late.append(copy(far_b.at[jnp.maximum(s - 2, 0), self.matrix], 3))
        return plain, early, late

    def each(self, s, act):
        plain, early, late = self.copies(s)
        for copy in plain:
            act(copy)

        @pl.when(s < 2)
        def _():
            for copy in early:
                act(copy)

        @pl.when(s >= 2)
        def _():
            for copy in late:
                act(copy)

    def start(self, s):
        self.each(s, lambda copy: copy.start())

    def wait(self, s):
        self.each(s, lambda copy: copy.wait())

    def turn(self, s, count):
        @pl.when(s == 0)
        def _():
            self.start(s)

        @pl.when(s + 1 < count)
        def _():
            self.start(s + 1)


def piece_shapes(width):
    return [pltpu.VMEM((2, D, width), BF16), pltpu.SemaphoreType.DMA((2, 8))]


def gelu_parts(u):
    size = jnp.abs(u)
    t = 1.0 / (1.0 + 0.2316419 * size)
    poly = t * (0.127414796 + t * (-0.142248368 + t * (0.7107068705 + t * (-0.7265760135 + t * 0.5307027145))))
    bell = jnp.exp(-0.5 * (u * u))
    tail = poly * bell
    cdf = jnp.where(u >= 0, 1.0 - tail, tail)
    return u * cdf, cdf + u * (0.3989422804014327 * bell)


def tiles(tokens, width):
    for i in range(2):
        for j in range(2):
            yield slice(i * tokens // 2, (i + 1) * tokens // 2), slice(j * width // 2, (j + 1) * width // 2)


def norm_up(flow, prev, parts, vec, rows_used, weight, matrix, bias, count):
    tokens = prev.shape[0]
    width = FF // count

    def body(scal_ref, prev_ref, *refs):
        part_refs, refs = refs[: len(parts)], refs[len(parts) :]
        vec_ref, bias_ref, refs = refs[0], refs[1], refs[2:]
        pieces, (n_ref, low_ref, inv_ref, act_ref, slope_ref, buffer, sems) = refs[:10], refs[10:]
        s = pl.program_id(0)
        stream = Streamed(pieces, matrix, buffer, sems, scal_ref)
        stream.turn(s, count)

        @pl.when(s == 0)
        def _():
            def total(rows):
                attn = read(part_refs[0], rows)
                for part in part_refs[1:]:
                    attn = attn + read(part, rows)
                before = read(prev_ref, rows) * row_of(vec_ref, rows_used[0]) + row_of(vec_ref, rows_used[1])
                return before + (attn + row_of(vec_ref, rows_used[2]))

            norm_forward(total, tokens, vec_ref, *rows_used[3:], n_ref, low_ref, inv_ref)

        stream.wait(s)
        slot = lax.rem(s, 2)
        for rows, cols in tiles(tokens, width):
            act, slope = gelu_parts(mm(low_ref[rows, :], buffer[slot, :, cols]) + bias_ref[0, :, cols])
            act_ref[rows, cols] = act.astype(BF16)
            slope_ref[rows, cols] = slope.astype(BF16)

    column = pl.BlockSpec((tokens, width), lambda s, _: (0, s))
    return call(
        flow, body, (count,),
        [full((tokens, D))] + [part_spec(part) for part in parts]
        + [full((TABLE, D)), pl.BlockSpec((1, 1, width), lambda s, scal_ref: (scal_ref[S_Z] ^ away(s), 0, 0))] + [ANY] * 10,
        [full((tokens, D)), full((tokens, D)), full((tokens, 128)), column, column],
        [sds((tokens, D), F32), sds((tokens, D), BF16), sds((tokens, 128), F32)] + [sds((tokens, FF), BF16)] * 2,
        piece_shapes(width), [prev, *parts, vec, bias, *weight], 2 * tokens * D * FF,
        2 * (D * FF + tokens * (10 * D + 2 * FF)), "norm_up",
    )


def down_norm(flow, act, weight, matrix, prev, vec, rows_used, count):
    tokens = prev.shape[0]
    width = FF // count

    def body(scal_ref, act_ref, prev_ref, vec_ref, *refs):
        pieces, (n_ref, low_ref, inv_ref, buffer, sems, acc) = refs[:10], refs[10:]
        s = pl.program_id(0)
        stream = Streamed(pieces, matrix, buffer, sems, scal_ref)
        stream.turn(s, count)
        stream.wait(s)
        value = mm(act_ref[...], buffer[lax.rem(s, 2)], NT)

        @pl.when(s == 0)
        def _():
            acc[...] = value

        @pl.when(s > 0)
        def _():
            acc[...] += value

        @pl.when(s == count - 1)
        def _():
            def total(rows):
                before = prev_ref[rows, :] * row_of(vec_ref, rows_used[0]) + row_of(vec_ref, rows_used[1])
                return before + (acc[rows, :] + row_of(vec_ref, rows_used[2]))

            norm_forward(total, tokens, vec_ref, *rows_used[3:], n_ref, low_ref, inv_ref)

    return call(
        flow, body, (count,),
        [pl.BlockSpec((tokens, width), lambda s, _: (0, s)), full((tokens, D)), full((TABLE, D))] + [ANY] * 10,
        [full((tokens, D)), full((tokens, D)), full((tokens, 128))],
        [sds((tokens, D), F32), sds((tokens, D), BF16), sds((tokens, 128), F32)],
        piece_shapes(width) + [pltpu.VMEM((tokens, D), F32)], [act, prev, vec, *weight], 2 * tokens * D * FF,
        2 * (D * FF + tokens * (5 * D + FF)), "down_norm",
    )


def units_back(flow, residual, parts, normed, inverse, vec, gain, weight, matrix, slope, count):
    tokens = residual.shape[0]
    width = FF // count

    def body(scal_ref, res_ref, *refs):
        part_refs, refs = refs[: len(parts)], refs[len(parts) :]
        n_ref, inv_ref, vec_ref, slope_ref, refs = refs[0], refs[1], refs[2], refs[3], refs[4:]
        pieces, (g_ref, low_ref, sums_ref, out_ref, sum_ref, buffer, sems) = refs[:10], refs[10:]
        s = pl.program_id(0)
        stream = Streamed(pieces, matrix, buffer, sems, scal_ref)
        stream.turn(s, count)

        @pl.when(s == 0)
        def _():
            def grad(rows):
                total = read(res_ref, rows)
                for part in part_refs:
                    total = total + read(part, rows)
                return total

            norm_backward(grad, tokens, n_ref, inv_ref, vec_ref, gain, g_ref, low_ref, sums_ref)

        stream.wait(s)
        slot = lax.rem(s, 2)
        sums = {}
        for rows, cols in tiles(tokens, width):
            low = (mm(low_ref[rows, :], buffer[slot, :, cols]) * slope_ref[rows, cols].astype(F32)).astype(BF16)
            out_ref[rows, cols] = low
            part = fold_rows(low.astype(F32))
            sums[cols.start] = sums[cols.start] + part if cols.start in sums else part
            if rows.start > 0:
                sum_ref[0, :, cols] = jnp.sum(sums[cols.start], 0, keepdims=True)

    column = pl.BlockSpec((tokens, width), lambda s, _: (0, s))
    return call(
        flow, body, (count,),
        [full((tokens, D))] + [part_spec(part) for part in parts]
        + [full((tokens, D)), full((tokens, 128)), full((TABLE, D)), column] + [ANY] * 10,
        [full((tokens, D)), full((tokens, D)), full((8, D)), column,
         pl.BlockSpec((1, 1, width), lambda s, scal_ref: (scal_ref[S_Z] ^ away(s), 0, 0))],
        [sds((tokens, D), F32), sds((tokens, D), BF16), sds((8, D), F32), sds((tokens, FF), BF16),
         sds((count, 1, width), F32)],
        piece_shapes(width), [residual, *parts, normed, inverse, vec, slope, *weight], 0, 0, "units_back",
    )


def up_back(flow, gu, weight, matrix, residual, normed, inverse, vec, gain, count):
    tokens = residual.shape[0]
    width = FF // count

    def body(scal_ref, gu_ref, res_ref, n_ref, inv_ref, vec_ref, *refs):
        pieces, (g_ref, low_ref, sums_ref, buffer, sems, acc) = refs[:10], refs[10:]
        s = pl.program_id(0)
        stream = Streamed(pieces, matrix, buffer, sems, scal_ref)
        stream.turn(s, count)
        stream.wait(s)
        value = mm(gu_ref[...], buffer[lax.rem(s, 2)], NT)

        @pl.when(s == 0)
        def _():
            acc[...] = value

        @pl.when(s > 0)
        def _():
            acc[...] += value

        @pl.when(s == count - 1)
        def _():
            norm_backward(
                lambda rows: res_ref[rows, :] + acc[rows, :], tokens, n_ref, inv_ref, vec_ref, gain, g_ref, low_ref,
                sums_ref,
            )

    return call(
        flow, body, (count,),
        [pl.BlockSpec((tokens, width), lambda s, _: (0, s)), full((tokens, D)), full((tokens, D)), full((tokens, 128)),
         full((TABLE, D))] + [ANY] * 10,
        [full((tokens, D)), full((tokens, D)), full((8, D))],
        [sds((tokens, D), F32), sds((tokens, D), BF16), sds((8, D), F32)],
        piece_shapes(width) + [pltpu.VMEM((tokens, D), F32)], [gu, residual, normed, inverse, vec, *weight],
        2 * tokens * D * FF, 2 * (D * FF + tokens * (8 * D + FF)), "up_back",
    )


def turn_rows(scal_ref, x_ref, turned, core):
    for r in range(4):
        row = ((scal_ref[S_Q] ^ r) * 2 + core) * ROWS
        turned[r * ROWS : (r + 1) * ROWS, :] = x_ref[:, pl.ds(pl.multiple_of(row, ROWS), ROWS)].T


def unit_grads(flow, down, up, received, count, sibling):
    tokens = down[0].shape[0]
    width = down[1].shape[1] // count
    half = count // 2
    steps = 2 * count

    def body(scal_ref, x0_ref, y0_ref, x1_ref, y1_ref, *refs):
        turned, t = refs[-1], pl.program_id(0)
        m, s = t // count, lax.rem(t, count)
        core = scal_ref[S_C] ^ 1 if sibling else scal_ref[S_C]

        @pl.when(t == 0)
        def _():
            turn_rows(scal_ref, x0_ref, turned, core)

        @pl.when(t == count)
        def _():
            turn_rows(scal_ref, x1_ref, turned, core)

        def store(y_ref):
            value = mm(turned[...], y_ref[...]).reshape(4, ROWS, width)
            if sibling:
                refs[0][:, 0] = value.astype(BF16)
                return
            if received is not None:
                value = value + refs[0][:, 0].astype(F32)
            value = value.astype(BF16)
            own, to_x, to_y, rest_x, rest_y = refs[-6:-1]
            spot = lax.rem(s, half) * 2 + m
            own[s // half * count + spot] = value[0]

            @pl.when(s < half)
            def _():
                to_x[spot] = value[1]
                to_x[count + spot] = value[3]
                rest_y[spot] = value[2]

            @pl.when(s >= half)
            def _():
                rest_x[spot] = value[1]
                to_y[spot] = value[2]
                to_y[count + spot] = value[3]

        @pl.when(m == 0)
        def _():
            store(y0_ref)

        @pl.when(m == 1)
        def _():
            store(y1_ref)

    left = full((tokens, D))
    pick_down = lambda t, _: (0, jnp.minimum(t, count - 1))
    pick_up = lambda t, _: (0, jnp.maximum(t - count, 0))
    specs = [left, pl.BlockSpec((tokens, width), pick_down), left, pl.BlockSpec((tokens, width), pick_up)]
    args = [*down, *up]
    one = pl.BlockSpec((4, 1, ROWS, width), lambda t, _: (0, t, 0, 0))
    if sibling:
        out_specs, out_shape = one, sds((4, steps, ROWS, width), BF16)
    else:
        if received is not None:
            specs.append(one)
            args.append(received)
        shapes = [(steps, ROWS, width)] * 3 + [(count, ROWS, width)] * 2
        out_specs, out_shape = [full(shape) for shape in shapes], [sds(shape, BF16) for shape in shapes]
    return call(
        flow, body, (steps,), specs, out_specs, out_shape, [pltpu.VMEM((4 * ROWS, tokens), BF16)], args,
        0, 0, "grads_theirs" if sibling else "grads_mine",
    )


def finish(flow, units, heads, small):
    layers = len(units)
    rows, cols = heads[0][0].shape
    in_width = cols * 3 // 4
    pairs = in_width // (3 * PAIR)
    width = units[0][0].shape[2]

    def body(scal_ref, *refs):
        qkv_ref, out_ref, up_ref, down_ref, square_ref = refs[-5:]
        small_ref, refs = refs[-6], refs[:-6]
        squares = jnp.sum(small_ref[...] * small_ref[...], keepdims=True)
        for l in range(layers):
            unit_refs, (first, second) = refs[7 * l : 7 * l + 5], refs[7 * l + 5 : 7 * l + 7]
            for m, target in enumerate((down_ref, up_ref)):
                total = unit_refs[0][m].astype(F32)
                for part in unit_refs[1:]:
                    total = total + part[m].astype(F32)
                target[l] = total
                squares = squares + jnp.sum(jnp.sum(total * total, 0, keepdims=True), 1, keepdims=True)
            total = first[...].astype(F32) + second[...].astype(F32)
            squares = squares + jnp.sum(jnp.sum(total * total, 0, keepdims=True), 1, keepdims=True)
            out_ref[l] = total[:, in_width:]
            for pair in range(pairs):
                for which in range(3):
                    base = (3 * pair + which) * PAIR
                    qkv_ref[l, which, :, pair * PAIR : (pair + 1) * PAIR] = total[:, base : base + PAIR]
        square_ref[...] = jnp.broadcast_to(squares, (8, 128))

    specs, args = [], []
    for l in range(layers):
        specs += [pl.BlockSpec((2, rows, width), lambda *_: (0, 0, 0))] * 5 + [full((rows, cols))] * 2
        args += [*units[l], *heads[l]]
    shapes = [(layers, 3, rows, in_width // 3), (layers, rows, cols - in_width), (layers, rows, width), (layers, rows, width),
              (8, 128)]
    return call(
        flow, body, (1,), specs + [full(small.shape)], [full(shape) for shape in shapes],
        [sds(shape, F32) for shape in shapes], [], args + [small], 0, 0, "finish",
    )


def place_heads_weight(scal_ref, pieces, buffer):
    for r in range(4):
        for k in range(2):
            row = ((scal_ref[S_Q] ^ r) * 2 + (scal_ref[S_ZH] ^ k)) * ROWS
            buffer[pl.ds(pl.multiple_of(row, ROWS), ROWS), :] = pieces[r // 2][r % 2, k, :ROWS, :]


def heads_weight_specs(weight, cols):
    width = cols.stop - cols.start
    return [pl.BlockSpec((2, 2, piece.shape[2], width), lambda *_: (0, 0, 0, cols.start // width)) for piece in weight]


def by_member(shape):
    return pl.BlockSpec((1,) + shape, lambda r, scal_ref: (scal_ref[S_P] ^ r, 0, 0))


def heads_weight_scratch(width):
    return [pltpu.VMEM((D, width), BF16)]


def project_in(flow, lefts, across, weight, cols, bias, name):
    tokens = lefts[0].shape[0]
    width = cols.stop - cols.start

    def body(scal_ref, left_ref, right_ref, *refs):
        if bias is not None:
            bias_ref, refs = refs[0], refs[1:]
        pieces, (out_ref, buffer) = refs[:2], refs[2:]
        step = pl.program_id(0)

        @pl.when(step == 0)
        def _():
            place_heads_weight(scal_ref, pieces, buffer)

        for r, left in enumerate((left_ref, right_ref)):

            @pl.when(step == r)
            def _(left=left):
                value = mm(left[...], buffer[...])
                if bias is not None:
                    value = value + bias_ref[...]
                out_ref[0] = value.astype(BF16)

    extra, extra_specs = ([], []) if bias is None else ([bias], [full((1, width))])
    return call(
        flow, body, (2,), [full((tokens, D))] * 2 + extra_specs + heads_weight_specs(weight, cols),
        pl.BlockSpec((1, tokens, width), lambda r, scal_ref: ((scal_ref[S_P] >> 1) ^ r, 0, 0)),
        sds((2, tokens, width), BF16), heads_weight_scratch(width), [*lefts, *extra, *weight], 0, 0, name,
    )


def project_out(flow, blocks, members, weight, cols, stacked, name):
    count, tokens, width = blocks[0].shape

    def body(scal_ref, *refs):
        block_refs, refs = refs[: len(blocks)], refs[len(blocks) :]
        pieces, outs, buffer = refs[:2], refs[2:-1], refs[-1]
        step = pl.program_id(0)

        @pl.when(step == 0)
        def _():
            place_heads_weight(scal_ref, pieces, buffer)

        value = mm(block_refs[0][0], buffer[:, :width], NT)
        for index in range(1, len(blocks)):
            value = value + mm(block_refs[index][0], buffer[:, index * width : (index + 1) * width], NT)
        value = value.astype(BF16)
        if stacked:
            outs[0][0] = value
            return
        for r, out in enumerate(outs):

            @pl.when(step == r)
            def _(out=out):
                out[...] = value

    first, last = members
    pick = lambda r, scal_ref: (scal_ref[S_P] ^ (first + r * (last - first)), 0, 0)
    if stacked:
        out_specs, out_shape = pl.BlockSpec((1, tokens, D), lambda r, _: (r, 0, 0)), sds((2, tokens, D), BF16)
    else:
        out_specs, out_shape = [full((tokens, D))] * 2, [sds((tokens, D), BF16)] * 2
    return call(
        flow, body, (2,), [pl.BlockSpec((1, tokens, width), pick)] * len(blocks) + heads_weight_specs(weight, cols), out_specs,
        out_shape,
        heads_weight_scratch(width * len(blocks)), [*blocks, *weight], 0, 0, name,
    )


def heads_grad(flow, xs, parts, gas, ctx):
    count, tokens, width = parts[0].shape
    out_width = ctx.shape[2]
    cuts = [slice(i * width, (i + 1) * width) for i in range(len(parts))]
    total = width * len(parts)

    def body(scal_ref, *refs):
        x_refs, refs = refs[:count], refs[count:]
        ga_refs, refs = refs[:count], refs[count:]
        part_refs, refs = refs[: len(parts)], refs[len(parts) :]
        ctx_ref, outs, (sum_ref, acc, acc_out) = refs[0], refs[1:3], refs[3:]
        step = pl.program_id(0)
        for r in range(count):

            @pl.when(step == r)
            def _(r=r):
                turned = x_refs[r][...].T
                value_out = mm(ga_refs[r][...].T, ctx_ref[0])
                for cut, part in zip(cuts, part_refs):
                    value = mm(turned, part[0])
                    sums = jnp.sum(part[0].astype(F32), 0, keepdims=True)
                    acc[:, cut] = value if r == 0 else acc[:, cut] + value
                    sum_ref[:, cut] = sums if r == 0 else sum_ref[:, cut] + sums
                acc_out[...] = value_out if r == 0 else acc_out[...] + value_out

        @pl.when(step == count - 1)
        def _():
            for r in range(4):
                for k in range(2):
                    row = ((scal_ref[S_Q] ^ r) * 2 + (scal_ref[S_ZH] ^ k)) * ROWS
                    rows = pl.ds(pl.multiple_of(row, ROWS), ROWS)
                    outs[r % 2][r // 2, k, :, :total] = acc[rows, :].astype(BF16)
                    outs[r % 2][r // 2, k, :, total:] = acc_out[rows, :].astype(BF16)

    shape = (2, 2, ROWS, total + out_width)
    return call(
        flow, body, (count,),
        [full((tokens, D))] * (2 * count) + [by_member((tokens, width))] * len(parts) + [by_member((tokens, out_width))],
        [full(shape)] * 2 + [full((1, total))], [sds(shape, BF16)] * 2 + [sds((1, total), F32)],
        [pltpu.VMEM((D, total), F32), pltpu.VMEM((D, out_width), F32)], [*xs, *gas, *parts, ctx], 0, 0, "heads_grad",
    )


def reach(ends_ref, row):
    first = jnp.zeros_like(row)
    for index in range(3):
        first = jnp.where(row >= ends_ref[index], ends_ref[index], first)
    last = jnp.full_like(row, SEQLEN)
    for index in (2, 1, 0):
        last = jnp.where(row < ends_ref[index], ends_ref[index], last)
    return jnp.maximum(first, row - (WINDOW - 1)), jnp.minimum(last, row + WINDOW)


def chunks_of(scal_ref, near_ref, far_ref):
    here = scal_ref[S_P] & 1
    for core in range(2):
        yield 2 * core + here, near_ref.at[core]
        yield 2 * core + 1 - here, far_ref.at[core]


def over_keys(ends_ref, start, chunk, keys_first, block):
    low_first, high_first = reach(ends_ref, start)
    low_last, high_last = reach(ends_ref, start + BQ - 1)
    axis = 1 if keys_first else 0
    low_row, high_row = reach(ends_ref, start + lax.broadcasted_iota(jnp.int32, (1, BQ) if keys_first else (BQ, 1), axis))
    shape = (chunk, BQ) if keys_first else (BQ, chunk)

    def one(b, carry):
        open_all = (b * chunk >= low_last) & ((b + 1) * chunk <= high_first)

        @pl.when(open_all)
        def _():
            block(b, None)

        @pl.when(jnp.logical_not(open_all))
        def _():
            key = b * chunk + lax.broadcasted_iota(jnp.int32, shape, 1 - axis)
            block(b, (key >= low_row) & (key < high_row))

        return carry

    lax.fori_loop(low_first // chunk, (high_last + chunk - 1) // chunk, one, 0)


def attend_forward(flow, ends, qkv):
    _, chunk, width3 = qkv[0].shape
    count = SEQLEN // chunk
    width = width3 // 3
    heads = width // HD
    steps = SEQLEN // BQ
    per = chunk // BQ

    def body(scal_ref, ends_ref, near_ref, far_ref, ctx_ref, wide_ref, lse_ref, qt, kh, vt, acc, tops, sums, scores):
        step = pl.program_id(0)

        @pl.when(step == 0)
        def _():
            for j, block in chunks_of(scal_ref, near_ref, far_ref):
                rows = pl.ds(pl.multiple_of(j * chunk, chunk), chunk)
                for pair in range(heads // 2):
                    base = 3 * PAIR * pair
                    part = slice(pair * PAIR, (pair + 1) * PAIR)
                    vt[j, part, :] = block[:, base + 2 * PAIR : base + 3 * PAIR].T
                    for s in range(per):
                        queries = block[s * BQ : (s + 1) * BQ, base : base + PAIR] * BF16(HD**-0.5)
                        qt[j * per + s, part, :] = queries.T
                    for h in range(2):
                        kh[2 * pair + h, rows, :] = block[:, base + PAIR + h * HD : base + PAIR + (h + 1) * HD]

        start = step * BQ
        acc[...] = jnp.zeros(acc.shape, F32)
        tops[...] = jnp.full(tops.shape, -3.0e38, F32)
        sums[...] = jnp.zeros(sums.shape, F32)

        def score(b, allowed):
            keys = pl.ds(pl.multiple_of(b * chunk, chunk), chunk)
            for h in range(heads):
                value = mm(kh[h, keys, :], qt[step, h * HD : (h + 1) * HD, :])
                if allowed is not None:
                    value = jnp.where(allowed, value, FILL)
                scores[h, b] = value
                tops[h] = jnp.maximum(tops[h], jnp.max(value.reshape(-1, 8, BQ), 0))

        over_keys(ends_ref, start, chunk, True, score)
        top = [jnp.max(tops[h], 0, keepdims=True) for h in range(heads)]

        def weigh(b, carry):
            for h in range(heads):
                part = slice(h * HD, (h + 1) * HD)
                weight = jnp.exp(scores[h, b] - top[h])
                sums[h] += fold_rows(weight)
                acc[part, :] += mm(vt[b, part, :], weight.astype(BF16))
            return carry

        low_first, _ = reach(ends_ref, start)
        _, high_last = reach(ends_ref, start + BQ - 1)
        lax.fori_loop(low_first // chunk, (high_last + chunk - 1) // chunk, weigh, 0)
        lse_ref[...] = jnp.zeros(lse_ref.shape, F32)
        for h in range(heads):
            part = slice(h * HD, (h + 1) * HD)
            total = jnp.sum(sums[h], 0, keepdims=True)
            acc[part, :] = acc[part, :] / total
            lse_ref[0, h : h + 1, :] = top[h] + jnp.log(total)
        wide = acc[...].T
        wide_ref[0] = wide
        ctx_ref[0] = wide.astype(BF16)

    row_block = lambda i, *_: (i // per, i % per, 0)
    return call(
        flow, body, (steps,), [full((2, chunk, width3))] * 2,
        [pl.BlockSpec((1, BQ, width), row_block), pl.BlockSpec((1, BQ, width), row_block),
         pl.BlockSpec((1, 8, BQ), lambda i, *_: (i, 0, 0))],
        [sds((count, chunk, width), BF16), sds((count, chunk, width), F32), sds((steps, 8, BQ), F32)],
        [
            pltpu.VMEM((steps, width, BQ), BF16),
            pltpu.VMEM((heads, SEQLEN, HD), BF16),
            pltpu.VMEM((count, width, chunk), BF16),
            pltpu.VMEM((width, BQ), F32),
            pltpu.VMEM((heads, 8, BQ), F32),
            pltpu.VMEM((heads, 8, BQ), F32),
            pltpu.VMEM((heads, count, chunk, BQ), F32),
        ],
        [*qkv], 0, 0, "attend_forward", (flow.scal, ends),
    )


def attend_backward(flow, ends, pair, qkv, grads, wide, lse):
    chunk = qkv[0].shape[1]
    count = SEQLEN // chunk
    steps = SEQLEN // BQ
    per = chunk // BQ

    def body(
        scal_ref, ends_ref, near_ref, far_ref, grad_near, grad_far, wide_ref, lse_ref, out_ref, qh, gh, kt, vt, qt, gt,
        gq, gk, gv,
    ):
        step = pl.program_id(0)

        @pl.when(step == 0)
        def _():
            blocks = chunks_of(scal_ref, near_ref, far_ref)
            grad_blocks = chunks_of(scal_ref, grad_near, grad_far)
            for (j, block), (_, grad_block) in zip(blocks, grad_blocks):
                rows = pl.ds(pl.multiple_of(j * chunk, chunk), chunk)
                queries = block[:, :PAIR] * BF16(HD**-0.5)
                keys = block[:, PAIR : 2 * PAIR]
                back = grad_block[...]
                for h in range(2):
                    cols = slice(h * HD, (h + 1) * HD)
                    qh[h, rows, :] = queries[:, cols]
                    gh[h, rows, :] = back[:, cols]
                kt[j] = keys.T
                vt[j] = block[:, 2 * PAIR :].T
                for s in range(per):
                    sub = slice(s * BQ, (s + 1) * BQ)
                    qt[j * per + s] = queries[sub, :].T
                    gt[j * per + s] = back[sub, :].T
            gk[...] = jnp.zeros(gk.shape, F32)
            gv[...] = jnp.zeros(gv.shape, F32)

        start = step * BQ
        rows = pl.ds(pl.multiple_of(start, BQ), BQ)
        gq[...] = jnp.zeros(gq.shape, F32)
        sums = lse_ref[0].T
        inner, logs = [], []
        for h in range(2):
            product = gh[h, rows, :].astype(F32) * wide_ref[0, :, h * HD : (h + 1) * HD]
            inner.append(jnp.sum(product, 1, keepdims=True))
            logs.append(sums[:, 2 * pair + h : 2 * pair + h + 1])

        def block(b, allowed):
            for h in range(2):
                part = slice(h * HD, (h + 1) * HD)
                score = mm(qh[h, rows, :], kt[b, part, :])
                grad_weight = mm(gh[h, rows, :], vt[b, part, :])
                if allowed is not None:
                    score = jnp.where(allowed, score, FILL)
                weight = jnp.exp(score - logs[h])
                grad_score = (weight * (grad_weight - inner[h])).astype(BF16)
                gv[b, part, :] += mm(gt[step, part, :], weight.astype(BF16))
                gk[b, part, :] += mm(qt[step, part, :], grad_score)
                gq[part, :] += mm(kt[b, part, :], grad_score, NT)

        over_keys(ends_ref, start, chunk, False, block)
        place = pl.ds(pl.multiple_of((step % per) * BQ, BQ), BQ)
        out_ref[step // per, place, :PAIR] = (gq[...] * HD**-0.5).T.astype(BF16)

        @pl.when(step == steps - 1)
        def _():
            for j in range(count):
                out_ref[j, :, PAIR : 2 * PAIR] = gk[j].T.astype(BF16)
                out_ref[j, :, 2 * PAIR :] = gv[j].T.astype(BF16)

    out = (count, chunk, 3 * PAIR)
    return call(
        flow, body, (steps,),
        [pl.BlockSpec((2, chunk, 3 * PAIR), lambda i, *_: (0, 0, pair))] * 2
        + [pl.BlockSpec((2, chunk, PAIR), lambda i, *_: (0, 0, pair))] * 2
        + [pl.BlockSpec((1, BQ, PAIR), lambda i, *_: (i // per, i % per, pair)),
           pl.BlockSpec((1, 8, BQ), lambda i, *_: (i, 0, 0))],
        full(out), sds(out, BF16),
        [pltpu.VMEM((2, SEQLEN, HD), BF16)] * 2
        + [pltpu.VMEM((count, PAIR, chunk), BF16)] * 2
        + [pltpu.VMEM((steps, PAIR, BQ), BF16)] * 2
        + [pltpu.VMEM((PAIR, BQ), F32)]
        + [pltpu.VMEM((count, PAIR, chunk), F32)] * 2,
        [*qkv, *grads, wide, lse], 0, 0, "attend_backward", (flow.scal, ends),
    )


def flip(values_in, axes, mask):
    return lax.ppermute(values_in, axes, [(a, a ^ mask) for a in range(lax.axis_size(axes))])


def turn(values_in):
    return lax.ppermute(values_in, ("c", "zh"), [(2 * a + b, 2 * b + a) for a in range(2) for b in range(2)])


def uncross(values_in):
    return lax.ppermute(values_in, ("c", "zh"), [(2 * b + 1 - a, 2 * a + b) for a in range(2) for b in range(2)])


def from_members(values_in, axes):
    return [values_in] + [flip(values_in, axes, r) for r in range(1, lax.axis_size(axes))]


def to_members(parts, axes):
    return [parts[0]] + [flip(part, axes, r) for r, part in enumerate(parts) if r > 0]


def add(*parts):
    total = parts[0].astype(F32)
    for part in parts[1:]:
        total = total + part.astype(F32)
    return total


def is_small():
    return lax.axis_size("q") == 4


def order_by(values_in, axis, position, count):
    bit = 1
    while bit < count:
        shape = values_in.shape
        split = shape[:axis] + (count // (2 * bit), 2, bit) + shape[axis + 1 :]
        cut = values_in.reshape(split)
        values_in = jnp.where((position & bit) != 0, jnp.flip(cut, axis + 1), cut).reshape(shape)
        bit *= 2
    return values_in


def gather_group(values_in):
    across, sibling = flip(values_in, GROUP, 1), flip(values_in, GROUP, 2)
    return [values_in, across, sibling]


def forward(flow, members, *before):
    flow.wait(*before)
    flow.hold(across=members[1])
    gate(flow)
    members[1] = flow.free("across")
    members.append(flip(members[1], GROUP, 2))


def sum_group(keep, send):
    got = flip(send, GROUP, 2)
    passed = add(keep[1], got[1]).astype(BF16)
    return [keep[0], got, flip(passed, GROUP, 1)], passed


EXTRA = 16


def heads_shard_of(qkv, out, bias):
    rows = out.shape[0]
    paired = qkv.reshape(3, rows, -1, PAIR).transpose(1, 2, 0, 3).reshape(rows, -1)
    weights = jnp.concatenate([paired, out], axis=1)
    below = jnp.pad(bias.reshape(1, -1), ((0, EXTRA - 1), (0, weights.shape[1] - bias.size)))
    return jnp.concatenate([weights, below])


def heads_bias(rows, heads):
    bias = rows.reshape(rows.shape[0], 2, heads, -1).transpose(1, 2, 0, 3).reshape(2, -1).astype(F32)
    bias = jnp.stack([bias[0], jnp.zeros_like(bias[0]), bias[1]])
    return bias.reshape(3, -1, PAIR).transpose(1, 0, 2).reshape(1, -1)


def with_sibling(shard):
    return jnp.stack([shard, flip(shard, "c", 1)])


def heads_along_x(pair):
    return jnp.stack([pair, flip(pair, "q", 1)])


def heads_along_y(near, size, heads, where, zh):
    return heads_pieces(near, flip(near, "q", 2), size, heads, where, zh)


def heads_pieces(near, far, size, heads, where, zh):
    rows = jnp.concatenate([near[:, :, ROWS, :size], far[:, :, ROWS, :size]])
    return [near, far], heads_bias(order_by(order_by(rows, 0, where[0], 4), 1, zh, 2).reshape(8, size), heads)


def all_heads_weight(shard, size, heads, zh):
    pair = turn(with_sibling(shard))
    every = order_by(lax.all_gather(pair, "q"), 1, zh, 2)
    count = shard.shape[0] - EXTRA
    weights = every[:, :, :count].reshape(4, 2, ROWS, -1)
    return [weights[:2], weights[2:]], heads_bias(every[:, :, count, :size].reshape(-1, size), heads)


class HeadsGrad:
    def __init__(self, keep, send):
        self.keep, self.send = keep, send

    def along_x(self):
        self.got = flip(self.send, "q", 1)
        return self.got

    def along_y(self):
        self.got_x = self.got
        self.got = flip(add(self.keep[1], self.got[1]).astype(BF16), "q", 2)
        return self.got

    def halves(self, zh):
        if is_small():
            return tuple(add(self.keep[0, k], self.got_x[0, k], self.got[k]).astype(BF16) for k in range(2))
        buckets = [self.keep[0], self.send[0], self.keep[1], self.send[1]]
        every = jnp.stack(buckets).reshape(lax.axis_size("q"), 2, -1, buckets[0].shape[-1])
        rows = order_by(lax.psum_scatter(every, "q", scatter_dimension=0, tiled=False), 0, zh, 2)
        return rows[0], rows[1]


SLOTS = (0, 2, 1, 3)


def all_units_weight(shard):
    matrices, _, width = shard.shape
    members = lax.axis_size(MODEL)
    every = lax.all_gather(shard, ALL).reshape(members, -1, matrices, shard.shape[1], width).transpose(0, 2, 1, 3, 4)
    every = every.reshape(members, matrices, 4, 2, ROWS, width)
    every = jnp.stack([every[slot] for slot in SLOTS])
    pieces = []
    for k in range(2):
        pieces += [every[:, :, r, k] for r in range(3)] + [every[:2, :, 3, k], every[2:, :, 3, k]]
    return pieces


class UnitsWeight:
    def __init__(self, shard):
        self.shard, self.theirs = shard, {}

    def start_far_z(self):
        self.other = flip(self.shard, "zh", 1)

    def join_far_z(self, shard):
        self.two = jnp.stack([shard, self.other])

    def far_z(self):
        self.start_far_z()
        self.join_far_z(self.shard)

    def start_z(self):
        self.other = flip(self.two, "zl", 1)

    def join_z(self, two):
        self.own = jnp.concatenate([two, self.other])

    def near_z(self):
        self.start_z()
        self.join_z(self.two)

    def near(self):
        self.near_x, self.near_y = flip(self.own, "q", 1), flip(self.own, "q", 2)

    def corner(self):
        self.far_a, self.far_b = flip(self.near_y[:2], "q", 1), flip(self.near_x[2:], "q", 2)

    def swap(self, *names):
        for name in names:
            self.theirs[name] = flip(getattr(self, name), "c", 1)

    def pieces(self):
        names = ("own", "near_x", "near_y", "far_a", "far_b")
        return [getattr(self, name) for name in names] + [self.theirs[name] for name in names]


class UnitsGrads:
    def __init__(self, flow, down, up, count):
        self.flow, self.down, self.up, self.count = flow, down, up, count

    def compute_theirs(self):
        self.theirs = unit_grads(self.flow, self.down, self.up, None, self.count, True)

    def send_theirs(self):
        self.got = flip(self.theirs, "c", 1) if is_small() else None

    def sibling(self):
        self.compute_theirs()
        self.send_theirs()

    def mine(self):
        self.made = unit_grads(self.flow, self.down, self.up, self.got, self.count, False)
        self.own, self.to_x, self.to_y, self.rest_x, self.rest_y = self.made

    def near(self):
        self.from_x, self.from_y = flip(self.to_x, "q", 1), flip(self.to_y, "q", 2)
        return [self.from_x, self.from_y]

    def far(self):
        half = self.count
        self.late_x = flip(add(self.rest_x, self.from_y[half:]).astype(BF16), "q", 1)
        self.late_y = flip(add(self.rest_y, self.from_x[half:]).astype(BF16), "q", 2)
        return [self.late_x, self.late_y]

    def near_z(self):
        half = self.count
        self.passing = add(self.own[half:], self.late_x, self.from_y[:half]).astype(BF16)
        self.there = flip(self.passing, "zl", 1)
        return [self.there]

    def far_z(self):
        self.last = flip(self.near_sum(slice(self.count // 2, self.count)).astype(BF16), "zh", 1)
        return [self.last]

    def near_sum(self, blocks):
        return add(self.own[blocks], self.from_x[blocks], self.late_y[blocks], self.there[blocks])

    def parts(self):
        return self.own, self.from_x, self.late_y, self.there, self.last

    def total(self):
        half = self.count
        mine = jnp.stack(
            [self.own, jnp.concatenate([self.to_x[:half], self.rest_x]), jnp.concatenate([self.rest_y, self.to_y[:half]]),
             jnp.concatenate([self.to_x[half:], self.to_y[half:]])]
        ).reshape(4, self.count, 2, ROWS, -1)
        theirs = self.theirs.reshape(4, 2, self.count, ROWS, -1).transpose(0, 2, 1, 3, 4)
        every = jnp.stack([mine, theirs], axis=1)
        every = every.transpose(2, 0, 1, 4, 3, 5)
        every = jnp.stack([every[slot] for slot in SLOTS]).reshape(-1, 2, mine.shape[-1])
        return lax.psum_scatter(every, ALL, scatter_dimension=0, tiled=True).astype(F32).transpose(1, 0, 2)


SMALL_AXES = ("q", MODEL, "c")
SMALL_STEPS = (("q", 1), ("q", 2), ("zl", 1), ("zh", 1), ("c", 1))
SMALL_SHAPE = (128, 256)


def spread_by_distance(values_in, where):
    every = values_in.reshape(4, 4, 2, -1).transpose(1, 0, 2, 3)
    for axis, position in enumerate(where):
        every = order_by(every, axis, position, every.shape[axis])
    return every.transpose(2, 1, 0, 3).reshape(32, -1)


def fold_small(every, first, last):
    for axis, mask in SMALL_STEPS[::-1][first:last]:
        half = every.shape[0] // 2
        every = every[:half] + flip(every[half:], axis, mask)
    return every


def sum_all(value):
    if not is_small():
        return lax.psum(value, ALL)
    for axes in SMALL_AXES:
        parts = jnp.stack(from_members(value, axes))
        value = jnp.sum(order_by(parts, 0, lax.axis_index(axes), parts.shape[0]), 0)
    return value[0, 0]


def on_device(
    tokens, doc_lengths, qkv_weight, qv_bias, out_weight, up_weight, up_bias, down_weight, gains, shifts, cotangent
):
    layers = qkv_weight.shape[0]
    tz, dp = lax.axis_size(MODEL), lax.axis_size(("q", "c"))
    place, zh = lax.axis_index(GROUP), lax.axis_index("zh")
    where = (lax.axis_index("q"), lax.axis_index(MODEL), lax.axis_index("c"))
    if is_small():
        spots = [place, where[0], where[2], zh, where[1]]
    else:
        spots = [place] + [jnp.zeros((), jnp.int32)] * 4
    scal = jnp.stack([spot.astype(jnp.int32) for spot in spots])

    flow = Flow(scal)
    small_slice = is_small()
    qkv_cols, out_cols = 3 * out_weight.shape[2], out_weight.shape[2]
    in_cols, out_cols = slice(0, qkv_cols), slice(qkv_cols, qkv_cols + out_cols)
    hz, bias_size = qv_bias.shape[2], qv_bias.size // layers
    heads_shard = [heads_shard_of(qkv_weight[l], out_weight[l], qv_bias[l]) for l in range(layers)]
    pieces = [up_bias, gains, shifts]
    sizes = [piece.size // layers for piece in pieces]
    cuts = [0]
    for size in sizes:
        cuts.append(cuts[-1] + size)
    small = jnp.concatenate([piece.reshape(layers, -1) for piece in pieces], axis=1).reshape(-1)
    padded = jnp.pad(small, (0, SMALL_SHAPE[0] * SMALL_SHAPE[1] - small.size)).reshape(SMALL_SHAPE)
    gathered = lax.all_gather(padded, ALL)
    small_all = gathered.reshape(tz * dp, -1)[:, : small.size]

    def spread_small():
        every = small_all.reshape(tz, dp, layers, -1).astype(F32)
        parts = [every[..., cuts[i] : cuts[i + 1]] for i in range(3)]
        biases = parts[0].reshape(tz, dp, layers, up_bias.shape[1], -1).transpose(2, 0, 3, 1, 4)
        gain = parts[1].reshape(tz, dp, layers, 2, -1).transpose(2, 3, 1, 0, 4).reshape(layers, 2, D)
        shift = parts[2].reshape(tz, dp, layers, 4, -1).transpose(2, 3, 1, 0, 4).reshape(layers, 4, D)
        table = jnp.concatenate([gain, shift], axis=1).reshape(layers * 6, D)
        head = jnp.concatenate([jnp.ones((1, D), F32), jnp.zeros((1, D), F32)])
        return biases.reshape(layers, tz, 1, -1), jnp.pad(jnp.concatenate([head, table]), ((0, TABLE - 2 - 6 * layers), (0, 0)))

    up_bias_full, table = spread_small()
    if small_slice:
        pair = with_sibling(heads_shard[0])
        bundle = turn(jnp.concatenate([tokens, pair.reshape(-1, D)]))
        x_low, pair = bundle[: tokens.shape[0]], bundle[tokens.shape[0] :].reshape(pair.shape)
        ends = jnp.cumsum(turn(doc_lengths)[0], dtype=jnp.int32)
        members = from_members(pair, "q")
        weights_of = [heads_pieces(jnp.stack(members[:2]), jnp.stack(members[2:]), bias_size, hz, where, zh)]
        up0, down0 = UnitsWeight(up_weight[0][None]), UnitsWeight(down_weight[0][None])
        both1 = UnitsWeight(jnp.stack([up_weight[1], down_weight[1]]))
        flow.hold(
            up0=up0.shard, up0_twin=up0.shard, up0_last=up0.shard, down0=down0.shard, down0_twin=down0.shard, both1=both1.shard,
            heads1=heads_shard[1], low=x_low,
        )
        gate(flow)
        x_low = flow.free("low")
    else:
        x_low = turn(tokens)
        ends = jnp.cumsum(turn(doc_lengths)[0], dtype=jnp.int32)
        weights_of = [all_heads_weight(shard, bias_size, hz, zh) for shard in heads_shard]
        every = [all_units_weight(jnp.stack([up_weight[l], down_weight[l]])) for l in range(layers)]
        top_grad = turn(cotangent)

    prev, prev_gain, prev_shift = x_low, ONE, ZERO
    kept = []
    for l in range(layers):
        first, last = small_slice and l == 0, small_slice and l == 1
        xs = gather_group(x_low)
        w_heads, bias = weights_of[l]
        if last:
            flow.hold(top=cotangent[:ROWS])
        qkv_near = project_in(flow, (xs[0], xs[2]), False, w_heads, in_cols, bias, "project_qkv")
        if first:
            up0.shard = flow.free("up0")
            up0.start_far_z()
            flow.wait(up0.other)
        if last:
            flow.hold(top=jnp.concatenate([flow.free("top"), cotangent[ROWS:]]), own=both1.own)
        forward(flow, xs, qkv_near)
        if first:
            twin, down0.shard = flow.free("up0_twin"), flow.free("down0")
            up0.join_far_z(twin)
            across = up0.other
            up0.start_z()
            down0.start_far_z()
        if last:
            both1.own = flow.free("own")
            both1.near()
        qkv_far = project_in(flow, (xs[1], xs[3]), True, w_heads, in_cols, bias, "project_qkv")
        qkv = (qkv_near, qkv_far)
        if first:
            down0.join_far_z(flow.free("down0_twin"))
            up0.join_z(jnp.stack([flow.free("up0_last"), across]))
            up0.near()
            down0.near_z()
            both1.shard = flow.free("both1")
            both1.far_z()
        if last:
            top_grad = turn(flow.free("top"))
            both1.swap("own")
        ctx, wide, lse = attend_forward(flow, ends, qkv)
        if first:
            flow.wait(up0.near_x, up0.near_y)
            flow.hold(both1=both1.two, down0=down0.own)
            up0.swap("own", "near_x", "near_y")
        if last:
            flow.wait(both1.near_x, both1.near_y, top_grad)
        send = project_out(flow, [ctx], (2, 3), w_heads, out_cols, True, "project_attn")
        flow.wait(send)
        if first:
            pair = with_sibling(flow.free("heads1"))
        if last:
            flow.hold(near_x=both1.near_x, near_y=both1.near_y)
        keep = project_out(flow, [ctx], (0, 1), w_heads, out_cols, False, "project_attn")
        if last:
            both1.near_x, both1.near_y = flow.free("near_x"), flow.free("near_y")
            both1.corner()
            both1.swap("near_x", "near_y")
        attn, passed = sum_group(keep, send)
        if first:
            flow.wait(passed, gathered, pair, *up0.theirs.values())
            flow.hold(near_x=up0.near_x, near_y=up0.near_y)
            gate(flow)
            down0.own, up0.near_x, up0.near_y = flow.free("down0"), flow.free("near_x"), flow.free("near_y")
            up0.corner()
            up0.swap("far_a", "far_b")
            down0.near()
            down0.swap("own")
            flow.wait(down0.near_x, down0.near_y)
            down0.corner()
            down0.swap("near_x", "near_y")
            flow.hold(pair=pair)
            w_up = up0.pieces(), 0
        elif last:
            flow.wait(passed)
            flow.hold(ends=ends)
            gate(flow)
            ends = flow.free("ends")
            flow.hold(far_a=both1.far_a, far_b=both1.far_b)
            flow.wait(attn[2])
            gate(flow)
            both1.far_a, both1.far_b = flow.free("far_a"), flow.free("far_b")
            both1.swap("far_a", "far_b")
            w_up, w_down = (both1.pieces(), 0), (both1.pieces(), 1)
        else:
            w_up, w_down = (every[l], 0), (every[l], 1)
        used = (prev_gain, prev_shift, shift_row(l, 0), gain_row(l, 0), shift_row(l, 1))
        n1, hs, r1, act, slope = norm_up(flow, prev, attn, table, used, *w_up, up_bias_full[l], tz)
        if first:
            pair = turn(flow.free("pair"))
            flow.wait(n1, *down0.theirs.values())
            flow.hold(far_a=down0.far_a, far_b=down0.far_b)
            gate(flow)
            down0.far_a, down0.far_b = flow.free("far_a"), flow.free("far_b")
            down0.swap("far_a", "far_b")
            both1.two = flow.free("both1")
            both1.near_z()
            flow.hold(pair=pair, pair_twin=pair)
            gate(flow)
            across = flip(flow.free("pair"), "q", 1)
            w_down = down0.pieces(), 0
        used = (gain_row(l, 0), shift_row(l, 1), shift_row(l, 2), gain_row(l, 1), shift_row(l, 3))
        n2, y_low, r2 = down_norm(flow, act, *w_down, n1, table, used, tz)
        if first:
            near = jnp.stack([flow.free("pair_twin"), across])
            weights_of.append(heads_along_y(near, bias_size, hz, where, zh))
        kept.append((xs, qkv, ctx, wide, lse, n1, hs, r1, act, slope, n2, r2, w_heads, w_up, w_down))
        x_low, prev, prev_gain, prev_shift = y_low, n2, gain_row(l, 1), shift_row(l, 3)
    layer_output = turn(x_low)

    residual, back = top_grad, []
    small_grads = [None] * layers
    units_of, heads_of = [None] * layers, [None] * layers
    above = above_heads = None
    for l in reversed(range(layers)):
        top = l == layers - 1
        xs, qkv, ctx, wide, lse, n1, hs, r1, act, slope, n2, r2, w_heads, w_up, w_down = kept[l]
        beside = small_slice and not top
        g2, gf, sums2, gu, up_bias_sum = units_back(
            flow, residual, back, n2, r2, table, gain_row(l, 1), *w_down, slope, tz
        )
        units = UnitsGrads(flow, (gf, act), (hs, gu), tz)
        if top:
            flow.hold(output=layer_output)
        else:
            if beside:
                flow.wait(*above.near())
                flow.hold(heads=above_heads.send)
            units.sibling()
            flow.wait(units.theirs)
            if beside:
                above_heads.send = flow.free("heads")
                above_heads.along_x()
                late = above.far()
        g1, ga, sums1 = up_back(flow, gu, *w_up, g2, n1, r1, table, gain_row(l, 0), tz)
        gas = gather_group(ga)
        flow.wait(ga)
        if top:
            layer_output = flow.free("output")
            units.compute_theirs()
            forward(flow, gas, units.theirs)
        else:
            units.mine()
            if beside:
                flow.wait(*late, above_heads.got)
            forward(flow, gas, *units.made)
        gc_near = project_in(flow, (gas[0], gas[2]), False, w_heads, out_cols, None, "project_gc")
        flow.wait(gc_near)
        if top:
            flow.hold(theirs=units.theirs)
        gc_far = project_in(flow, (gas[1], gas[3]), True, w_heads, out_cols, None, "project_gc")
        if top:
            units.theirs = flow.free("theirs")
            units.send_theirs()
        gcs = (gc_near, gc_far)
        if beside:
            early = above.near_z()
            flow.hold(rest_x=units.rest_x, rest_y=units.rest_y, keep=above_heads.keep, above=above.own)
        gqkv = [attend_backward(flow, ends, 0, qkv, gcs, wide, lse)]
        if beside:
            units.rest_x, units.rest_y = flow.free("rest_x"), flow.free("rest_y")
            above_heads.keep, above.own = flow.free("keep"), flow.free("above")
        flow.wait(gqkv[0])
        if beside:
            flow.wait(*units.near(), *early)
            above.far_z()
            units.far()
            above_heads.along_y()
            flow.hold(own=units.own, keep=above_heads.keep)
        gqkv.append(attend_backward(flow, ends, 1, qkv, gcs, wide, lse))
        if beside:
            units.own, above_heads.keep = flow.free("own"), flow.free("keep")
            units.near_z()
            flow.wait(units.passing, units.late_y, above.last, above_heads.got)
            above_halves = above_heads.halves(zh)
            done = turn(above_halves[0]), uncross(above_halves[1])
        send = project_out(flow, gqkv, (2, 3), w_heads, in_cols, True, "project_gx")
        flow.wait(send)
        if beside:
            flow.hold(own=units.own)
        keep = project_out(flow, gqkv, (0, 1), w_heads, in_cols, False, "project_gx")
        back, passed = sum_group(keep, send)
        flow.wait(passed)
        if top:
            units.mine()
            flow.wait(*units.made)
        elif small_slice:
            units.own = flow.free("own")
            units.far_z()
            flow.wait(*done)
        *buckets, qkv_sums = heads_grad(flow, xs, gqkv, gas, ctx)
        heads = HeadsGrad(*buckets)
        units_of[l], heads_of[l] = units, heads
        qv_sums = qkv_sums.reshape(-1, 3, PAIR).transpose(1, 0, 2).reshape(3, hz, dp, -1)
        qv_sums = jnp.stack([qv_sums[0], qv_sums[2]]).transpose(2, 0, 1, 3).reshape(1, dp, -1)
        mine = (jnp.arange(tz) == place).astype(F32).reshape(tz, 1, 1)
        small_grads[l] = jnp.concatenate(
            [
                mine * qv_sums,
                up_bias_sum.reshape(tz, up_bias.shape[1], dp, -1).transpose(0, 2, 1, 3).reshape(tz, dp, -1),
                jnp.stack([sums1[0], sums2[0]]).reshape(2, dp, tz, -1).transpose(2, 1, 0, 3).reshape(tz, dp, -1),
                jnp.stack([sums1[2], sums1[1], sums2[2], sums2[1]])
                .reshape(4, dp, tz, -1).transpose(2, 1, 0, 3).reshape(tz, dp, -1),
            ],
            axis=-1,
        )
        if l > 0:
            above, above_heads = units, heads
            flow.wait(heads.send)
            residual = g1
    small_sums = jnp.stack(small_grads, axis=2).reshape(tz, dp, -1)
    if small_slice:
        heads.along_x()
        small_sums = fold_small(spread_by_distance(small_sums, where), 0, 1)
        flow.wait(back[2])
        flow.hold(small=small_sums, got=heads.got)
        gate(flow)
        small_sums, heads.got = flow.free("small"), flow.free("got")
        input_grad = turn(add(g1, back[0], back[1][0], back[2]).astype(BF16))
        heads.along_y()
        small_sums = fold_small(small_sums, 1, 2)
        flow.wait(heads.got, units.last)
        flow.hold(small=small_sums)
        gate(flow)
        small_sums = fold_small(flow.free("small"), 2, 3)
        halves = heads.halves(zh)
        small_out = fold_small(small_sums, 3, 5).reshape(layers, -1)
        arrived = [(turn(halves[0]), uncross(halves[1])), done]
        flow.hold(grad=input_grad, output=layer_output)
        qkv_grad, out_grad, up_grad, down_grad, squares = finish(
            flow, [member.parts() for member in units_of], arrived, small_out
        )
        input_grad, layer_output = flow.free("grad"), flow.free("output")
    else:
        halves = [member.halves(zh) for member in heads_of]
        d_heads = jnp.stack([add(turn(half[0]), uncross(half[1])) for half in halves])
        input_grad = turn(add(g1, back[0], back[1][0], back[2]).astype(BF16))
        small_out = lax.psum_scatter(small_sums.reshape(tz * dp, -1), ALL, scatter_dimension=0, tiled=True)
        small_out = small_out.reshape(layers, -1)
        qkv_grad = d_heads[:, :, : in_cols.stop].reshape(layers, d_heads.shape[1], -1, 3, PAIR)
        qkv_grad = qkv_grad.transpose(0, 3, 1, 2, 4).reshape(qkv_weight.shape)
        out_grad = d_heads[:, :, in_cols.stop :]
        totals = [member.total() for member in units_of]
        down_grad, up_grad = (jnp.stack([total[i] for total in totals]) for i in range(2))
        squares = sum(jnp.sum(member * member) for member in (qkv_grad, out_grad, up_grad, down_grad, small_out))

    rest = small_out[:, bias_size:]
    qv_bias_grad = small_out[:, :bias_size].reshape(qv_bias.shape)
    up_bias_grad = rest[:, cuts[0] : cuts[1]].reshape(up_bias.shape)
    gains_grad = rest[:, cuts[1] : cuts[2]].reshape(gains.shape)
    shifts_grad = rest[:, cuts[2] : cuts[3]].reshape(shifts.shape)
    entry_count = LAYERS * (4 * D * D + 2 * D * FF + FF + 8 * D)
    grad_rms = jnp.sqrt(sum_all(squares) / entry_count)
    return (
        layer_output, input_grad, qkv_grad, qv_bias_grad, out_grad, up_grad, up_bias_grad, down_grad, gains_grad,
        shifts_grad, grad_rms,
    )


def solution(mesh):
    dp, tensor = mesh.shape["dp"], mesh.shape["tensor"]
    fine = Mesh(mesh.devices.reshape(dp // 2, 2, 2, tensor // 2), ("q", "c", "zh", "zl"))
    data, model = ("q", "c"), ("zh", "zl")
    both = data + model
    weight3, weight4 = P(None, data, model), P(None, None, data, model)
    in_specs = (
        P(both, None), P(data, None), weight4, P(None, None, model, data), weight3, weight3, P(None, model, data),
        weight3, P(None, None, both), P(None, None, both), P(both, None),
    )
    out_specs = (
        P(both, None), P(both, None), weight4, P(None, None, model, data), weight3, weight3, P(None, model, data),
        weight3, P(None, None, both), P(None, None, both), P(),
    )
    return jax.shard_map(on_device, mesh=fine, in_specs=in_specs, out_specs=out_specs, check_vma=False)
```
